32 devices in a mesh: gx: 8 (over z, x), gy: 4 (over y, core).
Axes of the slice: x: 2, y: 2, z: 4, core: 2. Of those that a mesh axis runs over, the one named last changes fastest.
Arguments:
- source: float32 [8, 32, 64, 128], P(None, 'gx', 'gy'), may hold values from -30 to 30
- reaction: float32 [32, 64, 128], P('gx', 'gy'), may hold values from 0.02 to 2
- shifts: float32 [8], replicated, may hold values from 0.05 to 2
- shift_index: int32 [8], replicated, may hold values from 0 to 7, each once
- velocity: float32 [3], replicated, may hold values from -2 to 2
Outputs:
- solution: float32 [8, 32, 64, 128], P(None, 'gx', 'gy')
- residual: float32 [8, 32, 64, 128], P(None, 'gx', 'gy')
- residual_rms: float32 [8], replicated
The draws below stay inside these ranges and needn't reach their ends.
Inputs may be any that keep to these rules, and one draw needn't show every extreme that they name: `shift_index`: each column takes a different shift.
All inputs are finite; a program needn't handle non-finite values.
Results may differ from the reference program's by a relative error of at most 0.00021.
Values sent between devices are 32-bit elements; how exact they have to be, the bound alone decides.
No kernel may reach another device: no remote copies, remote signals or barrier semaphores. Data moves between devices by JAX's collectives and lax.ppermute only.
A program may use at most 64 MiB of HBM per device.

```python
import math
import jax
import jax.numpy as jnp
from jax import lax

CH = 8
LEVELS = 3
COARSE_SWEEPS = 6
NX = 32
NY = 64
NZ = 128


def draw_source(key, part):
    key = jax.random.fold_in(key, 11)
    across_x = (jnp.arange(NX, dtype=jnp.float32) / NX).reshape(1, NX, 1, 1)
    scale_ramp = 0.5 * jnp.exp(2.302585 * across_x)
    rough_part = jnp.clip(jax.random.normal(key, (CH, NX, NY, NZ), jnp.float32), -6.0, 6.0)
    return rough_part * scale_ramp


def block_scale(key, extent, split, low, top_value):
    gain, own = 1.0, jax.random.fold_in(key, 6)
    for dim, blocks in split:
        draws = jnp.exp(jax.random.uniform(jax.random.fold_in(own, dim), (blocks,), jnp.float32, low / len(split), top_value / len(split)))
        gain = gain * jnp.repeat(draws, extent[dim] // blocks).reshape([-1 if axis == dim else 1 for axis in range(len(extent))])
    return gain


def setup_inputs(seed: int = 0) -> dict:
    key_list = jax.random.split(jax.random.key(seed), 6)
    return {
        "source": draw_source(jax.random.fold_in(key_list[5], 71), 0),
        "reaction": jnp.clip(jnp.exp(math.log(2.0) - 4.6051702 * jax.random.uniform(key_list[1], (NX, NY, NZ), jnp.float32) ** block_scale(key_list[1], (NX, NY, NZ), ((0, 8), (1, 4)), -0.2, 0.2)), 0.02, 2.0),
        "shifts": jnp.clip(jnp.exp(jax.random.uniform(key_list[2], (CH,), jnp.float32, math.log(0.05), math.log(2.0))), 0.05, 2.0),
        "shift_index": jax.random.permutation(key_list[3], CH).astype(jnp.int32),
        "velocity": jnp.clip(jax.random.uniform(key_list[4], (3,), jnp.float32, -2.0, 2.0), -2.0, 2.0),
    }


DAMPING = 0.8
EPSILON = 1e-06

def select_shifts(shifts, shift_index):
    columns = jnp.arange(shifts.shape[0], dtype=jnp.int32)
    picked = jnp.where(shift_index[:, None] == columns[None, :], shifts[None, :], 0.0)
    return lax.optimization_barrier(jnp.sum(picked, axis=1))

def coefficients(velocity, spacing):
    scale_a = 1.0 / (spacing * spacing)
    backward = scale_a + jnp.maximum(velocity, 0.0) / spacing
    forward = scale_a - jnp.minimum(velocity, 0.0) / spacing
    centre = 6.0 * scale_a + jnp.sum(jnp.abs(velocity)) / spacing
    return (backward, forward, centre)

def apply_stencil(padded, backward, forward, diagonal):
    middle = padded[:, 1:-1, 1:-1, :]
    along_z = jnp.pad(middle, ((0, 0), (0, 0), (0, 0), (1, 1)))
    others = backward[0] * padded[:, :-2, 1:-1, :] + forward[0] * padded[:, 2:, 1:-1, :]
    others = others + backward[1] * padded[:, 1:-1, :-2, :] + forward[1] * padded[:, 1:-1, 2:, :]
    others = others + backward[2] * along_z[:, :, :, :-2] + forward[2] * along_z[:, :, :, 2:]
    return diagonal * middle - others

def pad_rim(values):
    return jnp.pad(values, ((0, 0), (1, 1), (1, 1), (0, 0)))

def coarsen(values):
    count, size_x, size_y, size_z = values.shape
    blocks = values.reshape(count, size_x // 2, 2, size_y // 2, 2, size_z // 2, 2)
    return lax.optimization_barrier(jnp.sum(blocks, axis=(2, 4, 6))) * 0.125

def refine(values):
    return jnp.repeat(jnp.repeat(jnp.repeat(values, 2, 1), 2, 2), 2, 3)

def multigrid_cycle(level_index, rhs_field, reaction_l, shift_value, velocity):
    backward, forward, centre = coefficients(velocity, 2.0 ** level_index)
    diagonal = centre + reaction_l + shift_value[:, None, None, None]

    def operate(iterate):
        return apply_stencil(pad_rim(iterate), backward, forward, diagonal)

    def smooth_step(iterate):
        return iterate + DAMPING * (rhs_field - operate(iterate)) / diagonal
    iterate = DAMPING * rhs_field / diagonal
    if level_index == LEVELS - 1:
        for repeat in range(COARSE_SWEEPS - 1):
            iterate = smooth_step(iterate)
        return iterate
    iterate = smooth_step(iterate)
    defect = rhs_field - operate(iterate)
    correction = multigrid_cycle(level_index + 1, coarsen(defect), coarsen(reaction_l), shift_value, velocity)
    iterate = iterate + refine(correction)
    iterate = smooth_step(iterate)
    iterate = smooth_step(iterate)
    return iterate

def reference(source, reaction, shifts, shift_index, velocity):
    shift_value = select_shifts(shifts, shift_index)
    reaction_top = reaction[None]

    def single_column(column_item):
        rhs_field, shift_one = column_item
        shift_vector = shift_one[None]
        solved = multigrid_cycle(0, rhs_field, reaction_top, shift_vector, velocity)
        backward, forward, centre = coefficients(velocity, 1.0)
        diagonal = centre + reaction_top + shift_vector[:, None, None, None]
        defect = rhs_field - apply_stencil(pad_rim(solved), backward, forward, diagonal)
        return (solved[0], defect[0], jnp.sum(defect * defect))
    solution, residual, squares = lax.map(single_column, (source[:, None], shift_value))
    residual_rms = jnp.sqrt(squares / (NX * NY * NZ) + EPSILON)
    return (solution, residual, residual_rms)
```

```python
import functools

import jax
import jax.numpy as jnp
from jax import lax
from jax.experimental import pallas as pl
from jax.experimental.pallas import tpu as pltpu
from jax.sharding import PartitionSpec as P

LEVELS = 3
COARSE_SWEEPS = 6

DAMPING = 0.8
EPSILON = 1e-06
VMEM_LIMIT = 40 * 1024 * 1024
LANES = 128


def with_halo(x, sides, width):
    for axis, dim in sides:
        peers, length = (lax.axis_size(axis), x.shape[dim])
        up = [(i, (i + 1) % peers) for i in range(peers - 1)]
        down = [(j, i) for i, j in up]
        last = lax.slice_in_dim(x, length - width, length, axis=dim)
        leading = lax.slice_in_dim(x, 0, width, axis=dim)
        before = lax.ppermute(last, axis, up)
        after = lax.ppermute(leading, axis, down)
        x = jnp.concatenate([before, x, after], axis=dim)
    return x


def select_shifts(shifts, shift_index):
    columns = jnp.arange(shifts.shape[0], dtype=jnp.int32)
    picked = jnp.where(shift_index[:, None] == columns[None, :], shifts[None, :], 0.0)
    return jnp.sum(picked, axis=1)


def coefficients(velocity, spacing):
    scale_a = 1.0 / (spacing * spacing)
    backward = scale_a + jnp.maximum(velocity, 0.0) / spacing
    forward = scale_a - jnp.minimum(velocity, 0.0) / spacing
    centre = 6.0 * scale_a + jnp.sum(jnp.abs(velocity)) / spacing
    return (backward, forward, centre)


def apply_stencil(padded, backward, forward, diagonal):
    middle = padded[:, 1:-1, 1:-1, :]
    along_z = jnp.pad(middle, ((0, 0), (0, 0), (0, 0), (1, 1)))
    others = backward[0] * padded[:, :-2, 1:-1, :] + forward[0] * padded[:, 2:, 1:-1, :]
    others = others + backward[1] * padded[:, 1:-1, :-2, :] + forward[1] * padded[:, 1:-1, 2:, :]
    others = others + backward[2] * along_z[:, :, :, :-2] + forward[2] * along_z[:, :, :, 2:]
    return diagonal * middle - others


def face_halo(iterate):
    return with_halo(iterate, (("gx", 1), ("gy", 2)), 1)


def coarsen(values):
    count, size_x, size_y, size_z = values.shape
    blocks = values.reshape(count, size_x // 2, 2, size_y // 2, 2, size_z // 2, 2)
    return jnp.sum(blocks, axis=(2, 4, 6)) * 0.125


def refine(values):
    return jnp.repeat(jnp.repeat(jnp.repeat(values, 2, 1), 2, 2), 2, 3)


def coarsest_solve(rhs_field, backward, forward, diagonal):
    iterate = DAMPING * rhs_field / diagonal
    for repeat in range(COARSE_SWEEPS - 1):
        applied = apply_stencil(face_halo(iterate), backward, forward, diagonal)
        iterate = iterate + DAMPING * (rhs_field - applied) / diagonal
    return iterate


def multigrid_cycle(level_index, rhs_field, reaction_l, shift_value, velocity):
    backward, forward, centre = coefficients(velocity, 2.0**level_index)
    diagonal = centre + reaction_l + shift_value[:, None, None, None]
    if level_index == LEVELS - 1:
        return coarsest_solve(rhs_field, backward, forward, diagonal)

    def operate(iterate):
        return apply_stencil(face_halo(iterate), backward, forward, diagonal)

    def smooth_step(iterate):
        return iterate + DAMPING * (rhs_field - operate(iterate)) / diagonal

    iterate = DAMPING * rhs_field / diagonal
    iterate = smooth_step(iterate)
    defect = rhs_field - operate(iterate)
    correction = multigrid_cycle(
        level_index + 1, coarsen(defect), coarsen(reaction_l), shift_value, velocity
    )
    iterate = iterate + refine(correction)
    iterate = smooth_step(iterate)
    iterate = smooth_step(iterate)
    return iterate


def halo_body(source, reaction, shifts, shift_index, velocity):
    columns, cells_x, cells_y, cells_z = source.shape
    shift_value = select_shifts(shifts, shift_index)
    reaction_top = reaction[None]
    backward, forward, centre = coefficients(velocity, 1.0)
    diagonal = centre + reaction_top + shift_value[:, None, None, None]

    iterate = multigrid_cycle(0, source, reaction_top, shift_value, velocity)
    residual = source - apply_stencil(face_halo(iterate), backward, forward, diagonal)
    local_squares = jnp.sum(residual * residual, axis=(1, 2, 3))
    squares = lax.psum(local_squares, ("gx", "gy"))
    total_cells = cells_x * cells_y * cells_z * lax.axis_size("gx") * lax.axis_size("gy")
    residual_rms = jnp.sqrt(squares / total_cells + EPSILON)
    return (iterate, residual, residual_rms)


def split_dot(values, matrix):
    high = values.astype(jnp.bfloat16)
    low = (values - high.astype(jnp.float32)).astype(jnp.bfloat16)
    return jnp.dot(high, matrix, preferred_element_type=jnp.float32) + jnp.dot(
        low, matrix, preferred_element_type=jnp.float32
    )


class Level:
    def __init__(self, index, sizes, velocity_ref, shift, f, r, w):
        self.nx, self.ny, self.nz = (s >> index for s in sizes)
        self.f, self.r, self.w = f, r, w
        spacing = 2.0**index
        scale_a = 1.0 / (spacing * spacing)
        inverse = 1.0 / spacing
        speed = [velocity_ref[d] for d in range(3)]
        self.backward = [scale_a + jnp.maximum(v, 0.0) * inverse for v in speed]
        self.forward = [scale_a - jnp.minimum(v, 0.0) * inverse for v in speed]
        total = jnp.abs(speed[0]) + jnp.abs(speed[1]) + jnp.abs(speed[2])
        self.centre = 6.0 * scale_a + total * inverse + shift
        lane = lax.broadcasted_iota(jnp.int32, (1, LANES), 1)
        inside = lane < self.nz
        self.low_z = jnp.where((lane > 0) & inside, self.backward[2], 0.0)
        self.high_z = jnp.where(lane < self.nz - 1, self.forward[2], 0.0)

    def plane(self, v, x):
        return v[x + 1, pl.ds(8, self.ny), :]

    def neighbours(self, v, x, middle):
        ny = self.ny
        out = self.backward[0] * v[x, pl.ds(8, ny), :]
        out += self.forward[0] * v[x + 2, pl.ds(8, ny), :]
        out += self.backward[1] * v[x + 1, pl.ds(7, ny), :]
        out += self.forward[1] * v[x + 1, pl.ds(9, ny), :]
        out += self.low_z * pltpu.roll(middle, 1, 1)
        out += self.high_z * pltpu.roll(middle, LANES - 1, 1)
        return out

    def smooth(self, src, dst):
        def step(x, carry):
            middle = self.plane(src, x)
            pulled = self.f[x] + self.neighbours(src, x, middle)
            dst[x + 1, pl.ds(8, self.ny), :] = (1.0 - DAMPING) * middle + self.w[x] * pulled
            return carry

        lax.fori_loop(0, self.nx, step, 0)

    def defect(self, v, x):
        middle = self.plane(v, x)
        pulled = self.f[x] + self.neighbours(v, x, middle)
        return pulled - (self.r[x] + self.centre) * middle

    def start(self, v):
        def step(x, carry):
            weight = DAMPING / (self.r[x] + self.centre)
            self.w[x] = weight
            v[x + 1, pl.ds(8, self.ny), :] = weight * self.f[x]
            return carry

        lax.fori_loop(0, self.nx, step, 0)

    def pair_rows(self, tmp, values, slot):
        rows = tmp.at[slot]
        rows[pl.ds(0, self.ny), :] = values
        half = self.ny // 2
        return rows[pl.ds(0, half, stride=2), :] + rows[pl.ds(1, half, stride=2), :]

    def coarsen_defect(self, v, tmp, pooled):
        half = self.ny // 2

        def step(x, carry):
            both = self.defect(v, 2 * x) + self.defect(v, 2 * x + 1)
            pooled[pl.ds(pl.multiple_of(x * half, 8), half), :] = self.pair_rows(tmp, both, 0)
            return carry

        lax.fori_loop(0, self.nx // 2, step, 0)

    def coarsen_reaction(self, tmp, pooled):
        half = self.ny // 2

        def step(x, carry):
            both = self.r[2 * x] + self.r[2 * x + 1]
            pooled[pl.ds(pl.multiple_of(x * half, 8), half), :] = self.pair_rows(tmp, both, 1)
            return carry

        lax.fori_loop(0, self.nx // 2, step, 0)

    def add_refined(self, v, spread, tmp):
        half = self.ny // 2

        def step(x, carry):
            part = spread[pl.ds(pl.multiple_of(x * half, 8), half), :]
            rows = tmp.at[0]
            rows[pl.ds(0, half, stride=2), :] = part
            rows[pl.ds(1, half, stride=2), :] = part
            full = rows[pl.ds(0, self.ny), :]
            for k in range(2):
                v[2 * x + 1 + k, pl.ds(8, self.ny), :] += full
            return carry

        lax.fori_loop(0, self.nx // 2, step, 0)


def zero_rim(v, nx, ny):
    rows = v.shape[1]
    blank = jnp.zeros((rows, LANES), jnp.float32)
    v[0] = blank
    v[nx + 1] = blank
    edge = jnp.zeros((nx + 2, 8, LANES), jnp.float32)
    v[:, pl.ds(0, 8), :] = edge
    v[:, pl.ds(8 + ny, 8), :] = edge


def cycle_kernel(
    sizes, blocks, place_ref, shifts_ref, index_ref, velocity_ref, pool_ref, spread_ref, *refs
):
    gx_size, gy_size = blocks
    nx, ny, nz = sizes
    bx, by = nx // gx_size, ny // gy_size
    pieces = refs[:gy_size]
    out_ref = refs[gy_size]
    f0, r0, w0, va, vb, f1, r1, w1, v1a, v1b, f2, r2, w2, v2a, v2b, pooled, tmp = refs[gy_size + 1 :]
    column, row_block = place_ref[0], place_ref[1]
    shift = shifts_ref[index_ref[column]]
    pool, spread = pool_ref[...], spread_ref[...]

    fine = Level(0, sizes, velocity_ref, shift, f0, r0, w0)
    mid = Level(1, sizes, velocity_ref, shift, f1, r1, w1)
    deep = Level(2, sizes, velocity_ref, shift, f2, r2, w2)
    for v, level in ((va, fine), (vb, fine), (v1a, mid), (v1b, mid), (v2a, deep), (v2b, deep)):
        zero_rim(v, level.nx, level.ny)

    for j, piece in enumerate(pieces):
        for i in range(gx_size):
            f0[pl.ds(i * bx, bx), pl.ds(j * by, by), :] = piece[i, 0]
            r0[pl.ds(i * bx, bx), pl.ds(j * by, by), :] = piece[i, 1]

    rows1, rows2 = mid.nx * mid.ny, deep.nx * deep.ny
    fine.start(va)
    fine.smooth(va, vb)
    fine.coarsen_defect(vb, tmp, pooled)
    f1[...] = split_dot(pooled[pl.ds(0, rows1), :], pool).reshape(f1.shape)
    fine.coarsen_reaction(tmp, pooled)
    r1[...] = split_dot(pooled[pl.ds(0, rows1), :], pool).reshape(r1.shape)

    mid.start(v1a)
    mid.smooth(v1a, v1b)
    mid.coarsen_defect(v1b, tmp, pooled)
    f2[...] = split_dot(pooled[pl.ds(0, rows2), :], pool).reshape(f2.shape)
    mid.coarsen_reaction(tmp, pooled)
    r2[...] = split_dot(pooled[pl.ds(0, rows2), :], pool).reshape(r2.shape)

    deep.start(v2a)
    src, dst = v2a, v2b
    for _ in range(COARSE_SWEEPS - 1):
        deep.smooth(src, dst)
        src, dst = dst, src

    values = src[pl.ds(1, deep.nx), pl.ds(8, deep.ny), :].reshape(rows2, LANES)
    pooled[pl.ds(0, rows2), :] = split_dot(values, spread)
    mid.add_refined(v1b, pooled, tmp)
    mid.smooth(v1b, v1a)
    mid.smooth(v1a, v1b)
    values = v1b[pl.ds(1, mid.nx), pl.ds(8, mid.ny), :].reshape(rows1, LANES)
    pooled[pl.ds(0, rows1), :] = split_dot(values, spread)
    fine.add_refined(vb, pooled, tmp)
    fine.smooth(vb, va)
    fine.smooth(va, vb)

    area = bx * by
    row0 = pl.multiple_of(row_block * by, 8)

    def finish(i, total):
        for k in range(bx):
            x = i * bx + k
            rest = fine.defect(vb, x)
            total = total + jnp.sum((rest * rest).reshape(ny // 8, 8, LANES), axis=0)
            tmp[0, pl.ds(0, ny), :] = rest
            out_ref[i, pl.ds(k * by, by), :] = vb[x + 1, pl.ds(8 + row0, by), :]
            out_ref[i, pl.ds(area + k * by, by), :] = tmp[0, pl.ds(row0, by), :]
        return total

    squares = lax.fori_loop(0, gx_size, finish, jnp.zeros((8, LANES), jnp.float32))
    mean = jnp.sum(squares) / (nx * ny * nz) + EPSILON
    rms = jnp.sqrt(jnp.full((8, LANES), mean, jnp.float32))
    for i in range(gx_size):
        out_ref[i, pl.ds(2 * area, 8), :] = rms


def pooling_matrices():
    row = lax.broadcasted_iota(jnp.int32, (LANES, LANES), 0)
    col = lax.broadcasted_iota(jnp.int32, (LANES, LANES), 1)
    pool = jnp.where(row // 2 == col, 0.125, 0.0).astype(jnp.bfloat16)
    spread = jnp.where(col // 2 == row, 1.0, 0.0).astype(jnp.bfloat16)
    return pool, spread


def column_cycle(pieces, place, shifts, shift_index, velocity, sizes, blocks):
    gx_size, gy_size = blocks
    nx, ny, nz = sizes
    area = (nx // gx_size) * (ny // gy_size)
    f32 = jnp.float32

    def grid(index):
        return pltpu.VMEM((nx >> index, ny >> index, LANES), f32)

    def rimmed(index):
        return pltpu.VMEM(((nx >> index) + 2, (ny >> index) + 16, LANES), f32)

    scratch = []
    for index in range(LEVELS):
        scratch += [grid(index)] * 3 + [rimmed(index)] * 2
    scratch += [pltpu.VMEM(((nx // 2) * (ny // 2), LANES), f32), pltpu.VMEM((2, ny, LANES), f32)]
    smem = pl.BlockSpec(memory_space=pltpu.SMEM)
    vmem = pl.BlockSpec(memory_space=pltpu.VMEM)
    pool, spread = pooling_matrices()
    return pl.pallas_call(
        functools.partial(cycle_kernel, sizes, blocks),
        out_shape=jax.ShapeDtypeStruct((gx_size, 2 * area + 8, LANES), f32),
        in_specs=[smem] * 4 + [vmem] * (2 + gy_size),
        out_specs=vmem,
        scratch_shapes=scratch,
        compiler_params=pltpu.CompilerParams(vmem_limit_bytes=VMEM_LIMIT),
        name="cycle",
    )(place, shifts, shift_index, velocity, pool, spread, *pieces)


def column_body(source, reaction, shifts, shift_index, velocity):
    columns, bx, by, nz = source.shape
    gx_size, gy_size = lax.axis_size("gx"), lax.axis_size("gy")
    sizes = (bx * gx_size, by * gy_size, nz)
    place = jnp.stack([lax.axis_index("gx"), lax.axis_index("gy")]).astype(jnp.int32)

    both = jnp.stack([source, jnp.broadcast_to(reaction[None], source.shape)], axis=1)
    mine = lax.all_to_all(both, "gx", 0, 0)
    gathered = lax.all_gather(mine, "gy")
    pieces = [gathered[j] for j in range(gy_size)]
    results = column_cycle(
        pieces, place, shifts, shift_index, velocity, sizes, (gx_size, gy_size)
    )
    back = lax.all_to_all(results, "gx", 0, 0)
    area = bx * by
    iterate = back[:, :area].reshape(source.shape)
    residual = back[:, area : 2 * area].reshape(source.shape)
    return iterate, residual, back[:, 2 * area, 0]


def solution(mesh):
    gx_size, gy_size = mesh.shape["gx"], mesh.shape["gy"]

    def body(source, reaction, shifts, shift_index, velocity):
        columns, bx, by, nz = source.shape
        cells = bx * gx_size * by * gy_size
        fits = nz == LANES and bx % 4 == 0 and by % 16 == 0 and cells * nz * 4 <= 2**20
        plan = column_body if columns == gx_size and fits else halo_body
        return plan(source, reaction, shifts, shift_index, velocity)

    return jax.shard_map(
        body,
        mesh=mesh,
        in_specs=(P(None, "gx", "gy", None), P("gx", "gy", None), P(), P(), P()),
        out_specs=(P(None, "gx", "gy", None), P(None, "gx", "gy", None), P()),
        check_vma=False,
    )
```

```python
import functools

import jax
import jax.numpy as jnp
from jax import lax
from jax.experimental import pallas as pl
from jax.experimental.pallas import tpu as pltpu
from jax.sharding import PartitionSpec as P

LEVELS = 3
COARSE_SWEEPS = 6

DAMPING = 0.8
EPSILON = 1e-06
VMEM_LIMIT = 40 * 1024 * 1024
LANES = 128
UNROLL = 4


def with_halo(x, sides, width):
    for axis, dim in sides:
        peers, length = (lax.axis_size(axis), x.shape[dim])
        up = [(i, (i + 1) % peers) for i in range(peers - 1)]
        down = [(j, i) for i, j in up]
        last = lax.slice_in_dim(x, length - width, length, axis=dim)
        leading = lax.slice_in_dim(x, 0, width, axis=dim)
        before = lax.ppermute(last, axis, up)
        after = lax.ppermute(leading, axis, down)
        x = jnp.concatenate([before, x, after], axis=dim)
    return x


def select_shifts(shifts, shift_index):
    columns = jnp.arange(shifts.shape[0], dtype=jnp.int32)
    picked = jnp.where(shift_index[:, None] == columns[None, :], shifts[None, :], 0.0)
    return jnp.sum(picked, axis=1)


def coefficients(velocity, spacing):
    scale_a = 1.0 / (spacing * spacing)
    backward = scale_a + jnp.maximum(velocity, 0.0) / spacing
    forward = scale_a - jnp.minimum(velocity, 0.0) / spacing
    centre = 6.0 * scale_a + jnp.sum(jnp.abs(velocity)) / spacing
    return (backward, forward, centre)


def apply_stencil(padded, backward, forward, diagonal):
    middle = padded[:, 1:-1, 1:-1, :]
    along_z = jnp.pad(middle, ((0, 0), (0, 0), (0, 0), (1, 1)))
    others = backward[0] * padded[:, :-2, 1:-1, :] + forward[0] * padded[:, 2:, 1:-1, :]
    others = others + backward[1] * padded[:, 1:-1, :-2, :] + forward[1] * padded[:, 1:-1, 2:, :]
    others = others + backward[2] * along_z[:, :, :, :-2] + forward[2] * along_z[:, :, :, 2:]
    return diagonal * middle - others


def face_halo(iterate):
    return with_halo(iterate, (("gx", 1), ("gy", 2)), 1)


def coarsen(values):
    count, size_x, size_y, size_z = values.shape
    blocks = values.reshape(count, size_x // 2, 2, size_y // 2, 2, size_z // 2, 2)
    return jnp.sum(blocks, axis=(2, 4, 6)) * 0.125


def refine(values):
    return jnp.repeat(jnp.repeat(jnp.repeat(values, 2, 1), 2, 2), 2, 3)


def coarsest_solve(rhs_field, backward, forward, diagonal):
    iterate = DAMPING * rhs_field / diagonal
    for repeat in range(COARSE_SWEEPS - 1):
        applied = apply_stencil(face_halo(iterate), backward, forward, diagonal)
        iterate = iterate + DAMPING * (rhs_field - applied) / diagonal
    return iterate


def multigrid_cycle(level_index, rhs_field, reaction_l, shift_value, velocity):
    backward, forward, centre = coefficients(velocity, 2.0**level_index)
    diagonal = centre + reaction_l + shift_value[:, None, None, None]
    if level_index == LEVELS - 1:
        return coarsest_solve(rhs_field, backward, forward, diagonal)

    def operate(iterate):
        return apply_stencil(face_halo(iterate), backward, forward, diagonal)

    def smooth_step(iterate):
        return iterate + DAMPING * (rhs_field - operate(iterate)) / diagonal

    iterate = DAMPING * rhs_field / diagonal
    iterate = smooth_step(iterate)
    defect = rhs_field - operate(iterate)
    correction = multigrid_cycle(
        level_index + 1, coarsen(defect), coarsen(reaction_l), shift_value, velocity
    )
    iterate = iterate + refine(correction)
    iterate = smooth_step(iterate)
    iterate = smooth_step(iterate)
    return iterate


def halo_body(source, reaction, shifts, shift_index, velocity):
    columns, cells_x, cells_y, cells_z = source.shape
    shift_value = select_shifts(shifts, shift_index)
    reaction_top = reaction[None]
    backward, forward, centre = coefficients(velocity, 1.0)
    diagonal = centre + reaction_top + shift_value[:, None, None, None]

    iterate = multigrid_cycle(0, source, reaction_top, shift_value, velocity)
    residual = source - apply_stencil(face_halo(iterate), backward, forward, diagonal)
    local_squares = jnp.sum(residual * residual, axis=(1, 2, 3))
    squares = lax.psum(local_squares, ("gx", "gy"))
    total_cells = cells_x * cells_y * cells_z * lax.axis_size("gx") * lax.axis_size("gy")
    residual_rms = jnp.sqrt(squares / total_cells + EPSILON)
    return (iterate, residual, residual_rms)


def split_dot(values, matrix):
    high = values.astype(jnp.bfloat16)
    low = (values - high.astype(jnp.float32)).astype(jnp.bfloat16)
    return jnp.dot(high, matrix, preferred_element_type=jnp.float32) + jnp.dot(
        low, matrix, preferred_element_type=jnp.float32
    )


def sweep(count, get, put):
    def step(group, carry):
        planes = [group * UNROLL + k for k in range(UNROLL)]
        values = [get(x) for x in planes]
        for x, value in zip(planes, values):
            put(x, value)
        return carry

    lax.fori_loop(0, count // UNROLL, step, 0)


class Level:
    def __init__(self, index, sizes, velocity_ref, shift, f, r, w):
        self.nx, self.ny, self.nz = (s >> index for s in sizes)
        self.f, self.r, self.w = f, r, w
        spacing = 2.0**index
        scale_a = 1.0 / (spacing * spacing)
        inverse = 1.0 / spacing
        speed = [velocity_ref[d] for d in range(3)]
        self.backward = [scale_a + jnp.maximum(v, 0.0) * inverse for v in speed]
        self.forward = [scale_a - jnp.minimum(v, 0.0) * inverse for v in speed]
        total = jnp.abs(speed[0]) + jnp.abs(speed[1]) + jnp.abs(speed[2])
        self.centre = 6.0 * scale_a + total * inverse + shift
        lane = lax.broadcasted_iota(jnp.int32, (1, LANES), 1)
        inside = lane < self.nz
        self.low_z = jnp.where((lane > 0) & inside, self.backward[2], 0.0)
        self.high_z = jnp.where(lane < self.nz - 1, self.forward[2], 0.0)

    def plane(self, v, x):
        return v[x + 1, pl.ds(8, self.ny), :]

    def neighbours(self, v, x, middle):
        ny = self.ny
        along_x = self.backward[0] * v[x, pl.ds(8, ny), :] + self.forward[0] * v[x + 2, pl.ds(8, ny), :]
        along_y = self.backward[1] * v[x + 1, pl.ds(7, ny), :] + self.forward[1] * v[x + 1, pl.ds(9, ny), :]
        along_z = self.low_z * pltpu.roll(middle, 1, 1) + self.high_z * pltpu.roll(middle, LANES - 1, 1)
        return along_x + along_y + along_z

    def smoothed(self, v, x):
        middle = self.plane(v, x)
        pulled = self.f[x] + self.neighbours(v, x, middle)
        return (1.0 - DAMPING) * middle + self.w[x] * pulled

    def smooth(self, src, dst):
        def put(x, value):
            dst[x + 1, pl.ds(8, self.ny), :] = value

        sweep(self.nx, lambda x: self.smoothed(src, x), put)

    def defect(self, v, x):
        middle = self.plane(v, x)
        pulled = self.f[x] + self.neighbours(v, x, middle)
        return pulled - (self.r[x] + self.centre) * middle

    def start(self, v):
        def put(x, weight):
            self.w[x] = weight
            v[x + 1, pl.ds(8, self.ny), :] = weight * self.f[x]

        sweep(self.nx, lambda x: DAMPING / (self.r[x] + self.centre), put)

    def pool_pairs(self, plane_of, tmp, pooled):
        half, ny = self.ny // 2, self.ny

        def put(x, value):
            rows = tmp.at[lax.rem(x, UNROLL)]
            rows[pl.ds(0, ny), :] = value
            both = rows[pl.ds(0, half, stride=2), :] + rows[pl.ds(1, half, stride=2), :]
            pooled[pl.ds(pl.multiple_of(x * half, 8), half), :] = both

        sweep(self.nx // 2, lambda x: plane_of(2 * x) + plane_of(2 * x + 1), put)

    def add_refined(self, v, spread, tmp):
        half, ny = self.ny // 2, self.ny

        def get(x):
            part = spread[pl.ds(pl.multiple_of(x * half, 8), half), :]
            rows = tmp.at[lax.rem(x, UNROLL)]
            rows[pl.ds(0, half, stride=2), :] = part
            rows[pl.ds(1, half, stride=2), :] = part
            return rows[pl.ds(0, ny), :]

        def put(x, value):
            for k in range(2):
                v[2 * x + 1 + k, pl.ds(8, ny), :] += value

        sweep(self.nx // 2, get, put)

    def solve_in_registers(self):
        row = lax.broadcasted_iota(jnp.int32, (self.ny, 1), 0)
        low_y = jnp.where(row > 0, self.backward[1], 0.0)
        high_y = jnp.where(row < self.ny - 1, self.forward[1], 0.0)
        weight = [DAMPING / (self.r[x] + self.centre) for x in range(self.nx)]
        rhs = [self.f[x] for x in range(self.nx)]
        v = [w * f for w, f in zip(weight, rhs)]
        for _ in range(COARSE_SWEEPS - 1):
            new = []
            for x, here in enumerate(v):
                along_z = self.low_z * pltpu.roll(here, 1, 1) + self.high_z * pltpu.roll(here, LANES - 1, 1)
                along_y = low_y * pltpu.roll(here, 1, 0) + high_y * pltpu.roll(here, self.ny - 1, 0)
                pulled = rhs[x] + along_z + along_y
                if x > 0:
                    pulled += self.backward[0] * v[x - 1]
                if x < self.nx - 1:
                    pulled += self.forward[0] * v[x + 1]
                new.append((1.0 - DAMPING) * here + weight[x] * pulled)
            v = new
        return jnp.concatenate(v, axis=0)


def zero_rim(v, nx, ny):
    rows = v.shape[1]
    blank = jnp.zeros((rows, LANES), jnp.float32)
    v[0] = blank
    v[nx + 1] = blank
    edge = jnp.zeros((nx + 2, 8, LANES), jnp.float32)
    v[:, pl.ds(0, 8), :] = edge
    v[:, pl.ds(8 + ny, 8), :] = edge


def cycle_kernel(
    sizes, blocks, place_ref, shifts_ref, index_ref, velocity_ref, pool_ref, spread_ref, *refs
):
    gx_size, gy_size = blocks
    nx, ny, nz = sizes
    bx, by = nx // gx_size, ny // gy_size
    pieces = refs[:gy_size]
    out_ref = refs[gy_size]
    f0, r0, w0, va, vb, f1, r1, w1, v1a, v1b, f2, r2, pooled, tmp = refs[gy_size + 1 :]
    column, row_block = place_ref[0], place_ref[1]
    shift = shifts_ref[index_ref[column]]
    pool, spread = pool_ref[...], spread_ref[...]

    fine = Level(0, sizes, velocity_ref, shift, f0, r0, w0)
    mid = Level(1, sizes, velocity_ref, shift, f1, r1, w1)
    deep = Level(2, sizes, velocity_ref, shift, f2, r2, None)
    for v, level in ((va, fine), (vb, fine), (v1a, mid), (v1b, mid)):
        zero_rim(v, level.nx, level.ny)

    for k, piece in enumerate(pieces):
        rows = pl.ds(pl.multiple_of(place_ref[1 + k] * by, 8), by)
        for i in range(gx_size):
            f0[pl.ds(i * bx, bx), rows, :] = piece[i, 0]
            r0[pl.ds(i * bx, bx), rows, :] = piece[i, 1]

    rows1, rows2 = mid.nx * mid.ny, deep.nx * deep.ny
    fine.start(va)
    fine.smooth(va, vb)
    fine.pool_pairs(lambda x: fine.defect(vb, x), tmp, pooled)
    f1[...] = split_dot(pooled[pl.ds(0, rows1), :], pool).reshape(f1.shape)
    fine.pool_pairs(lambda x: r0[x], tmp, pooled)
    r1[...] = split_dot(pooled[pl.ds(0, rows1), :], pool).reshape(r1.shape)

    mid.start(v1a)
    mid.smooth(v1a, v1b)
    mid.pool_pairs(lambda x: mid.defect(v1b, x), tmp, pooled)
    f2[...] = split_dot(pooled[pl.ds(0, rows2), :], pool).reshape(f2.shape)
    mid.pool_pairs(lambda x: r1[x], tmp, pooled)
    r2[...] = split_dot(pooled[pl.ds(0, rows2), :], pool).reshape(r2.shape)

    values = deep.solve_in_registers()

    pooled[pl.ds(0, rows2), :] = split_dot(values, spread)
    mid.add_refined(v1b, pooled, tmp)
    mid.smooth(v1b, v1a)
    mid.smooth(v1a, v1b)
    values = v1b[pl.ds(1, mid.nx), pl.ds(8, mid.ny), :].reshape(rows1, LANES)
    pooled[pl.ds(0, rows1), :] = split_dot(values, spread)
    fine.add_refined(vb, pooled, tmp)
    fine.smooth(vb, va)
    fine.smooth(va, vb)

    area = bx * by
    row0 = pl.multiple_of(row_block * by, 8)

    def finish(i, total):
        for k in range(bx):
            x = i * bx + k
            rest = fine.defect(vb, x)
            total = total + jnp.sum((rest * rest).reshape(ny // 8, 8, LANES), axis=0)
            tmp[k, pl.ds(0, ny), :] = rest
        for k in range(bx):
            x = i * bx + k
            out_ref[i, pl.ds(k * by, by), :] = vb[x + 1, pl.ds(8 + row0, by), :]
            out_ref[i, pl.ds(area + k * by, by), :] = tmp[k, pl.ds(row0, by), :]
        return total

    squares = lax.fori_loop(0, gx_size, finish, jnp.zeros((8, LANES), jnp.float32))
    mean = jnp.sum(squares) / (nx * ny * nz) + EPSILON
    rms = jnp.sqrt(jnp.full((8, LANES), mean, jnp.float32))
    for i in range(gx_size):
        out_ref[i, pl.ds(2 * area, 8), :] = rms


def pooling_matrices():
    row = lax.broadcasted_iota(jnp.int32, (LANES, LANES), 0)
    col = lax.broadcasted_iota(jnp.int32, (LANES, LANES), 1)
    pool = jnp.where(row // 2 == col, 0.125, 0.0).astype(jnp.bfloat16)
    spread = jnp.where(col // 2 == row, 1.0, 0.0).astype(jnp.bfloat16)
    return pool, spread


def column_cycle(pieces, place, shifts, shift_index, velocity, sizes, blocks):
    gx_size, gy_size = blocks
    nx, ny, nz = sizes
    area = (nx // gx_size) * (ny // gy_size)
    f32 = jnp.float32

    def grid(index):
        return pltpu.VMEM((nx >> index, ny >> index, LANES), f32)

    def rimmed(index):
        return pltpu.VMEM(((nx >> index) + 2, (ny >> index) + 16, LANES), f32)

    scratch = []
    for index in range(LEVELS - 1):
        scratch += [grid(index)] * 3 + [rimmed(index)] * 2
    scratch += [grid(LEVELS - 1)] * 2
    scratch += [pltpu.VMEM(((nx // 2) * (ny // 2), LANES), f32), pltpu.VMEM((UNROLL, ny, LANES), f32)]
    smem = pl.BlockSpec(memory_space=pltpu.SMEM)
    vmem = pl.BlockSpec(memory_space=pltpu.VMEM)
    pool, spread = pooling_matrices()
    return pl.pallas_call(
        functools.partial(cycle_kernel, sizes, blocks),
        out_shape=jax.ShapeDtypeStruct((gx_size, 2 * area + 8, LANES), f32),
        in_specs=[smem] * 4 + [vmem] * (2 + gy_size),
        out_specs=vmem,
        scratch_shapes=scratch,
        compiler_params=pltpu.CompilerParams(vmem_limit_bytes=VMEM_LIMIT),
        name="cycle",
    )(place, shifts, shift_index, velocity, pool, spread, *pieces)


def column_body(source, reaction, shifts, shift_index, velocity):
    columns, bx, by, nz = source.shape
    gx_size, gy_size = lax.axis_size("gx"), lax.axis_size("gy")
    sizes = (bx * gx_size, by * gy_size, nz)
    both = jnp.stack([source, jnp.broadcast_to(reaction[None], source.shape)], axis=1)
    mine = lax.all_to_all(both, "gx", 0, 0)

    row_block = lax.axis_index("gy")
    pieces, owners, stride = [mine], [row_block], gy_size // 2
    while stride:
        pairs = [(i, i ^ stride) for i in range(gy_size)]
        pieces = pieces + [lax.ppermute(piece, "gy", pairs) for piece in pieces]
        owners = owners + [jnp.bitwise_xor(owner, stride) for owner in owners]
        stride //= 2
    place = jnp.stack([lax.axis_index("gx")] + owners).astype(jnp.int32)
    results = column_cycle(
        pieces, place, shifts, shift_index, velocity, sizes, (gx_size, gy_size)
    )
    back = lax.all_to_all(results, "gx", 0, 0)
    area = bx * by
    iterate = back[:, :area].reshape(source.shape)
    residual = back[:, area : 2 * area].reshape(source.shape)
    return iterate, residual, back[:, 2 * area, 0]


def solution(mesh):
    gx_size, gy_size = mesh.shape["gx"], mesh.shape["gy"]

    def body(source, reaction, shifts, shift_index, velocity):
        columns, bx, by, nz = source.shape
        cells = bx * gx_size * by * gy_size
        fits = nz == LANES and by % 16 == 0 and cells * nz * 4 <= 2**20
        dealt = columns == gx_size and gx_size % UNROLL == 0 and bx == UNROLL
        dealt = dealt and gy_size & (gy_size - 1) == 0
        plan = column_body if dealt and fits else halo_body
        return plan(source, reaction, shifts, shift_index, velocity)

    return jax.shard_map(
        body,
        mesh=mesh,
        in_specs=(P(None, "gx", "gy", None), P("gx", "gy", None), P(), P(), P()),
        out_specs=(P(None, "gx", "gy", None), P(None, "gx", "gy", None), P()),
        check_vma=False,
    )
```

```python
import functools

import jax
import jax.numpy as jnp
from jax import lax
from jax.experimental import pallas as pl
from jax.experimental.pallas import tpu as pltpu
from jax.sharding import PartitionSpec as P

LEVELS = 3
COARSE_SWEEPS = 6

DAMPING = 0.8
EPSILON = 1e-06
VMEM_LIMIT = 40 * 1024 * 1024
LANES = 128
UNROLL = 4


def with_halo(x, sides, width):
    for axis, dim in sides:
        peers, length = (lax.axis_size(axis), x.shape[dim])
        up = [(i, (i + 1) % peers) for i in range(peers - 1)]
        down = [(j, i) for i, j in up]
        last = lax.slice_in_dim(x, length - width, length, axis=dim)
        leading = lax.slice_in_dim(x, 0, width, axis=dim)
        before = lax.ppermute(last, axis, up)
        after = lax.ppermute(leading, axis, down)
        x = jnp.concatenate([before, x, after], axis=dim)
    return x


def select_shifts(shifts, shift_index):
    columns = jnp.arange(shifts.shape[0], dtype=jnp.int32)
    picked = jnp.where(shift_index[:, None] == columns[None, :], shifts[None, :], 0.0)
    return jnp.sum(picked, axis=1)


def coefficients(velocity, spacing):
    scale_a = 1.0 / (spacing * spacing)
    backward = scale_a + jnp.maximum(velocity, 0.0) / spacing
    forward = scale_a - jnp.minimum(velocity, 0.0) / spacing
    centre = 6.0 * scale_a + jnp.sum(jnp.abs(velocity)) / spacing
    return (backward, forward, centre)


def apply_stencil(padded, backward, forward, diagonal):
    middle = padded[:, 1:-1, 1:-1, :]
    along_z = jnp.pad(middle, ((0, 0), (0, 0), (0, 0), (1, 1)))
    others = backward[0] * padded[:, :-2, 1:-1, :] + forward[0] * padded[:, 2:, 1:-1, :]
    others = others + backward[1] * padded[:, 1:-1, :-2, :] + forward[1] * padded[:, 1:-1, 2:, :]
    others = others + backward[2] * along_z[:, :, :, :-2] + forward[2] * along_z[:, :, :, 2:]
    return diagonal * middle - others


def face_halo(iterate):
    return with_halo(iterate, (("gx", 1), ("gy", 2)), 1)


def coarsen(values):
    count, size_x, size_y, size_z = values.shape
    blocks = values.reshape(count, size_x // 2, 2, size_y // 2, 2, size_z // 2, 2)
    return jnp.sum(blocks, axis=(2, 4, 6)) * 0.125


def refine(values):
    return jnp.repeat(jnp.repeat(jnp.repeat(values, 2, 1), 2, 2), 2, 3)


def coarsest_solve(rhs_field, backward, forward, diagonal):
    iterate = DAMPING * rhs_field / diagonal
    for repeat in range(COARSE_SWEEPS - 1):
        applied = apply_stencil(face_halo(iterate), backward, forward, diagonal)
        iterate = iterate + DAMPING * (rhs_field - applied) / diagonal
    return iterate


def multigrid_cycle(level_index, rhs_field, reaction_l, shift_value, velocity):
    backward, forward, centre = coefficients(velocity, 2.0**level_index)
    diagonal = centre + reaction_l + shift_value[:, None, None, None]
    if level_index == LEVELS - 1:
        return coarsest_solve(rhs_field, backward, forward, diagonal)

    def operate(iterate):
        return apply_stencil(face_halo(iterate), backward, forward, diagonal)

    def smooth_step(iterate):
        return iterate + DAMPING * (rhs_field - operate(iterate)) / diagonal

    iterate = DAMPING * rhs_field / diagonal
    iterate = smooth_step(iterate)
    defect = rhs_field - operate(iterate)
    correction = multigrid_cycle(
        level_index + 1, coarsen(defect), coarsen(reaction_l), shift_value, velocity
    )
    iterate = iterate + refine(correction)
    iterate = smooth_step(iterate)
    iterate = smooth_step(iterate)
    return iterate


def halo_body(source, reaction, shifts, shift_index, velocity):
    columns, cells_x, cells_y, cells_z = source.shape
    shift_value = select_shifts(shifts, shift_index)
    reaction_top = reaction[None]
    backward, forward, centre = coefficients(velocity, 1.0)
    diagonal = centre + reaction_top + shift_value[:, None, None, None]

    iterate = multigrid_cycle(0, source, reaction_top, shift_value, velocity)
    residual = source - apply_stencil(face_halo(iterate), backward, forward, diagonal)
    local_squares = jnp.sum(residual * residual, axis=(1, 2, 3))
    squares = lax.psum(local_squares, ("gx", "gy"))
    total_cells = cells_x * cells_y * cells_z * lax.axis_size("gx") * lax.axis_size("gy")
    residual_rms = jnp.sqrt(squares / total_cells + EPSILON)
    return (iterate, residual, residual_rms)


def split_dot(values, matrix):
    high = values.astype(jnp.bfloat16)
    low = (values - high.astype(jnp.float32)).astype(jnp.bfloat16)
    return jnp.dot(high, matrix, preferred_element_type=jnp.float32) + jnp.dot(
        low, matrix, preferred_element_type=jnp.float32
    )


def sweep(count, get, put):
    def step(group, carry):
        planes = [group * UNROLL + k for k in range(UNROLL)]
        values = [get(x) for x in planes]
        for x, value in zip(planes, values):
            put(x, value)
        return carry

    lax.fori_loop(0, count // UNROLL, step, 0)


class Level:
    def __init__(self, index, sizes, velocity_ref, shift, f, r, w):
        self.nx, self.ny, self.nz = (s >> index for s in sizes)
        self.f, self.r, self.w = f, r, w
        spacing = 2.0**index
        scale_a = 1.0 / (spacing * spacing)
        inverse = 1.0 / spacing
        speed = [velocity_ref[d] for d in range(3)]
        self.backward = [scale_a + jnp.maximum(v, 0.0) * inverse for v in speed]
        self.forward = [scale_a - jnp.minimum(v, 0.0) * inverse for v in speed]
        total = jnp.abs(speed[0]) + jnp.abs(speed[1]) + jnp.abs(speed[2])
        self.centre = 6.0 * scale_a + total * inverse + shift
        lane = lax.broadcasted_iota(jnp.int32, (1, LANES), 1)
        inside = lane < self.nz
        self.low_z = jnp.where((lane > 0) & inside, self.backward[2], 0.0)
        self.high_z = jnp.where(lane < self.nz - 1, self.forward[2], 0.0)

    def plane(self, v, x):
        return v[x + 1, pl.ds(8, self.ny), :]

    def neighbours(self, v, x, middle):
        ny = self.ny
        along_x = self.backward[0] * v[x, pl.ds(8, ny), :] + self.forward[0] * v[x + 2, pl.ds(8, ny), :]
        along_y = self.backward[1] * v[x + 1, pl.ds(7, ny), :] + self.forward[1] * v[x + 1, pl.ds(9, ny), :]
        along_z = self.low_z * pltpu.roll(middle, 1, 1) + self.high_z * pltpu.roll(middle, LANES - 1, 1)
        return along_x + along_y + along_z

    def smoothed(self, v, x):
        middle = self.plane(v, x)
        pulled = self.f[x] + self.neighbours(v, x, middle)
        return (1.0 - DAMPING) * middle + self.w[x] * pulled

    def smooth(self, src, dst):
        def put(x, value):
            dst[x + 1, pl.ds(8, self.ny), :] = value

        sweep(self.nx, lambda x: self.smoothed(src, x), put)

    def defect(self, v, x):
        middle = self.plane(v, x)
        pulled = self.f[x] + self.neighbours(v, x, middle)
        return pulled - (self.r[x] + self.centre) * middle

    def start(self, v):
        def put(x, weight):
            self.w[x] = weight
            v[x + 1, pl.ds(8, self.ny), :] = weight * self.f[x]

        sweep(self.nx, lambda x: DAMPING / (self.r[x] + self.centre), put)

    def pool_pairs(self, plane_of, tmp, pooled):
        half, ny = self.ny // 2, self.ny

        def put(x, value):
            rows = tmp.at[lax.rem(x, UNROLL)]
            rows[pl.ds(0, ny), :] = value
            both = rows[pl.ds(0, half, stride=2), :] + rows[pl.ds(1, half, stride=2), :]
            pooled[pl.ds(pl.multiple_of(x * half, 8), half), :] = both

        sweep(self.nx // 2, lambda x: plane_of(2 * x) + plane_of(2 * x + 1), put)

    def add_refined(self, v, spread, tmp):
        half, ny = self.ny // 2, self.ny

        def get(x):
            part = spread[pl.ds(pl.multiple_of(x * half, 8), half), :]
            rows = tmp.at[lax.rem(x, UNROLL)]
            rows[pl.ds(0, half, stride=2), :] = part
            rows[pl.ds(1, half, stride=2), :] = part
            return rows[pl.ds(0, ny), :]

        def put(x, value):
            for k in range(2):
                v[2 * x + 1 + k, pl.ds(8, ny), :] += value

        sweep(self.nx // 2, get, put)

    def solve_in_registers(self):
        row = lax.broadcasted_iota(jnp.int32, (self.ny, 1), 0)
        low_y = jnp.where(row > 0, self.backward[1], 0.0)
        high_y = jnp.where(row < self.ny - 1, self.forward[1], 0.0)
        weight = [DAMPING / (self.r[x] + self.centre) for x in range(self.nx)]
        rhs = [self.f[x] for x in range(self.nx)]
        v = [w * f for w, f in zip(weight, rhs)]
        for _ in range(COARSE_SWEEPS - 1):
            new = []
            for x, here in enumerate(v):
                along_z = self.low_z * pltpu.roll(here, 1, 1) + self.high_z * pltpu.roll(here, LANES - 1, 1)
                along_y = low_y * pltpu.roll(here, 1, 0) + high_y * pltpu.roll(here, self.ny - 1, 0)
                pulled = rhs[x] + along_z + along_y
                if x > 0:
                    pulled += self.backward[0] * v[x - 1]
                if x < self.nx - 1:
                    pulled += self.forward[0] * v[x + 1]
                new.append((1.0 - DAMPING) * here + weight[x] * pulled)
            v = new
        return jnp.concatenate(v, axis=0)


def zero_rim(v, nx, ny):
    rows = v.shape[1]
    blank = jnp.zeros((rows, LANES), jnp.float32)
    v[0] = blank
    v[nx + 1] = blank
    edge = jnp.zeros((nx + 2, 8, LANES), jnp.float32)
    v[:, pl.ds(0, 8), :] = edge
    v[:, pl.ds(8 + ny, 8), :] = edge


def cycle_kernel(
    sizes, blocks, place_ref, shifts_ref, index_ref, velocity_ref, pool_ref, spread_ref, *refs
):
    gx_size, gy_size = blocks
    nx, ny, nz = sizes
    bx, by = nx // gx_size, ny // gy_size
    f_pieces, r_pieces = refs[:gy_size], refs[gy_size : 2 * gy_size]
    out_refs = refs[2 * gy_size : 2 * gy_size + gx_size]
    f0, r0, w0, va, vb, f1, r1, w1, v1a, v1b, f2, r2, pooled, tmp = refs[2 * gy_size + gx_size :]
    column, row_block = place_ref[0], place_ref[1]
    shift = shifts_ref[index_ref[column]]
    pool, spread = pool_ref[...], spread_ref[...]

    fine = Level(0, sizes, velocity_ref, shift, f0, r0, w0)
    mid = Level(1, sizes, velocity_ref, shift, f1, r1, w1)
    deep = Level(2, sizes, velocity_ref, shift, f2, r2, None)
    for v, level in ((va, fine), (vb, fine), (v1a, mid), (v1b, mid)):
        zero_rim(v, level.nx, level.ny)

    for j, (f_piece, r_piece) in enumerate(zip(f_pieces, r_pieces)):
        rows = pl.ds(pl.multiple_of(place_ref[1 + j] * by, 8), by)
        for k in range(gx_size):
            planes = pl.ds(lax.rem(column + gx_size - k, gx_size) * bx, bx)
            f0[planes, rows, :] = f_piece[k]
            r0[planes, rows, :] = r_piece[k]

    rows1, rows2 = mid.nx * mid.ny, deep.nx * deep.ny
    fine.start(va)
    fine.smooth(va, vb)
    fine.pool_pairs(lambda x: fine.defect(vb, x), tmp, pooled)
    f1[...] = split_dot(pooled[pl.ds(0, rows1), :], pool).reshape(f1.shape)
    fine.pool_pairs(lambda x: r0[x], tmp, pooled)
    r1[...] = split_dot(pooled[pl.ds(0, rows1), :], pool).reshape(r1.shape)

    mid.start(v1a)
    mid.smooth(v1a, v1b)
    mid.pool_pairs(lambda x: mid.defect(v1b, x), tmp, pooled)
    f2[...] = split_dot(pooled[pl.ds(0, rows2), :], pool).reshape(f2.shape)
    mid.pool_pairs(lambda x: r1[x], tmp, pooled)
    r2[...] = split_dot(pooled[pl.ds(0, rows2), :], pool).reshape(r2.shape)

    values = deep.solve_in_registers()

    pooled[pl.ds(0, rows2), :] = split_dot(values, spread)
    mid.add_refined(v1b, pooled, tmp)
    mid.smooth(v1b, v1a)
    mid.smooth(v1a, v1b)
    values = v1b[pl.ds(1, mid.nx), pl.ds(8, mid.ny), :].reshape(rows1, LANES)
    pooled[pl.ds(0, rows1), :] = split_dot(values, spread)
    fine.add_refined(vb, pooled, tmp)
    fine.smooth(vb, va)
    fine.smooth(va, vb)

    area = bx * by
    row0 = pl.multiple_of(row_block * by, 8)

    total = jnp.zeros((8, LANES), jnp.float32)
    for k, out_ref in enumerate(out_refs):
        first = lax.rem(column + k, gx_size) * bx
        rest = [fine.defect(vb, first + p) for p in range(bx)]
        for p in range(bx):
            total = total + jnp.sum((rest[p] * rest[p]).reshape(ny // 8, 8, LANES), axis=0)
            tmp[p, pl.ds(0, ny), :] = rest[p]
        for p in range(bx):
            out_ref[pl.ds(p * by, by), :] = vb[first + p + 1, pl.ds(8 + row0, by), :]
            out_ref[pl.ds(area + p * by, by), :] = tmp[p, pl.ds(row0, by), :]
    mean = jnp.sum(total) / (nx * ny * nz) + EPSILON
    rms = jnp.sqrt(jnp.full((8, LANES), mean, jnp.float32))
    for out_ref in out_refs:
        out_ref[pl.ds(2 * area, 8), :] = rms


def collect_kernel(bx, by, place_ref, *refs):
    count = len(refs) - 3
    parts, (iterate_ref, residual_ref, rms_ref) = refs[:count], refs[count:]
    area = bx * by
    for k, part in enumerate(parts):
        column = lax.rem(place_ref[0] + count - k, count)
        iterate_ref[column] = part[pl.ds(0, area), :].reshape(bx, by, LANES)
        residual_ref[column] = part[pl.ds(area, area), :].reshape(bx, by, LANES)
        rms_ref[column] = jnp.max(part[pl.ds(2 * area, 8), :])


def collect(parts, place, shape):
    columns, bx, by, nz = shape
    smem = pl.BlockSpec(memory_space=pltpu.SMEM)
    vmem = pl.BlockSpec(memory_space=pltpu.VMEM)
    block = jax.ShapeDtypeStruct(shape, jnp.float32)
    return pl.pallas_call(
        functools.partial(collect_kernel, bx, by),
        out_shape=(block, block, jax.ShapeDtypeStruct((columns,), jnp.float32)),
        in_specs=[smem] + [vmem] * len(parts),
        out_specs=(vmem, vmem, smem),
        name="collect",
    )(place, *parts)


def pooling_matrices():
    row = lax.broadcasted_iota(jnp.int32, (LANES, LANES), 0)
    col = lax.broadcasted_iota(jnp.int32, (LANES, LANES), 1)
    pool = jnp.where(row // 2 == col, 0.125, 0.0).astype(jnp.bfloat16)
    spread = jnp.where(col // 2 == row, 1.0, 0.0).astype(jnp.bfloat16)
    return pool, spread


def column_cycle(pieces, place, shifts, shift_index, velocity, sizes, blocks):
    gx_size, gy_size = blocks
    nx, ny, nz = sizes
    area = (nx // gx_size) * (ny // gy_size)
    f32 = jnp.float32

    def grid(index):
        return pltpu.VMEM((nx >> index, ny >> index, LANES), f32)

    def rimmed(index):
        return pltpu.VMEM(((nx >> index) + 2, (ny >> index) + 16, LANES), f32)

    scratch = []
    for index in range(LEVELS - 1):
        scratch += [grid(index)] * 3 + [rimmed(index)] * 2
    scratch += [grid(LEVELS - 1)] * 2
    scratch += [pltpu.VMEM(((nx // 2) * (ny // 2), LANES), f32), pltpu.VMEM((UNROLL, ny, LANES), f32)]
    smem = pl.BlockSpec(memory_space=pltpu.SMEM)
    vmem = pl.BlockSpec(memory_space=pltpu.VMEM)
    pool, spread = pooling_matrices()
    return pl.pallas_call(
        functools.partial(cycle_kernel, sizes, blocks),
        out_shape=[jax.ShapeDtypeStruct((2 * area + 8, LANES), f32)] * gx_size,
        in_specs=[smem] * 4 + [vmem] * (2 + 2 * gy_size),
        out_specs=[vmem] * gx_size,
        scratch_shapes=scratch,
        compiler_params=pltpu.CompilerParams(vmem_limit_bytes=VMEM_LIMIT),
        name="cycle",
    )(place, shifts, shift_index, velocity, pool, spread, *pieces)


def deal(block_for):
    size = lax.axis_size("gx")
    moved = [block_for(0)]
    for k in range(1, size):
        pairs = [(i, (i + k) % size) for i in range(size)]
        moved.append(lax.ppermute(block_for(k), "gx", pairs))
    return moved


def gather_rows(piece):
    size = lax.axis_size("gy")
    pieces, stride = [piece], size // 2
    while stride:
        pairs = [(i, i ^ stride) for i in range(size)]
        pieces = pieces + [lax.ppermute(p, "gy", pairs) for p in pieces]
        stride //= 2
    return pieces


def row_owners():
    owners, stride = [lax.axis_index("gy")], lax.axis_size("gy") // 2
    while stride:
        owners = owners + [jnp.bitwise_xor(owner, stride) for owner in owners]
        stride //= 2
    return owners


def column_body(source, reaction, shifts, shift_index, velocity):
    columns, bx, by, nz = source.shape
    gx_size, gy_size = lax.axis_size("gx"), lax.axis_size("gy")
    sizes = (bx * gx_size, by * gy_size, nz)
    column = lax.axis_index("gx")
    place = jnp.stack([column] + row_owners()).astype(jnp.int32)

    def column_for(k):
        return lax.dynamic_index_in_dim(source, lax.rem(column + k, columns), 0, keepdims=False)

    r_pieces = gather_rows(jnp.stack(deal(lambda k: reaction)))
    f_pieces = gather_rows(jnp.stack(deal(column_for)))
    results = column_cycle(
        f_pieces + r_pieces, place, shifts, shift_index, velocity, sizes, (gx_size, gy_size)
    )
    return collect(deal(lambda k: results[k]), place, source.shape)


def solution(mesh):
    gx_size, gy_size = mesh.shape["gx"], mesh.shape["gy"]

    def body(source, reaction, shifts, shift_index, velocity):
        columns, bx, by, nz = source.shape
        cells = bx * gx_size * by * gy_size
        fits = nz == LANES and by % 16 == 0 and cells * nz * 4 <= 2**20
        dealt = columns == gx_size and gx_size % UNROLL == 0 and bx == UNROLL
        dealt = dealt and gy_size & (gy_size - 1) == 0
        plan = column_body if dealt and fits else halo_body
        return plan(source, reaction, shifts, shift_index, velocity)

    return jax.shard_map(
        body,
        mesh=mesh,
        in_specs=(P(None, "gx", "gy", None), P("gx", "gy", None), P(), P(), P()),
        out_specs=(P(None, "gx", "gy", None), P(None, "gx", "gy", None), P()),
        check_vma=False,
    )
```

```python
import functools

import jax
import jax.numpy as jnp
from jax import lax
from jax.experimental import pallas as pl
from jax.experimental.pallas import tpu as pltpu
from jax.sharding import PartitionSpec as P

LEVELS = 3
COARSE_SWEEPS = 6

DAMPING = 0.8
EPSILON = 1e-06
VMEM_LIMIT = 32 * 1024 * 1024
LANES = 128
GROUP = 4
SLAB = 8
HALO = 4


def with_halo(x, sides, width):
    for axis, dim in sides:
        peers, length = (lax.axis_size(axis), x.shape[dim])
        up = [(i, (i + 1) % peers) for i in range(peers - 1)]
        down = [(j, i) for i, j in up]
        last = lax.slice_in_dim(x, length - width, length, axis=dim)
        leading = lax.slice_in_dim(x, 0, width, axis=dim)
        before = lax.ppermute(last, axis, up)
        after = lax.ppermute(leading, axis, down)
        x = jnp.concatenate([before, x, after], axis=dim)
    return x


def select_shifts(shifts, shift_index):
    columns = jnp.arange(shifts.shape[0], dtype=jnp.int32)
    picked = jnp.where(shift_index[:, None] == columns[None, :], shifts[None, :], 0.0)
    return jnp.sum(picked, axis=1)


def coefficients(velocity, spacing):
    scale_a = 1.0 / (spacing * spacing)
    backward = scale_a + jnp.maximum(velocity, 0.0) / spacing
    forward = scale_a - jnp.minimum(velocity, 0.0) / spacing
    centre = 6.0 * scale_a + jnp.sum(jnp.abs(velocity)) / spacing
    return (backward, forward, centre)


def apply_stencil(padded, backward, forward, diagonal):
    middle = padded[:, 1:-1, 1:-1, :]
    along_z = jnp.pad(middle, ((0, 0), (0, 0), (0, 0), (1, 1)))
    others = backward[0] * padded[:, :-2, 1:-1, :] + forward[0] * padded[:, 2:, 1:-1, :]
    others = others + backward[1] * padded[:, 1:-1, :-2, :] + forward[1] * padded[:, 1:-1, 2:, :]
    others = others + backward[2] * along_z[:, :, :, :-2] + forward[2] * along_z[:, :, :, 2:]
    return diagonal * middle - others


def face_halo(iterate):
    return with_halo(iterate, (("gx", 1), ("gy", 2)), 1)


def coarsen(values):
    count, size_x, size_y, size_z = values.shape
    blocks = values.reshape(count, size_x // 2, 2, size_y // 2, 2, size_z // 2, 2)
    return jnp.sum(blocks, axis=(2, 4, 6)) * 0.125


def refine(values):
    return jnp.repeat(jnp.repeat(jnp.repeat(values, 2, 1), 2, 2), 2, 3)


def coarsest_solve(rhs_field, backward, forward, diagonal):
    iterate = DAMPING * rhs_field / diagonal
    for repeat in range(COARSE_SWEEPS - 1):
        applied = apply_stencil(face_halo(iterate), backward, forward, diagonal)
        iterate = iterate + DAMPING * (rhs_field - applied) / diagonal
    return iterate


def multigrid_cycle(level_index, rhs_field, reaction_l, shift_value, velocity):
    backward, forward, centre = coefficients(velocity, 2.0**level_index)
    diagonal = centre + reaction_l + shift_value[:, None, None, None]
    if level_index == LEVELS - 1:
        return coarsest_solve(rhs_field, backward, forward, diagonal)

    def operate(iterate):
        return apply_stencil(face_halo(iterate), backward, forward, diagonal)

    def smooth_step(iterate):
        return iterate + DAMPING * (rhs_field - operate(iterate)) / diagonal

    iterate = DAMPING * rhs_field / diagonal
    iterate = smooth_step(iterate)
    defect = rhs_field - operate(iterate)
    correction = multigrid_cycle(
        level_index + 1, coarsen(defect), coarsen(reaction_l), shift_value, velocity
    )
    iterate = iterate + refine(correction)
    iterate = smooth_step(iterate)
    iterate = smooth_step(iterate)
    return iterate


def halo_body(source, reaction, shifts, shift_index, velocity):
    columns, cells_x, cells_y, cells_z = source.shape
    shift_value = select_shifts(shifts, shift_index)
    reaction_top = reaction[None]
    backward, forward, centre = coefficients(velocity, 1.0)
    diagonal = centre + reaction_top + shift_value[:, None, None, None]

    iterate = multigrid_cycle(0, source, reaction_top, shift_value, velocity)
    residual = source - apply_stencil(face_halo(iterate), backward, forward, diagonal)
    local_squares = jnp.sum(residual * residual, axis=(1, 2, 3))
    squares = lax.psum(local_squares, ("gx", "gy"))
    total_cells = cells_x * cells_y * cells_z * lax.axis_size("gx") * lax.axis_size("gy")
    residual_rms = jnp.sqrt(squares / total_cells + EPSILON)
    return (iterate, residual, residual_rms)


def split_dot(values, matrix):
    high = values.astype(jnp.bfloat16)
    low = (values - high.astype(jnp.float32)).astype(jnp.bfloat16)
    return jnp.dot(high, matrix, preferred_element_type=jnp.float32) + jnp.dot(
        low, matrix, preferred_element_type=jnp.float32
    )


def sweep(planes, get, put):
    planes = list(planes)
    for first in range(0, len(planes), GROUP):
        group = planes[first : first + GROUP]
        values = [get(x) for x in group]
        for x, value in zip(group, values):
            put(x, value)


class Level:
    def __init__(self, index, ny, nz, rim, velocity_ref, shift, f, r, w):
        self.ny, self.nz, self.rim = ny, nz, rim
        self.f, self.r, self.w = f, r, w
        spacing = 2.0**index
        scale_a = 1.0 / (spacing * spacing)
        inverse = 1.0 / spacing
        speed = [velocity_ref[d] for d in range(3)]
        self.backward = [scale_a + jnp.maximum(v, 0.0) * inverse for v in speed]
        self.forward = [scale_a - jnp.minimum(v, 0.0) * inverse for v in speed]
        total = jnp.abs(speed[0]) + jnp.abs(speed[1]) + jnp.abs(speed[2])
        self.centre = 6.0 * scale_a + total * inverse + shift
        lane = lax.broadcasted_iota(jnp.int32, (1, LANES), 1)
        inside = lane < nz
        self.low_z = jnp.where((lane > 0) & inside, self.backward[2], 0.0)
        self.high_z = jnp.where(lane < nz - 1, self.forward[2], 0.0)

    def plane(self, v, x):
        return v[x + self.rim, pl.ds(8, self.ny), :]

    def put(self, v):
        def write(x, value):
            v[x + self.rim, pl.ds(8, self.ny), :] = value

        return write

    def along_z(self, middle):
        return self.low_z * pltpu.roll(middle, 1, 1) + self.high_z * pltpu.roll(middle, LANES - 1, 1)

    def neighbours(self, v, x, middle):
        at, ny = x + self.rim, self.ny
        along_x = self.backward[0] * v[at - 1, pl.ds(8, ny), :] + self.forward[0] * v[at + 1, pl.ds(8, ny), :]
        along_y = self.backward[1] * v[at, pl.ds(7, ny), :] + self.forward[1] * v[at, pl.ds(9, ny), :]
        return along_x + along_y + self.along_z(middle)

    def smoothed(self, v, x):
        middle = self.plane(v, x)
        pulled = self.f[x] + self.neighbours(v, x, middle)
        return (1.0 - DAMPING) * middle + self.w[x] * pulled

    def smooth(self, src, dst, planes):
        sweep(planes, lambda x: self.smoothed(src, x), self.put(dst))

    def defect(self, v, x):
        middle = self.plane(v, x)
        pulled = self.f[x] + self.neighbours(v, x, middle)
        return pulled - (self.r[x] + self.centre) * middle

    def pool_rows(self, value, rows):
        half, ny = self.ny // 2, self.ny
        rows[pl.ds(0, ny), :] = value
        return rows[pl.ds(0, half, stride=2), :] + rows[pl.ds(1, half, stride=2), :]

    def spread_rows(self, part, rows):
        half, ny = self.ny // 2, self.ny
        rows[pl.ds(0, half, stride=2), :] = part
        rows[pl.ds(1, half, stride=2), :] = part
        return rows[pl.ds(0, ny), :]

    def solve_in_registers(self, rhs, reaction):
        row = lax.broadcasted_iota(jnp.int32, (self.ny, 1), 0)
        low_y = jnp.where(row > 0, self.backward[1], 0.0)
        high_y = jnp.where(row < self.ny - 1, self.forward[1], 0.0)
        weight = [DAMPING / (r + self.centre) for r in reaction]
        v = [w * f for w, f in zip(weight, rhs)]
        for _ in range(COARSE_SWEEPS - 1):
            new = []
            for x, here in enumerate(v):
                along_y = low_y * pltpu.roll(here, 1, 0) + high_y * pltpu.roll(here, self.ny - 1, 0)
                pulled = rhs[x] + self.along_z(here) + along_y
                if x > 0:
                    pulled += self.backward[0] * v[x - 1]
                if x < len(v) - 1:
                    pulled += self.forward[0] * v[x + 1]
                new.append((1.0 - DAMPING) * here + weight[x] * pulled)
            v = new
        return jnp.concatenate(v, axis=0)


def zero_rows(v, ny):
    edge = jnp.zeros((v.shape[0], 8, LANES), jnp.float32)
    v[:, pl.ds(0, 8), :] = edge
    v[:, pl.ds(8 + ny, 8), :] = edge


def pool_matrix(offset):
    row = lax.broadcasted_iota(jnp.int32, (LANES, LANES), 0)
    col = lax.broadcasted_iota(jnp.int32, (LANES, LANES), 1)
    return jnp.where(row // 2 + offset == col, 0.125, 0.0).astype(jnp.bfloat16)


def spread_matrix():
    row = lax.broadcasted_iota(jnp.int32, (LANES, LANES), 0)
    col = lax.broadcasted_iota(jnp.int32, (LANES, LANES), 1)
    return jnp.where(col // 2 == row, 1.0, 0.0).astype(jnp.bfloat16)


def pack_kernel(place_ref, source_ref, reaction_ref, *out_refs):
    for k, out_ref in enumerate(out_refs):
        out_ref[0] = source_ref[jnp.bitwise_xor(place_ref[0], k)]
        out_ref[1] = reaction_ref[...]


def arrange_kernel(gy_size, place_ref, *refs):
    pieces, (low_ref, high_ref, both) = refs[:-3], refs[-3:]
    _, bx, by, _ = pieces[0].shape
    for k, piece in enumerate(pieces):
        owner = jnp.bitwise_xor(place_ref[0], k)
        planes = pl.ds((owner // gy_size) * bx, bx)
        rows = pl.ds(pl.multiple_of(lax.rem(owner, gy_size) * by, 8), by)
        both[:, planes, rows, :] = piece[...]
    low_ref[...] = both[:, pl.ds(0, HALO)]
    high_ref[...] = both[:, pl.ds(HALO, HALO)]


def pre_kernel(slabs, place_ref, shifts_ref, index_ref, velocity_ref, *refs):
    pool_ref, pool_up_ref = refs[:2]
    parts = refs[2:6]
    f, r, w, v1, coarse_ref, v0, tmp, pooled = refs[6:]
    ny = f.shape[1]
    slab = place_ref[1]
    shift = shifts_ref[index_ref[place_ref[0]]]
    fine = Level(0, ny, LANES, 0, velocity_ref, shift, f, r, w)
    zero_rows(v0, ny)
    zero_rows(v1, ny)
    count = SLAB + 2 * HALO
    inside = [jnp.where(slab > 0, DAMPING, 0.0)] * HALO
    inside += [DAMPING] * SLAB
    inside += [jnp.where(slab < slabs - 1, DAMPING, 0.0)] * HALO

    def begin(x):
        part, at = parts[x // HALO], x % HALO
        return part[0, at], part[1, at]

    def put(x, pair):
        f[x], r[x] = pair
        weight = inside[x] / (pair[1] + fine.centre)
        w[x] = weight
        v0[x, pl.ds(8, ny), :] = weight * pair[0]

    sweep(range(count), begin, put)
    fine.smooth(v0, v1, range(1, count - 1))
    half = ny // 2

    def coarsened(x):
        at = HALO + 2 * x
        return fine.defect(v1, at) + fine.defect(v1, at + 1), r[at] + r[at + 1]

    def put_pooled(x, pair):
        for n in range(2):
            pooled[n, pl.ds(x * half, half), :] = fine.pool_rows(pair[n], tmp.at[2 * x + n])

    sweep(range(SLAB // 2), coarsened, put_pooled)
    packed = split_dot(pooled[0], pool_ref[...]) + split_dot(pooled[1], pool_up_ref[...])
    coarse_ref[...] = packed.reshape(coarse_ref.shape)


def post_kernel(grid, gy_size, bx, by, place_ref, shifts_ref, index_ref, velocity_ref, *refs):
    slabs, nx, ny, nz = grid
    pool_ref, spread_ref, f, r, w, v1 = refs[:6]
    coarse = refs[6 : 6 + slabs]
    columns = SLAB // bx * gy_size
    out_refs = refs[6 + slabs : 6 + slabs + columns]
    va, vb, f1, r1, w1, v1a, v1b, pooled, tmp = refs[6 + slabs + columns :]
    pool, spread = pool_ref[...], spread_ref[...]
    slab = place_ref[1]
    shift = shifts_ref[index_ref[place_ref[0]]]
    rim = HALO // 2
    nx1, ny1, nx2, ny2 = nx // 2, ny // 2, nx // 4, ny // 4
    fine = Level(0, ny, nz, 0, velocity_ref, shift, f, r, w)
    mid = Level(1, ny1, nz // 2, rim, velocity_ref, shift, f1, r1, w1)
    deep = Level(2, ny2, nz // 4, 0, velocity_ref, shift, None, None, None)
    for v in (va, vb):
        zero_rows(v, ny)
    for v in (v1a, v1b):
        zero_rows(v, ny1)
        blank = jnp.zeros((rim,) + v.shape[1:], jnp.float32)
        v[pl.ds(0, rim)] = blank
        v[pl.ds(rim + nx1, rim)] = blank

    lower = lax.broadcasted_iota(jnp.int32, (1, LANES), 1) < LANES // 2
    own = SLAB // 2
    for k in range(slabs):
        first = jnp.bitwise_xor(slab, k) * own
        both = coarse[k][...]
        f1[pl.ds(first, own)] = jnp.where(lower, both, 0.0)
        r1[pl.ds(first, own)] = jnp.where(lower, pltpu.roll(both, LANES // 2, 2), 0.0)

    def put_start(x, weight):
        w1[x] = weight
        v1a[x + rim, pl.ds(8, ny1), :] = weight * f1[x]

    sweep(range(nx1), lambda x: DAMPING / (r1[x] + mid.centre), put_start)
    mid.smooth(v1a, v1b, range(nx1))

    def coarsened(x):
        return mid.defect(v1b, 2 * x) + mid.defect(v1b, 2 * x + 1), r1[2 * x] + r1[2 * x + 1]

    rows2 = nx2 * ny2

    def put_pooled(x, pair):
        for n in range(2):
            value = mid.pool_rows(pair[n], tmp.at[2 * x + n])
            pooled[pl.ds(n * rows2 + x * ny2, ny2), :] = value

    sweep(range(nx2), coarsened, put_pooled)
    deeper = split_dot(pooled[pl.ds(0, 2 * rows2), :], pool)
    planes = [deeper[n * ny2 : (n + 1) * ny2] for n in range(2 * nx2)]
    values = deep.solve_in_registers(planes[:nx2], planes[nx2:])

    pooled[pl.ds(0, rows2), :] = split_dot(values, spread)

    def refined1(x):
        return mid.spread_rows(pooled[pl.ds(x * ny2, ny2), :], tmp.at[x])

    def put_refined1(x, value):
        for n in range(2):
            v1b[2 * x + n + rim, pl.ds(8, ny1), :] += value

    sweep(range(nx2), refined1, put_refined1)
    mid.smooth(v1b, v1a, range(nx1))
    mid.smooth(v1a, v1b, range(nx1))

    window = own + 2 * rim
    values = v1b[pl.ds(slab * own, window), pl.ds(8, ny1), :].reshape(window * ny1, LANES)
    pooled[pl.ds(0, window * ny1), :] = split_dot(values, spread)
    count = SLAB + 2 * HALO

    def refined(x):
        return fine.spread_rows(pooled[pl.ds(x * ny1, ny1), :], tmp.at[x])

    def put_refined(x, value):
        for at in (2 * x, 2 * x + 1):
            if 0 < at < count - 1:
                va[at, pl.ds(8, ny), :] = v1[at, pl.ds(8, ny), :] + value

    sweep(range(window), refined, put_refined)
    fine.smooth(va, vb, range(2, count - 2))
    fine.smooth(vb, va, range(3, count - 3))

    total = jnp.zeros((8, LANES), jnp.float32)
    for x in range(SLAB):
        rest = fine.defect(va, HALO + x)
        total = total + jnp.sum((rest * rest).reshape(ny // 8, 8, LANES), axis=0)
        tmp[x] = rest
    squares = jnp.full((8, LANES), jnp.sum(total), jnp.float32)
    area = bx * by
    for k, out_ref in enumerate(out_refs):
        owner = jnp.bitwise_xor(place_ref[0], k)
        first = (owner // gy_size) * bx
        row = pl.multiple_of(lax.rem(owner, gy_size) * by, 8)
        for p in range(bx):
            out_ref[pl.ds(p * by, by), :] = va[HALO + first + p, pl.ds(8 + row, by), :]
            out_ref[pl.ds(area + p * by, by), :] = tmp[first + p, pl.ds(row, by), :]
        out_ref[pl.ds(2 * area, 8), :] = squares


def collect_kernel(bx, by, place_ref, *refs):
    parts, (iterate_ref, residual_ref) = refs[:-2], refs[-2:]
    area = bx * by
    for k, part in enumerate(parts):
        column = jnp.bitwise_xor(place_ref[0], k)
        iterate_ref[column] = part[pl.ds(0, area), :].reshape(bx, by, LANES)
        residual_ref[column] = part[pl.ds(area, area), :].reshape(bx, by, LANES)


SMEM = pl.BlockSpec(memory_space=pltpu.SMEM)
VMEM = pl.BlockSpec(memory_space=pltpu.VMEM)


def local_kernel(kernel, name, scalars, arrays, outs, scratch=()):
    return pl.pallas_call(
        kernel,
        out_shape=[jax.ShapeDtypeStruct(shape, jnp.float32) for shape in outs],
        in_specs=[SMEM] * len(scalars) + [VMEM] * len(arrays),
        out_specs=[VMEM] * len(outs),
        scratch_shapes=[pltpu.VMEM(shape, jnp.float32) for shape in scratch],
        compiler_params=pltpu.CompilerParams(vmem_limit_bytes=VMEM_LIMIT),
        name=name,
    )(*scalars, *arrays)


def swap_in_plane(pieces, columns):
    devices = lax.axis_size("gx") * lax.axis_size("gy")
    moved = [pieces[0]]
    for k in range(1, columns):
        pairs = [(i, i ^ k) for i in range(devices)]
        moved.append(lax.ppermute(pieces[k], ("gx", "gy"), pairs))
    return moved


def swap_slabs(piece, step, slabs):
    size = lax.axis_size("gx")
    moved = [piece]
    for k in range(1, slabs):
        pairs = [(i, i ^ (k * step)) for i in range(size)]
        moved.append(lax.ppermute(piece, "gx", pairs))
    return moved


def column_body(source, reaction, shifts, shift_index, velocity):
    columns, bx, by, nz = source.shape
    gx_size, gy_size = lax.axis_size("gx"), lax.axis_size("gy")
    nx, ny = bx * gx_size, by * gy_size
    step = columns // gy_size
    slabs = gx_size // step
    along, across = lax.axis_index("gx"), lax.axis_index("gy")
    column = lax.rem(along, step) * gy_size + across
    place = jnp.stack([column, along // step]).astype(jnp.int32)
    scalars = (place, shifts, shift_index, velocity)
    count = SLAB + 2 * HALO
    area = bx * by

    pieces = local_kernel(
        pack_kernel, "pack", (place,), (source, reaction), [(2, bx, by, nz)] * columns
    )
    pieces = swap_in_plane(pieces, columns)
    low, high = local_kernel(
        functools.partial(arrange_kernel, gy_size),
        "arrange",
        (place,),
        pieces,
        [(2, HALO, ny, nz)] * 2,
        [(2, SLAB, ny, nz)],
    )
    before = lax.ppermute(high, "gx", [(i, i + step) for i in range(gx_size - step)])
    after = lax.ppermute(low, "gx", [(i + step, i) for i in range(gx_size - step)])

    grid, rimmed = (count, ny, nz), (count, ny + 16, nz)
    f, r, w, v1, coarse = local_kernel(
        functools.partial(pre_kernel, slabs),
        "pre",
        scalars,
        (pool_matrix(0), pool_matrix(LANES // 2), before, low, high, after),
        [grid, grid, grid, rimmed, (SLAB // 2, ny // 2, nz)],
        [rimmed, (SLAB, ny, nz), (2, SLAB // 2 * ny // 2, nz)],
    )
    gathered = swap_slabs(coarse, step, slabs)

    coarse_grid = (nx // 2, ny // 2, nz)
    coarse_rimmed = (nx // 2 + HALO, ny // 2 + 16, nz)
    rows = max((SLAB // 2 + HALO) * ny // 2, nx // 4 * ny // 2)
    results = local_kernel(
        functools.partial(post_kernel, (slabs, nx, ny, nz), gy_size, bx, by),
        "post",
        scalars,
        (pool_matrix(0), spread_matrix(), f, r, w, v1, *gathered),
        [(2 * area + 8, nz)] * columns,
        [rimmed] * 2 + [coarse_grid] * 3 + [coarse_rimmed] * 2 + [(rows, nz), (nx // 2, ny, nz)],
    )
    parts = swap_in_plane(results, columns)

    squares = jnp.stack([part[2 * area, 0] for part in parts])
    total = sum(swap_slabs(squares, step, slabs))
    rms = jnp.sqrt(total / (nx * ny * nz) + EPSILON)
    slots = jnp.arange(columns, dtype=jnp.int32)
    mine = jnp.bitwise_xor(slots, column)[None, :] == slots[:, None]
    residual_rms = jnp.sum(jnp.where(mine, rms[None, :], 0.0), axis=1)
    iterate, residual = local_kernel(
        functools.partial(collect_kernel, bx, by), "collect", (place,), parts, [source.shape] * 2
    )
    return iterate, residual, residual_rms


def power_of_two(n):
    return n > 0 and n & (n - 1) == 0


def column_plan_fits(columns, bx, by, nz, gx_size, gy_size):
    if columns % gy_size or gx_size % (columns // gy_size):
        return False
    step = columns // gy_size
    slabs, ny = gx_size // step, by * gy_size
    whole = power_of_two(columns) and power_of_two(step) and power_of_two(slabs)
    small = slabs * ny * nz <= 2**15
    return whole and small and bx * step == SLAB and nz == LANES and by % 16 == 0


def solution(mesh):
    gx_size, gy_size = mesh.shape["gx"], mesh.shape["gy"]

    def body(source, reaction, shifts, shift_index, velocity):
        fits = column_plan_fits(*source.shape, gx_size, gy_size)
        plan = column_body if fits else halo_body
        return plan(source, reaction, shifts, shift_index, velocity)

    return jax.shard_map(
        body,
        mesh=mesh,
        in_specs=(P(None, "gx", "gy", None), P("gx", "gy", None), P(), P(), P()),
        out_specs=(P(None, "gx", "gy", None), P(None, "gx", "gy", None), P()),
        check_vma=False,
    )
```

```python
import functools

import jax
import jax.numpy as jnp
from jax import lax
from jax.experimental import pallas as pl
from jax.experimental.pallas import tpu as pltpu
from jax.sharding import PartitionSpec as P

LEVELS = 3
COARSE_SWEEPS = 6

DAMPING = 0.8
EPSILON = 1e-06
VMEM_LIMIT = 32 * 1024 * 1024
LANES = 128
GROUP = 4
SLAB = 8
HALO = 4


def with_halo(x, sides, width):
    for axis, dim in sides:
        peers, length = (lax.axis_size(axis), x.shape[dim])
        up = [(i, (i + 1) % peers) for i in range(peers - 1)]
        down = [(j, i) for i, j in up]
        last = lax.slice_in_dim(x, length - width, length, axis=dim)
        leading = lax.slice_in_dim(x, 0, width, axis=dim)
        before = lax.ppermute(last, axis, up)
        after = lax.ppermute(leading, axis, down)
        x = jnp.concatenate([before, x, after], axis=dim)
    return x


def select_shifts(shifts, shift_index):
    columns = jnp.arange(shifts.shape[0], dtype=jnp.int32)
    picked = jnp.where(shift_index[:, None] == columns[None, :], shifts[None, :], 0.0)
    return jnp.sum(picked, axis=1)


def coefficients(velocity, spacing):
    scale_a = 1.0 / (spacing * spacing)
    backward = scale_a + jnp.maximum(velocity, 0.0) / spacing
    forward = scale_a - jnp.minimum(velocity, 0.0) / spacing
    centre = 6.0 * scale_a + jnp.sum(jnp.abs(velocity)) / spacing
    return (backward, forward, centre)


def apply_stencil(padded, backward, forward, diagonal):
    middle = padded[:, 1:-1, 1:-1, :]
    along_z = jnp.pad(middle, ((0, 0), (0, 0), (0, 0), (1, 1)))
    others = backward[0] * padded[:, :-2, 1:-1, :] + forward[0] * padded[:, 2:, 1:-1, :]
    others = others + backward[1] * padded[:, 1:-1, :-2, :] + forward[1] * padded[:, 1:-1, 2:, :]
    others = others + backward[2] * along_z[:, :, :, :-2] + forward[2] * along_z[:, :, :, 2:]
    return diagonal * middle - others


def face_halo(iterate):
    return with_halo(iterate, (("gx", 1), ("gy", 2)), 1)


def coarsen(values):
    count, size_x, size_y, size_z = values.shape
    blocks = values.reshape(count, size_x // 2, 2, size_y // 2, 2, size_z // 2, 2)
    return jnp.sum(blocks, axis=(2, 4, 6)) * 0.125


def refine(values):
    return jnp.repeat(jnp.repeat(jnp.repeat(values, 2, 1), 2, 2), 2, 3)


def coarsest_solve(rhs_field, backward, forward, diagonal):
    iterate = DAMPING * rhs_field / diagonal
    for repeat in range(COARSE_SWEEPS - 1):
        applied = apply_stencil(face_halo(iterate), backward, forward, diagonal)
        iterate = iterate + DAMPING * (rhs_field - applied) / diagonal
    return iterate


def multigrid_cycle(level_index, rhs_field, reaction_l, shift_value, velocity):
    backward, forward, centre = coefficients(velocity, 2.0**level_index)
    diagonal = centre + reaction_l + shift_value[:, None, None, None]
    if level_index == LEVELS - 1:
        return coarsest_solve(rhs_field, backward, forward, diagonal)

    def operate(iterate):
        return apply_stencil(face_halo(iterate), backward, forward, diagonal)

    def smooth_step(iterate):
        return iterate + DAMPING * (rhs_field - operate(iterate)) / diagonal

    iterate = DAMPING * rhs_field / diagonal
    iterate = smooth_step(iterate)
    defect = rhs_field - operate(iterate)
    correction = multigrid_cycle(
        level_index + 1, coarsen(defect), coarsen(reaction_l), shift_value, velocity
    )
    iterate = iterate + refine(correction)
    iterate = smooth_step(iterate)
    iterate = smooth_step(iterate)
    return iterate


def halo_body(source, reaction, shifts, shift_index, velocity):
    columns, cells_x, cells_y, cells_z = source.shape
    shift_value = select_shifts(shifts, shift_index)
    reaction_top = reaction[None]
    backward, forward, centre = coefficients(velocity, 1.0)
    diagonal = centre + reaction_top + shift_value[:, None, None, None]

    iterate = multigrid_cycle(0, source, reaction_top, shift_value, velocity)
    residual = source - apply_stencil(face_halo(iterate), backward, forward, diagonal)
    local_squares = jnp.sum(residual * residual, axis=(1, 2, 3))
    squares = lax.psum(local_squares, ("gx", "gy"))
    total_cells = cells_x * cells_y * cells_z * lax.axis_size("gx") * lax.axis_size("gy")
    residual_rms = jnp.sqrt(squares / total_cells + EPSILON)
    return (iterate, residual, residual_rms)


def split_dot(values, matrix):
    high = values.astype(jnp.bfloat16)
    low = (values - high.astype(jnp.float32)).astype(jnp.bfloat16)
    return jnp.dot(high, matrix, preferred_element_type=jnp.float32) + jnp.dot(
        low, matrix, preferred_element_type=jnp.float32
    )


def sweep(planes, get, put):
    planes = list(planes)
    for first in range(0, len(planes), GROUP):
        group = planes[first : first + GROUP]
        values = [get(x) for x in group]
        for x, value in zip(group, values):
            put(x, value)


class Level:
    def __init__(self, index, ny, nz, rim, velocity_ref, shift, f, r, w):
        self.ny, self.nz, self.rim = ny, nz, rim
        self.f, self.r, self.w = f, r, w
        spacing = 2.0**index
        scale_a = 1.0 / (spacing * spacing)
        inverse = 1.0 / spacing
        speed = [velocity_ref[d] for d in range(3)]
        self.backward = [scale_a + jnp.maximum(v, 0.0) * inverse for v in speed]
        self.forward = [scale_a - jnp.minimum(v, 0.0) * inverse for v in speed]
        total = jnp.abs(speed[0]) + jnp.abs(speed[1]) + jnp.abs(speed[2])
        self.centre = 6.0 * scale_a + total * inverse + shift
        lane = lax.broadcasted_iota(jnp.int32, (1, LANES), 1)
        inside = lane < nz
        self.low_z = jnp.where((lane > 0) & inside, self.backward[2], 0.0)
        self.high_z = jnp.where(lane < nz - 1, self.forward[2], 0.0)

    def plane(self, v, x):
        return v[x + self.rim, pl.ds(8, self.ny), :]

    def put(self, v):
        def write(x, value):
            v[x + self.rim, pl.ds(8, self.ny), :] = value

        return write

    def along_z(self, middle):
        return self.low_z * pltpu.roll(middle, 1, 1) + self.high_z * pltpu.roll(middle, LANES - 1, 1)

    def neighbours(self, v, x, middle):
        at, ny = x + self.rim, self.ny
        along_x = self.backward[0] * v[at - 1, pl.ds(8, ny), :] + self.forward[0] * v[at + 1, pl.ds(8, ny), :]
        along_y = self.backward[1] * v[at, pl.ds(7, ny), :] + self.forward[1] * v[at, pl.ds(9, ny), :]
        return along_x + along_y + self.along_z(middle)

    def smoothed(self, v, x):
        middle = self.plane(v, x)
        pulled = self.f[x] + self.neighbours(v, x, middle)
        return (1.0 - DAMPING) * middle + self.w[x] * pulled

    def smooth(self, src, dst, planes):
        sweep(planes, lambda x: self.smoothed(src, x), self.put(dst))

    def defect(self, v, x):
        middle = self.plane(v, x)
        pulled = self.f[x] + self.neighbours(v, x, middle)
        return pulled - (self.r[x] + self.centre) * middle

    def pool_rows(self, value, rows):
        half, ny = self.ny // 2, self.ny
        rows[pl.ds(0, ny), :] = value
        return rows[pl.ds(0, half, stride=2), :] + rows[pl.ds(1, half, stride=2), :]

    def spread_rows(self, part, rows):
        half, ny = self.ny // 2, self.ny
        rows[pl.ds(0, half, stride=2), :] = part
        rows[pl.ds(1, half, stride=2), :] = part
        return rows[pl.ds(0, ny), :]

    def solve_in_registers(self, rhs, reaction):
        row = lax.broadcasted_iota(jnp.int32, (self.ny, 1), 0)
        low_y = jnp.where(row > 0, self.backward[1], 0.0)
        high_y = jnp.where(row < self.ny - 1, self.forward[1], 0.0)
        weight = [DAMPING / (r + self.centre) for r in reaction]
        v = [w * f for w, f in zip(weight, rhs)]
        for _ in range(COARSE_SWEEPS - 1):
            new = []
            for x, here in enumerate(v):
                along_y = low_y * pltpu.roll(here, 1, 0) + high_y * pltpu.roll(here, self.ny - 1, 0)
                pulled = rhs[x] + self.along_z(here) + along_y
                if x > 0:
                    pulled += self.backward[0] * v[x - 1]
                if x < len(v) - 1:
                    pulled += self.forward[0] * v[x + 1]
                new.append((1.0 - DAMPING) * here + weight[x] * pulled)
            v = new
        return jnp.concatenate(v, axis=0)


def zero_rows(v, ny):
    edge = jnp.zeros((v.shape[0], 8, LANES), jnp.float32)
    v[:, pl.ds(0, 8), :] = edge
    v[:, pl.ds(8 + ny, 8), :] = edge


def pool_matrix(offset):
    row = lax.broadcasted_iota(jnp.int32, (LANES, LANES), 0)
    col = lax.broadcasted_iota(jnp.int32, (LANES, LANES), 1)
    return jnp.where(row // 2 + offset == col, 0.125, 0.0).astype(jnp.bfloat16)


def spread_matrix():
    row = lax.broadcasted_iota(jnp.int32, (LANES, LANES), 0)
    col = lax.broadcasted_iota(jnp.int32, (LANES, LANES), 1)
    return jnp.where(col // 2 == row, 1.0, 0.0).astype(jnp.bfloat16)


def pack_kernel(place_ref, source_ref, reaction_ref, out_ref, sems):
    columns = out_ref.shape[0] - 1
    other = jnp.bitwise_xor(place_ref[0], 1) & 1
    copies = [pltpu.make_async_copy(reaction_ref, out_ref.at[columns], sems.at[columns])]
    for i in range(columns):
        copies.append(pltpu.make_async_copy(source_ref.at[2 * i + other], out_ref.at[i], sems.at[i]))
    for copy in copies:
        copy.start()
    for copy in copies:
        copy.wait()


def merge_kernel(place_ref, source_ref, reaction_ref, theirs_ref, *out_refs):
    chip, core = place_ref[0] // 2, place_ref[0] & 1
    columns, by = theirs_ref.shape[0] - 1, source_ref.shape[2]
    mine = pl.ds(pl.multiple_of(core * by, 8), by)
    theirs = pl.ds(pl.multiple_of((1 - core) * by, 8), by)
    for m, out_ref in enumerate(out_refs):
        target = jnp.bitwise_xor(chip, m)
        out_ref[0, :, mine, :] = source_ref[2 * target + core]
        out_ref[0, :, theirs, :] = theirs_ref[target]
        out_ref[1, :, mine, :] = reaction_ref[...]
        out_ref[1, :, theirs, :] = theirs_ref[columns]


def squares_kernel(row, *refs):
    for k, part in enumerate(refs[:-1]):
        refs[-1][pl.ds(k, 1), :] = part[pl.ds(row, 1), :]


def pre_kernel(slabs, chips_y, place_ref, shifts_ref, index_ref, velocity_ref, *refs):
    pool_ref, pool_up_ref = refs[:2]
    parts, refs = refs[2:-8], refs[-8:]
    f, r, w, v1, coarse_ref, v0, tmp, pooled = refs
    ny = f.shape[1]
    chip, slab = place_ref[0] // 2, place_ref[1]
    shift = shifts_ref[index_ref[place_ref[0]]]
    fine = Level(0, ny, LANES, 0, velocity_ref, shift, f, r, w)
    zero_rows(v0, ny)
    zero_rows(v1, ny)
    count = SLAB + 2 * HALO

    chips = len(parts) // 2
    rows = parts[0].shape[2]
    for k, part in enumerate(parts):
        owner = jnp.bitwise_xor(chip, k % chips)
        x = owner // chips_y
        first = HALO * (1 + x) if k < chips else (HALO + SLAB) * (1 - x)
        to = pl.ds(pl.multiple_of(lax.rem(owner, chips_y) * rows, 8), rows)
        f[pl.ds(first, HALO), to, :] = part[0]
        r[pl.ds(first, HALO), to, :] = part[1]

    inside = [jnp.where(slab > 0, DAMPING, 0.0)] * HALO
    inside += [DAMPING] * SLAB
    inside += [jnp.where(slab < slabs - 1, DAMPING, 0.0)] * HALO

    def put(x, weight):
        w[x] = weight
        v0[x, pl.ds(8, ny), :] = weight * f[x]

    sweep(range(count), lambda x: inside[x] / (r[x] + fine.centre), put)
    fine.smooth(v0, v1, range(1, count - 1))
    half = ny // 2

    def coarsened(x):
        at = HALO + 2 * x
        return fine.defect(v1, at) + fine.defect(v1, at + 1), r[at] + r[at + 1]

    def put_pooled(x, pair):
        for n in range(2):
            pooled[n, pl.ds(x * half, half), :] = fine.pool_rows(pair[n], tmp.at[2 * x + n])

    sweep(range(SLAB // 2), coarsened, put_pooled)
    packed = split_dot(pooled[0], pool_ref[...]) + split_dot(pooled[1], pool_up_ref[...])
    coarse_ref[...] = packed.reshape(coarse_ref.shape)


def post_kernel(grid, gy_size, bx, by, place_ref, shifts_ref, index_ref, velocity_ref, *refs):
    slabs, nx, ny, nz = grid
    pool_ref, spread_ref, f, r, w, v1 = refs[:6]
    coarse = refs[6 : 6 + slabs]
    columns = SLAB // bx * gy_size
    out_refs = refs[6 + slabs : 6 + slabs + columns]
    va, vb, f1, r1, w1, v1a, v1b, pooled, tmp = refs[6 + slabs + columns :]
    pool, spread = pool_ref[...], spread_ref[...]
    slab = place_ref[1]
    shift = shifts_ref[index_ref[place_ref[0]]]
    rim = HALO // 2
    nx1, ny1, nx2, ny2 = nx // 2, ny // 2, nx // 4, ny // 4
    fine = Level(0, ny, nz, 0, velocity_ref, shift, f, r, w)
    mid = Level(1, ny1, nz // 2, rim, velocity_ref, shift, f1, r1, w1)
    deep = Level(2, ny2, nz // 4, 0, velocity_ref, shift, None, None, None)
    for v in (va, vb):
        zero_rows(v, ny)
    for v in (v1a, v1b):
        zero_rows(v, ny1)
        blank = jnp.zeros((rim,) + v.shape[1:], jnp.float32)
        v[pl.ds(0, rim)] = blank
        v[pl.ds(rim + nx1, rim)] = blank

    lower = lax.broadcasted_iota(jnp.int32, (1, LANES), 1) < LANES // 2
    own = SLAB // 2
    for k in range(slabs):
        first = jnp.bitwise_xor(slab, k) * own
        both = coarse[k][...]
        f1[pl.ds(first, own)] = jnp.where(lower, both, 0.0)
        r1[pl.ds(first, own)] = jnp.where(lower, pltpu.roll(both, LANES // 2, 2), 0.0)

    def put_start(x, weight):
        w1[x] = weight
        v1a[x + rim, pl.ds(8, ny1), :] = weight * f1[x]

    sweep(range(nx1), lambda x: DAMPING / (r1[x] + mid.centre), put_start)
    mid.smooth(v1a, v1b, range(nx1))

    def coarsened(x):
        return mid.defect(v1b, 2 * x) + mid.defect(v1b, 2 * x + 1), r1[2 * x] + r1[2 * x + 1]

    rows2 = nx2 * ny2

    def put_pooled(x, pair):
        for n in range(2):
            value = mid.pool_rows(pair[n], tmp.at[2 * x + n])
            pooled[pl.ds(n * rows2 + x * ny2, ny2), :] = value

    sweep(range(nx2), coarsened, put_pooled)
    deeper = split_dot(pooled[pl.ds(0, 2 * rows2), :], pool)
    planes = [deeper[n * ny2 : (n + 1) * ny2] for n in range(2 * nx2)]
    values = deep.solve_in_registers(planes[:nx2], planes[nx2:])

    pooled[pl.ds(0, rows2), :] = split_dot(values, spread)

    def refined1(x):
        return mid.spread_rows(pooled[pl.ds(x * ny2, ny2), :], tmp.at[x])

    def put_refined1(x, value):
        for n in range(2):
            v1b[2 * x + n + rim, pl.ds(8, ny1), :] += value

    sweep(range(nx2), refined1, put_refined1)
    mid.smooth(v1b, v1a, range(nx1))
    mid.smooth(v1a, v1b, range(nx1))

    window = own + 2 * rim
    values = v1b[pl.ds(slab * own, window), pl.ds(8, ny1), :].reshape(window * ny1, LANES)
    pooled[pl.ds(0, window * ny1), :] = split_dot(values, spread)
    count = SLAB + 2 * HALO

    def refined(x):
        return fine.spread_rows(pooled[pl.ds(x * ny1, ny1), :], tmp.at[x])

    def put_refined(x, value):
        for at in (2 * x, 2 * x + 1):
            if 0 < at < count - 1:
                va[at, pl.ds(8, ny), :] = v1[at, pl.ds(8, ny), :] + value

    sweep(range(window), refined, put_refined)
    fine.smooth(va, vb, range(2, count - 2))
    fine.smooth(vb, va, range(3, count - 3))

    total = jnp.zeros((8, LANES), jnp.float32)
    for x in range(SLAB):
        rest = fine.defect(va, HALO + x)
        total = total + jnp.sum((rest * rest).reshape(ny // 8, 8, LANES), axis=0)
        tmp[x] = rest
    squares = jnp.full((8, LANES), jnp.sum(total), jnp.float32)
    area = bx * by
    for k, out_ref in enumerate(out_refs):
        owner = jnp.bitwise_xor(place_ref[0], k)
        first = (owner // gy_size) * bx
        row = pl.multiple_of(lax.rem(owner, gy_size) * by, 8)
        for p in range(bx):
            out_ref[pl.ds(p * by, by), :] = va[HALO + first + p, pl.ds(8 + row, by), :]
            out_ref[pl.ds(area + p * by, by), :] = tmp[first + p, pl.ds(row, by), :]
        out_ref[pl.ds(2 * area, 8), :] = squares


def collect_kernel(bx, by, place_ref, *refs):
    parts, (iterate_ref, residual_ref) = refs[:-2], refs[-2:]
    area = bx * by
    for k, part in enumerate(parts):
        column = jnp.bitwise_xor(place_ref[0], k)
        iterate_ref[column] = part[pl.ds(0, area), :].reshape(bx, by, LANES)
        residual_ref[column] = part[pl.ds(area, area), :].reshape(bx, by, LANES)


HBM = pl.BlockSpec(memory_space=pltpu.HBM)
SMEM = pl.BlockSpec(memory_space=pltpu.SMEM)
VMEM = pl.BlockSpec(memory_space=pltpu.VMEM)


def local_kernel(kernel, name, scalars, arrays, outs, scratch=()):
    return pl.pallas_call(
        kernel,
        out_shape=[jax.ShapeDtypeStruct(shape, jnp.float32) for shape in outs],
        in_specs=[SMEM] * len(scalars) + [VMEM] * len(arrays),
        out_specs=[VMEM] * len(outs),
        scratch_shapes=[pltpu.VMEM(shape, jnp.float32) for shape in scratch],
        compiler_params=pltpu.CompilerParams(vmem_limit_bytes=VMEM_LIMIT),
        name=name,
    )(*scalars, *arrays)


def swap_in_plane(pieces, unit):
    devices = lax.axis_size("gx") * lax.axis_size("gy")
    moved = [pieces[0]]
    for k in range(1, len(pieces)):
        pairs = [(i, i ^ (k * unit)) for i in range(devices)]
        moved.append(lax.ppermute(pieces[k], ("gx", "gy"), pairs))
    return moved


def send_beside(pieces, columns, chips_y):
    devices = lax.axis_size("gx") * lax.axis_size("gy")
    moved = []
    for m, piece in enumerate(pieces):
        pairs = []
        for i in range(devices):
            up = (i % columns) // 2 // chips_y
            target = (i ^ (2 * m)) + (columns if up else -columns)
            if 0 <= target < devices:
                pairs.append((i, target))
        moved.append(lax.ppermute(piece, ("gx", "gy"), pairs))
    return moved


def swap_slabs(piece, step, slabs):
    size = lax.axis_size("gx")
    moved = [piece]
    for k in range(1, slabs):
        pairs = [(i, i ^ (k * step)) for i in range(size)]
        moved.append(lax.ppermute(piece, "gx", pairs))
    return moved


def column_body(source, reaction, shifts, shift_index, velocity):
    columns, bx, by, nz = source.shape
    gx_size, gy_size = lax.axis_size("gx"), lax.axis_size("gy")
    nx, ny = bx * gx_size, by * gy_size
    step = columns // gy_size
    slabs = gx_size // step
    along, across = lax.axis_index("gx"), lax.axis_index("gy")
    column = lax.rem(along, step) * gy_size + across
    place = jnp.stack([column, along // step]).astype(jnp.int32)
    scalars = (place, shifts, shift_index, velocity)
    count = SLAB + 2 * HALO
    area = bx * by

    chips, chips_y = columns // 2, gy_size // 2
    packed = pl.pallas_call(
        pack_kernel,
        out_shape=jax.ShapeDtypeStruct((chips + 1, bx, by, nz), jnp.float32),
        in_specs=[SMEM, HBM, HBM],
        out_specs=VMEM,
        scratch_shapes=[pltpu.SemaphoreType.DMA((chips + 1,))],
        compiler_params=pltpu.CompilerParams(vmem_limit_bytes=63 * 1024 * 1024),
        name="pack",
    )(place, source, reaction)
    theirs = lax.ppermute(packed, "gy", [(i, i ^ 1) for i in range(gy_size)])
    blocks = local_kernel(
        merge_kernel,
        "merge",
        (place,),
        (source, reaction, theirs),
        [(2, bx, 2 * by, nz)] * chips,
    )
    parts = swap_in_plane(blocks, 2) + send_beside(blocks, columns, chips_y)

    grid, rimmed = (count, ny, nz), (count, ny + 16, nz)
    f, r, w, v1, coarse = local_kernel(
        functools.partial(pre_kernel, slabs, chips_y),
        "pre",
        scalars,
        (pool_matrix(0), pool_matrix(LANES // 2), *parts),
        [grid, grid, grid, rimmed, (SLAB // 2, ny // 2, nz)],
        [rimmed, (SLAB, ny, nz), (2, SLAB // 2 * ny // 2, nz)],
    )
    gathered = swap_slabs(coarse, step, slabs)

    coarse_grid = (nx // 2, ny // 2, nz)
    coarse_rimmed = (nx // 2 + HALO, ny // 2 + 16, nz)
    rows = max((SLAB // 2 + HALO) * ny // 2, nx // 4 * ny // 2)
    results = local_kernel(
        functools.partial(post_kernel, (slabs, nx, ny, nz), gy_size, bx, by),
        "post",
        scalars,
        (pool_matrix(0), spread_matrix(), f, r, w, v1, *gathered),
        [(2 * area + 8, nz)] * columns,
        [rimmed] * 2 + [coarse_grid] * 3 + [coarse_rimmed] * 2 + [(rows, nz), (nx // 2, ny, nz)],
    )
    parts = swap_in_plane(results, 1)

    (squares,) = local_kernel(
        functools.partial(squares_kernel, 2 * area), "squares", (), parts, [(columns, nz)]
    )
    total = sum(swap_slabs(squares, step, slabs))
    rms = jnp.sqrt(total[:, 0] / (nx * ny * nz) + EPSILON)
    slots = jnp.arange(columns, dtype=jnp.int32)
    mine = jnp.bitwise_xor(slots, column)[None, :] == slots[:, None]
    residual_rms = jnp.sum(jnp.where(mine, rms[None, :], 0.0), axis=1)
    iterate, residual = local_kernel(
        functools.partial(collect_kernel, bx, by), "collect", (place,), parts, [source.shape] * 2
    )
    return iterate, residual, residual_rms


def power_of_two(n):
    return n > 0 and n & (n - 1) == 0


def column_plan_fits(columns, bx, by, nz, gx_size, gy_size):
    if columns % gy_size or gx_size % (columns // gy_size):
        return False
    step = columns // gy_size
    slabs, ny = gx_size // step, by * gy_size
    whole = power_of_two(columns) and power_of_two(step) and power_of_two(slabs)
    small = slabs * ny * nz <= 2**15
    paired = step == 2 and bx == HALO and gy_size % 2 == 0
    return whole and small and paired and bx * step == SLAB and nz == LANES and by % 16 == 0


def solution(mesh):
    gx_size, gy_size = mesh.shape["gx"], mesh.shape["gy"]

    def body(source, reaction, shifts, shift_index, velocity):
        fits = column_plan_fits(*source.shape, gx_size, gy_size)
        plan = column_body if fits else halo_body
        return plan(source, reaction, shifts, shift_index, velocity)

    return jax.shard_map(
        body,
        mesh=mesh,
        in_specs=(P(None, "gx", "gy", None), P("gx", "gy", None), P(), P(), P()),
        out_specs=(P(None, "gx", "gy", None), P(None, "gx", "gy", None), P()),
        check_vma=False,
    )
```

```python
import functools

import jax
import jax.numpy as jnp
from jax import lax
from jax.experimental import pallas as pl
from jax.experimental.pallas import tpu as pltpu
from jax.sharding import PartitionSpec as P

LEVELS = 3
COARSE_SWEEPS = 6

DAMPING = 0.8
EPSILON = 1e-06
VMEM_LIMIT = 32 * 1024 * 1024
LANES = 128
GROUP = 4
SLAB = 8
HALO = 4


def with_halo(x, sides, width):
    for axis, dim in sides:
        peers, length = (lax.axis_size(axis), x.shape[dim])
        up = [(i, (i + 1) % peers) for i in range(peers - 1)]
        down = [(j, i) for i, j in up]
        last = lax.slice_in_dim(x, length - width, length, axis=dim)
        leading = lax.slice_in_dim(x, 0, width, axis=dim)
        before = lax.ppermute(last, axis, up)
        after = lax.ppermute(leading, axis, down)
        x = jnp.concatenate([before, x, after], axis=dim)
    return x


def select_shifts(shifts, shift_index):
    columns = jnp.arange(shifts.shape[0], dtype=jnp.int32)
    picked = jnp.where(shift_index[:, None] == columns[None, :], shifts[None, :], 0.0)
    return jnp.sum(picked, axis=1)


def coefficients(velocity, spacing):
    scale_a = 1.0 / (spacing * spacing)
    backward = scale_a + jnp.maximum(velocity, 0.0) / spacing
    forward = scale_a - jnp.minimum(velocity, 0.0) / spacing
    centre = 6.0 * scale_a + jnp.sum(jnp.abs(velocity)) / spacing
    return (backward, forward, centre)


def apply_stencil(padded, backward, forward, diagonal):
    middle = padded[:, 1:-1, 1:-1, :]
    along_z = jnp.pad(middle, ((0, 0), (0, 0), (0, 0), (1, 1)))
    others = backward[0] * padded[:, :-2, 1:-1, :] + forward[0] * padded[:, 2:, 1:-1, :]
    others = others + backward[1] * padded[:, 1:-1, :-2, :] + forward[1] * padded[:, 1:-1, 2:, :]
    others = others + backward[2] * along_z[:, :, :, :-2] + forward[2] * along_z[:, :, :, 2:]
    return diagonal * middle - others


def face_halo(iterate):
    return with_halo(iterate, (("gx", 1), ("gy", 2)), 1)


def coarsen(values):
    count, size_x, size_y, size_z = values.shape
    blocks = values.reshape(count, size_x // 2, 2, size_y // 2, 2, size_z // 2, 2)
    return jnp.sum(blocks, axis=(2, 4, 6)) * 0.125


def refine(values):
    return jnp.repeat(jnp.repeat(jnp.repeat(values, 2, 1), 2, 2), 2, 3)


def coarsest_solve(rhs_field, backward, forward, diagonal):
    iterate = DAMPING * rhs_field / diagonal
    for repeat in range(COARSE_SWEEPS - 1):
        applied = apply_stencil(face_halo(iterate), backward, forward, diagonal)
        iterate = iterate + DAMPING * (rhs_field - applied) / diagonal
    return iterate


def multigrid_cycle(level_index, rhs_field, reaction_l, shift_value, velocity):
    backward, forward, centre = coefficients(velocity, 2.0**level_index)
    diagonal = centre + reaction_l + shift_value[:, None, None, None]
    if level_index == LEVELS - 1:
        return coarsest_solve(rhs_field, backward, forward, diagonal)

    def operate(iterate):
        return apply_stencil(face_halo(iterate), backward, forward, diagonal)

    def smooth_step(iterate):
        return iterate + DAMPING * (rhs_field - operate(iterate)) / diagonal

    iterate = DAMPING * rhs_field / diagonal
    iterate = smooth_step(iterate)
    defect = rhs_field - operate(iterate)
    correction = multigrid_cycle(
        level_index + 1, coarsen(defect), coarsen(reaction_l), shift_value, velocity
    )
    iterate = iterate + refine(correction)
    iterate = smooth_step(iterate)
    iterate = smooth_step(iterate)
    return iterate


def halo_body(source, reaction, shifts, shift_index, velocity):
    columns, cells_x, cells_y, cells_z = source.shape
    shift_value = select_shifts(shifts, shift_index)
    reaction_top = reaction[None]
    backward, forward, centre = coefficients(velocity, 1.0)
    diagonal = centre + reaction_top + shift_value[:, None, None, None]

    iterate = multigrid_cycle(0, source, reaction_top, shift_value, velocity)
    residual = source - apply_stencil(face_halo(iterate), backward, forward, diagonal)
    local_squares = jnp.sum(residual * residual, axis=(1, 2, 3))
    squares = lax.psum(local_squares, ("gx", "gy"))
    total_cells = cells_x * cells_y * cells_z * lax.axis_size("gx") * lax.axis_size("gy")
    residual_rms = jnp.sqrt(squares / total_cells + EPSILON)
    return (iterate, residual, residual_rms)


def split_dot(values, matrix):
    high = values.astype(jnp.bfloat16)
    low = (values - high.astype(jnp.float32)).astype(jnp.bfloat16)
    return jnp.dot(high, matrix, preferred_element_type=jnp.float32) + jnp.dot(
        low, matrix, preferred_element_type=jnp.float32
    )


def sweep(planes, get, put):
    planes = list(planes)
    for first in range(0, len(planes), GROUP):
        group = planes[first : first + GROUP]
        values = [get(x) for x in group]
        for x, value in zip(group, values):
            put(x, value)


class Level:
    def __init__(self, index, ny, nz, rim, scalar_ref, f, r, w):
        self.ny, self.nz, self.rim = ny, nz, rim
        self.f, self.r, self.w = f, r, w
        spacing = 2.0**index
        scale_a = 1.0 / (spacing * spacing)
        inverse = 1.0 / spacing
        shift = scalar_ref[0, 0]
        speed = [scalar_ref[1 + d, 0] for d in range(3)]
        self.backward = [scale_a + jnp.maximum(v, 0.0) * inverse for v in speed]
        self.forward = [scale_a - jnp.minimum(v, 0.0) * inverse for v in speed]
        total = jnp.abs(speed[0]) + jnp.abs(speed[1]) + jnp.abs(speed[2])
        self.centre = 6.0 * scale_a + total * inverse + shift
        lane = lax.broadcasted_iota(jnp.int32, (1, LANES), 1)
        inside = lane < nz
        self.low_z = jnp.where((lane > 0) & inside, self.backward[2], 0.0)
        self.high_z = jnp.where(lane < nz - 1, self.forward[2], 0.0)

    def plane(self, v, x):
        return v[x + self.rim, pl.ds(8, self.ny), :]

    def put(self, v):
        def write(x, value):
            v[x + self.rim, pl.ds(8, self.ny), :] = value

        return write

    def along_z(self, middle):
        return self.low_z * pltpu.roll(middle, 1, 1) + self.high_z * pltpu.roll(middle, LANES - 1, 1)

    def neighbours(self, v, x, middle):
        at, ny = x + self.rim, self.ny
        along_x = self.backward[0] * v[at - 1, pl.ds(8, ny), :] + self.forward[0] * v[at + 1, pl.ds(8, ny), :]
        along_y = self.backward[1] * v[at, pl.ds(7, ny), :] + self.forward[1] * v[at, pl.ds(9, ny), :]
        return along_x + along_y + self.along_z(middle)

    def smoothed(self, v, x):
        middle = self.plane(v, x)
        pulled = self.f[x] + self.neighbours(v, x, middle)
        return (1.0 - DAMPING) * middle + self.w[x] * pulled

    def smooth(self, src, dst, planes):
        sweep(planes, lambda x: self.smoothed(src, x), self.put(dst))

    def defect(self, v, x):
        middle = self.plane(v, x)
        pulled = self.f[x] + self.neighbours(v, x, middle)
        return pulled - (self.r[x] + self.centre) * middle

    def pool_rows(self, value, rows):
        half, ny = self.ny // 2, self.ny
        rows[pl.ds(0, ny), :] = value
        return rows[pl.ds(0, half, stride=2), :] + rows[pl.ds(1, half, stride=2), :]

    def spread_rows(self, part, rows):
        half, ny = self.ny // 2, self.ny
        rows[pl.ds(0, half, stride=2), :] = part
        rows[pl.ds(1, half, stride=2), :] = part
        return rows[pl.ds(0, ny), :]

    def solve_in_registers(self, rhs, reaction):
        row = lax.broadcasted_iota(jnp.int32, (self.ny, 1), 0)
        low_y = jnp.where(row > 0, self.backward[1], 0.0)
        high_y = jnp.where(row < self.ny - 1, self.forward[1], 0.0)
        weight = [DAMPING / (r + self.centre) for r in reaction]
        v = [w * f for w, f in zip(weight, rhs)]
        for _ in range(COARSE_SWEEPS - 1):
            new = []
            for x, here in enumerate(v):
                along_y = low_y * pltpu.roll(here, 1, 0) + high_y * pltpu.roll(here, self.ny - 1, 0)
                pulled = rhs[x] + self.along_z(here) + along_y
                if x > 0:
                    pulled += self.backward[0] * v[x - 1]
                if x < len(v) - 1:
                    pulled += self.forward[0] * v[x + 1]
                new.append((1.0 - DAMPING) * here + weight[x] * pulled)
            v = new
        return jnp.concatenate(v, axis=0)


def zero_rows(v, ny):
    edge = jnp.zeros((v.shape[0], 8, LANES), jnp.float32)
    v[:, pl.ds(0, 8), :] = edge
    v[:, pl.ds(8 + ny, 8), :] = edge


def pool_matrix(offset):
    row = lax.broadcasted_iota(jnp.int32, (LANES, LANES), 0)
    col = lax.broadcasted_iota(jnp.int32, (LANES, LANES), 1)
    return jnp.where(row // 2 + offset == col, 0.125, 0.0).astype(jnp.bfloat16)


def spread_matrix():
    row = lax.broadcasted_iota(jnp.int32, (LANES, LANES), 0)
    col = lax.broadcasted_iota(jnp.int32, (LANES, LANES), 1)
    return jnp.where(col // 2 == row, 1.0, 0.0).astype(jnp.bfloat16)


def pack_kernel(first, place_ref, source_ref, reaction_ref, *out_refs):
    for k, out_ref in enumerate(out_refs):
        out_ref[0] = source_ref[jnp.bitwise_xor(place_ref[0], first + k)]
        out_ref[1] = reaction_ref[...]


def pack_rest_kernel(first, place_ref, shifts_ref, index_ref, velocity_ref, source_ref, reaction_ref, _, *refs):
    pack_kernel(first, place_ref, source_ref, reaction_ref, *refs[:-1])
    scalars = [shifts_ref[index_ref[place_ref[0]]]] + [velocity_ref[d] for d in range(3)]
    for n, scalar in enumerate(scalars):
        refs[-1][pl.ds(n, 1), :] = jnp.full((1, LANES), scalar, jnp.float32)


def arrange_kernel(gy_size, first, place_ref, *refs):
    half_ref = refs[-1]
    for k, piece in enumerate(refs[:-1]):
        owner = jnp.bitwise_xor(place_ref[0], first + k)
        by = piece.shape[2]
        rows = pl.ds(pl.multiple_of(lax.rem(owner, gy_size) * by, 8), by)
        half_ref[:, :, rows, :] = piece[...]


def pre_kernel(slabs, gy_size, place_ref, scalar_ref, *refs):
    pool_ref, pool_up_ref = refs[:2]
    parts = refs[2:6]
    f, r, w, v1, coarse_ref, v0, tmp, pooled = refs[6:]
    ny = f.shape[1]
    slab = place_ref[1]
    fine = Level(0, ny, LANES, 0, scalar_ref, f, r, w)
    zero_rows(v0, ny)
    zero_rows(v1, ny)
    count = SLAB + 2 * HALO
    inside = [jnp.where(slab > 0, DAMPING, 0.0)] * HALO
    inside += [DAMPING] * SLAB
    inside += [jnp.where(slab < slabs - 1, DAMPING, 0.0)] * HALO

    x = place_ref[0] // gy_size
    firsts = (HALO * (1 + x), HALO * (2 - x), (HALO + SLAB) * (1 - x), (HALO + SLAB) * x)
    for part, first in zip(parts, firsts):
        f[pl.ds(first, HALO)] = part[0]
        r[pl.ds(first, HALO)] = part[1]

    def put(x, weight):
        w[x] = weight
        v0[x, pl.ds(8, ny), :] = weight * f[x]

    sweep(range(count), lambda x: inside[x] / (r[x] + fine.centre), put)
    fine.smooth(v0, v1, range(1, count - 1))
    half = ny // 2

    def coarsened(x):
        at = HALO + 2 * x
        return fine.defect(v1, at) + fine.defect(v1, at + 1), r[at] + r[at + 1]

    def put_pooled(x, pair):
        for n in range(2):
            pooled[n, pl.ds(x * half, half), :] = fine.pool_rows(pair[n], tmp.at[2 * x + n])

    sweep(range(SLAB // 2), coarsened, put_pooled)
    packed = split_dot(pooled[0], pool_ref[...]) + split_dot(pooled[1], pool_up_ref[...])
    coarse_ref[...] = packed.reshape(coarse_ref.shape)


def post_kernel(grid, gy_size, bx, by, place_ref, scalar_ref, *refs):
    slabs, nx, ny, nz = grid
    pool_ref, spread_ref, f, r, w, v1 = refs[:6]
    coarse = refs[6 : 6 + slabs]
    columns = SLAB // bx * gy_size
    out_refs = refs[6 + slabs : 6 + slabs + columns]
    va, vb, f1, r1, w1, v1a, v1b, pooled, tmp = refs[6 + slabs + columns :]
    pool, spread = pool_ref[...], spread_ref[...]
    slab = place_ref[1]
    rim = HALO // 2
    nx1, ny1, nx2, ny2 = nx // 2, ny // 2, nx // 4, ny // 4
    fine = Level(0, ny, nz, 0, scalar_ref, f, r, w)
    mid = Level(1, ny1, nz // 2, rim, scalar_ref, f1, r1, w1)
    deep = Level(2, ny2, nz // 4, 0, scalar_ref, None, None, None)
    for v in (va, vb):
        zero_rows(v, ny)
    for v in (v1a, v1b):
        zero_rows(v, ny1)
        blank = jnp.zeros((rim,) + v.shape[1:], jnp.float32)
        v[pl.ds(0, rim)] = blank
        v[pl.ds(rim + nx1, rim)] = blank

    lower = lax.broadcasted_iota(jnp.int32, (1, LANES), 1) < LANES // 2
    own = SLAB // 2
    for k in range(slabs):
        first = jnp.bitwise_xor(slab, k) * own
        both = coarse[k][...]
        f1[pl.ds(first, own)] = jnp.where(lower, both, 0.0)
        r1[pl.ds(first, own)] = jnp.where(lower, pltpu.roll(both, LANES // 2, 2), 0.0)

    def put_start(x, weight):
        w1[x] = weight
        v1a[x + rim, pl.ds(8, ny1), :] = weight * f1[x]

    sweep(range(nx1), lambda x: DAMPING / (r1[x] + mid.centre), put_start)
    mid.smooth(v1a, v1b, range(nx1))

    def coarsened(x):
        return mid.defect(v1b, 2 * x) + mid.defect(v1b, 2 * x + 1), r1[2 * x] + r1[2 * x + 1]

    rows2 = nx2 * ny2

    def put_pooled(x, pair):
        for n in range(2):
            value = mid.pool_rows(pair[n], tmp.at[2 * x + n])
            pooled[pl.ds(n * rows2 + x * ny2, ny2), :] = value

    sweep(range(nx2), coarsened, put_pooled)
    deeper = split_dot(pooled[pl.ds(0, 2 * rows2), :], pool)
    planes = [deeper[n * ny2 : (n + 1) * ny2] for n in range(2 * nx2)]
    values = deep.solve_in_registers(planes[:nx2], planes[nx2:])

    pooled[pl.ds(0, rows2), :] = split_dot(values, spread)

    def refined1(x):
        return mid.spread_rows(pooled[pl.ds(x * ny2, ny2), :], tmp.at[x])

    def put_refined1(x, value):
        for n in range(2):
            v1b[2 * x + n + rim, pl.ds(8, ny1), :] += value

    sweep(range(nx2), refined1, put_refined1)
    mid.smooth(v1b, v1a, range(nx1))
    mid.smooth(v1a, v1b, range(nx1))

    window = own + 2 * rim
    values = v1b[pl.ds(slab * own, window), pl.ds(8, ny1), :].reshape(window * ny1, LANES)
    pooled[pl.ds(0, window * ny1), :] = split_dot(values, spread)
    count = SLAB + 2 * HALO

    def refined(x):
        return fine.spread_rows(pooled[pl.ds(x * ny1, ny1), :], tmp.at[x])

    def put_refined(x, value):
        for at in (2 * x, 2 * x + 1):
            if 0 < at < count - 1:
                va[at, pl.ds(8, ny), :] = v1[at, pl.ds(8, ny), :] + value

    sweep(range(window), refined, put_refined)
    fine.smooth(va, vb, range(2, count - 2))
    fine.smooth(vb, va, range(3, count - 3))

    total = jnp.zeros((8, LANES), jnp.float32)
    for x in range(SLAB):
        rest = fine.defect(va, HALO + x)
        total = total + jnp.sum((rest * rest).reshape(ny // 8, 8, LANES), axis=0)
        tmp[x] = rest
    squares = jnp.full((8, LANES), jnp.sum(total), jnp.float32)
    area = bx * by
    for k, out_ref in enumerate(out_refs):
        owner = jnp.bitwise_xor(place_ref[0], k)
        first = (owner // gy_size) * bx
        row = pl.multiple_of(lax.rem(owner, gy_size) * by, 8)
        for p in range(bx):
            out_ref[pl.ds(p * by, by), :] = va[HALO + first + p, pl.ds(8 + row, by), :]
            out_ref[pl.ds(area + p * by, by), :] = tmp[first + p, pl.ds(row, by), :]
        out_ref[pl.ds(2 * area, 8), :] = squares


def collect_kernel(bx, by, place_ref, *refs):
    parts, (iterate_ref, residual_ref) = refs[:-2], refs[-2:]
    area = bx * by
    for k, part in enumerate(parts):
        column = jnp.bitwise_xor(place_ref[0], k)
        iterate_ref[column] = part[pl.ds(0, area), :].reshape(bx, by, LANES)
        residual_ref[column] = part[pl.ds(area, area), :].reshape(bx, by, LANES)


def squares_kernel(row, *refs):
    for k, part in enumerate(refs[:-1]):
        refs[-1][pl.ds(k, 1), :] = part[pl.ds(row, 1), :]


SMEM = pl.BlockSpec(memory_space=pltpu.SMEM)
VMEM = pl.BlockSpec(memory_space=pltpu.VMEM)


def local_kernel(kernel, name, scalars, arrays, outs, scratch=()):
    return pl.pallas_call(
        kernel,
        out_shape=[jax.ShapeDtypeStruct(shape, jnp.float32) for shape in outs],
        in_specs=[SMEM] * len(scalars) + [VMEM] * len(arrays),
        out_specs=[VMEM] * len(outs),
        scratch_shapes=[pltpu.VMEM(shape, jnp.float32) for shape in scratch],
        compiler_params=pltpu.CompilerParams(vmem_limit_bytes=VMEM_LIMIT),
        name=name,
    )(*scalars, *arrays)


def swap_in_plane(pieces, first):
    devices = lax.axis_size("gx") * lax.axis_size("gy")
    moved = []
    for k, piece in enumerate(pieces, first):
        pairs = [(i, i ^ k) for i in range(devices)]
        moved.append(lax.ppermute(piece, ("gx", "gy"), pairs) if k else piece)
    return moved


def swap_slabs(piece, step, slabs):
    size = lax.axis_size("gx")
    moved = [piece]
    for k in range(1, slabs):
        pairs = [(i, i ^ (k * step)) for i in range(size)]
        moved.append(lax.ppermute(piece, "gx", pairs))
    return moved


def column_body(source, reaction, shifts, shift_index, velocity):
    columns, bx, by, nz = source.shape
    gx_size, gy_size = lax.axis_size("gx"), lax.axis_size("gy")
    nx, ny = bx * gx_size, by * gy_size
    step = columns // gy_size
    slabs = gx_size // step
    along, across = lax.axis_index("gx"), lax.axis_index("gy")
    column = lax.rem(along, step) * gy_size + across
    place = jnp.stack([column, along // step]).astype(jnp.int32)
    count = SLAB + 2 * HALO
    area = bx * by

    piece = (2, bx, by, nz)
    pieces = local_kernel(
        functools.partial(pack_kernel, 0), "pack", (place,), (source, reaction), [piece] * gy_size
    )
    pieces = swap_in_plane(pieces, 0)
    *rest, scalar_rows = local_kernel(
        functools.partial(pack_rest_kernel, gy_size),
        "pack_rest",
        (place, shifts, shift_index, velocity),
        (source, reaction, pieces[1]),
        [piece] * gy_size + [(8, LANES)],
    )
    scalars = (place, scalar_rows)
    pieces = pieces + swap_in_plane(rest, gy_size)
    halves, beside = [], []
    for n in range(2):
        first = n * gy_size
        (half,) = local_kernel(
            functools.partial(arrange_kernel, gy_size, first),
            "arrange",
            (place,),
            pieces[first : first + gy_size],
            [(2, HALO, ny, nz)],
        )
        pairs = []
        for i in range(gx_size):
            target = i + step if i % step != n else i - step
            if 0 <= target < gx_size:
                pairs.append((i, target))
        halves.append(half)
        beside.append(lax.ppermute(half, "gx", pairs))

    grid, rimmed = (count, ny, nz), (count, ny + 16, nz)
    f, r, w, v1, coarse = local_kernel(
        functools.partial(pre_kernel, slabs, gy_size),
        "pre",
        scalars,
        (pool_matrix(0), pool_matrix(LANES // 2), *halves, *beside),
        [grid, grid, grid, rimmed, (SLAB // 2, ny // 2, nz)],
        [rimmed, (SLAB, ny, nz), (2, SLAB // 2 * ny // 2, nz)],
    )
    gathered = swap_slabs(coarse, step, slabs)

    coarse_grid = (nx // 2, ny // 2, nz)
    coarse_rimmed = (nx // 2 + HALO, ny // 2 + 16, nz)
    rows = max((SLAB // 2 + HALO) * ny // 2, nx // 4 * ny // 2)
    results = local_kernel(
        functools.partial(post_kernel, (slabs, nx, ny, nz), gy_size, bx, by),
        "post",
        scalars,
        (pool_matrix(0), spread_matrix(), f, r, w, v1, *gathered),
        [(2 * area + 8, nz)] * columns,
        [rimmed] * 2 + [coarse_grid] * 3 + [coarse_rimmed] * 2 + [(rows, nz), (nx // 2, ny, nz)],
    )
    parts = swap_in_plane(results, 0)

    (squares,) = local_kernel(
        functools.partial(squares_kernel, 2 * area), "squares", (), parts, [(columns, nz)]
    )
    total = sum(swap_slabs(squares, step, slabs))
    rms = jnp.sqrt(total[:, 0] / (nx * ny * nz) + EPSILON)
    slots = jnp.arange(columns, dtype=jnp.int32)
    mine = jnp.bitwise_xor(slots, column)[None, :] == slots[:, None]
    residual_rms = jnp.sum(jnp.where(mine, rms[None, :], 0.0), axis=1)
    iterate, residual = local_kernel(
        functools.partial(collect_kernel, bx, by), "collect", (place,), parts, [source.shape] * 2
    )
    return iterate, residual, residual_rms


def power_of_two(n):
    return n > 0 and n & (n - 1) == 0


def column_plan_fits(columns, bx, by, nz, gx_size, gy_size):
    if columns % gy_size or gx_size % (columns // gy_size):
        return False
    step = columns // gy_size
    slabs, ny = gx_size // step, by * gy_size
    whole = power_of_two(columns) and power_of_two(step) and power_of_two(slabs)
    small = slabs * ny * nz <= 2**15
    paired = step == 2 and bx == HALO
    return whole and small and paired and bx * step == SLAB and nz == LANES and by % 16 == 0


def solution(mesh):
    gx_size, gy_size = mesh.shape["gx"], mesh.shape["gy"]

    def body(source, reaction, shifts, shift_index, velocity):
        fits = column_plan_fits(*source.shape, gx_size, gy_size)
        plan = column_body if fits else halo_body
        return plan(source, reaction, shifts, shift_index, velocity)

    return jax.shard_map(
        body,
        mesh=mesh,
        in_specs=(P(None, "gx", "gy", None), P("gx", "gy", None), P(), P(), P()),
        out_specs=(P(None, "gx", "gy", None), P(None, "gx", "gy", None), P()),
        check_vma=False,
    )
```

```python
import functools

import jax
import jax.numpy as jnp
from jax import lax
from jax.experimental import pallas as pl
from jax.experimental.pallas import tpu as pltpu
from jax.sharding import PartitionSpec as P

LEVELS = 3
COARSE_SWEEPS = 6

DAMPING = 0.8
EPSILON = 1e-06
VMEM_LIMIT = 32 * 1024 * 1024
LANES = 128
GROUP = 4
SLAB = 8
HALO = 4


def with_halo(x, sides, width):
    for axis, dim in sides:
        peers, length = (lax.axis_size(axis), x.shape[dim])
        up = [(i, (i + 1) % peers) for i in range(peers - 1)]
        down = [(j, i) for i, j in up]
        last = lax.slice_in_dim(x, length - width, length, axis=dim)
        leading = lax.slice_in_dim(x, 0, width, axis=dim)
        before = lax.ppermute(last, axis, up)
        after = lax.ppermute(leading, axis, down)
        x = jnp.concatenate([before, x, after], axis=dim)
    return x


def select_shifts(shifts, shift_index):
    columns = jnp.arange(shifts.shape[0], dtype=jnp.int32)
    picked = jnp.where(shift_index[:, None] == columns[None, :], shifts[None, :], 0.0)
    return jnp.sum(picked, axis=1)


def coefficients(velocity, spacing):
    scale_a = 1.0 / (spacing * spacing)
    backward = scale_a + jnp.maximum(velocity, 0.0) / spacing
    forward = scale_a - jnp.minimum(velocity, 0.0) / spacing
    centre = 6.0 * scale_a + jnp.sum(jnp.abs(velocity)) / spacing
    return (backward, forward, centre)


def apply_stencil(padded, backward, forward, diagonal):
    middle = padded[:, 1:-1, 1:-1, :]
    along_z = jnp.pad(middle, ((0, 0), (0, 0), (0, 0), (1, 1)))
    others = backward[0] * padded[:, :-2, 1:-1, :] + forward[0] * padded[:, 2:, 1:-1, :]
    others = others + backward[1] * padded[:, 1:-1, :-2, :] + forward[1] * padded[:, 1:-1, 2:, :]
    others = others + backward[2] * along_z[:, :, :, :-2] + forward[2] * along_z[:, :, :, 2:]
    return diagonal * middle - others


def face_halo(iterate):
    return with_halo(iterate, (("gx", 1), ("gy", 2)), 1)


def coarsen(values):
    count, size_x, size_y, size_z = values.shape
    blocks = values.reshape(count, size_x // 2, 2, size_y // 2, 2, size_z // 2, 2)
    return jnp.sum(blocks, axis=(2, 4, 6)) * 0.125


def refine(values):
    return jnp.repeat(jnp.repeat(jnp.repeat(values, 2, 1), 2, 2), 2, 3)


def coarsest_solve(rhs_field, backward, forward, diagonal):
    iterate = DAMPING * rhs_field / diagonal
    for repeat in range(COARSE_SWEEPS - 1):
        applied = apply_stencil(face_halo(iterate), backward, forward, diagonal)
        iterate = iterate + DAMPING * (rhs_field - applied) / diagonal
    return iterate


def multigrid_cycle(level_index, rhs_field, reaction_l, shift_value, velocity):
    backward, forward, centre = coefficients(velocity, 2.0**level_index)
    diagonal = centre + reaction_l + shift_value[:, None, None, None]
    if level_index == LEVELS - 1:
        return coarsest_solve(rhs_field, backward, forward, diagonal)

    def operate(iterate):
        return apply_stencil(face_halo(iterate), backward, forward, diagonal)

    def smooth_step(iterate):
        return iterate + DAMPING * (rhs_field - operate(iterate)) / diagonal

    iterate = DAMPING * rhs_field / diagonal
    iterate = smooth_step(iterate)
    defect = rhs_field - operate(iterate)
    correction = multigrid_cycle(
        level_index + 1, coarsen(defect), coarsen(reaction_l), shift_value, velocity
    )
    iterate = iterate + refine(correction)
    iterate = smooth_step(iterate)
    iterate = smooth_step(iterate)
    return iterate


def halo_body(source, reaction, shifts, shift_index, velocity):
    columns, cells_x, cells_y, cells_z = source.shape
    shift_value = select_shifts(shifts, shift_index)
    reaction_top = reaction[None]
    backward, forward, centre = coefficients(velocity, 1.0)
    diagonal = centre + reaction_top + shift_value[:, None, None, None]

    iterate = multigrid_cycle(0, source, reaction_top, shift_value, velocity)
    residual = source - apply_stencil(face_halo(iterate), backward, forward, diagonal)
    local_squares = jnp.sum(residual * residual, axis=(1, 2, 3))
    squares = lax.psum(local_squares, ("gx", "gy"))
    total_cells = cells_x * cells_y * cells_z * lax.axis_size("gx") * lax.axis_size("gy")
    residual_rms = jnp.sqrt(squares / total_cells + EPSILON)
    return (iterate, residual, residual_rms)


def split_dot(values, matrix):
    high = values.astype(jnp.bfloat16)
    low = (values - high.astype(jnp.float32)).astype(jnp.bfloat16)
    return jnp.dot(high, matrix, preferred_element_type=jnp.float32) + jnp.dot(
        low, matrix, preferred_element_type=jnp.float32
    )


def sweep(planes, get, put):
    planes = list(planes)
    for first in range(0, len(planes), GROUP):
        group = planes[first : first + GROUP]
        values = [get(x) for x in group]
        for x, value in zip(group, values):
            put(x, value)


class Level:
    def __init__(self, index, ny, nz, rim, scalar_ref, f, r, w):
        self.ny, self.nz, self.rim = ny, nz, rim
        self.f, self.r, self.w = f, r, w
        spacing = 2.0**index
        scale_a = 1.0 / (spacing * spacing)
        inverse = 1.0 / spacing
        shift = scalar_ref[0, 0]
        speed = [scalar_ref[1 + d, 0] for d in range(3)]
        self.backward = [scale_a + jnp.maximum(v, 0.0) * inverse for v in speed]
        self.forward = [scale_a - jnp.minimum(v, 0.0) * inverse for v in speed]
        total = jnp.abs(speed[0]) + jnp.abs(speed[1]) + jnp.abs(speed[2])
        self.centre = 6.0 * scale_a + total * inverse + shift
        lane = lax.broadcasted_iota(jnp.int32, (1, LANES), 1)
        inside = lane < nz
        self.low_z = jnp.where((lane > 0) & inside, self.backward[2], 0.0)
        self.high_z = jnp.where(lane < nz - 1, self.forward[2], 0.0)

    def plane(self, v, x):
        return v[x + self.rim, pl.ds(8, self.ny), :]

    def put(self, v):
        def write(x, value):
            v[x + self.rim, pl.ds(8, self.ny), :] = value

        return write

    def along_z(self, middle):
        return self.low_z * pltpu.roll(middle, 1, 1) + self.high_z * pltpu.roll(middle, LANES - 1, 1)

    def neighbours(self, v, x, middle):
        at, ny = x + self.rim, self.ny
        along_x = self.backward[0] * v[at - 1, pl.ds(8, ny), :] + self.forward[0] * v[at + 1, pl.ds(8, ny), :]
        along_y = self.backward[1] * v[at, pl.ds(7, ny), :] + self.forward[1] * v[at, pl.ds(9, ny), :]
        return along_x + along_y + self.along_z(middle)

    def smoothed(self, v, x):
        middle = self.plane(v, x)
        pulled = self.f[x] + self.neighbours(v, x, middle)
        return (1.0 - DAMPING) * middle + self.w[x] * pulled

    def smooth(self, src, dst, planes):
        sweep(planes, lambda x: self.smoothed(src, x), self.put(dst))

    def defect(self, v, x):
        middle = self.plane(v, x)
        pulled = self.f[x] + self.neighbours(v, x, middle)
        return pulled - (self.r[x] + self.centre) * middle

    def pool_rows(self, value, rows):
        half, ny = self.ny // 2, self.ny
        rows[pl.ds(0, ny), :] = value
        return rows[pl.ds(0, half, stride=2), :] + rows[pl.ds(1, half, stride=2), :]

    def spread_rows(self, part, rows):
        half, ny = self.ny // 2, self.ny
        rows[pl.ds(0, half, stride=2), :] = part
        rows[pl.ds(1, half, stride=2), :] = part
        return rows[pl.ds(0, ny), :]

    def solve_in_registers(self, rhs, reaction):
        row = lax.broadcasted_iota(jnp.int32, (self.ny, 1), 0)
        low_y = jnp.where(row > 0, self.backward[1], 0.0)
        high_y = jnp.where(row < self.ny - 1, self.forward[1], 0.0)
        weight = [DAMPING / (r + self.centre) for r in reaction]
        v = [w * f for w, f in zip(weight, rhs)]
        for _ in range(COARSE_SWEEPS - 1):
            new = []
            for x, here in enumerate(v):
                along_y = low_y * pltpu.roll(here, 1, 0) + high_y * pltpu.roll(here, self.ny - 1, 0)
                pulled = rhs[x] + self.along_z(here) + along_y
                if x > 0:
                    pulled += self.backward[0] * v[x - 1]
                if x < len(v) - 1:
                    pulled += self.forward[0] * v[x + 1]
                new.append((1.0 - DAMPING) * here + weight[x] * pulled)
            v = new
        return jnp.concatenate(v, axis=0)


def zero_rows(v, ny):
    edge = jnp.zeros((v.shape[0], 8, LANES), jnp.float32)
    v[:, pl.ds(0, 8), :] = edge
    v[:, pl.ds(8 + ny, 8), :] = edge


def pool_matrix(offset):
    row = lax.broadcasted_iota(jnp.int32, (LANES, LANES), 0)
    col = lax.broadcasted_iota(jnp.int32, (LANES, LANES), 1)
    return jnp.where(row // 2 + offset == col, 0.125, 0.0).astype(jnp.bfloat16)


def spread_matrix():
    row = lax.broadcasted_iota(jnp.int32, (LANES, LANES), 0)
    col = lax.broadcasted_iota(jnp.int32, (LANES, LANES), 1)
    return jnp.where(col // 2 == row, 1.0, 0.0).astype(jnp.bfloat16)


def merge_kernel(place_ref, shifts_ref, index_ref, velocity_ref, *refs):
    source_ref, reaction_ref, other_source_ref, other_reaction_ref = refs[:4]
    out_refs, scalar_ref = refs[4:-1], refs[-1]
    chip, core = place_ref[0] // 2, place_ref[0] & 1
    by = source_ref.shape[2]
    mine = pl.ds(pl.multiple_of(core * by, 8), by)
    theirs = pl.ds(pl.multiple_of((1 - core) * by, 8), by)
    for m, out_ref in enumerate(out_refs):
        column = 2 * jnp.bitwise_xor(chip, m) + core
        out_ref[0, :, mine, :] = source_ref[column]
        out_ref[0, :, theirs, :] = other_source_ref[column]
        out_ref[1, :, mine, :] = reaction_ref[...]
        out_ref[1, :, theirs, :] = other_reaction_ref[...]
    scalars = [shifts_ref[index_ref[place_ref[0]]]] + [velocity_ref[d] for d in range(3)]
    for n, scalar in enumerate(scalars):
        scalar_ref[pl.ds(n, 1), :] = jnp.full((1, LANES), scalar, jnp.float32)


def arrange_kernel(chips_y, first, place_ref, *refs):
    half_ref = refs[-1]
    for m, block in enumerate(refs[:-1]):
        owner = jnp.bitwise_xor(place_ref[0] // 2, first + m)
        size = block.shape[2]
        rows = pl.ds(pl.multiple_of(lax.rem(owner, chips_y) * size, 8), size)
        half_ref[:, :, rows, :] = block[...]


def pre_kernel(slabs, gy_size, place_ref, scalar_ref, *refs):
    pool_ref, pool_up_ref = refs[:2]
    parts = refs[2:6]
    f, r, w, v1, coarse_ref, v0, tmp, pooled = refs[6:]
    ny = f.shape[1]
    slab = place_ref[1]
    fine = Level(0, ny, LANES, 0, scalar_ref, f, r, w)
    zero_rows(v0, ny)
    zero_rows(v1, ny)
    count = SLAB + 2 * HALO
    inside = [jnp.where(slab > 0, DAMPING, 0.0)] * HALO
    inside += [DAMPING] * SLAB
    inside += [jnp.where(slab < slabs - 1, DAMPING, 0.0)] * HALO

    x = place_ref[0] // gy_size
    firsts = (HALO * (1 + x), HALO * (2 - x), (HALO + SLAB) * (1 - x), (HALO + SLAB) * x)
    for part, first in zip(parts, firsts):
        f[pl.ds(first, HALO)] = part[0]
        r[pl.ds(first, HALO)] = part[1]

    def put(x, weight):
        w[x] = weight
        v0[x, pl.ds(8, ny), :] = weight * f[x]

    sweep(range(count), lambda x: inside[x] / (r[x] + fine.centre), put)
    fine.smooth(v0, v1, range(1, count - 1))
    half = ny // 2

    def coarsened(x):
        at = HALO + 2 * x
        return fine.defect(v1, at) + fine.defect(v1, at + 1), r[at] + r[at + 1]

    def put_pooled(x, pair):
        for n in range(2):
            pooled[n, pl.ds(x * half, half), :] = fine.pool_rows(pair[n], tmp.at[2 * x + n])

    sweep(range(SLAB // 2), coarsened, put_pooled)
    packed = split_dot(pooled[0], pool_ref[...]) + split_dot(pooled[1], pool_up_ref[...])
    coarse_ref[...] = packed.reshape(coarse_ref.shape)


def post_kernel(grid, gy_size, bx, by, place_ref, scalar_ref, *refs):
    slabs, nx, ny, nz = grid
    pool_ref, spread_ref, f, r, w, v1 = refs[:6]
    coarse = refs[6 : 6 + slabs]
    columns = SLAB // bx * gy_size
    out_refs = refs[6 + slabs : 6 + slabs + columns]
    va, vb, f1, r1, w1, v1a, v1b, pooled, tmp = refs[6 + slabs + columns :]
    pool, spread = pool_ref[...], spread_ref[...]
    slab = place_ref[1]
    rim = HALO // 2
    nx1, ny1, nx2, ny2 = nx // 2, ny // 2, nx // 4, ny // 4
    fine = Level(0, ny, nz, 0, scalar_ref, f, r, w)
    mid = Level(1, ny1, nz // 2, rim, scalar_ref, f1, r1, w1)
    deep = Level(2, ny2, nz // 4, 0, scalar_ref, None, None, None)
    for v in (va, vb):
        zero_rows(v, ny)
    for v in (v1a, v1b):
        zero_rows(v, ny1)
        blank = jnp.zeros((rim,) + v.shape[1:], jnp.float32)
        v[pl.ds(0, rim)] = blank
        v[pl.ds(rim + nx1, rim)] = blank

    lower = lax.broadcasted_iota(jnp.int32, (1, LANES), 1) < LANES // 2
    own = SLAB // 2
    for k in range(slabs):
        first = jnp.bitwise_xor(slab, k) * own
        both = coarse[k][...]
        f1[pl.ds(first, own)] = jnp.where(lower, both, 0.0)
        r1[pl.ds(first, own)] = jnp.where(lower, pltpu.roll(both, LANES // 2, 2), 0.0)

    def put_start(x, weight):
        w1[x] = weight
        v1a[x + rim, pl.ds(8, ny1), :] = weight * f1[x]

    sweep(range(nx1), lambda x: DAMPING / (r1[x] + mid.centre), put_start)
    mid.smooth(v1a, v1b, range(nx1))

    def coarsened(x):
        return mid.defect(v1b, 2 * x) + mid.defect(v1b, 2 * x + 1), r1[2 * x] + r1[2 * x + 1]

    rows2 = nx2 * ny2

    def put_pooled(x, pair):
        for n in range(2):
            value = mid.pool_rows(pair[n], tmp.at[2 * x + n])
            pooled[pl.ds(n * rows2 + x * ny2, ny2), :] = value

    sweep(range(nx2), coarsened, put_pooled)
    deeper = split_dot(pooled[pl.ds(0, 2 * rows2), :], pool)
    planes = [deeper[n * ny2 : (n + 1) * ny2] for n in range(2 * nx2)]
    values = deep.solve_in_registers(planes[:nx2], planes[nx2:])

    pooled[pl.ds(0, rows2), :] = split_dot(values, spread)

    def refined1(x):
        return mid.spread_rows(pooled[pl.ds(x * ny2, ny2), :], tmp.at[x])

    def put_refined1(x, value):
        for n in range(2):
            v1b[2 * x + n + rim, pl.ds(8, ny1), :] += value

    sweep(range(nx2), refined1, put_refined1)
    mid.smooth(v1b, v1a, range(nx1))
    mid.smooth(v1a, v1b, range(nx1))

    window = own + 2 * rim
    values = v1b[pl.ds(slab * own, window), pl.ds(8, ny1), :].reshape(window * ny1, LANES)
    pooled[pl.ds(0, window * ny1), :] = split_dot(values, spread)
    count = SLAB + 2 * HALO

    def refined(x):
        return fine.spread_rows(pooled[pl.ds(x * ny1, ny1), :], tmp.at[x])

    def put_refined(x, value):
        for at in (2 * x, 2 * x + 1):
            if 0 < at < count - 1:
                va[at, pl.ds(8, ny), :] = v1[at, pl.ds(8, ny), :] + value

    sweep(range(window), refined, put_refined)
    fine.smooth(va, vb, range(2, count - 2))
    fine.smooth(vb, va, range(3, count - 3))

    total = jnp.zeros((8, LANES), jnp.float32)
    for x in range(SLAB):
        rest = fine.defect(va, HALO + x)
        total = total + jnp.sum((rest * rest).reshape(ny // 8, 8, LANES), axis=0)
        tmp[x] = rest
    squares = jnp.full((8, LANES), jnp.sum(total), jnp.float32)
    area = bx * by
    for k, out_ref in enumerate(out_refs):
        owner = jnp.bitwise_xor(place_ref[0], k)
        first = (owner // gy_size) * bx
        row = pl.multiple_of(lax.rem(owner, gy_size) * by, 8)
        for p in range(bx):
            out_ref[pl.ds(p * by, by), :] = va[HALO + first + p, pl.ds(8 + row, by), :]
            out_ref[pl.ds(area + p * by, by), :] = tmp[first + p, pl.ds(row, by), :]
        out_ref[pl.ds(2 * area, 8), :] = squares


def collect_kernel(bx, by, place_ref, *refs):
    parts, (iterate_ref, residual_ref) = refs[:-2], refs[-2:]
    area = bx * by
    for k, part in enumerate(parts):
        column = jnp.bitwise_xor(place_ref[0], k)
        iterate_ref[column] = part[pl.ds(0, area), :].reshape(bx, by, LANES)
        residual_ref[column] = part[pl.ds(area, area), :].reshape(bx, by, LANES)


def squares_kernel(row, *refs):
    for k, part in enumerate(refs[:-1]):
        refs[-1][pl.ds(k, 1), :] = part[pl.ds(row, 1), :]


SMEM = pl.BlockSpec(memory_space=pltpu.SMEM)
VMEM = pl.BlockSpec(memory_space=pltpu.VMEM)


def local_kernel(kernel, name, scalars, arrays, outs, scratch=()):
    return pl.pallas_call(
        kernel,
        out_shape=[jax.ShapeDtypeStruct(shape, jnp.float32) for shape in outs],
        in_specs=[SMEM] * len(scalars) + [VMEM] * len(arrays),
        out_specs=[VMEM] * len(outs),
        scratch_shapes=[pltpu.VMEM(shape, jnp.float32) for shape in scratch],
        compiler_params=pltpu.CompilerParams(vmem_limit_bytes=VMEM_LIMIT),
        name=name,
    )(*scalars, *arrays)


def swap_in_plane(pieces, unit):
    devices = lax.axis_size("gx") * lax.axis_size("gy")
    moved = [pieces[0]]
    for k in range(1, len(pieces)):
        pairs = [(i, i ^ (k * unit)) for i in range(devices)]
        moved.append(lax.ppermute(pieces[k], ("gx", "gy"), pairs))
    return moved


def swap_slabs(piece, step, slabs):
    size = lax.axis_size("gx")
    moved = [piece]
    for k in range(1, slabs):
        pairs = [(i, i ^ (k * step)) for i in range(size)]
        moved.append(lax.ppermute(piece, "gx", pairs))
    return moved


def column_body(source, reaction, shifts, shift_index, velocity):
    columns, bx, by, nz = source.shape
    gx_size, gy_size = lax.axis_size("gx"), lax.axis_size("gy")
    nx, ny = bx * gx_size, by * gy_size
    step = columns // gy_size
    slabs = gx_size // step
    along, across = lax.axis_index("gx"), lax.axis_index("gy")
    column = lax.rem(along, step) * gy_size + across
    place = jnp.stack([column, along // step]).astype(jnp.int32)
    count = SLAB + 2 * HALO
    area = bx * by

    chips, chips_y = columns // 2, gy_size // 2
    cores = [(i, i ^ 1) for i in range(gy_size)]
    others = [lax.ppermute(source, "gy", cores), lax.ppermute(reaction, "gy", cores)]
    *blocks, scalar_rows = local_kernel(
        merge_kernel,
        "merge",
        (place, shifts, shift_index, velocity),
        (source, reaction, *others),
        [(2, bx, 2 * by, nz)] * chips + [(8, LANES)],
    )
    scalars = (place, scalar_rows)
    blocks = swap_in_plane(blocks, 2)
    halves, beside = [], []
    for n in range(2):
        first = n * chips_y
        (half,) = local_kernel(
            functools.partial(arrange_kernel, chips_y, first),
            "arrange",
            (place,),
            blocks[first : first + chips_y],
            [(2, HALO, ny, nz)],
        )
        pairs = []
        for i in range(gx_size):
            target = i + step if i % step != n else i - step
            if 0 <= target < gx_size:
                pairs.append((i, target))
        halves.append(half)
        beside.append(lax.ppermute(half, "gx", pairs))

    grid, rimmed = (count, ny, nz), (count, ny + 16, nz)
    f, r, w, v1, coarse = local_kernel(
        functools.partial(pre_kernel, slabs, gy_size),
        "pre",
        scalars,
        (pool_matrix(0), pool_matrix(LANES // 2), *halves, *beside),
        [grid, grid, grid, rimmed, (SLAB // 2, ny // 2, nz)],
        [rimmed, (SLAB, ny, nz), (2, SLAB // 2 * ny // 2, nz)],
    )
    gathered = swap_slabs(coarse, step, slabs)

    coarse_grid = (nx // 2, ny // 2, nz)
    coarse_rimmed = (nx // 2 + HALO, ny // 2 + 16, nz)
    rows = max((SLAB // 2 + HALO) * ny // 2, nx // 4 * ny // 2)
    results = local_kernel(
        functools.partial(post_kernel, (slabs, nx, ny, nz), gy_size, bx, by),
        "post",
        scalars,
        (pool_matrix(0), spread_matrix(), f, r, w, v1, *gathered),
        [(2 * area + 8, nz)] * columns,
        [rimmed] * 2 + [coarse_grid] * 3 + [coarse_rimmed] * 2 + [(rows, nz), (nx // 2, ny, nz)],
    )
    parts = swap_in_plane(results, 1)

    (squares,) = local_kernel(
        functools.partial(squares_kernel, 2 * area), "squares", (), parts, [(columns, nz)]
    )
    total = sum(swap_slabs(squares, step, slabs))
    rms = jnp.sqrt(total[:, 0] / (nx * ny * nz) + EPSILON)
    slots = jnp.arange(columns, dtype=jnp.int32)
    mine = jnp.bitwise_xor(slots, column)[None, :] == slots[:, None]
    residual_rms = jnp.sum(jnp.where(mine, rms[None, :], 0.0), axis=1)
    iterate, residual = local_kernel(
        functools.partial(collect_kernel, bx, by), "collect", (place,), parts, [source.shape] * 2
    )
    return iterate, residual, residual_rms


def power_of_two(n):
    return n > 0 and n & (n - 1) == 0


def column_plan_fits(columns, bx, by, nz, gx_size, gy_size):
    if columns % gy_size or gx_size % (columns // gy_size):
        return False
    step = columns // gy_size
    slabs, ny = gx_size // step, by * gy_size
    whole = power_of_two(columns) and power_of_two(step) and power_of_two(slabs)
    small = slabs * ny * nz <= 2**15
    paired = step == 2 and bx == HALO and gy_size % 2 == 0
    return whole and small and paired and bx * step == SLAB and nz == LANES and by % 16 == 0


def solution(mesh):
    gx_size, gy_size = mesh.shape["gx"], mesh.shape["gy"]

    def body(source, reaction, shifts, shift_index, velocity):
        fits = column_plan_fits(*source.shape, gx_size, gy_size)
        plan = column_body if fits else halo_body
        return plan(source, reaction, shifts, shift_index, velocity)

    return jax.shard_map(
        body,
        mesh=mesh,
        in_specs=(P(None, "gx", "gy", None), P("gx", "gy", None), P(), P(), P()),
        out_specs=(P(None, "gx", "gy", None), P(None, "gx", "gy", None), P()),
        check_vma=False,
    )
```

```python
import functools

import jax
import jax.numpy as jnp
from jax import lax
from jax.experimental import pallas as pl
from jax.experimental.pallas import tpu as pltpu
from jax.sharding import PartitionSpec as P

LEVELS = 3
COARSE_SWEEPS = 6

DAMPING = 0.8
EPSILON = 1e-06
VMEM_LIMIT = 32 * 1024 * 1024
LANES = 128
GROUP = 4
SLAB = 8
HALO = 4


def with_halo(x, sides, width):
    for axis, dim in sides:
        peers, length = (lax.axis_size(axis), x.shape[dim])
        up = [(i, (i + 1) % peers) for i in range(peers - 1)]
        down = [(j, i) for i, j in up]
        last = lax.slice_in_dim(x, length - width, length, axis=dim)
        leading = lax.slice_in_dim(x, 0, width, axis=dim)
        before = lax.ppermute(last, axis, up)
        after = lax.ppermute(leading, axis, down)
        x = jnp.concatenate([before, x, after], axis=dim)
    return x


def select_shifts(shifts, shift_index):
    columns = jnp.arange(shifts.shape[0], dtype=jnp.int32)
    picked = jnp.where(shift_index[:, None] == columns[None, :], shifts[None, :], 0.0)
    return jnp.sum(picked, axis=1)


def coefficients(velocity, spacing):
    scale_a = 1.0 / (spacing * spacing)
    backward = scale_a + jnp.maximum(velocity, 0.0) / spacing
    forward = scale_a - jnp.minimum(velocity, 0.0) / spacing
    centre = 6.0 * scale_a + jnp.sum(jnp.abs(velocity)) / spacing
    return (backward, forward, centre)


def apply_stencil(padded, backward, forward, diagonal):
    middle = padded[:, 1:-1, 1:-1, :]
    along_z = jnp.pad(middle, ((0, 0), (0, 0), (0, 0), (1, 1)))
    others = backward[0] * padded[:, :-2, 1:-1, :] + forward[0] * padded[:, 2:, 1:-1, :]
    others = others + backward[1] * padded[:, 1:-1, :-2, :] + forward[1] * padded[:, 1:-1, 2:, :]
    others = others + backward[2] * along_z[:, :, :, :-2] + forward[2] * along_z[:, :, :, 2:]
    return diagonal * middle - others


def face_halo(iterate):
    return with_halo(iterate, (("gx", 1), ("gy", 2)), 1)


def coarsen(values):
    count, size_x, size_y, size_z = values.shape
    blocks = values.reshape(count, size_x // 2, 2, size_y // 2, 2, size_z // 2, 2)
    return jnp.sum(blocks, axis=(2, 4, 6)) * 0.125


def refine(values):
    return jnp.repeat(jnp.repeat(jnp.repeat(values, 2, 1), 2, 2), 2, 3)


def coarsest_solve(rhs_field, backward, forward, diagonal):
    iterate = DAMPING * rhs_field / diagonal
    for repeat in range(COARSE_SWEEPS - 1):
        applied = apply_stencil(face_halo(iterate), backward, forward, diagonal)
        iterate = iterate + DAMPING * (rhs_field - applied) / diagonal
    return iterate


def multigrid_cycle(level_index, rhs_field, reaction_l, shift_value, velocity):
    backward, forward, centre = coefficients(velocity, 2.0**level_index)
    diagonal = centre + reaction_l + shift_value[:, None, None, None]
    if level_index == LEVELS - 1:
        return coarsest_solve(rhs_field, backward, forward, diagonal)

    def operate(iterate):
        return apply_stencil(face_halo(iterate), backward, forward, diagonal)

    def smooth_step(iterate):
        return iterate + DAMPING * (rhs_field - operate(iterate)) / diagonal

    iterate = DAMPING * rhs_field / diagonal
    iterate = smooth_step(iterate)
    defect = rhs_field - operate(iterate)
    correction = multigrid_cycle(
        level_index + 1, coarsen(defect), coarsen(reaction_l), shift_value, velocity
    )
    iterate = iterate + refine(correction)
    iterate = smooth_step(iterate)
    iterate = smooth_step(iterate)
    return iterate


def halo_body(source, reaction, shifts, shift_index, velocity):
    columns, cells_x, cells_y, cells_z = source.shape
    shift_value = select_shifts(shifts, shift_index)
    reaction_top = reaction[None]
    backward, forward, centre = coefficients(velocity, 1.0)
    diagonal = centre + reaction_top + shift_value[:, None, None, None]

    iterate = multigrid_cycle(0, source, reaction_top, shift_value, velocity)
    residual = source - apply_stencil(face_halo(iterate), backward, forward, diagonal)
    local_squares = jnp.sum(residual * residual, axis=(1, 2, 3))
    squares = lax.psum(local_squares, ("gx", "gy"))
    total_cells = cells_x * cells_y * cells_z * lax.axis_size("gx") * lax.axis_size("gy")
    residual_rms = jnp.sqrt(squares / total_cells + EPSILON)
    return (iterate, residual, residual_rms)


def split_dot(values, matrix):
    high = values.astype(jnp.bfloat16)
    low = (values - high.astype(jnp.float32)).astype(jnp.bfloat16)
    return jnp.dot(high, matrix, preferred_element_type=jnp.float32) + jnp.dot(
        low, matrix, preferred_element_type=jnp.float32
    )


def sweep(planes, get, put):
    planes = list(planes)
    for first in range(0, len(planes), GROUP):
        group = planes[first : first + GROUP]
        values = [get(x) for x in group]
        for x, value in zip(group, values):
            put(x, value)


class Level:
    def __init__(self, index, ny, nz, rim, scalar_ref, f, r, w):
        self.ny, self.nz, self.rim = ny, nz, rim
        self.f, self.r, self.w = f, r, w
        spacing = 2.0**index
        scale_a = 1.0 / (spacing * spacing)
        inverse = 1.0 / spacing
        shift = scalar_ref[0, 0]
        speed = [scalar_ref[1 + d, 0] for d in range(3)]
        self.backward = [scale_a + jnp.maximum(v, 0.0) * inverse for v in speed]
        self.forward = [scale_a - jnp.minimum(v, 0.0) * inverse for v in speed]
        total = jnp.abs(speed[0]) + jnp.abs(speed[1]) + jnp.abs(speed[2])
        self.centre = 6.0 * scale_a + total * inverse + shift
        lane = lax.broadcasted_iota(jnp.int32, (1, LANES), 1)
        inside = lane < nz
        self.low_z = jnp.where((lane > 0) & inside, self.backward[2], 0.0)
        self.high_z = jnp.where(lane < nz - 1, self.forward[2], 0.0)

    def plane(self, v, x):
        return v[x + self.rim, pl.ds(8, self.ny), :]

    def put(self, v):
        def write(x, value):
            v[x + self.rim, pl.ds(8, self.ny), :] = value

        return write

    def along_z(self, middle):
        return self.low_z * pltpu.roll(middle, 1, 1) + self.high_z * pltpu.roll(middle, LANES - 1, 1)

    def neighbours(self, v, x, middle):
        at, ny = x + self.rim, self.ny
        along_x = self.backward[0] * v[at - 1, pl.ds(8, ny), :] + self.forward[0] * v[at + 1, pl.ds(8, ny), :]
        along_y = self.backward[1] * v[at, pl.ds(7, ny), :] + self.forward[1] * v[at, pl.ds(9, ny), :]
        return along_x + along_y + self.along_z(middle)

    def smoothed(self, v, x):
        middle = self.plane(v, x)
        pulled = self.f[x] + self.neighbours(v, x, middle)
        return (1.0 - DAMPING) * middle + self.w[x] * pulled

    def smooth(self, src, dst, planes):
        sweep(planes, lambda x: self.smoothed(src, x), self.put(dst))

    def defect(self, v, x):
        middle = self.plane(v, x)
        pulled = self.f[x] + self.neighbours(v, x, middle)
        return pulled - (self.r[x] + self.centre) * middle

    def pool_rows(self, value, rows):
        half, ny = self.ny // 2, self.ny
        rows[pl.ds(0, ny), :] = value
        return rows[pl.ds(0, half, stride=2), :] + rows[pl.ds(1, half, stride=2), :]

    def spread_rows(self, part, rows):
        half, ny = self.ny // 2, self.ny
        rows[pl.ds(0, half, stride=2), :] = part
        rows[pl.ds(1, half, stride=2), :] = part
        return rows[pl.ds(0, ny), :]

    def solve_in_registers(self, rhs, reaction):
        row = lax.broadcasted_iota(jnp.int32, (self.ny, 1), 0)
        low_y = jnp.where(row > 0, self.backward[1], 0.0)
        high_y = jnp.where(row < self.ny - 1, self.forward[1], 0.0)
        weight = [DAMPING / (r + self.centre) for r in reaction]
        v = [w * f for w, f in zip(weight, rhs)]
        for _ in range(COARSE_SWEEPS - 1):
            new = []
            for x, here in enumerate(v):
                along_y = low_y * pltpu.roll(here, 1, 0) + high_y * pltpu.roll(here, self.ny - 1, 0)
                pulled = rhs[x] + self.along_z(here) + along_y
                if x > 0:
                    pulled += self.backward[0] * v[x - 1]
                if x < len(v) - 1:
                    pulled += self.forward[0] * v[x + 1]
                new.append((1.0 - DAMPING) * here + weight[x] * pulled)
            v = new
        return jnp.concatenate(v, axis=0)


def zero_rows(v, ny):
    edge = jnp.zeros((v.shape[0], 8, LANES), jnp.float32)
    v[:, pl.ds(0, 8), :] = edge
    v[:, pl.ds(8 + ny, 8), :] = edge


def pool_matrix(offset):
    row = lax.broadcasted_iota(jnp.int32, (LANES, LANES), 0)
    col = lax.broadcasted_iota(jnp.int32, (LANES, LANES), 1)
    return jnp.where(row // 2 + offset == col, 0.125, 0.0).astype(jnp.bfloat16)


def spread_matrix():
    row = lax.broadcasted_iota(jnp.int32, (LANES, LANES), 0)
    col = lax.broadcasted_iota(jnp.int32, (LANES, LANES), 1)
    return jnp.where(col // 2 == row, 1.0, 0.0).astype(jnp.bfloat16)


def merge_kernel(place_ref, mine_ref, theirs_ref, *out_refs):
    chip, core = place_ref[0] // 2, place_ref[0] & 1
    by = mine_ref.shape[2]
    for first, ref in ((core * by, mine_ref), ((1 - core) * by, theirs_ref)):
        rows = pl.ds(pl.multiple_of(first, 8), by)
        for m, out_ref in enumerate(out_refs):
            target = jnp.bitwise_xor(chip, m)
            whole = ref.shape[0] > len(out_refs) + 1
            out_ref[0, :, rows, :] = ref[2 * target + core if whole else target]
            out_ref[1, :, rows, :] = ref[ref.shape[0] - 1]


def pack_kernel(place_ref, block_ref, *refs):
    out_ref = refs[-1]
    other, chips = 1 - (place_ref[0] & 1), out_ref.shape[0] - 1
    for n in range(chips):
        out_ref[n] = block_ref[2 * n + other]
    out_ref[chips] = block_ref[2 * chips]


def scalars_kernel(place_ref, shifts_ref, index_ref, velocity_ref, out_ref):
    scalars = [shifts_ref[index_ref[place_ref[0]]]] + [velocity_ref[d] for d in range(3)]
    for n, scalar in enumerate(scalars):
        out_ref[pl.ds(n, 1), :] = jnp.full((1, LANES), scalar, jnp.float32)


def pre_kernel(slabs, chips_y, place_ref, scalar_ref, *refs):
    pool_ref, pool_up_ref = refs[:2]
    parts, refs = refs[2:-8], refs[-8:]
    f, r, w, v1, coarse_ref, v0, tmp, pooled = refs
    ny = f.shape[1]
    chip, slab = place_ref[0] // 2, place_ref[1]
    fine = Level(0, ny, LANES, 0, scalar_ref, f, r, w)
    zero_rows(v0, ny)
    zero_rows(v1, ny)
    count = SLAB + 2 * HALO
    inside = [jnp.where(slab > 0, DAMPING, 0.0)] * HALO
    inside += [DAMPING] * SLAB
    inside += [jnp.where(slab < slabs - 1, DAMPING, 0.0)] * HALO

    chips = len(parts) // 2
    rows = parts[0].shape[2]
    for k, part in enumerate(parts):
        owner = jnp.bitwise_xor(chip, k % chips)
        x = owner // chips_y
        first = HALO * (1 + x) if k < chips else (HALO + SLAB) * (1 - x)
        to = pl.ds(pl.multiple_of(lax.rem(owner, chips_y) * rows, 8), rows)
        f[pl.ds(first, HALO), to, :] = part[0]
        r[pl.ds(first, HALO), to, :] = part[1]

    def put(x, weight):
        w[x] = weight
        v0[x, pl.ds(8, ny), :] = weight * f[x]

    sweep(range(count), lambda x: inside[x] / (r[x] + fine.centre), put)
    fine.smooth(v0, v1, range(1, count - 1))
    half = ny // 2

    def coarsened(x):
        at = HALO + 2 * x
        return fine.defect(v1, at) + fine.defect(v1, at + 1), r[at] + r[at + 1]

    def put_pooled(x, pair):
        for n in range(2):
            pooled[n, pl.ds(x * half, half), :] = fine.pool_rows(pair[n], tmp.at[2 * x + n])

    sweep(range(SLAB // 2), coarsened, put_pooled)
    packed = split_dot(pooled[0], pool_ref[...]) + split_dot(pooled[1], pool_up_ref[...])
    coarse_ref[...] = packed.reshape(coarse_ref.shape)


def post_kernel(grid, gy_size, bx, by, place_ref, scalar_ref, *refs):
    slabs, nx, ny, nz = grid
    pool_ref, spread_ref, f, r, w, v1 = refs[:6]
    coarse = refs[6 : 6 + slabs]
    columns = SLAB // bx * gy_size
    out_refs = refs[6 + slabs : 6 + slabs + columns]
    va, vb, f1, r1, w1, v1a, v1b, pooled, tmp = refs[6 + slabs + columns :]
    pool, spread = pool_ref[...], spread_ref[...]
    slab = place_ref[1]
    rim = HALO // 2
    nx1, ny1, nx2, ny2 = nx // 2, ny // 2, nx // 4, ny // 4
    fine = Level(0, ny, nz, 0, scalar_ref, f, r, w)
    mid = Level(1, ny1, nz // 2, rim, scalar_ref, f1, r1, w1)
    deep = Level(2, ny2, nz // 4, 0, scalar_ref, None, None, None)
    for v in (va, vb):
        zero_rows(v, ny)
    for v in (v1a, v1b):
        zero_rows(v, ny1)
        blank = jnp.zeros((rim,) + v.shape[1:], jnp.float32)
        v[pl.ds(0, rim)] = blank
        v[pl.ds(rim + nx1, rim)] = blank

    lower = lax.broadcasted_iota(jnp.int32, (1, LANES), 1) < LANES // 2
    own = SLAB // 2
    for k in range(slabs):
        first = jnp.bitwise_xor(slab, k) * own
        both = coarse[k][...]
        f1[pl.ds(first, own)] = jnp.where(lower, both, 0.0)
        r1[pl.ds(first, own)] = jnp.where(lower, pltpu.roll(both, LANES // 2, 2), 0.0)

    def put_start(x, weight):
        w1[x] = weight
        v1a[x + rim, pl.ds(8, ny1), :] = weight * f1[x]

    sweep(range(nx1), lambda x: DAMPING / (r1[x] + mid.centre), put_start)
    mid.smooth(v1a, v1b, range(nx1))

    def coarsened(x):
        return mid.defect(v1b, 2 * x) + mid.defect(v1b, 2 * x + 1), r1[2 * x] + r1[2 * x + 1]

    rows2 = nx2 * ny2

    def put_pooled(x, pair):
        for n in range(2):
            value = mid.pool_rows(pair[n], tmp.at[2 * x + n])
            pooled[pl.ds(n * rows2 + x * ny2, ny2), :] = value

    sweep(range(nx2), coarsened, put_pooled)
    deeper = split_dot(pooled[pl.ds(0, 2 * rows2), :], pool)
    planes = [deeper[n * ny2 : (n + 1) * ny2] for n in range(2 * nx2)]
    values = deep.solve_in_registers(planes[:nx2], planes[nx2:])

    pooled[pl.ds(0, rows2), :] = split_dot(values, spread)

    def refined1(x):
        return mid.spread_rows(pooled[pl.ds(x * ny2, ny2), :], tmp.at[x])

    def put_refined1(x, value):
        for n in range(2):
            v1b[2 * x + n + rim, pl.ds(8, ny1), :] += value

    sweep(range(nx2), refined1, put_refined1)
    mid.smooth(v1b, v1a, range(nx1))
    mid.smooth(v1a, v1b, range(nx1))

    window = own + 2 * rim
    values = v1b[pl.ds(slab * own, window), pl.ds(8, ny1), :].reshape(window * ny1, LANES)
    pooled[pl.ds(0, window * ny1), :] = split_dot(values, spread)
    count = SLAB + 2 * HALO

    def refined(x):
        return fine.spread_rows(pooled[pl.ds(x * ny1, ny1), :], tmp.at[x])

    def put_refined(x, value):
        for at in (2 * x, 2 * x + 1):
            if 0 < at < count - 1:
                va[at, pl.ds(8, ny), :] = v1[at, pl.ds(8, ny), :] + value

    sweep(range(window), refined, put_refined)
    fine.smooth(va, vb, range(2, count - 2))
    fine.smooth(vb, va, range(3, count - 3))

    total = jnp.zeros((8, LANES), jnp.float32)
    for x in range(SLAB):
        rest = fine.defect(va, HALO + x)
        total = total + jnp.sum((rest * rest).reshape(ny // 8, 8, LANES), axis=0)
        tmp[x] = rest
    squares = jnp.full((8, LANES), jnp.sum(total), jnp.float32)
    area = bx * by
    for k, out_ref in enumerate(out_refs):
        owner = jnp.bitwise_xor(place_ref[0], k)
        first = (owner // gy_size) * bx
        row = pl.multiple_of(lax.rem(owner, gy_size) * by, 8)
        for p in range(bx):
            out_ref[pl.ds(p * by, by), :] = va[HALO + first + p, pl.ds(8 + row, by), :]
            out_ref[pl.ds(area + p * by, by), :] = tmp[first + p, pl.ds(row, by), :]
        out_ref[pl.ds(2 * area, 8), :] = squares


def collect_kernel(bx, by, place_ref, *refs):
    parts, (iterate_ref, residual_ref) = refs[:-2], refs[-2:]
    area = bx * by
    for k, part in enumerate(parts):
        column = jnp.bitwise_xor(place_ref[0], k)
        iterate_ref[column] = part[pl.ds(0, area), :].reshape(bx, by, LANES)
        residual_ref[column] = part[pl.ds(area, area), :].reshape(bx, by, LANES)


def squares_kernel(row, *refs):
    for k, part in enumerate(refs[:-1]):
        refs[-1][pl.ds(k, 1), :] = part[pl.ds(row, 1), :]


SMEM = pl.BlockSpec(memory_space=pltpu.SMEM)
VMEM = pl.BlockSpec(memory_space=pltpu.VMEM)


def local_kernel(kernel, name, scalars, arrays, outs, scratch=()):
    return pl.pallas_call(
        kernel,
        out_shape=[jax.ShapeDtypeStruct(shape, jnp.float32) for shape in outs],
        in_specs=[SMEM] * len(scalars) + [VMEM] * len(arrays),
        out_specs=[VMEM] * len(outs),
        scratch_shapes=[pltpu.VMEM(shape, jnp.float32) for shape in scratch],
        compiler_params=pltpu.CompilerParams(vmem_limit_bytes=VMEM_LIMIT),
        name=name,
    )(*scalars, *arrays)


def swap_in_plane(pieces, unit):
    devices = lax.axis_size("gx") * lax.axis_size("gy")
    moved = [pieces[0]]
    for k in range(1, len(pieces)):
        pairs = [(i, i ^ (k * unit)) for i in range(devices)]
        moved.append(lax.ppermute(pieces[k], ("gx", "gy"), pairs))
    return moved


def swap_slabs(piece, step, slabs):
    size = lax.axis_size("gx")
    moved = [piece]
    for k in range(1, slabs):
        pairs = [(i, i ^ (k * step)) for i in range(size)]
        moved.append(lax.ppermute(piece, "gx", pairs))
    return moved


def column_body(source, reaction, shifts, shift_index, velocity):
    columns, bx, by, nz = source.shape
    gx_size, gy_size = lax.axis_size("gx"), lax.axis_size("gy")
    nx, ny = bx * gx_size, by * gy_size
    step = columns // gy_size
    slabs = gx_size // step
    along, across = lax.axis_index("gx"), lax.axis_index("gy")
    column = lax.rem(along, step) * gy_size + across
    place = jnp.stack([column, along // step]).astype(jnp.int32)
    count = SLAB + 2 * HALO
    area = bx * by

    chips, chips_y = columns // 2, gy_size // 2
    cores = [(i, i ^ 1) for i in range(gy_size)]
    onward = [(i, i + step if i % step else i - step) for i in range(gx_size)]
    onward = [(i, j) for i, j in onward if 0 <= j < gx_size]

    def deal(block, sent):
        theirs = lax.ppermute(sent, "gy", cores)
        merged = local_kernel(
            merge_kernel, "merge", (place,), (block, theirs), [(2, bx, 2 * by, nz)] * chips
        )
        return swap_in_plane(merged, 2)

    joined = jnp.concatenate([source, reaction[None]])
    beside = lax.ppermute(joined, "gx", onward)
    parts = deal(joined, joined)
    (sent,) = local_kernel(
        pack_kernel, "pack", (place,), (beside, *parts[1:]), [(chips + 1, bx, by, nz)]
    )
    parts = parts + deal(beside, sent)
    (scalar_rows,) = local_kernel(
        scalars_kernel, "scalars", (place, shifts, shift_index, velocity), (), [(8, LANES)]
    )
    scalars = (place, scalar_rows)

    grid, rimmed = (count, ny, nz), (count, ny + 16, nz)
    f, r, w, v1, coarse = local_kernel(
        functools.partial(pre_kernel, slabs, chips_y),
        "pre",
        scalars,
        (pool_matrix(0), pool_matrix(LANES // 2), *parts),
        [grid, grid, grid, rimmed, (SLAB // 2, ny // 2, nz)],
        [rimmed, (SLAB, ny, nz), (2, SLAB // 2 * ny // 2, nz)],
    )
    gathered = swap_slabs(coarse, step, slabs)

    coarse_grid = (nx // 2, ny // 2, nz)
    coarse_rimmed = (nx // 2 + HALO, ny // 2 + 16, nz)
    rows = max((SLAB // 2 + HALO) * ny // 2, nx // 4 * ny // 2)
    results = local_kernel(
        functools.partial(post_kernel, (slabs, nx, ny, nz), gy_size, bx, by),
        "post",
        scalars,
        (pool_matrix(0), spread_matrix(), f, r, w, v1, *gathered),
        [(2 * area + 8, nz)] * columns,
        [rimmed] * 2 + [coarse_grid] * 3 + [coarse_rimmed] * 2 + [(rows, nz), (nx // 2, ny, nz)],
    )
    parts = swap_in_plane(results, 1)

    (squares,) = local_kernel(
        functools.partial(squares_kernel, 2 * area), "squares", (), parts, [(columns, nz)]
    )
    total = sum(swap_slabs(squares, step, slabs))
    rms = jnp.sqrt(total[:, 0] / (nx * ny * nz) + EPSILON)
    slots = jnp.arange(columns, dtype=jnp.int32)
    mine = jnp.bitwise_xor(slots, column)[None, :] == slots[:, None]
    residual_rms = jnp.sum(jnp.where(mine, rms[None, :], 0.0), axis=1)
    iterate, residual = local_kernel(
        functools.partial(collect_kernel, bx, by), "collect", (place,), parts, [source.shape] * 2
    )
    return iterate, residual, residual_rms


def power_of_two(n):
    return n > 0 and n & (n - 1) == 0


def column_plan_fits(columns, bx, by, nz, gx_size, gy_size):
    if columns % gy_size or gx_size % (columns // gy_size):
        return False
    step = columns // gy_size
    slabs, ny = gx_size // step, by * gy_size
    whole = power_of_two(columns) and power_of_two(step) and power_of_two(slabs)
    small = slabs * ny * nz <= 2**15
    paired = step == 2 and bx == HALO and gy_size % 2 == 0
    return whole and small and paired and bx * step == SLAB and nz == LANES and by % 16 == 0


def solution(mesh):
    gx_size, gy_size = mesh.shape["gx"], mesh.shape["gy"]

    def body(source, reaction, shifts, shift_index, velocity):
        fits = column_plan_fits(*source.shape, gx_size, gy_size)
        plan = column_body if fits else halo_body
        return plan(source, reaction, shifts, shift_index, velocity)

    return jax.shard_map(
        body,
        mesh=mesh,
        in_specs=(P(None, "gx", "gy", None), P("gx", "gy", None), P(), P(), P()),
        out_specs=(P(None, "gx", "gy", None), P(None, "gx", "gy", None), P()),
        check_vma=False,
    )
```

```python
import functools

import jax
import jax.numpy as jnp
from jax import lax
from jax.experimental import pallas as pl
from jax.experimental.pallas import tpu as pltpu
from jax.sharding import PartitionSpec as P

LEVELS = 3
COARSE_SWEEPS = 6

DAMPING = 0.8
EPSILON = 1e-06
VMEM_LIMIT = 32 * 1024 * 1024
LANES = 128
GROUP = 4
SLAB = 8
HALO = 4


def with_halo(x, sides, width):
    for axis, dim in sides:
        peers, length = (lax.axis_size(axis), x.shape[dim])
        up = [(i, (i + 1) % peers) for i in range(peers - 1)]
        down = [(j, i) for i, j in up]
        last = lax.slice_in_dim(x, length - width, length, axis=dim)
        leading = lax.slice_in_dim(x, 0, width, axis=dim)
        before = lax.ppermute(last, axis, up)
        after = lax.ppermute(leading, axis, down)
        x = jnp.concatenate([before, x, after], axis=dim)
    return x


def select_shifts(shifts, shift_index):
    columns = jnp.arange(shifts.shape[0], dtype=jnp.int32)
    picked = jnp.where(shift_index[:, None] == columns[None, :], shifts[None, :], 0.0)
    return jnp.sum(picked, axis=1)


def coefficients(velocity, spacing):
    scale_a = 1.0 / (spacing * spacing)
    backward = scale_a + jnp.maximum(velocity, 0.0) / spacing
    forward = scale_a - jnp.minimum(velocity, 0.0) / spacing
    centre = 6.0 * scale_a + jnp.sum(jnp.abs(velocity)) / spacing
    return (backward, forward, centre)


def apply_stencil(padded, backward, forward, diagonal):
    middle = padded[:, 1:-1, 1:-1, :]
    along_z = jnp.pad(middle, ((0, 0), (0, 0), (0, 0), (1, 1)))
    others = backward[0] * padded[:, :-2, 1:-1, :] + forward[0] * padded[:, 2:, 1:-1, :]
    others = others + backward[1] * padded[:, 1:-1, :-2, :] + forward[1] * padded[:, 1:-1, 2:, :]
    others = others + backward[2] * along_z[:, :, :, :-2] + forward[2] * along_z[:, :, :, 2:]
    return diagonal * middle - others


def face_halo(iterate):
    return with_halo(iterate, (("gx", 1), ("gy", 2)), 1)


def coarsen(values):
    count, size_x, size_y, size_z = values.shape
    blocks = values.reshape(count, size_x // 2, 2, size_y // 2, 2, size_z // 2, 2)
    return jnp.sum(blocks, axis=(2, 4, 6)) * 0.125


def refine(values):
    return jnp.repeat(jnp.repeat(jnp.repeat(values, 2, 1), 2, 2), 2, 3)


def coarsest_solve(rhs_field, backward, forward, diagonal):
    iterate = DAMPING * rhs_field / diagonal
    for repeat in range(COARSE_SWEEPS - 1):
        applied = apply_stencil(face_halo(iterate), backward, forward, diagonal)
        iterate = iterate + DAMPING * (rhs_field - applied) / diagonal
    return iterate


def multigrid_cycle(level_index, rhs_field, reaction_l, shift_value, velocity):
    backward, forward, centre = coefficients(velocity, 2.0**level_index)
    diagonal = centre + reaction_l + shift_value[:, None, None, None]
    if level_index == LEVELS - 1:
        return coarsest_solve(rhs_field, backward, forward, diagonal)

    def operate(iterate):
        return apply_stencil(face_halo(iterate), backward, forward, diagonal)

    def smooth_step(iterate):
        return iterate + DAMPING * (rhs_field - operate(iterate)) / diagonal

    iterate = DAMPING * rhs_field / diagonal
    iterate = smooth_step(iterate)
    defect = rhs_field - operate(iterate)
    correction = multigrid_cycle(
        level_index + 1, coarsen(defect), coarsen(reaction_l), shift_value, velocity
    )
    iterate = iterate + refine(correction)
    iterate = smooth_step(iterate)
    iterate = smooth_step(iterate)
    return iterate


def halo_body(source, reaction, shifts, shift_index, velocity):
    columns, cells_x, cells_y, cells_z = source.shape
    shift_value = select_shifts(shifts, shift_index)
    reaction_top = reaction[None]
    backward, forward, centre = coefficients(velocity, 1.0)
    diagonal = centre + reaction_top + shift_value[:, None, None, None]

    iterate = multigrid_cycle(0, source, reaction_top, shift_value, velocity)
    residual = source - apply_stencil(face_halo(iterate), backward, forward, diagonal)
    local_squares = jnp.sum(residual * residual, axis=(1, 2, 3))
    squares = lax.psum(local_squares, ("gx", "gy"))
    total_cells = cells_x * cells_y * cells_z * lax.axis_size("gx") * lax.axis_size("gy")
    residual_rms = jnp.sqrt(squares / total_cells + EPSILON)
    return (iterate, residual, residual_rms)


def split_dot(values, matrix):
    high = values.astype(jnp.bfloat16)
    low = (values - high.astype(jnp.float32)).astype(jnp.bfloat16)
    return jnp.dot(high, matrix, preferred_element_type=jnp.float32) + jnp.dot(
        low, matrix, preferred_element_type=jnp.float32
    )


def sweep(planes, get, put):
    planes = list(planes)
    for first in range(0, len(planes), GROUP):
        group = planes[first : first + GROUP]
        values = [get(x) for x in group]
        for x, value in zip(group, values):
            put(x, value)


class Level:
    def __init__(self, index, ny, nz, rim, scalar_ref, f, r, w):
        self.ny, self.nz, self.rim = ny, nz, rim
        self.f, self.r, self.w = f, r, w
        spacing = 2.0**index
        scale_a = 1.0 / (spacing * spacing)
        inverse = 1.0 / spacing
        shift = scalar_ref[0, 0]
        speed = [scalar_ref[1 + d, 0] for d in range(3)]
        self.backward = [scale_a + jnp.maximum(v, 0.0) * inverse for v in speed]
        self.forward = [scale_a - jnp.minimum(v, 0.0) * inverse for v in speed]
        total = jnp.abs(speed[0]) + jnp.abs(speed[1]) + jnp.abs(speed[2])
        self.centre = 6.0 * scale_a + total * inverse + shift
        lane = lax.broadcasted_iota(jnp.int32, (1, LANES), 1)
        inside = lane < nz
        self.low_z = jnp.where((lane > 0) & inside, self.backward[2], 0.0)
        self.high_z = jnp.where(lane < nz - 1, self.forward[2], 0.0)

    def plane(self, v, x):
        return v[x + self.rim, pl.ds(8, self.ny), :]

    def put(self, v):
        def write(x, value):
            v[x + self.rim, pl.ds(8, self.ny), :] = value

        return write

    def along_z(self, middle):
        return self.low_z * pltpu.roll(middle, 1, 1) + self.high_z * pltpu.roll(middle, LANES - 1, 1)

    def neighbours(self, v, x, middle):
        at, ny = x + self.rim, self.ny
        along_x = self.backward[0] * v[at - 1, pl.ds(8, ny), :] + self.forward[0] * v[at + 1, pl.ds(8, ny), :]
        along_y = self.backward[1] * v[at, pl.ds(7, ny), :] + self.forward[1] * v[at, pl.ds(9, ny), :]
        return along_x + along_y + self.along_z(middle)

    def smoothed(self, v, x):
        middle = self.plane(v, x)
        pulled = self.f[x] + self.neighbours(v, x, middle)
        return (1.0 - DAMPING) * middle + self.w[x] * pulled

    def smooth(self, src, dst, planes):
        sweep(planes, lambda x: self.smoothed(src, x), self.put(dst))

    def defect(self, v, x):
        middle = self.plane(v, x)
        pulled = self.f[x] + self.neighbours(v, x, middle)
        return pulled - (self.r[x] + self.centre) * middle

    def pool_rows(self, value, rows):
        half, ny = self.ny // 2, self.ny
        rows[pl.ds(0, ny), :] = value
        return rows[pl.ds(0, half, stride=2), :] + rows[pl.ds(1, half, stride=2), :]

    def spread_rows(self, part, rows):
        half, ny = self.ny // 2, self.ny
        rows[pl.ds(0, half, stride=2), :] = part
        rows[pl.ds(1, half, stride=2), :] = part
        return rows[pl.ds(0, ny), :]

    def solve_in_registers(self, rhs, reaction):
        row = lax.broadcasted_iota(jnp.int32, (self.ny, 1), 0)
        low_y = jnp.where(row > 0, self.backward[1], 0.0)
        high_y = jnp.where(row < self.ny - 1, self.forward[1], 0.0)
        weight = [DAMPING / (r + self.centre) for r in reaction]
        v = [w * f for w, f in zip(weight, rhs)]
        for _ in range(COARSE_SWEEPS - 1):
            new = []
            for x, here in enumerate(v):
                along_y = low_y * pltpu.roll(here, 1, 0) + high_y * pltpu.roll(here, self.ny - 1, 0)
                pulled = rhs[x] + self.along_z(here) + along_y
                if x > 0:
                    pulled += self.backward[0] * v[x - 1]
                if x < len(v) - 1:
                    pulled += self.forward[0] * v[x + 1]
                new.append((1.0 - DAMPING) * here + weight[x] * pulled)
            v = new
        return jnp.concatenate(v, axis=0)


def zero_rows(v, ny):
    edge = jnp.zeros((v.shape[0], 8, LANES), jnp.float32)
    v[:, pl.ds(0, 8), :] = edge
    v[:, pl.ds(8 + ny, 8), :] = edge


def pool_matrix(offset):
    row = lax.broadcasted_iota(jnp.int32, (LANES, LANES), 0)
    col = lax.broadcasted_iota(jnp.int32, (LANES, LANES), 1)
    return jnp.where(row // 2 + offset == col, 0.125, 0.0).astype(jnp.bfloat16)


def spread_matrix():
    row = lax.broadcasted_iota(jnp.int32, (LANES, LANES), 0)
    col = lax.broadcasted_iota(jnp.int32, (LANES, LANES), 1)
    return jnp.where(col // 2 == row, 1.0, 0.0).astype(jnp.bfloat16)


def keep_kernel(place_ref, source_ref, out_ref):
    for n in range(out_ref.shape[0]):
        out_ref[n] = source_ref[2 * n + (place_ref[0] & 1)]


def merge_kernel(place_ref, shifts_ref, index_ref, velocity_ref, *refs):
    mine_ref, theirs_ref, reaction_ref, beside_ref = refs[:4]
    out_refs, scalar_ref = refs[4:-1], refs[-1]
    chip, core = place_ref[0] // 2, place_ref[0] & 1
    by = mine_ref.shape[2]
    mine = pl.ds(pl.multiple_of(core * by, 8), by)
    theirs = pl.ds(pl.multiple_of((1 - core) * by, 8), by)
    for m, out_ref in enumerate(out_refs):
        target = jnp.bitwise_xor(chip, m)
        out_ref[:, mine, :] = mine_ref[target]
        out_ref[:, theirs, :] = theirs_ref[2 * target + core]
        out_ref[:, pl.ds(2 * by, by), :] = reaction_ref[...]
        out_ref[:, pl.ds(3 * by, by), :] = beside_ref[...]
    scalars = [shifts_ref[index_ref[place_ref[0]]]] + [velocity_ref[d] for d in range(3)]
    for n, scalar in enumerate(scalars):
        scalar_ref[pl.ds(n, 1), :] = jnp.full((1, LANES), scalar, jnp.float32)


def arrange_kernel(chips_y, place_ref, *refs):
    blocks, (first_ref, second_ref, reaction_ref, halves) = refs[:-4], refs[-4:]
    by = blocks[0].shape[1] // 4
    for m, block in enumerate(blocks):
        owner = jnp.bitwise_xor(place_ref[0] // 2, m)
        x, y = owner // chips_y, lax.rem(owner, chips_y)
        rows = pl.ds(pl.multiple_of(2 * y * by, 8), 2 * by)
        halves[x, :, rows, :] = block[:, pl.ds(0, 2 * by), :]
        rows = pl.ds(pl.multiple_of(y * by, 8), by)
        reaction_ref[pl.ds(HALO * (1 + x), HALO), rows, :] = block[:, pl.ds(2 * by, by), :]
        reaction_ref[pl.ds((HALO + SLAB) * (1 - x), HALO), rows, :] = block[:, pl.ds(3 * by, by), :]
    even = 1 - (place_ref[1] & 1)
    first_ref[...] = halves[even]
    second_ref[...] = halves[1 - even]


def pre_kernel(slabs, gy_size, by, place_ref, scalar_ref, *refs):
    pool_ref, pool_up_ref = refs[:2]
    parts, reactions = refs[2:6], refs[6:8]
    f, r, w, v1, coarse_ref, v0, tmp, pooled = refs[8:]
    ny = f.shape[1]
    slab = place_ref[1]
    fine = Level(0, ny, LANES, 0, scalar_ref, f, r, w)
    zero_rows(v0, ny)
    zero_rows(v1, ny)
    count = SLAB + 2 * HALO
    inside = [jnp.where(slab > 0, DAMPING, 0.0)] * HALO
    inside += [DAMPING] * SLAB
    inside += [jnp.where(slab < slabs - 1, DAMPING, 0.0)] * HALO

    even = 1 - (slab & 1)
    firsts = (HALO * (1 + even), HALO * (2 - even), (HALO + SLAB) * even, (HALO + SLAB) * (1 - even))
    for part, first in zip(parts, firsts):
        f[pl.ds(first, HALO)] = part[...]
    core = place_ref[0] & 1
    for n, reaction in enumerate(reactions):
        for y in range(gy_size // 2):
            to = pl.multiple_of((2 * y + jnp.bitwise_xor(core, n)) * by, 8)
            r[:, pl.ds(to, by), :] = reaction[:, pl.ds(y * by, by), :]

    def put(x, weight):
        w[x] = weight
        v0[x, pl.ds(8, ny), :] = weight * f[x]

    sweep(range(count), lambda x: inside[x] / (r[x] + fine.centre), put)
    fine.smooth(v0, v1, range(1, count - 1))
    half = ny // 2

    def coarsened(x):
        at = HALO + 2 * x
        return fine.defect(v1, at) + fine.defect(v1, at + 1), r[at] + r[at + 1]

    def put_pooled(x, pair):
        for n in range(2):
            pooled[n, pl.ds(x * half, half), :] = fine.pool_rows(pair[n], tmp.at[2 * x + n])

    sweep(range(SLAB // 2), coarsened, put_pooled)
    packed = split_dot(pooled[0], pool_ref[...]) + split_dot(pooled[1], pool_up_ref[...])
    coarse_ref[...] = packed.reshape(coarse_ref.shape)


def post_kernel(grid, gy_size, bx, by, place_ref, scalar_ref, *refs):
    slabs, nx, ny, nz = grid
    pool_ref, spread_ref, f, r, w, v1 = refs[:6]
    coarse = refs[6 : 6 + slabs]
    columns = SLAB // bx * gy_size
    out_refs = refs[6 + slabs : 6 + slabs + columns]
    va, vb, f1, r1, w1, v1a, v1b, pooled, tmp = refs[6 + slabs + columns :]
    pool, spread = pool_ref[...], spread_ref[...]
    slab = place_ref[1]
    rim = HALO // 2
    nx1, ny1, nx2, ny2 = nx // 2, ny // 2, nx // 4, ny // 4
    fine = Level(0, ny, nz, 0, scalar_ref, f, r, w)
    mid = Level(1, ny1, nz // 2, rim, scalar_ref, f1, r1, w1)
    deep = Level(2, ny2, nz // 4, 0, scalar_ref, None, None, None)
    for v in (va, vb):
        zero_rows(v, ny)
    for v in (v1a, v1b):
        zero_rows(v, ny1)
        blank = jnp.zeros((rim,) + v.shape[1:], jnp.float32)
        v[pl.ds(0, rim)] = blank
        v[pl.ds(rim + nx1, rim)] = blank

    lower = lax.broadcasted_iota(jnp.int32, (1, LANES), 1) < LANES // 2
    own = SLAB // 2
    for k in range(slabs):
        first = jnp.bitwise_xor(slab, k) * own
        both = coarse[k][...]
        f1[pl.ds(first, own)] = jnp.where(lower, both, 0.0)
        r1[pl.ds(first, own)] = jnp.where(lower, pltpu.roll(both, LANES // 2, 2), 0.0)

    def put_start(x, weight):
        w1[x] = weight
        v1a[x + rim, pl.ds(8, ny1), :] = weight * f1[x]

    sweep(range(nx1), lambda x: DAMPING / (r1[x] + mid.centre), put_start)
    mid.smooth(v1a, v1b, range(nx1))

    def coarsened(x):
        return mid.defect(v1b, 2 * x) + mid.defect(v1b, 2 * x + 1), r1[2 * x] + r1[2 * x + 1]

    rows2 = nx2 * ny2

    def put_pooled(x, pair):
        for n in range(2):
            value = mid.pool_rows(pair[n], tmp.at[2 * x + n])
            pooled[pl.ds(n * rows2 + x * ny2, ny2), :] = value

    sweep(range(nx2), coarsened, put_pooled)
    deeper = split_dot(pooled[pl.ds(0, 2 * rows2), :], pool)
    planes = [deeper[n * ny2 : (n + 1) * ny2] for n in range(2 * nx2)]
    values = deep.solve_in_registers(planes[:nx2], planes[nx2:])

    pooled[pl.ds(0, rows2), :] = split_dot(values, spread)

    def refined1(x):
        return mid.spread_rows(pooled[pl.ds(x * ny2, ny2), :], tmp.at[x])

    def put_refined1(x, value):
        for n in range(2):
            v1b[2 * x + n + rim, pl.ds(8, ny1), :] += value

    sweep(range(nx2), refined1, put_refined1)
    mid.smooth(v1b, v1a, range(nx1))
    mid.smooth(v1a, v1b, range(nx1))

    window = own + 2 * rim
    values = v1b[pl.ds(slab * own, window), pl.ds(8, ny1), :].reshape(window * ny1, LANES)
    pooled[pl.ds(0, window * ny1), :] = split_dot(values, spread)
    count = SLAB + 2 * HALO

    def refined(x):
        return fine.spread_rows(pooled[pl.ds(x * ny1, ny1), :], tmp.at[x])

    def put_refined(x, value):
        for at in (2 * x, 2 * x + 1):
            if 0 < at < count - 1:
                va[at, pl.ds(8, ny), :] = v1[at, pl.ds(8, ny), :] + value

    sweep(range(window), refined, put_refined)
    fine.smooth(va, vb, range(2, count - 2))
    fine.smooth(vb, va, range(3, count - 3))

    total = jnp.zeros((8, LANES), jnp.float32)
    for x in range(SLAB):
        rest = fine.defect(va, HALO + x)
        total = total + jnp.sum((rest * rest).reshape(ny // 8, 8, LANES), axis=0)
        tmp[x] = rest
    squares = jnp.full((8, LANES), jnp.sum(total), jnp.float32)
    area = bx * by
    for k, out_ref in enumerate(out_refs):
        owner = jnp.bitwise_xor(place_ref[0], k)
        first = (owner // gy_size) * bx
        row = pl.multiple_of(lax.rem(owner, gy_size) * by, 8)
        for p in range(bx):
            out_ref[pl.ds(p * by, by), :] = va[HALO + first + p, pl.ds(8 + row, by), :]
            out_ref[pl.ds(area + p * by, by), :] = tmp[first + p, pl.ds(row, by), :]
        out_ref[pl.ds(2 * area, 8), :] = squares


def collect_kernel(bx, by, place_ref, *refs):
    parts, (iterate_ref, residual_ref) = refs[:-2], refs[-2:]
    area = bx * by
    for k, part in enumerate(parts):
        column = jnp.bitwise_xor(place_ref[0], k)
        iterate_ref[column] = part[pl.ds(0, area), :].reshape(bx, by, LANES)
        residual_ref[column] = part[pl.ds(area, area), :].reshape(bx, by, LANES)


def squares_kernel(row, *refs):
    for k, part in enumerate(refs[:-1]):
        refs[-1][pl.ds(k, 1), :] = part[pl.ds(row, 1), :]


SMEM = pl.BlockSpec(memory_space=pltpu.SMEM)
VMEM = pl.BlockSpec(memory_space=pltpu.VMEM)


def local_kernel(kernel, name, scalars, arrays, outs, scratch=()):
    return pl.pallas_call(
        kernel,
        out_shape=[jax.ShapeDtypeStruct(shape, jnp.float32) for shape in outs],
        in_specs=[SMEM] * len(scalars) + [VMEM] * len(arrays),
        out_specs=[VMEM] * len(outs),
        scratch_shapes=[pltpu.VMEM(shape, jnp.float32) for shape in scratch],
        compiler_params=pltpu.CompilerParams(vmem_limit_bytes=VMEM_LIMIT),
        name=name,
    )(*scalars, *arrays)


def swap_in_plane(pieces, unit):
    devices = lax.axis_size("gx") * lax.axis_size("gy")
    moved = [pieces[0]]
    for k in range(1, len(pieces)):
        pairs = [(i, i ^ (k * unit)) for i in range(devices)]
        moved.append(lax.ppermute(pieces[k], ("gx", "gy"), pairs))
    return moved


def swap_slabs(piece, step, slabs):
    size = lax.axis_size("gx")
    moved = [piece]
    for k in range(1, slabs):
        pairs = [(i, i ^ (k * step)) for i in range(size)]
        moved.append(lax.ppermute(piece, "gx", pairs))
    return moved


def column_body(source, reaction, shifts, shift_index, velocity):
    columns, bx, by, nz = source.shape
    gx_size, gy_size = lax.axis_size("gx"), lax.axis_size("gy")
    nx, ny = bx * gx_size, by * gy_size
    step = columns // gy_size
    slabs = gx_size // step
    along, across = lax.axis_index("gx"), lax.axis_index("gy")
    column = lax.rem(along, step) * gy_size + across
    place = jnp.stack([column, along // step]).astype(jnp.int32)
    count = SLAB + 2 * HALO
    area = bx * by

    chips, chips_y = columns // 2, gy_size // 2
    cores = [(i, i ^ 1) for i in range(gy_size)]
    onward = [(i, i + step if i % step else i - step) for i in range(gx_size)]
    onward = [(i, j) for i, j in onward if 0 <= j < gx_size]
    theirs = lax.ppermute(source, "gy", cores)
    reaction_beside = lax.ppermute(reaction, "gx", onward)
    (mine,) = local_kernel(keep_kernel, "keep", (place,), (source,), [(chips, bx, by, nz)])
    *blocks, scalar_rows = local_kernel(
        merge_kernel,
        "merge",
        (place, shifts, shift_index, velocity),
        (mine, theirs, reaction, reaction_beside),
        [(bx, 4 * by, nz)] * chips + [(8, LANES)],
    )
    scalars = (place, scalar_rows)
    blocks = swap_in_plane(blocks, 2)

    half = (HALO, ny, nz)
    *halves, rows = local_kernel(
        functools.partial(arrange_kernel, chips_y),
        "arrange",
        (place,),
        blocks,
        [half, half, (count, ny // 2, nz)],
        [(2, *half)],
    )
    beside = []
    for n, half in enumerate(halves):
        pairs = []
        for i in range(gx_size):
            j = i + step if i // step % 2 == n else i - step
            if 0 <= j < gx_size:
                pairs.append((i, j))
        beside.append(lax.ppermute(half, "gx", pairs))
    reactions = [rows, lax.ppermute(rows, "gy", cores)]

    grid, rimmed = (count, ny, nz), (count, ny + 16, nz)
    f, r, w, v1, coarse = local_kernel(
        functools.partial(pre_kernel, slabs, gy_size, by),
        "pre",
        scalars,
        (pool_matrix(0), pool_matrix(LANES // 2), *halves, *beside, *reactions),
        [grid, grid, grid, rimmed, (SLAB // 2, ny // 2, nz)],
        [rimmed, (SLAB, ny, nz), (2, SLAB // 2 * ny // 2, nz)],
    )
    gathered = swap_slabs(coarse, step, slabs)

    coarse_grid = (nx // 2, ny // 2, nz)
    coarse_rimmed = (nx // 2 + HALO, ny // 2 + 16, nz)
    rows = max((SLAB // 2 + HALO) * ny // 2, nx // 4 * ny // 2)
    results = local_kernel(
        functools.partial(post_kernel, (slabs, nx, ny, nz), gy_size, bx, by),
        "post",
        scalars,
        (pool_matrix(0), spread_matrix(), f, r, w, v1, *gathered),
        [(2 * area + 8, nz)] * columns,
        [rimmed] * 2 + [coarse_grid] * 3 + [coarse_rimmed] * 2 + [(rows, nz), (nx // 2, ny, nz)],
    )
    parts = swap_in_plane(results, 1)

    (squares,) = local_kernel(
        functools.partial(squares_kernel, 2 * area), "squares", (), parts, [(columns, nz)]
    )
    total = sum(swap_slabs(squares, step, slabs))
    rms = jnp.sqrt(total[:, 0] / (nx * ny * nz) + EPSILON)
    slots = jnp.arange(columns, dtype=jnp.int32)
    mine = jnp.bitwise_xor(slots, column)[None, :] == slots[:, None]
    residual_rms = jnp.sum(jnp.where(mine, rms[None, :], 0.0), axis=1)
    iterate, residual = local_kernel(
        functools.partial(collect_kernel, bx, by), "collect", (place,), parts, [source.shape] * 2
    )
    return iterate, residual, residual_rms


def power_of_two(n):
    return n > 0 and n & (n - 1) == 0


def column_plan_fits(columns, bx, by, nz, gx_size, gy_size):
    if columns % gy_size or gx_size % (columns // gy_size):
        return False
    step = columns // gy_size
    slabs, ny = gx_size // step, by * gy_size
    whole = power_of_two(columns) and power_of_two(step) and power_of_two(slabs)
    small = slabs * ny * nz <= 2**15
    paired = step == 2 and bx == HALO and gy_size % 2 == 0
    return whole and small and paired and bx * step == SLAB and nz == LANES and by % 16 == 0


def solution(mesh):
    gx_size, gy_size = mesh.shape["gx"], mesh.shape["gy"]

    def body(source, reaction, shifts, shift_index, velocity):
        fits = column_plan_fits(*source.shape, gx_size, gy_size)
        plan = column_body if fits else halo_body
        return plan(source, reaction, shifts, shift_index, velocity)

    return jax.shard_map(
        body,
        mesh=mesh,
        in_specs=(P(None, "gx", "gy", None), P("gx", "gy", None), P(), P(), P()),
        out_specs=(P(None, "gx", "gy", None), P(None, "gx", "gy", None), P()),
        check_vma=False,
    )
```

```python
import functools

import jax
import jax.numpy as jnp
from jax import lax
from jax.experimental import pallas as pl
from jax.experimental.pallas import tpu as pltpu
from jax.sharding import PartitionSpec as P

LEVELS = 3
COARSE_SWEEPS = 6

DAMPING = 0.8
EPSILON = 1e-06
VMEM_LIMIT = 32 * 1024 * 1024
LANES = 128
GROUP = 4
SLAB = 8
HALO = 4


def with_halo(x, sides, width):
    for axis, dim in sides:
        peers, length = (lax.axis_size(axis), x.shape[dim])
        up = [(i, (i + 1) % peers) for i in range(peers - 1)]
        down = [(j, i) for i, j in up]
        last = lax.slice_in_dim(x, length - width, length, axis=dim)
        leading = lax.slice_in_dim(x, 0, width, axis=dim)
        before = lax.ppermute(last, axis, up)
        after = lax.ppermute(leading, axis, down)
        x = jnp.concatenate([before, x, after], axis=dim)
    return x


def select_shifts(shifts, shift_index):
    columns = jnp.arange(shifts.shape[0], dtype=jnp.int32)
    picked = jnp.where(shift_index[:, None] == columns[None, :], shifts[None, :], 0.0)
    return jnp.sum(picked, axis=1)


def coefficients(velocity, spacing):
    scale_a = 1.0 / (spacing * spacing)
    backward = scale_a + jnp.maximum(velocity, 0.0) / spacing
    forward = scale_a - jnp.minimum(velocity, 0.0) / spacing
    centre = 6.0 * scale_a + jnp.sum(jnp.abs(velocity)) / spacing
    return (backward, forward, centre)


def apply_stencil(padded, backward, forward, diagonal):
    middle = padded[:, 1:-1, 1:-1, :]
    along_z = jnp.pad(middle, ((0, 0), (0, 0), (0, 0), (1, 1)))
    others = backward[0] * padded[:, :-2, 1:-1, :] + forward[0] * padded[:, 2:, 1:-1, :]
    others = others + backward[1] * padded[:, 1:-1, :-2, :] + forward[1] * padded[:, 1:-1, 2:, :]
    others = others + backward[2] * along_z[:, :, :, :-2] + forward[2] * along_z[:, :, :, 2:]
    return diagonal * middle - others


def face_halo(iterate):
    return with_halo(iterate, (("gx", 1), ("gy", 2)), 1)


def coarsen(values):
    count, size_x, size_y, size_z = values.shape
    blocks = values.reshape(count, size_x // 2, 2, size_y // 2, 2, size_z // 2, 2)
    return jnp.sum(blocks, axis=(2, 4, 6)) * 0.125


def refine(values):
    return jnp.repeat(jnp.repeat(jnp.repeat(values, 2, 1), 2, 2), 2, 3)


def coarsest_solve(rhs_field, backward, forward, diagonal):
    iterate = DAMPING * rhs_field / diagonal
    for repeat in range(COARSE_SWEEPS - 1):
        applied = apply_stencil(face_halo(iterate), backward, forward, diagonal)
        iterate = iterate + DAMPING * (rhs_field - applied) / diagonal
    return iterate


def multigrid_cycle(level_index, rhs_field, reaction_l, shift_value, velocity):
    backward, forward, centre = coefficients(velocity, 2.0**level_index)
    diagonal = centre + reaction_l + shift_value[:, None, None, None]
    if level_index == LEVELS - 1:
        return coarsest_solve(rhs_field, backward, forward, diagonal)

    def operate(iterate):
        return apply_stencil(face_halo(iterate), backward, forward, diagonal)

    def smooth_step(iterate):
        return iterate + DAMPING * (rhs_field - operate(iterate)) / diagonal

    iterate = DAMPING * rhs_field / diagonal
    iterate = smooth_step(iterate)
    defect = rhs_field - operate(iterate)
    correction = multigrid_cycle(
        level_index + 1, coarsen(defect), coarsen(reaction_l), shift_value, velocity
    )
    iterate = iterate + refine(correction)
    iterate = smooth_step(iterate)
    iterate = smooth_step(iterate)
    return iterate


def halo_body(source, reaction, shifts, shift_index, velocity):
    columns, cells_x, cells_y, cells_z = source.shape
    shift_value = select_shifts(shifts, shift_index)
    reaction_top = reaction[None]
    backward, forward, centre = coefficients(velocity, 1.0)
    diagonal = centre + reaction_top + shift_value[:, None, None, None]

    iterate = multigrid_cycle(0, source, reaction_top, shift_value, velocity)
    residual = source - apply_stencil(face_halo(iterate), backward, forward, diagonal)
    local_squares = jnp.sum(residual * residual, axis=(1, 2, 3))
    squares = lax.psum(local_squares, ("gx", "gy"))
    total_cells = cells_x * cells_y * cells_z * lax.axis_size("gx") * lax.axis_size("gy")
    residual_rms = jnp.sqrt(squares / total_cells + EPSILON)
    return (iterate, residual, residual_rms)


def split_dot(values, matrix):
    high = values.astype(jnp.bfloat16)
    low = (values - high.astype(jnp.float32)).astype(jnp.bfloat16)
    return jnp.dot(high, matrix, preferred_element_type=jnp.float32) + jnp.dot(
        low, matrix, preferred_element_type=jnp.float32
    )


def sweep(planes, get, put):
    planes = list(planes)
    for first in range(0, len(planes), GROUP):
        group = planes[first : first + GROUP]
        values = [get(x) for x in group]
        for x, value in zip(group, values):
            put(x, value)


class Level:
    def __init__(self, index, ny, nz, rim, scalar_ref, f, r, w):
        self.ny, self.nz, self.rim = ny, nz, rim
        self.f, self.r, self.w = f, r, w
        spacing = 2.0**index
        scale_a = 1.0 / (spacing * spacing)
        inverse = 1.0 / spacing
        shift = scalar_ref[0, 0]
        speed = [scalar_ref[1 + d, 0] for d in range(3)]
        self.backward = [scale_a + jnp.maximum(v, 0.0) * inverse for v in speed]
        self.forward = [scale_a - jnp.minimum(v, 0.0) * inverse for v in speed]
        total = jnp.abs(speed[0]) + jnp.abs(speed[1]) + jnp.abs(speed[2])
        self.centre = 6.0 * scale_a + total * inverse + shift
        lane = lax.broadcasted_iota(jnp.int32, (1, LANES), 1)
        inside = lane < nz
        self.low_z = jnp.where((lane > 0) & inside, self.backward[2], 0.0)
        self.high_z = jnp.where(lane < nz - 1, self.forward[2], 0.0)

    def plane(self, v, x):
        return v[x + self.rim, pl.ds(8, self.ny), :]

    def put(self, v):
        def write(x, value):
            v[x + self.rim, pl.ds(8, self.ny), :] = value

        return write

    def along_z(self, middle):
        return self.low_z * pltpu.roll(middle, 1, 1) + self.high_z * pltpu.roll(middle, LANES - 1, 1)

    def neighbours(self, v, x, middle):
        at, ny = x + self.rim, self.ny
        along_x = self.backward[0] * v[at - 1, pl.ds(8, ny), :] + self.forward[0] * v[at + 1, pl.ds(8, ny), :]
        along_y = self.backward[1] * v[at, pl.ds(7, ny), :] + self.forward[1] * v[at, pl.ds(9, ny), :]
        return along_x + along_y + self.along_z(middle)

    def smoothed(self, v, x):
        middle = self.plane(v, x)
        pulled = self.f[x] + self.neighbours(v, x, middle)
        return (1.0 - DAMPING) * middle + self.w[x] * pulled

    def smooth(self, src, dst, planes):
        sweep(planes, lambda x: self.smoothed(src, x), self.put(dst))

    def defect(self, v, x):
        middle = self.plane(v, x)
        pulled = self.f[x] + self.neighbours(v, x, middle)
        return pulled - (self.r[x] + self.centre) * middle

    def pool_rows(self, value, rows):
        half, ny = self.ny // 2, self.ny
        rows[pl.ds(0, ny), :] = value
        return rows[pl.ds(0, half, stride=2), :] + rows[pl.ds(1, half, stride=2), :]

    def spread_rows(self, part, rows):
        half, ny = self.ny // 2, self.ny
        rows[pl.ds(0, half, stride=2), :] = part
        rows[pl.ds(1, half, stride=2), :] = part
        return rows[pl.ds(0, ny), :]

    def solve_in_registers(self, rhs, reaction):
        row = lax.broadcasted_iota(jnp.int32, (self.ny, 1), 0)
        low_y = jnp.where(row > 0, self.backward[1], 0.0)
        high_y = jnp.where(row < self.ny - 1, self.forward[1], 0.0)
        weight = [DAMPING / (r + self.centre) for r in reaction]
        v = [w * f for w, f in zip(weight, rhs)]
        for _ in range(COARSE_SWEEPS - 1):
            new = []
            for x, here in enumerate(v):
                along_y = low_y * pltpu.roll(here, 1, 0) + high_y * pltpu.roll(here, self.ny - 1, 0)
                pulled = rhs[x] + self.along_z(here) + along_y
                if x > 0:
                    pulled += self.backward[0] * v[x - 1]
                if x < len(v) - 1:
                    pulled += self.forward[0] * v[x + 1]
                new.append((1.0 - DAMPING) * here + weight[x] * pulled)
            v = new
        return jnp.concatenate(v, axis=0)


def zero_rows(v, ny):
    edge = jnp.zeros((v.shape[0], 8, LANES), jnp.float32)
    v[:, pl.ds(0, 8), :] = edge
    v[:, pl.ds(8 + ny, 8), :] = edge


def pool_matrix(offset):
    row = lax.broadcasted_iota(jnp.int32, (LANES, LANES), 0)
    col = lax.broadcasted_iota(jnp.int32, (LANES, LANES), 1)
    return jnp.where(row // 2 + offset == col, 0.125, 0.0).astype(jnp.bfloat16)


def spread_matrix():
    row = lax.broadcasted_iota(jnp.int32, (LANES, LANES), 0)
    col = lax.broadcasted_iota(jnp.int32, (LANES, LANES), 1)
    return jnp.where(col // 2 == row, 1.0, 0.0).astype(jnp.bfloat16)


def keep_kernel(place_ref, source_ref, out_ref):
    for n in range(out_ref.shape[0]):
        out_ref[n] = source_ref[2 * n + (place_ref[0] & 1)]


def merge_kernel(place_ref, shifts_ref, index_ref, velocity_ref, *refs):
    mine_ref, theirs_ref, reaction_ref, other_reaction_ref = refs[:4]
    out_refs, scalar_ref = refs[4:-1], refs[-1]
    chip, core = place_ref[0] // 2, place_ref[0] & 1
    by = mine_ref.shape[2]
    mine = pl.ds(pl.multiple_of(core * by, 8), by)
    theirs = pl.ds(pl.multiple_of((1 - core) * by, 8), by)
    for m, out_ref in enumerate(out_refs):
        target = jnp.bitwise_xor(chip, m)
        out_ref[0, :, mine, :] = mine_ref[target]
        out_ref[0, :, theirs, :] = theirs_ref[2 * target + core]
        out_ref[1, :, mine, :] = reaction_ref[...]
        out_ref[1, :, theirs, :] = other_reaction_ref[...]
    scalars = [shifts_ref[index_ref[place_ref[0]]]] + [velocity_ref[d] for d in range(3)]
    for n, scalar in enumerate(scalars):
        scalar_ref[pl.ds(n, 1), :] = jnp.full((1, LANES), scalar, jnp.float32)


def arrange_kernel(chips_y, place_ref, *refs):
    blocks, (first_ref, second_ref, halves) = refs[:-3], refs[-3:]
    for m, block in enumerate(blocks):
        owner = jnp.bitwise_xor(place_ref[0] // 2, m)
        size = block.shape[2]
        rows = pl.ds(pl.multiple_of(lax.rem(owner, chips_y) * size, 8), size)
        halves[owner // chips_y, :, :, rows, :] = block[...]
    even = 1 - (place_ref[1] & 1)
    first_ref[...] = halves[even]
    second_ref[...] = halves[1 - even]


def pre_kernel(slabs, place_ref, scalar_ref, *refs):
    pool_ref, pool_up_ref = refs[:2]
    parts = refs[2:6]
    f, r, w, v1, coarse_ref, v0, tmp, pooled = refs[6:]
    ny = f.shape[1]
    slab = place_ref[1]
    fine = Level(0, ny, LANES, 0, scalar_ref, f, r, w)
    zero_rows(v0, ny)
    zero_rows(v1, ny)
    count = SLAB + 2 * HALO
    inside = [jnp.where(slab > 0, DAMPING, 0.0)] * HALO
    inside += [DAMPING] * SLAB
    inside += [jnp.where(slab < slabs - 1, DAMPING, 0.0)] * HALO

    even = 1 - (slab & 1)
    firsts = (HALO * (1 + even), HALO * (2 - even), (HALO + SLAB) * even, (HALO + SLAB) * (1 - even))
    for part, first in zip(parts, firsts):
        f[pl.ds(first, HALO)] = part[0]
        r[pl.ds(first, HALO)] = part[1]

    def put(x, weight):
        w[x] = weight
        v0[x, pl.ds(8, ny), :] = weight * f[x]

    sweep(range(count), lambda x: inside[x] / (r[x] + fine.centre), put)
    fine.smooth(v0, v1, range(1, count - 1))
    half = ny // 2

    def coarsened(x):
        at = HALO + 2 * x
        return fine.defect(v1, at) + fine.defect(v1, at + 1), r[at] + r[at + 1]

    def put_pooled(x, pair):
        for n in range(2):
            pooled[n, pl.ds(x * half, half), :] = fine.pool_rows(pair[n], tmp.at[2 * x + n])

    sweep(range(SLAB // 2), coarsened, put_pooled)
    packed = split_dot(pooled[0], pool_ref[...]) + split_dot(pooled[1], pool_up_ref[...])
    coarse_ref[...] = packed.reshape(coarse_ref.shape)


def post_kernel(grid, by, place_ref, scalar_ref, *refs):
    slabs, nx, ny, nz = grid
    pool_ref, spread_ref, f, r, w, v1 = refs[:6]
    coarse = refs[6 : 6 + slabs]
    kept_ref, sent_ref, squares_ref = refs[6 + slabs : 9 + slabs]
    va, vb, f1, r1, w1, v1a, v1b, pooled, tmp = refs[9 + slabs :]
    pool, spread = pool_ref[...], spread_ref[...]
    slab = place_ref[1]
    rim = HALO // 2
    nx1, ny1, nx2, ny2 = nx // 2, ny // 2, nx // 4, ny // 4
    fine = Level(0, ny, nz, 0, scalar_ref, f, r, w)
    mid = Level(1, ny1, nz // 2, rim, scalar_ref, f1, r1, w1)
    deep = Level(2, ny2, nz // 4, 0, scalar_ref, None, None, None)
    for v in (va, vb):
        zero_rows(v, ny)
    for v in (v1a, v1b):
        zero_rows(v, ny1)
        blank = jnp.zeros((rim,) + v.shape[1:], jnp.float32)
        v[pl.ds(0, rim)] = blank
        v[pl.ds(rim + nx1, rim)] = blank

    lower = lax.broadcasted_iota(jnp.int32, (1, LANES), 1) < LANES // 2
    own = SLAB // 2
    for k in range(slabs):
        first = jnp.bitwise_xor(slab, k) * own
        both = coarse[k][...]
        f1[pl.ds(first, own)] = jnp.where(lower, both, 0.0)
        r1[pl.ds(first, own)] = jnp.where(lower, pltpu.roll(both, LANES // 2, 2), 0.0)

    def put_start(x, weight):
        w1[x] = weight
        v1a[x + rim, pl.ds(8, ny1), :] = weight * f1[x]

    sweep(range(nx1), lambda x: DAMPING / (r1[x] + mid.centre), put_start)
    mid.smooth(v1a, v1b, range(nx1))

    def coarsened(x):
        return mid.defect(v1b, 2 * x) + mid.defect(v1b, 2 * x + 1), r1[2 * x] + r1[2 * x + 1]

    rows2 = nx2 * ny2

    def put_pooled(x, pair):
        for n in range(2):
            value = mid.pool_rows(pair[n], tmp.at[2 * x + n])
            pooled[pl.ds(n * rows2 + x * ny2, ny2), :] = value

    sweep(range(nx2), coarsened, put_pooled)
    deeper = split_dot(pooled[pl.ds(0, 2 * rows2), :], pool)
    planes = [deeper[n * ny2 : (n + 1) * ny2] for n in range(2 * nx2)]
    values = deep.solve_in_registers(planes[:nx2], planes[nx2:])

    pooled[pl.ds(0, rows2), :] = split_dot(values, spread)

    def refined1(x):
        return mid.spread_rows(pooled[pl.ds(x * ny2, ny2), :], tmp.at[x])

    def put_refined1(x, value):
        for n in range(2):
            v1b[2 * x + n + rim, pl.ds(8, ny1), :] += value

    sweep(range(nx2), refined1, put_refined1)
    mid.smooth(v1b, v1a, range(nx1))
    mid.smooth(v1a, v1b, range(nx1))

    window = own + 2 * rim
    values = v1b[pl.ds(slab * own, window), pl.ds(8, ny1), :].reshape(window * ny1, LANES)
    pooled[pl.ds(0, window * ny1), :] = split_dot(values, spread)
    count = SLAB + 2 * HALO

    def refined(x):
        return fine.spread_rows(pooled[pl.ds(x * ny1, ny1), :], tmp.at[x])

    def put_refined(x, value):
        for at in (2 * x, 2 * x + 1):
            if 0 < at < count - 1:
                va[at, pl.ds(8, ny), :] = v1[at, pl.ds(8, ny), :] + value

    sweep(range(window), refined, put_refined)
    fine.smooth(va, vb, range(2, count - 2))
    fine.smooth(vb, va, range(3, count - 3))

    total = jnp.zeros((8, LANES), jnp.float32)
    for x in range(SLAB):
        rest = fine.defect(va, HALO + x)
        total = total + jnp.sum((rest * rest).reshape(ny // 8, 8, LANES), axis=0)
        tmp[x] = rest
    squares_ref[...] = jnp.full((8, LANES), jnp.sum(total), jnp.float32)

    core = place_ref[0] & 1
    for ref, first in ((kept_ref, core * by), (sent_ref, (1 - core) * by)):
        for y in range(ny // (2 * by)):
            row, to = pl.multiple_of(2 * y * by + first, 8), pl.ds(y * by, by)
            for x in range(SLAB):
                ref[0, x, to, :] = va[HALO + x, pl.ds(8 + row, by), :]
                ref[1, x, to, :] = tmp[x, pl.ds(row, by), :]


def merge_back_kernel(bx, by, chips_y, chips, place_ref, kept_ref, got_ref, *refs):
    squares, out_refs = refs[:-chips], refs[-chips:]
    total = sum(square[...] for square in squares)
    chip, core = place_ref[0] // 2, place_ref[0] & 1
    area = bx * by
    for m, out_ref in enumerate(out_refs):
        target = jnp.bitwise_xor(chip, m)
        planes = pl.ds((target // chips_y) * bx, bx)
        rows = pl.ds(pl.multiple_of(lax.rem(target, chips_y) * by, 8), by)
        for ref, column in ((kept_ref, core), (got_ref, 1 - core)):
            for n in range(2):
                to = pl.multiple_of((2 * column + n) * area, 8)
                out_ref[pl.ds(to, area), :] = ref[n, planes, rows, :].reshape(area, LANES)
        out_ref[pl.ds(4 * area, 8), :] = total


def collect_kernel(place_ref, *refs):
    parts, (iterate_ref, residual_ref) = refs[:-2], refs[-2:]
    _, bx, by, _ = iterate_ref.shape
    area = bx * by
    for m, part in enumerate(parts):
        target = jnp.bitwise_xor(place_ref[0] // 2, m)
        for n in range(2):
            for k, ref in enumerate((iterate_ref, residual_ref)):
                rows = pl.ds((2 * n + k) * area, area)
                ref[2 * target + n] = part[rows, :].reshape(bx, by, LANES)


def totals_kernel(row, *refs):
    for m, part in enumerate(refs[:-1]):
        refs[-1][pl.ds(m, 1), :] = part[pl.ds(row, 1), :]


def rms_kernel(cells, place_ref, mine_ref, theirs_ref, out_ref):
    chip, core = place_ref[0] // 2, place_ref[0] & 1
    for ref, column in ((mine_ref, core), (theirs_ref, 1 - core)):
        rms = jnp.sqrt(ref[...] / cells + EPSILON)
        for m in range(out_ref.shape[0] // 2):
            out_ref[2 * jnp.bitwise_xor(chip, m) + column] = jnp.max(rms[m : m + 1])


SMEM = pl.BlockSpec(memory_space=pltpu.SMEM)
VMEM = pl.BlockSpec(memory_space=pltpu.VMEM)


def local_kernel(kernel, name, scalars, arrays, outs, scratch=()):
    return pl.pallas_call(
        kernel,
        out_shape=[jax.ShapeDtypeStruct(shape, jnp.float32) for shape in outs],
        in_specs=[SMEM] * len(scalars) + [VMEM] * len(arrays),
        out_specs=[VMEM] * len(outs),
        scratch_shapes=[pltpu.VMEM(shape, jnp.float32) for shape in scratch],
        compiler_params=pltpu.CompilerParams(vmem_limit_bytes=VMEM_LIMIT),
        name=name,
    )(*scalars, *arrays)


def swap_in_plane(pieces, unit):
    devices = lax.axis_size("gx") * lax.axis_size("gy")
    moved = [pieces[0]]
    for k in range(1, len(pieces)):
        pairs = [(i, i ^ (k * unit)) for i in range(devices)]
        moved.append(lax.ppermute(pieces[k], ("gx", "gy"), pairs))
    return moved


def swap_slabs(piece, step, slabs):
    size = lax.axis_size("gx")
    moved = [piece]
    for k in range(1, slabs):
        pairs = [(i, i ^ (k * step)) for i in range(size)]
        moved.append(lax.ppermute(piece, "gx", pairs))
    return moved


def column_body(source, reaction, shifts, shift_index, velocity):
    columns, bx, by, nz = source.shape
    gx_size, gy_size = lax.axis_size("gx"), lax.axis_size("gy")
    nx, ny = bx * gx_size, by * gy_size
    step = columns // gy_size
    slabs = gx_size // step
    along, across = lax.axis_index("gx"), lax.axis_index("gy")
    column = lax.rem(along, step) * gy_size + across
    place = jnp.stack([column, along // step]).astype(jnp.int32)
    count = SLAB + 2 * HALO
    area = bx * by

    chips, chips_y = columns // 2, gy_size // 2
    cores = [(i, i ^ 1) for i in range(gy_size)]
    theirs = [lax.ppermute(source, "gy", cores), lax.ppermute(reaction, "gy", cores)]
    (mine,) = local_kernel(keep_kernel, "keep", (place,), (source,), [(chips, bx, by, nz)])
    *blocks, scalar_rows = local_kernel(
        merge_kernel,
        "merge",
        (place, shifts, shift_index, velocity),
        (mine, theirs[0], reaction, theirs[1]),
        [(2, bx, 2 * by, nz)] * chips + [(8, LANES)],
    )
    scalars = (place, scalar_rows)
    blocks = swap_in_plane(blocks, 2)

    half = (2, HALO, ny, nz)
    halves = local_kernel(
        functools.partial(arrange_kernel, chips_y), "arrange", (place,), blocks, [half] * 2, [(2, *half)]
    )
    beside = []
    for n, half in enumerate(halves):
        pairs = []
        for i in range(gx_size):
            j = i + step if i // step % 2 == n else i - step
            if 0 <= j < gx_size:
                pairs.append((i, j))
        beside.append(lax.ppermute(half, "gx", pairs))

    grid, rimmed = (count, ny, nz), (count, ny + 16, nz)
    f, r, w, v1, coarse = local_kernel(
        functools.partial(pre_kernel, slabs),
        "pre",
        scalars,
        (pool_matrix(0), pool_matrix(LANES // 2), *halves, *beside),
        [grid, grid, grid, rimmed, (SLAB // 2, ny // 2, nz)],
        [rimmed, (SLAB, ny, nz), (2, SLAB // 2 * ny // 2, nz)],
    )
    gathered = swap_slabs(coarse, step, slabs)

    coarse_grid = (nx // 2, ny // 2, nz)
    coarse_rimmed = (nx // 2 + HALO, ny // 2 + 16, nz)
    rows = max((SLAB // 2 + HALO) * ny // 2, nx // 4 * ny // 2)
    result = (2, SLAB, ny // 2, nz)
    kept, sent, squares = local_kernel(
        functools.partial(post_kernel, (slabs, nx, ny, nz), by),
        "post",
        scalars,
        (pool_matrix(0), spread_matrix(), f, r, w, v1, *gathered),
        [result, result, (8, nz)],
        [rimmed] * 2 + [coarse_grid] * 3 + [coarse_rimmed] * 2 + [(rows, nz), (nx // 2, ny, nz)],
    )

    got = lax.ppermute(sent, "gy", cores)
    parts = local_kernel(
        functools.partial(merge_back_kernel, bx, by, chips_y, chips),
        "merge_back",
        (place,),
        (kept, got, *swap_slabs(squares, step, slabs)),
        [(4 * area + 8, nz)] * chips,
    )
    parts = swap_in_plane(parts, 2)
    (totals,) = local_kernel(
        functools.partial(totals_kernel, 4 * area), "totals", (), parts, [(chips, nz)]
    )
    other_totals = lax.ppermute(totals, "gy", cores)
    residual_rms = pl.pallas_call(
        functools.partial(rms_kernel, nx * ny * nz),
        out_shape=jax.ShapeDtypeStruct((columns,), jnp.float32),
        in_specs=[SMEM, VMEM, VMEM],
        out_specs=SMEM,
        name="rms",
    )(place, totals, other_totals)
    iterate, residual = local_kernel(
        collect_kernel, "collect", (place,), parts, [source.shape] * 2
    )
    return iterate, residual, residual_rms


def power_of_two(n):
    return n > 0 and n & (n - 1) == 0


def column_plan_fits(columns, bx, by, nz, gx_size, gy_size):
    if columns % gy_size or gx_size % (columns // gy_size):
        return False
    step = columns // gy_size
    slabs, ny = gx_size // step, by * gy_size
    whole = power_of_two(columns) and power_of_two(step) and power_of_two(slabs)
    small = slabs * ny * nz <= 2**15
    paired = step == 2 and bx == HALO and gy_size % 2 == 0
    return whole and small and paired and bx * step == SLAB and nz == LANES and by % 16 == 0


def solution(mesh):
    gx_size, gy_size = mesh.shape["gx"], mesh.shape["gy"]

    def body(source, reaction, shifts, shift_index, velocity):
        fits = column_plan_fits(*source.shape, gx_size, gy_size)
        plan = column_body if fits else halo_body
        return plan(source, reaction, shifts, shift_index, velocity)

    return jax.shard_map(
        body,
        mesh=mesh,
        in_specs=(P(None, "gx", "gy", None), P("gx", "gy", None), P(), P(), P()),
        out_specs=(P(None, "gx", "gy", None), P(None, "gx", "gy", None), P()),
        check_vma=False,
    )
```

```python
import functools

import jax
import jax.numpy as jnp
from jax import lax
from jax.experimental import pallas as pl
from jax.experimental.pallas import tpu as pltpu
from jax.sharding import PartitionSpec as P

LEVELS = 3
COARSE_SWEEPS = 6

DAMPING = 0.8
EPSILON = 1e-06
VMEM_LIMIT = 32 * 1024 * 1024
LANES = 128
GROUP = 4
SLAB = 8
HALO = 4
NEAR = 2


def with_halo(x, sides, width):
    for axis, dim in sides:
        peers, length = (lax.axis_size(axis), x.shape[dim])
        up = [(i, (i + 1) % peers) for i in range(peers - 1)]
        down = [(j, i) for i, j in up]
        last = lax.slice_in_dim(x, length - width, length, axis=dim)
        leading = lax.slice_in_dim(x, 0, width, axis=dim)
        before = lax.ppermute(last, axis, up)
        after = lax.ppermute(leading, axis, down)
        x = jnp.concatenate([before, x, after], axis=dim)
    return x


def select_shifts(shifts, shift_index):
    columns = jnp.arange(shifts.shape[0], dtype=jnp.int32)
    picked = jnp.where(shift_index[:, None] == columns[None, :], shifts[None, :], 0.0)
    return jnp.sum(picked, axis=1)


def coefficients(velocity, spacing):
    scale_a = 1.0 / (spacing * spacing)
    backward = scale_a + jnp.maximum(velocity, 0.0) / spacing
    forward = scale_a - jnp.minimum(velocity, 0.0) / spacing
    centre = 6.0 * scale_a + jnp.sum(jnp.abs(velocity)) / spacing
    return (backward, forward, centre)


def apply_stencil(padded, backward, forward, diagonal):
    middle = padded[:, 1:-1, 1:-1, :]
    along_z = jnp.pad(middle, ((0, 0), (0, 0), (0, 0), (1, 1)))
    others = backward[0] * padded[:, :-2, 1:-1, :] + forward[0] * padded[:, 2:, 1:-1, :]
    others = others + backward[1] * padded[:, 1:-1, :-2, :] + forward[1] * padded[:, 1:-1, 2:, :]
    others = others + backward[2] * along_z[:, :, :, :-2] + forward[2] * along_z[:, :, :, 2:]
    return diagonal * middle - others


def face_halo(iterate):
    return with_halo(iterate, (("gx", 1), ("gy", 2)), 1)


def coarsen(values):
    count, size_x, size_y, size_z = values.shape
    blocks = values.reshape(count, size_x // 2, 2, size_y // 2, 2, size_z // 2, 2)
    return jnp.sum(blocks, axis=(2, 4, 6)) * 0.125


def refine(values):
    return jnp.repeat(jnp.repeat(jnp.repeat(values, 2, 1), 2, 2), 2, 3)


def coarsest_solve(rhs_field, backward, forward, diagonal):
    iterate = DAMPING * rhs_field / diagonal
    for repeat in range(COARSE_SWEEPS - 1):
        applied = apply_stencil(face_halo(iterate), backward, forward, diagonal)
        iterate = iterate + DAMPING * (rhs_field - applied) / diagonal
    return iterate


def multigrid_cycle(level_index, rhs_field, reaction_l, shift_value, velocity):
    backward, forward, centre = coefficients(velocity, 2.0**level_index)
    diagonal = centre + reaction_l + shift_value[:, None, None, None]
    if level_index == LEVELS - 1:
        return coarsest_solve(rhs_field, backward, forward, diagonal)

    def operate(iterate):
        return apply_stencil(face_halo(iterate), backward, forward, diagonal)

    def smooth_step(iterate):
        return iterate + DAMPING * (rhs_field - operate(iterate)) / diagonal

    iterate = DAMPING * rhs_field / diagonal
    iterate = smooth_step(iterate)
    defect = rhs_field - operate(iterate)
    correction = multigrid_cycle(
        level_index + 1, coarsen(defect), coarsen(reaction_l), shift_value, velocity
    )
    iterate = iterate + refine(correction)
    iterate = smooth_step(iterate)
    iterate = smooth_step(iterate)
    return iterate


def halo_body(source, reaction, shifts, shift_index, velocity):
    columns, cells_x, cells_y, cells_z = source.shape
    shift_value = select_shifts(shifts, shift_index)
    reaction_top = reaction[None]
    backward, forward, centre = coefficients(velocity, 1.0)
    diagonal = centre + reaction_top + shift_value[:, None, None, None]

    iterate = multigrid_cycle(0, source, reaction_top, shift_value, velocity)
    residual = source - apply_stencil(face_halo(iterate), backward, forward, diagonal)
    local_squares = jnp.sum(residual * residual, axis=(1, 2, 3))
    squares = lax.psum(local_squares, ("gx", "gy"))
    total_cells = cells_x * cells_y * cells_z * lax.axis_size("gx") * lax.axis_size("gy")
    residual_rms = jnp.sqrt(squares / total_cells + EPSILON)
    return (iterate, residual, residual_rms)


def split_dot(values, matrix):
    high = values.astype(jnp.bfloat16)
    low = (values - high.astype(jnp.float32)).astype(jnp.bfloat16)
    return jnp.dot(high, matrix, preferred_element_type=jnp.float32) + jnp.dot(
        low, matrix, preferred_element_type=jnp.float32
    )


def sweep(planes, get, put):
    planes = list(planes)
    for first in range(0, len(planes), GROUP):
        group = planes[first : first + GROUP]
        values = [get(x) for x in group]
        for x, value in zip(group, values):
            put(x, value)


class Level:
    def __init__(self, index, ny, nz, rim, scalar_ref, f, r, w):
        self.ny, self.nz, self.rim = ny, nz, rim
        self.f, self.r, self.w = f, r, w
        spacing = 2.0**index
        scale_a = 1.0 / (spacing * spacing)
        inverse = 1.0 / spacing
        shift = scalar_ref[0, 0]
        speed = [scalar_ref[1 + d, 0] for d in range(3)]
        self.backward = [scale_a + jnp.maximum(v, 0.0) * inverse for v in speed]
        self.forward = [scale_a - jnp.minimum(v, 0.0) * inverse for v in speed]
        total = jnp.abs(speed[0]) + jnp.abs(speed[1]) + jnp.abs(speed[2])
        self.centre = 6.0 * scale_a + total * inverse + shift
        lane = lax.broadcasted_iota(jnp.int32, (1, LANES), 1)
        inside = lane < nz
        self.low_z = jnp.where((lane > 0) & inside, self.backward[2], 0.0)
        self.high_z = jnp.where(lane < nz - 1, self.forward[2], 0.0)

    def plane(self, v, x):
        return v[x + self.rim, pl.ds(8, self.ny), :]

    def put(self, v):
        def write(x, value):
            v[x + self.rim, pl.ds(8, self.ny), :] = value

        return write

    def along_z(self, middle):
        return self.low_z * pltpu.roll(middle, 1, 1) + self.high_z * pltpu.roll(middle, LANES - 1, 1)

    def neighbours(self, v, x, middle):
        at, ny = x + self.rim, self.ny
        along_x = self.backward[0] * v[at - 1, pl.ds(8, ny), :] + self.forward[0] * v[at + 1, pl.ds(8, ny), :]
        along_y = self.backward[1] * v[at, pl.ds(7, ny), :] + self.forward[1] * v[at, pl.ds(9, ny), :]
        return along_x + along_y + self.along_z(middle)

    def smoothed(self, v, x):
        middle = self.plane(v, x)
        pulled = self.f[x] + self.neighbours(v, x, middle)
        return (1.0 - DAMPING) * middle + self.w[x] * pulled

    def smooth(self, src, dst, planes):
        sweep(planes, lambda x: self.smoothed(src, x), self.put(dst))

    def defect(self, v, x):
        middle = self.plane(v, x)
        pulled = self.f[x] + self.neighbours(v, x, middle)
        return pulled - (self.r[x] + self.centre) * middle

    def pool_rows(self, value, rows):
        half, ny = self.ny // 2, self.ny
        rows[pl.ds(0, ny), :] = value
        return rows[pl.ds(0, half, stride=2), :] + rows[pl.ds(1, half, stride=2), :]

    def spread_rows(self, part, rows):
        half, ny = self.ny // 2, self.ny
        rows[pl.ds(0, half, stride=2), :] = part
        rows[pl.ds(1, half, stride=2), :] = part
        return rows[pl.ds(0, ny), :]

    def solve_in_registers(self, rhs, reaction):
        row = lax.broadcasted_iota(jnp.int32, (self.ny, 1), 0)
        low_y = jnp.where(row > 0, self.backward[1], 0.0)
        high_y = jnp.where(row < self.ny - 1, self.forward[1], 0.0)
        weight = [DAMPING / (r + self.centre) for r in reaction]
        v = [w * f for w, f in zip(weight, rhs)]
        for _ in range(COARSE_SWEEPS - 1):
            new = []
            for x, here in enumerate(v):
                along_y = low_y * pltpu.roll(here, 1, 0) + high_y * pltpu.roll(here, self.ny - 1, 0)
                pulled = rhs[x] + self.along_z(here) + along_y
                if x > 0:
                    pulled += self.backward[0] * v[x - 1]
                if x < len(v) - 1:
                    pulled += self.forward[0] * v[x + 1]
                new.append((1.0 - DAMPING) * here + weight[x] * pulled)
            v = new
        return jnp.concatenate(v, axis=0)


def zero_rows(v, ny):
    edge = jnp.zeros((v.shape[0], 8, LANES), jnp.float32)
    v[:, pl.ds(0, 8), :] = edge
    v[:, pl.ds(8 + ny, 8), :] = edge


def pool_matrix(offset):
    row = lax.broadcasted_iota(jnp.int32, (LANES, LANES), 0)
    col = lax.broadcasted_iota(jnp.int32, (LANES, LANES), 1)
    return jnp.where(row // 2 + offset == col, 0.125, 0.0).astype(jnp.bfloat16)


def spread_matrix():
    row = lax.broadcasted_iota(jnp.int32, (LANES, LANES), 0)
    col = lax.broadcasted_iota(jnp.int32, (LANES, LANES), 1)
    return jnp.where(col // 2 == row, 1.0, 0.0).astype(jnp.bfloat16)


def keep_kernel(place_ref, source_ref, out_ref):
    for n in range(out_ref.shape[0]):
        out_ref[n] = source_ref[2 * n + (place_ref[0] & 1)]


def merge_kernel(place_ref, shifts_ref, index_ref, velocity_ref, *refs):
    mine_ref, theirs_ref, reaction_ref, other_reaction_ref = refs[:4]
    out_refs, scalar_ref = refs[4:-1], refs[-1]
    chip, core = place_ref[0] // 2, place_ref[0] & 1
    by = mine_ref.shape[2]
    mine = pl.ds(pl.multiple_of(core * by, 8), by)
    theirs = pl.ds(pl.multiple_of((1 - core) * by, 8), by)
    for m, out_ref in enumerate(out_refs):
        target = jnp.bitwise_xor(chip, m)
        out_ref[0, :, mine, :] = mine_ref[target]
        out_ref[0, :, theirs, :] = theirs_ref[2 * target + core]
        out_ref[1, :, mine, :] = reaction_ref[...]
        out_ref[1, :, theirs, :] = other_reaction_ref[...]
    scalars = [shifts_ref[index_ref[place_ref[0]]]] + [velocity_ref[d] for d in range(3)]
    for n, scalar in enumerate(scalars):
        scalar_ref[pl.ds(n, 1), :] = jnp.full((1, LANES), scalar, jnp.float32)


def arrange_kernel(chips_y, place_ref, *refs):
    blocks, (slab_ref, first_ref, second_ref) = refs[:-3], refs[-3:]
    for m, block in enumerate(blocks):
        owner = jnp.bitwise_xor(place_ref[0] // 2, m)
        _, bx, size, _ = block.shape
        planes = pl.ds((owner // chips_y) * bx, bx)
        rows = pl.ds(pl.multiple_of(lax.rem(owner, chips_y) * size, 8), size)
        slab_ref[:, planes, rows, :] = block[...]
    even = 1 - (place_ref[1] & 1)
    first_ref[...] = slab_ref[:, pl.ds(even * (SLAB - NEAR), NEAR)]
    second_ref[...] = slab_ref[:, pl.ds((1 - even) * (SLAB - NEAR), NEAR)]


def pre_kernel(slabs, place_ref, scalar_ref, *refs):
    pool_ref, pool_up_ref, slab_ref, first_ref, second_ref = refs[:5]
    f, r, w, v1, coarse_ref, first_out, second_out, v0, tmp, pooled = refs[5:]
    ny = f.shape[1]
    slab = place_ref[1]
    fine = Level(0, ny, LANES, 0, scalar_ref, f, r, w)
    zero_rows(v0, ny)
    zero_rows(v1, ny)
    after = HALO + SLAB
    even = 1 - (slab & 1)

    f[pl.ds(HALO, SLAB)], r[pl.ds(HALO, SLAB)] = slab_ref[0], slab_ref[1]
    for ref, above in ((first_ref, even), (second_ref, 1 - even)):
        planes = pl.ds((HALO - NEAR) + above * (SLAB + NEAR), NEAR)
        f[planes], r[planes] = ref[0], ref[1]

    inside = [jnp.where(slab > 0, DAMPING, 0.0)] * HALO
    inside += [DAMPING] * SLAB
    inside += [jnp.where(slab < slabs - 1, DAMPING, 0.0)] * HALO

    def put(x, weight):
        w[x] = weight
        v0[x, pl.ds(8, ny), :] = weight * f[x]

    known = range(HALO - NEAR, after + NEAR)
    sweep(known, lambda x: inside[x] / (r[x] + fine.centre), put)
    fine.smooth(v0, v1, known[1:-1])
    for ref, above in ((first_out, even), (second_out, 1 - even)):
        ref[...] = v1[pl.ds(HALO + 1 + above * (SLAB - HALO), NEAR), pl.ds(8, ny), :]
    half = ny // 2

    def coarsened(x):
        at = HALO + 2 * x
        return fine.defect(v1, at) + fine.defect(v1, at + 1), r[at] + r[at + 1]

    def put_pooled(x, pair):
        for n in range(2):
            pooled[n, pl.ds(x * half, half), :] = fine.pool_rows(pair[n], tmp.at[2 * x + n])

    sweep(range(SLAB // 2), coarsened, put_pooled)
    packed = split_dot(pooled[0], pool_ref[...]) + split_dot(pooled[1], pool_up_ref[...])
    coarse_ref[...] = packed.reshape(coarse_ref.shape)


def coarse_kernel(grid, place_ref, scalar_ref, *refs):
    slabs, nx, ny, nz = grid
    pool_ref, spread_ref = refs[:2]
    coarse, out_ref = refs[2 : 2 + slabs], refs[2 + slabs]
    f1, r1, w1, v1a, v1b, pooled, tmp = refs[3 + slabs :]
    pool, spread = pool_ref[...], spread_ref[...]
    slab = place_ref[1]
    rim = HALO // 2
    nx1, ny1, nx2, ny2 = nx // 2, ny // 2, nx // 4, ny // 4
    mid = Level(1, ny1, nz // 2, rim, scalar_ref, f1, r1, w1)
    deep = Level(2, ny2, nz // 4, 0, scalar_ref, None, None, None)
    for v in (v1a, v1b):
        zero_rows(v, ny1)
        blank = jnp.zeros((rim,) + v.shape[1:], jnp.float32)
        v[pl.ds(0, rim)] = blank
        v[pl.ds(rim + nx1, rim)] = blank

    lower = lax.broadcasted_iota(jnp.int32, (1, LANES), 1) < LANES // 2
    own = SLAB // 2
    for k in range(slabs):
        first = jnp.bitwise_xor(slab, k) * own
        both = coarse[k][...]
        f1[pl.ds(first, own)] = jnp.where(lower, both, 0.0)
        r1[pl.ds(first, own)] = jnp.where(lower, pltpu.roll(both, LANES // 2, 2), 0.0)

    def put_start(x, weight):
        w1[x] = weight
        v1a[x + rim, pl.ds(8, ny1), :] = weight * f1[x]

    sweep(range(nx1), lambda x: DAMPING / (r1[x] + mid.centre), put_start)
    mid.smooth(v1a, v1b, range(nx1))

    def coarsened(x):
        return mid.defect(v1b, 2 * x) + mid.defect(v1b, 2 * x + 1), r1[2 * x] + r1[2 * x + 1]

    rows2 = nx2 * ny2

    def put_pooled(x, pair):
        for n in range(2):
            value = mid.pool_rows(pair[n], tmp.at[2 * x + n])
            pooled[pl.ds(n * rows2 + x * ny2, ny2), :] = value

    sweep(range(nx2), coarsened, put_pooled)
    deeper = split_dot(pooled[pl.ds(0, 2 * rows2), :], pool)
    planes = [deeper[n * ny2 : (n + 1) * ny2] for n in range(2 * nx2)]
    values = deep.solve_in_registers(planes[:nx2], planes[nx2:])

    pooled[pl.ds(0, rows2), :] = split_dot(values, spread)

    def refined1(x):
        return mid.spread_rows(pooled[pl.ds(x * ny2, ny2), :], tmp.at[x])

    def put_refined1(x, value):
        for n in range(2):
            v1b[2 * x + n + rim, pl.ds(8, ny1), :] += value

    sweep(range(nx2), refined1, put_refined1)
    mid.smooth(v1b, v1a, range(nx1))
    mid.smooth(v1a, v1b, range(nx1))

    window = own + 2 * rim
    values = v1b[pl.ds(slab * own, window), pl.ds(8, ny1), :].reshape(window * ny1, LANES)
    out_ref[...] = split_dot(values, spread)


def post_kernel(by, place_ref, scalar_ref, *refs):
    f, r, w, v1, correction, first_ref, second_ref, kept_ref, sent_ref, va, vb, tmp = refs
    count, ny = f.shape[:2]
    fine = Level(0, ny, LANES, 0, scalar_ref, f, r, w)
    for v in (va, vb):
        zero_rows(v, ny)
    even, half = 1 - (place_ref[1] & 1), ny // 2
    window = correction.shape[0] // half
    for ref, above in ((first_ref, even), (second_ref, 1 - even)):
        va[pl.ds(1 + above * (SLAB + HALO), NEAR), pl.ds(8, ny), :] = ref[...]

    def refined(x):
        return fine.spread_rows(correction[pl.ds(x * half, half), :], tmp.at[x])

    def put_refined(x, value):
        for at in (2 * x, 2 * x + 1):
            if 0 < at < count - 1:
                known = HALO - NEAR < at < HALO + SLAB + NEAR - 1
                here = v1 if known else va
                va[at, pl.ds(8, ny), :] = here[at, pl.ds(8, ny), :] + value

    sweep(range(window), refined, put_refined)
    fine.smooth(va, vb, range(2, count - 2))
    fine.smooth(vb, va, range(3, count - 3))

    total = jnp.zeros((8, LANES), jnp.float32)
    for x in range(SLAB):
        rest = fine.defect(va, HALO + x)
        total = total + jnp.sum((rest * rest).reshape(ny // 8, 8, LANES), axis=0)
        tmp[x] = rest
    squares = jnp.full((8, LANES), jnp.sum(total), jnp.float32)

    core, area = place_ref[0] & 1, half * SLAB
    for ref, first in ((kept_ref, core * by), (sent_ref, (1 - core) * by)):
        for y in range(half // by):
            row = pl.multiple_of(2 * y * by + first, 8)
            for x in range(SLAB):
                to = x * half + y * by
                ref[pl.ds(to, by), :] = va[HALO + x, pl.ds(8 + row, by), :]
                ref[pl.ds(area + to, by), :] = tmp[x, pl.ds(row, by), :]
        ref[pl.ds(2 * area, 8), :] = squares


def merge_back_kernel(bx, by, chips_y, place_ref, kept_ref, got_ref, *out_refs):
    chip, core = place_ref[0] // 2, place_ref[0] & 1
    area, half = bx * by, chips_y * by
    for m, out_ref in enumerate(out_refs):
        target = jnp.bitwise_xor(chip, m)
        first = (target // chips_y) * bx * half + lax.rem(target, chips_y) * by
        for ref, column in ((kept_ref, core), (got_ref, 1 - core)):
            for n in range(2):
                for p in range(bx):
                    at = pl.multiple_of(first + (n * SLAB + p) * half, 8)
                    to = pl.multiple_of((2 * column + n) * area + p * by, 8)
                    out_ref[pl.ds(to, by), :] = ref[pl.ds(at, by), :]
            to = pl.multiple_of(4 * area + 8 * column, 8)
            out_ref[pl.ds(to, 8), :] = ref[pl.ds(2 * SLAB * half, 8), :]


def collect_kernel(place_ref, *refs):
    parts, (iterate_ref, residual_ref) = refs[:-2], refs[-2:]
    _, bx, by, _ = iterate_ref.shape
    area = bx * by
    for m, part in enumerate(parts):
        target = jnp.bitwise_xor(place_ref[0] // 2, m)
        for n in range(2):
            for k, ref in enumerate((iterate_ref, residual_ref)):
                rows = pl.ds((2 * n + k) * area, area)
                ref[2 * target + n] = part[rows, :].reshape(bx, by, LANES)


def squares_kernel(row, *refs):
    for m, part in enumerate(refs[:-1]):
        for n in range(2):
            refs[-1][pl.ds(2 * m + n, 1), :] = part[pl.ds(row + 8 * n, 1), :]


SMEM = pl.BlockSpec(memory_space=pltpu.SMEM)
VMEM = pl.BlockSpec(memory_space=pltpu.VMEM)


def local_kernel(kernel, name, scalars, arrays, outs, scratch=()):
    return pl.pallas_call(
        kernel,
        out_shape=[jax.ShapeDtypeStruct(shape, jnp.float32) for shape in outs],
        in_specs=[SMEM] * len(scalars) + [VMEM] * len(arrays),
        out_specs=[VMEM] * len(outs),
        scratch_shapes=[pltpu.VMEM(shape, jnp.float32) for shape in scratch],
        compiler_params=pltpu.CompilerParams(vmem_limit_bytes=VMEM_LIMIT),
        name=name,
    )(*scalars, *arrays)


def swap_in_plane(pieces, unit):
    devices = lax.axis_size("gx") * lax.axis_size("gy")
    moved = [pieces[0]]
    for k in range(1, len(pieces)):
        pairs = [(i, i ^ (k * unit)) for i in range(devices)]
        moved.append(lax.ppermute(pieces[k], ("gx", "gy"), pairs))
    return moved


def swap_slabs(piece, step, slabs):
    size = lax.axis_size("gx")
    moved = [piece]
    for k in range(1, slabs):
        pairs = [(i, i ^ (k * step)) for i in range(size)]
        moved.append(lax.ppermute(piece, "gx", pairs))
    return moved


def column_body(source, reaction, shifts, shift_index, velocity):
    columns, bx, by, nz = source.shape
    gx_size, gy_size = lax.axis_size("gx"), lax.axis_size("gy")
    nx, ny = bx * gx_size, by * gy_size
    step = columns // gy_size
    slabs = gx_size // step
    along, across = lax.axis_index("gx"), lax.axis_index("gy")
    column = lax.rem(along, step) * gy_size + across
    place = jnp.stack([column, along // step]).astype(jnp.int32)
    count = SLAB + 2 * HALO
    area = bx * by

    chips, chips_y = columns // 2, gy_size // 2
    cores = [(i, i ^ 1) for i in range(gy_size)]
    theirs = [lax.ppermute(source, "gy", cores), lax.ppermute(reaction, "gy", cores)]
    (mine,) = local_kernel(keep_kernel, "keep", (place,), (source,), [(chips, bx, by, nz)])
    *blocks, scalar_rows = local_kernel(
        merge_kernel,
        "merge",
        (place, shifts, shift_index, velocity),
        (mine, theirs[0], reaction, theirs[1]),
        [(2, bx, 2 * by, nz)] * chips + [(8, LANES)],
    )
    scalars = (place, scalar_rows)
    blocks = swap_in_plane(blocks, 2)

    edge = (2, NEAR, ny, nz)
    slab, *edges = local_kernel(
        functools.partial(arrange_kernel, chips_y),
        "arrange",
        (place,),
        blocks,
        [(2, SLAB, ny, nz), edge, edge],
    )

    def exchange(pieces):
        got = []
        for n, piece in enumerate(pieces):
            pairs = [(i, i + step if i // step % 2 == n else i - step) for i in range(gx_size)]
            pairs = [(i, j) for i, j in pairs if 0 <= j < gx_size]
            got.append(lax.ppermute(piece, "gx", pairs))
        return got

    grid, rimmed = (count, ny, nz), (count, ny + 16, nz)
    f, r, w, v1, coarse, *beyond = local_kernel(
        functools.partial(pre_kernel, slabs),
        "pre",
        scalars,
        (pool_matrix(0), pool_matrix(LANES // 2), slab, *exchange(edges)),
        [grid, grid, grid, rimmed, (SLAB // 2, ny // 2, nz)] + [(NEAR, ny, nz)] * 2,
        [rimmed, (SLAB, ny, nz), (2, SLAB // 2 * ny // 2, nz)],
    )
    gathered = swap_slabs(coarse, step, slabs)

    coarse_grid = (nx // 2, ny // 2, nz)
    coarse_rimmed = (nx // 2 + HALO, ny // 2 + 16, nz)
    window = (SLAB // 2 + HALO) * ny // 2
    (correction,) = local_kernel(
        functools.partial(coarse_kernel, (slabs, nx, ny, nz)),
        "coarse",
        scalars,
        (pool_matrix(0), spread_matrix(), *gathered),
        [(window, nz)],
        [coarse_grid] * 3 + [coarse_rimmed] * 2 + [(nx // 4 * ny // 2, nz), (nx // 2, ny // 2, nz)],
    )
    result = (SLAB * ny + 8, nz)
    kept, sent = local_kernel(
        functools.partial(post_kernel, by),
        "post",
        scalars,
        (f, r, w, v1, correction, *exchange(beyond)),
        [result, result],
        [rimmed] * 2 + [(SLAB, ny, nz)],
    )

    parts = local_kernel(
        functools.partial(merge_back_kernel, bx, by, chips_y),
        "merge_back",
        (place,),
        (kept, lax.ppermute(sent, "gy", cores)),
        [(4 * area + 16, nz)] * chips,
    )
    parts = swap_in_plane(parts, 2)
    (squares,) = local_kernel(
        functools.partial(squares_kernel, 4 * area), "squares", (), parts, [(columns, nz)]
    )
    iterate, residual = local_kernel(
        collect_kernel, "collect", (place,), parts, [source.shape] * 2
    )
    total = sum(swap_slabs(squares, step, slabs))
    rms = jnp.sqrt(total[:, 0] / (nx * ny * nz) + EPSILON)
    slots = jnp.arange(columns, dtype=jnp.int32)
    mine = jnp.bitwise_xor(slots, column // 2 * 2)[:, None] == slots[None, :]
    residual_rms = jnp.sum(jnp.where(mine, rms[None, :], 0.0), axis=1)
    return iterate, residual, residual_rms


def power_of_two(n):
    return n > 0 and n & (n - 1) == 0


def column_plan_fits(columns, bx, by, nz, gx_size, gy_size):
    if columns % gy_size or gx_size % (columns // gy_size):
        return False
    step = columns // gy_size
    slabs, ny = gx_size // step, by * gy_size
    whole = power_of_two(columns) and power_of_two(step) and power_of_two(slabs)
    small = slabs * ny * nz <= 2**15
    paired = step == 2 and bx == HALO and gy_size % 2 == 0
    return whole and small and paired and bx * step == SLAB and nz == LANES and by % 16 == 0


def solution(mesh):
    gx_size, gy_size = mesh.shape["gx"], mesh.shape["gy"]

    def body(source, reaction, shifts, shift_index, velocity):
        fits = column_plan_fits(*source.shape, gx_size, gy_size)
        plan = column_body if fits else halo_body
        return plan(source, reaction, shifts, shift_index, velocity)

    return jax.shard_map(
        body,
        mesh=mesh,
        in_specs=(P(None, "gx", "gy", None), P("gx", "gy", None), P(), P(), P()),
        out_specs=(P(None, "gx", "gy", None), P(None, "gx", "gy", None), P()),
        check_vma=False,
    )
```

```python
import functools

import jax
import jax.numpy as jnp
from jax import lax
from jax.experimental import pallas as pl
from jax.experimental.pallas import tpu as pltpu
from jax.sharding import PartitionSpec as P

LEVELS = 3
COARSE_SWEEPS = 6

DAMPING = 0.8
EPSILON = 1e-06
VMEM_LIMIT = 32 * 1024 * 1024
LANES = 128
GROUP = 4
SLAB = 8
HALO = 4
NEAR = 2


def with_halo(x, sides, width):
    for axis, dim in sides:
        peers, length = (lax.axis_size(axis), x.shape[dim])
        up = [(i, (i + 1) % peers) for i in range(peers - 1)]
        down = [(j, i) for i, j in up]
        last = lax.slice_in_dim(x, length - width, length, axis=dim)
        leading = lax.slice_in_dim(x, 0, width, axis=dim)
        before = lax.ppermute(last, axis, up)
        after = lax.ppermute(leading, axis, down)
        x = jnp.concatenate([before, x, after], axis=dim)
    return x


def select_shifts(shifts, shift_index):
    columns = jnp.arange(shifts.shape[0], dtype=jnp.int32)
    picked = jnp.where(shift_index[:, None] == columns[None, :], shifts[None, :], 0.0)
    return jnp.sum(picked, axis=1)


def coefficients(velocity, spacing):
    scale_a = 1.0 / (spacing * spacing)
    backward = scale_a + jnp.maximum(velocity, 0.0) / spacing
    forward = scale_a - jnp.minimum(velocity, 0.0) / spacing
    centre = 6.0 * scale_a + jnp.sum(jnp.abs(velocity)) / spacing
    return (backward, forward, centre)


def apply_stencil(padded, backward, forward, diagonal):
    middle = padded[:, 1:-1, 1:-1, :]
    along_z = jnp.pad(middle, ((0, 0), (0, 0), (0, 0), (1, 1)))
    others = backward[0] * padded[:, :-2, 1:-1, :] + forward[0] * padded[:, 2:, 1:-1, :]
    others = others + backward[1] * padded[:, 1:-1, :-2, :] + forward[1] * padded[:, 1:-1, 2:, :]
    others = others + backward[2] * along_z[:, :, :, :-2] + forward[2] * along_z[:, :, :, 2:]
    return diagonal * middle - others


def face_halo(iterate):
    return with_halo(iterate, (("gx", 1), ("gy", 2)), 1)


def coarsen(values):
    count, size_x, size_y, size_z = values.shape
    blocks = values.reshape(count, size_x // 2, 2, size_y // 2, 2, size_z // 2, 2)
    return jnp.sum(blocks, axis=(2, 4, 6)) * 0.125


def refine(values):
    return jnp.repeat(jnp.repeat(jnp.repeat(values, 2, 1), 2, 2), 2, 3)


def coarsest_solve(rhs_field, backward, forward, diagonal):
    iterate = DAMPING * rhs_field / diagonal
    for repeat in range(COARSE_SWEEPS - 1):
        applied = apply_stencil(face_halo(iterate), backward, forward, diagonal)
        iterate = iterate + DAMPING * (rhs_field - applied) / diagonal
    return iterate


def multigrid_cycle(level_index, rhs_field, reaction_l, shift_value, velocity):
    backward, forward, centre = coefficients(velocity, 2.0**level_index)
    diagonal = centre + reaction_l + shift_value[:, None, None, None]
    if level_index == LEVELS - 1:
        return coarsest_solve(rhs_field, backward, forward, diagonal)

    def operate(iterate):
        return apply_stencil(face_halo(iterate), backward, forward, diagonal)

    def smooth_step(iterate):
        return iterate + DAMPING * (rhs_field - operate(iterate)) / diagonal

    iterate = DAMPING * rhs_field / diagonal
    iterate = smooth_step(iterate)
    defect = rhs_field - operate(iterate)
    correction = multigrid_cycle(
        level_index + 1, coarsen(defect), coarsen(reaction_l), shift_value, velocity
    )
    iterate = iterate + refine(correction)
    iterate = smooth_step(iterate)
    iterate = smooth_step(iterate)
    return iterate


def halo_body(source, reaction, shifts, shift_index, velocity):
    columns, cells_x, cells_y, cells_z = source.shape
    shift_value = select_shifts(shifts, shift_index)
    reaction_top = reaction[None]
    backward, forward, centre = coefficients(velocity, 1.0)
    diagonal = centre + reaction_top + shift_value[:, None, None, None]

    iterate = multigrid_cycle(0, source, reaction_top, shift_value, velocity)
    residual = source - apply_stencil(face_halo(iterate), backward, forward, diagonal)
    local_squares = jnp.sum(residual * residual, axis=(1, 2, 3))
    squares = lax.psum(local_squares, ("gx", "gy"))
    total_cells = cells_x * cells_y * cells_z * lax.axis_size("gx") * lax.axis_size("gy")
    residual_rms = jnp.sqrt(squares / total_cells + EPSILON)
    return (iterate, residual, residual_rms)


def split_dot(values, matrix):
    high = values.astype(jnp.bfloat16)
    low = (values - high.astype(jnp.float32)).astype(jnp.bfloat16)
    return jnp.dot(high, matrix, preferred_element_type=jnp.float32) + jnp.dot(
        low, matrix, preferred_element_type=jnp.float32
    )


def sweep(planes, get, put):
    planes = list(planes)
    for first in range(0, len(planes), GROUP):
        group = planes[first : first + GROUP]
        values = [get(x) for x in group]
        for x, value in zip(group, values):
            put(x, value)


class Level:
    def __init__(self, index, ny, nz, rim, scalar_ref, f, r, w):
        self.ny, self.nz, self.rim = ny, nz, rim
        self.f, self.r, self.w = f, r, w
        spacing = 2.0**index
        scale_a = 1.0 / (spacing * spacing)
        inverse = 1.0 / spacing
        shift = scalar_ref[0, 0]
        speed = [scalar_ref[1 + d, 0] for d in range(3)]
        self.backward = [scale_a + jnp.maximum(v, 0.0) * inverse for v in speed]
        self.forward = [scale_a - jnp.minimum(v, 0.0) * inverse for v in speed]
        total = jnp.abs(speed[0]) + jnp.abs(speed[1]) + jnp.abs(speed[2])
        self.centre = 6.0 * scale_a + total * inverse + shift
        lane = lax.broadcasted_iota(jnp.int32, (1, LANES), 1)
        inside = lane < nz
        self.low_z = jnp.where((lane > 0) & inside, self.backward[2], 0.0)
        self.high_z = jnp.where(lane < nz - 1, self.forward[2], 0.0)

    def plane(self, v, x):
        return v[x + self.rim, pl.ds(8, self.ny), :]

    def put(self, v):
        def write(x, value):
            v[x + self.rim, pl.ds(8, self.ny), :] = value

        return write

    def along_z(self, middle):
        return self.low_z * pltpu.roll(middle, 1, 1) + self.high_z * pltpu.roll(middle, LANES - 1, 1)

    def neighbours(self, v, x, middle):
        at, ny = x + self.rim, self.ny
        along_x = self.backward[0] * v[at - 1, pl.ds(8, ny), :] + self.forward[0] * v[at + 1, pl.ds(8, ny), :]
        along_y = self.backward[1] * v[at, pl.ds(7, ny), :] + self.forward[1] * v[at, pl.ds(9, ny), :]
        return along_x + along_y + self.along_z(middle)

    def smoothed(self, v, x):
        middle = self.plane(v, x)
        pulled = self.f[x] + self.neighbours(v, x, middle)
        return (1.0 - DAMPING) * middle + self.w[x] * pulled

    def smooth(self, src, dst, planes):
        sweep(planes, lambda x: self.smoothed(src, x), self.put(dst))

    def defect(self, v, x):
        middle = self.plane(v, x)
        pulled = self.f[x] + self.neighbours(v, x, middle)
        return pulled - (self.r[x] + self.centre) * middle

    def pool_rows(self, value, rows):
        half, ny = self.ny // 2, self.ny
        rows[pl.ds(0, ny), :] = value
        return rows[pl.ds(0, half, stride=2), :] + rows[pl.ds(1, half, stride=2), :]

    def spread_rows(self, part, rows):
        half, ny = self.ny // 2, self.ny
        rows[pl.ds(0, half, stride=2), :] = part
        rows[pl.ds(1, half, stride=2), :] = part
        return rows[pl.ds(0, ny), :]

    def solve_in_registers(self, rhs, reaction):
        row = lax.broadcasted_iota(jnp.int32, (self.ny, 1), 0)
        low_y = jnp.where(row > 0, self.backward[1], 0.0)
        high_y = jnp.where(row < self.ny - 1, self.forward[1], 0.0)
        weight = [DAMPING / (r + self.centre) for r in reaction]
        v = [w * f for w, f in zip(weight, rhs)]
        for _ in range(COARSE_SWEEPS - 1):
            new = []
            for x, here in enumerate(v):
                along_y = low_y * pltpu.roll(here, 1, 0) + high_y * pltpu.roll(here, self.ny - 1, 0)
                pulled = rhs[x] + self.along_z(here) + along_y
                if x > 0:
                    pulled += self.backward[0] * v[x - 1]
                if x < len(v) - 1:
                    pulled += self.forward[0] * v[x + 1]
                new.append((1.0 - DAMPING) * here + weight[x] * pulled)
            v = new
        return jnp.concatenate(v, axis=0)


def zero_rows(v, ny):
    edge = jnp.zeros((v.shape[0], 8, LANES), jnp.float32)
    v[:, pl.ds(0, 8), :] = edge
    v[:, pl.ds(8 + ny, 8), :] = edge


def pool_matrix(offset):
    row = lax.broadcasted_iota(jnp.int32, (LANES, LANES), 0)
    col = lax.broadcasted_iota(jnp.int32, (LANES, LANES), 1)
    return jnp.where(row // 2 + offset == col, 0.125, 0.0).astype(jnp.bfloat16)


def spread_matrix():
    row = lax.broadcasted_iota(jnp.int32, (LANES, LANES), 0)
    col = lax.broadcasted_iota(jnp.int32, (LANES, LANES), 1)
    return jnp.where(col // 2 == row, 1.0, 0.0).astype(jnp.bfloat16)


def step_of(k, count):
    return -k % count


def keep_kernel(place_ref, source_ref, out_ref):
    for n in range(out_ref.shape[0]):
        out_ref[n] = source_ref[2 * n + (place_ref[0] & 1)]


def merge_kernel(place_ref, shifts_ref, index_ref, velocity_ref, *refs):
    mine_ref, theirs_ref, reaction_ref, other_reaction_ref = refs[:4]
    out_refs, scalar_ref = refs[4:-1], refs[-1]
    chip, core = place_ref[0] // 2, place_ref[0] & 1
    by = mine_ref.shape[2]
    mine = pl.ds(pl.multiple_of(core * by, 8), by)
    theirs = pl.ds(pl.multiple_of((1 - core) * by, 8), by)
    for m, out_ref in enumerate(out_refs):
        target = jnp.bitwise_xor(chip, step_of(m, len(out_refs)))
        out_ref[0, :, mine, :] = mine_ref[target]
        out_ref[0, :, theirs, :] = theirs_ref[2 * target + core]
        out_ref[1, :, mine, :] = reaction_ref[...]
        out_ref[1, :, theirs, :] = other_reaction_ref[...]
    scalars = [shifts_ref[index_ref[place_ref[0]]]] + [velocity_ref[d] for d in range(3)]
    for n, scalar in enumerate(scalars):
        scalar_ref[pl.ds(n, 1), :] = jnp.full((1, LANES), scalar, jnp.float32)


def arrange_kernel(chips_y, place_ref, *refs):
    blocks, (slab_ref, first_ref, second_ref) = refs[:-3], refs[-3:]
    for m, block in enumerate(blocks):
        owner = jnp.bitwise_xor(place_ref[0] // 2, step_of(m, len(blocks)))
        _, bx, size, _ = block.shape
        planes = pl.ds((owner // chips_y) * bx, bx)
        rows = pl.ds(pl.multiple_of(lax.rem(owner, chips_y) * size, 8), size)
        slab_ref[:, planes, rows, :] = block[...]
    even = 1 - (place_ref[1] & 1)
    first_ref[...] = slab_ref[:, pl.ds(even * (SLAB - NEAR), NEAR)]
    second_ref[...] = slab_ref[:, pl.ds((1 - even) * (SLAB - NEAR), NEAR)]


def pre_kernel(slabs, place_ref, scalar_ref, *refs):
    pool_ref, pool_up_ref, slab_ref, first_ref, second_ref = refs[:5]
    f, r, w, v1, coarse_ref, first_out, second_out, v0, tmp, pooled = refs[5:]
    ny = f.shape[1]
    slab = place_ref[1]
    fine = Level(0, ny, LANES, 0, scalar_ref, f, r, w)
    zero_rows(v0, ny)
    zero_rows(v1, ny)
    after = HALO + SLAB
    even = 1 - (slab & 1)

    f[pl.ds(HALO, SLAB)], r[pl.ds(HALO, SLAB)] = slab_ref[0], slab_ref[1]
    for ref, above in ((first_ref, even), (second_ref, 1 - even)):
        planes = pl.ds((HALO - NEAR) + above * (SLAB + NEAR), NEAR)
        f[planes], r[planes] = ref[0], ref[1]

    inside = [jnp.where(slab > 0, DAMPING, 0.0)] * HALO
    inside += [DAMPING] * SLAB
    inside += [jnp.where(slab < slabs - 1, DAMPING, 0.0)] * HALO

    def put(x, weight):
        w[x] = weight
        v0[x, pl.ds(8, ny), :] = weight * f[x]

    known = range(HALO - NEAR, after + NEAR)
    sweep(known, lambda x: inside[x] / (r[x] + fine.centre), put)
    fine.smooth(v0, v1, known[1:-1])
    for ref, above in ((first_out, even), (second_out, 1 - even)):
        ref[...] = v1[pl.ds(HALO + 1 + above * (SLAB - HALO), NEAR), pl.ds(8, ny), :]
    half = ny // 2

    def coarsened(x):
        at = HALO + 2 * x
        return fine.defect(v1, at) + fine.defect(v1, at + 1), r[at] + r[at + 1]

    def put_pooled(x, pair):
        for n in range(2):
            pooled[n, pl.ds(x * half, half), :] = fine.pool_rows(pair[n], tmp.at[2 * x + n])

    sweep(range(SLAB // 2), coarsened, put_pooled)
    packed = split_dot(pooled[0], pool_ref[...]) + split_dot(pooled[1], pool_up_ref[...])
    coarse_ref[...] = packed.reshape(coarse_ref.shape)


def coarse_kernel(grid, place_ref, scalar_ref, *refs):
    slabs, nx, ny, nz = grid
    pool_ref, spread_ref = refs[:2]
    coarse, out_ref = refs[2 : 2 + slabs], refs[2 + slabs]
    f1, r1, w1, v1a, v1b, pooled, tmp = refs[3 + slabs :]
    pool, spread = pool_ref[...], spread_ref[...]
    slab = place_ref[1]
    rim = HALO // 2
    nx1, ny1, nx2, ny2 = nx // 2, ny // 2, nx // 4, ny // 4
    mid = Level(1, ny1, nz // 2, rim, scalar_ref, f1, r1, w1)
    deep = Level(2, ny2, nz // 4, 0, scalar_ref, None, None, None)
    for v in (v1a, v1b):
        zero_rows(v, ny1)
        blank = jnp.zeros((rim,) + v.shape[1:], jnp.float32)
        v[pl.ds(0, rim)] = blank
        v[pl.ds(rim + nx1, rim)] = blank

    lower = lax.broadcasted_iota(jnp.int32, (1, LANES), 1) < LANES // 2
    own = SLAB // 2
    for k in range(slabs):
        first = jnp.bitwise_xor(slab, k) * own
        both = coarse[k][...]
        f1[pl.ds(first, own)] = jnp.where(lower, both, 0.0)
        r1[pl.ds(first, own)] = jnp.where(lower, pltpu.roll(both, LANES // 2, 2), 0.0)

    def put_start(x, weight):
        w1[x] = weight
        v1a[x + rim, pl.ds(8, ny1), :] = weight * f1[x]

    sweep(range(nx1), lambda x: DAMPING / (r1[x] + mid.centre), put_start)
    mid.smooth(v1a, v1b, range(nx1))

    def coarsened(x):
        return mid.defect(v1b, 2 * x) + mid.defect(v1b, 2 * x + 1), r1[2 * x] + r1[2 * x + 1]

    rows2 = nx2 * ny2

    def put_pooled(x, pair):
        for n in range(2):
            value = mid.pool_rows(pair[n], tmp.at[2 * x + n])
            pooled[pl.ds(n * rows2 + x * ny2, ny2), :] = value

    sweep(range(nx2), coarsened, put_pooled)
    deeper = split_dot(pooled[pl.ds(0, 2 * rows2), :], pool)
    planes = [deeper[n * ny2 : (n + 1) * ny2] for n in range(2 * nx2)]
    values = deep.solve_in_registers(planes[:nx2], planes[nx2:])

    pooled[pl.ds(0, rows2), :] = split_dot(values, spread)

    def refined1(x):
        return mid.spread_rows(pooled[pl.ds(x * ny2, ny2), :], tmp.at[x])

    def put_refined1(x, value):
        for n in range(2):
            v1b[2 * x + n + rim, pl.ds(8, ny1), :] += value

    sweep(range(nx2), refined1, put_refined1)
    mid.smooth(v1b, v1a, range(nx1))
    mid.smooth(v1a, v1b, range(nx1))

    window = own + 2 * rim
    values = v1b[pl.ds(slab * own, window), pl.ds(8, ny1), :].reshape(window * ny1, LANES)
    out_ref[...] = split_dot(values, spread)


def post_kernel(by, place_ref, scalar_ref, *refs):
    f, r, w, v1, correction, first_ref, second_ref, kept_ref, sent_ref, va, vb, tmp = refs
    count, ny = f.shape[:2]
    fine = Level(0, ny, LANES, 0, scalar_ref, f, r, w)
    for v in (va, vb):
        zero_rows(v, ny)
    even, half = 1 - (place_ref[1] & 1), ny // 2
    window = correction.shape[0] // half
    for ref, above in ((first_ref, even), (second_ref, 1 - even)):
        va[pl.ds(1 + above * (SLAB + HALO), NEAR), pl.ds(8, ny), :] = ref[...]

    def refined(x):
        return fine.spread_rows(correction[pl.ds(x * half, half), :], tmp.at[x])

    def put_refined(x, value):
        for at in (2 * x, 2 * x + 1):
            if 0 < at < count - 1:
                known = HALO - NEAR < at < HALO + SLAB + NEAR - 1
                here = v1 if known else va
                va[at, pl.ds(8, ny), :] = here[at, pl.ds(8, ny), :] + value

    sweep(range(window), refined, put_refined)
    fine.smooth(va, vb, range(2, count - 2))
    fine.smooth(vb, va, range(3, count - 3))

    total = jnp.zeros((8, LANES), jnp.float32)
    for x in range(SLAB):
        rest = fine.defect(va, HALO + x)
        total = total + jnp.sum((rest * rest).reshape(ny // 8, 8, LANES), axis=0)
        tmp[x] = rest
    squares = jnp.full((8, LANES), jnp.sum(total), jnp.float32)

    core, area = place_ref[0] & 1, half * SLAB
    for ref, first in ((kept_ref, core * by), (sent_ref, (1 - core) * by)):
        for y in range(half // by):
            row = pl.multiple_of(2 * y * by + first, 8)
            for x in range(SLAB):
                to = x * half + y * by
                ref[pl.ds(to, by), :] = va[HALO + x, pl.ds(8 + row, by), :]
                ref[pl.ds(area + to, by), :] = tmp[x, pl.ds(row, by), :]
        ref[pl.ds(2 * area, 8), :] = squares


def merge_back_kernel(bx, by, chips_y, place_ref, kept_ref, got_ref, *out_refs):
    chip, core = place_ref[0] // 2, place_ref[0] & 1
    area, half = bx * by, chips_y * by
    for m, out_ref in enumerate(out_refs):
        target = jnp.bitwise_xor(chip, step_of(m, len(out_refs)))
        first = (target // chips_y) * bx * half + lax.rem(target, chips_y) * by
        for ref, column in ((kept_ref, core), (got_ref, 1 - core)):
            for n in range(2):
                for p in range(bx):
                    at = pl.multiple_of(first + (n * SLAB + p) * half, 8)
                    to = pl.multiple_of((2 * column + n) * area + p * by, 8)
                    out_ref[pl.ds(to, by), :] = ref[pl.ds(at, by), :]
            to = pl.multiple_of(4 * area + 8 * column, 8)
            out_ref[pl.ds(to, 8), :] = ref[pl.ds(2 * SLAB * half, 8), :]


def collect_kernel(place_ref, *refs):
    parts, (iterate_ref, residual_ref) = refs[:-2], refs[-2:]
    _, bx, by, _ = iterate_ref.shape
    area = bx * by
    for m, part in enumerate(parts):
        target = jnp.bitwise_xor(place_ref[0] // 2, step_of(m, len(parts)))
        for n in range(2):
            for k, ref in enumerate((iterate_ref, residual_ref)):
                rows = pl.ds((2 * n + k) * area, area)
                ref[2 * target + n] = part[rows, :].reshape(bx, by, LANES)


def squares_kernel(row, *refs):
    for m, part in enumerate(refs[:-1]):
        for n in range(2):
            refs[-1][pl.ds(2 * m + n, 1), :] = part[pl.ds(row + 8 * n, 1), :]


SMEM = pl.BlockSpec(memory_space=pltpu.SMEM)
VMEM = pl.BlockSpec(memory_space=pltpu.VMEM)


def local_kernel(kernel, name, scalars, arrays, outs, scratch=()):
    return pl.pallas_call(
        kernel,
        out_shape=[jax.ShapeDtypeStruct(shape, jnp.float32) for shape in outs],
        in_specs=[SMEM] * len(scalars) + [VMEM] * len(arrays),
        out_specs=[VMEM] * len(outs),
        scratch_shapes=[pltpu.VMEM(shape, jnp.float32) for shape in scratch],
        compiler_params=pltpu.CompilerParams(vmem_limit_bytes=VMEM_LIMIT),
        name=name,
    )(*scalars, *arrays)


def swap_in_plane(pieces, unit):
    devices = lax.axis_size("gx") * lax.axis_size("gy")
    moved = [pieces[0]]
    for k in range(1, len(pieces)):
        pairs = [(i, i ^ (step_of(k, len(pieces)) * unit)) for i in range(devices)]
        moved.append(lax.ppermute(pieces[k], ("gx", "gy"), pairs))
    return moved


def swap_slabs(piece, step, slabs):
    size = lax.axis_size("gx")
    moved = [piece]
    for k in range(1, slabs):
        pairs = [(i, i ^ (k * step)) for i in range(size)]
        moved.append(lax.ppermute(piece, "gx", pairs))
    return moved


def column_body(source, reaction, shifts, shift_index, velocity):
    columns, bx, by, nz = source.shape
    gx_size, gy_size = lax.axis_size("gx"), lax.axis_size("gy")
    nx, ny = bx * gx_size, by * gy_size
    step = columns // gy_size
    slabs = gx_size // step
    along, across = lax.axis_index("gx"), lax.axis_index("gy")
    column = lax.rem(along, step) * gy_size + across
    place = jnp.stack([column, along // step]).astype(jnp.int32)
    count = SLAB + 2 * HALO
    area = bx * by

    chips, chips_y = columns // 2, gy_size // 2
    cores = [(i, i ^ 1) for i in range(gy_size)]
    theirs = [lax.ppermute(source, "gy", cores), lax.ppermute(reaction, "gy", cores)]
    (mine,) = local_kernel(keep_kernel, "keep", (place,), (source,), [(chips, bx, by, nz)])
    *blocks, scalar_rows = local_kernel(
        merge_kernel,
        "merge",
        (place, shifts, shift_index, velocity),
        (mine, theirs[0], reaction, theirs[1]),
        [(2, bx, 2 * by, nz)] * chips + [(8, LANES)],
    )
    scalars = (place, scalar_rows)
    blocks = swap_in_plane(blocks, 2)

    edge = (2, NEAR, ny, nz)
    slab, *edges = local_kernel(
        functools.partial(arrange_kernel, chips_y),
        "arrange",
        (place,),
        blocks,
        [(2, SLAB, ny, nz), edge, edge],
    )

    def exchange(pieces):
        got = []
        for n, piece in enumerate(pieces):
            pairs = [(i, i + step if i // step % 2 == n else i - step) for i in range(gx_size)]
            pairs = [(i, j) for i, j in pairs if 0 <= j < gx_size]
            got.append(lax.ppermute(piece, "gx", pairs))
        return got

    grid, rimmed = (count, ny, nz), (count, ny + 16, nz)
    f, r, w, v1, coarse, *beyond = local_kernel(
        functools.partial(pre_kernel, slabs),
        "pre",
        scalars,
        (pool_matrix(0), pool_matrix(LANES // 2), slab, *exchange(edges)),
        [grid, grid, grid, rimmed, (SLAB // 2, ny // 2, nz)] + [(NEAR, ny, nz)] * 2,
        [rimmed, (SLAB, ny, nz), (2, SLAB // 2 * ny // 2, nz)],
    )
    gathered = swap_slabs(coarse, step, slabs)

    coarse_grid = (nx // 2, ny // 2, nz)
    coarse_rimmed = (nx // 2 + HALO, ny // 2 + 16, nz)
    window = (SLAB // 2 + HALO) * ny // 2
    (correction,) = local_kernel(
        functools.partial(coarse_kernel, (slabs, nx, ny, nz)),
        "coarse",
        scalars,
        (pool_matrix(0), spread_matrix(), *gathered),
        [(window, nz)],
        [coarse_grid] * 3 + [coarse_rimmed] * 2 + [(nx // 4 * ny // 2, nz), (nx // 2, ny // 2, nz)],
    )
    result = (SLAB * ny + 8, nz)
    kept, sent = local_kernel(
        functools.partial(post_kernel, by),
        "post",
        scalars,
        (f, r, w, v1, correction, *exchange(beyond)),
        [result, result],
        [rimmed] * 2 + [(SLAB, ny, nz)],
    )

    parts = local_kernel(
        functools.partial(merge_back_kernel, bx, by, chips_y),
        "merge_back",
        (place,),
        (kept, lax.ppermute(sent, "gy", cores)),
        [(4 * area + 16, nz)] * chips,
    )
    parts = swap_in_plane(parts, 2)
    (squares,) = local_kernel(
        functools.partial(squares_kernel, 4 * area), "squares", (), parts, [(columns, nz)]
    )
    iterate, residual = local_kernel(
        collect_kernel, "collect", (place,), parts, [source.shape] * 2
    )
    total = sum(swap_slabs(squares, step, slabs))
    rms = jnp.sqrt(total[:, 0] / (nx * ny * nz) + EPSILON)
    slots = jnp.arange(columns, dtype=jnp.int32)
    order = jnp.array([2 * step_of(k, chips) + n for k in range(chips) for n in range(2)], jnp.int32)
    mine = jnp.bitwise_xor(slots, column // 2 * 2)[:, None] == order[None, :]
    residual_rms = jnp.sum(jnp.where(mine, rms[None, :], 0.0), axis=1)
    return iterate, residual, residual_rms


def power_of_two(n):
    return n > 0 and n & (n - 1) == 0


def column_plan_fits(columns, bx, by, nz, gx_size, gy_size):
    if columns % gy_size or gx_size % (columns // gy_size):
        return False
    step = columns // gy_size
    slabs, ny = gx_size // step, by * gy_size
    whole = power_of_two(columns) and power_of_two(step) and power_of_two(slabs)
    small = slabs * ny * nz <= 2**15
    paired = step == 2 and bx == HALO and gy_size % 2 == 0
    return whole and small and paired and bx * step == SLAB and nz == LANES and by % 16 == 0


def solution(mesh):
    gx_size, gy_size = mesh.shape["gx"], mesh.shape["gy"]

    def body(source, reaction, shifts, shift_index, velocity):
        fits = column_plan_fits(*source.shape, gx_size, gy_size)
        plan = column_body if fits else halo_body
        return plan(source, reaction, shifts, shift_index, velocity)

    return jax.shard_map(
        body,
        mesh=mesh,
        in_specs=(P(None, "gx", "gy", None), P("gx", "gy", None), P(), P(), P()),
        out_specs=(P(None, "gx", "gy", None), P(None, "gx", "gy", None), P()),
        check_vma=False,
    )
```

```python
import functools

import jax
import jax.numpy as jnp
from jax import lax
from jax.experimental import pallas as pl
from jax.experimental.pallas import tpu as pltpu
from jax.sharding import PartitionSpec as P

LEVELS = 3
COARSE_SWEEPS = 6

DAMPING = 0.8
EPSILON = 1e-06
VMEM_LIMIT = 32 * 1024 * 1024
LANES = 128
GROUP = 4
SLAB = 8
HALO = 4
NEAR = 2


def with_halo(x, sides, width):
    for axis, dim in sides:
        peers, length = (lax.axis_size(axis), x.shape[dim])
        up = [(i, (i + 1) % peers) for i in range(peers - 1)]
        down = [(j, i) for i, j in up]
        last = lax.slice_in_dim(x, length - width, length, axis=dim)
        leading = lax.slice_in_dim(x, 0, width, axis=dim)
        before = lax.ppermute(last, axis, up)
        after = lax.ppermute(leading, axis, down)
        x = jnp.concatenate([before, x, after], axis=dim)
    return x


def select_shifts(shifts, shift_index):
    columns = jnp.arange(shifts.shape[0], dtype=jnp.int32)
    picked = jnp.where(shift_index[:, None] == columns[None, :], shifts[None, :], 0.0)
    return jnp.sum(picked, axis=1)


def coefficients(velocity, spacing):
    scale_a = 1.0 / (spacing * spacing)
    backward = scale_a + jnp.maximum(velocity, 0.0) / spacing
    forward = scale_a - jnp.minimum(velocity, 0.0) / spacing
    centre = 6.0 * scale_a + jnp.sum(jnp.abs(velocity)) / spacing
    return (backward, forward, centre)


def apply_stencil(padded, backward, forward, diagonal):
    middle = padded[:, 1:-1, 1:-1, :]
    along_z = jnp.pad(middle, ((0, 0), (0, 0), (0, 0), (1, 1)))
    others = backward[0] * padded[:, :-2, 1:-1, :] + forward[0] * padded[:, 2:, 1:-1, :]
    others = others + backward[1] * padded[:, 1:-1, :-2, :] + forward[1] * padded[:, 1:-1, 2:, :]
    others = others + backward[2] * along_z[:, :, :, :-2] + forward[2] * along_z[:, :, :, 2:]
    return diagonal * middle - others


def face_halo(iterate):
    return with_halo(iterate, (("gx", 1), ("gy", 2)), 1)


def coarsen(values):
    count, size_x, size_y, size_z = values.shape
    blocks = values.reshape(count, size_x // 2, 2, size_y // 2, 2, size_z // 2, 2)
    return jnp.sum(blocks, axis=(2, 4, 6)) * 0.125


def refine(values):
    return jnp.repeat(jnp.repeat(jnp.repeat(values, 2, 1), 2, 2), 2, 3)


def coarsest_solve(rhs_field, backward, forward, diagonal):
    iterate = DAMPING * rhs_field / diagonal
    for repeat in range(COARSE_SWEEPS - 1):
        applied = apply_stencil(face_halo(iterate), backward, forward, diagonal)
        iterate = iterate + DAMPING * (rhs_field - applied) / diagonal
    return iterate


def multigrid_cycle(level_index, rhs_field, reaction_l, shift_value, velocity):
    backward, forward, centre = coefficients(velocity, 2.0**level_index)
    diagonal = centre + reaction_l + shift_value[:, None, None, None]
    if level_index == LEVELS - 1:
        return coarsest_solve(rhs_field, backward, forward, diagonal)

    def operate(iterate):
        return apply_stencil(face_halo(iterate), backward, forward, diagonal)

    def smooth_step(iterate):
        return iterate + DAMPING * (rhs_field - operate(iterate)) / diagonal

    iterate = DAMPING * rhs_field / diagonal
    iterate = smooth_step(iterate)
    defect = rhs_field - operate(iterate)
    correction = multigrid_cycle(
        level_index + 1, coarsen(defect), coarsen(reaction_l), shift_value, velocity
    )
    iterate = iterate + refine(correction)
    iterate = smooth_step(iterate)
    iterate = smooth_step(iterate)
    return iterate


def halo_body(source, reaction, shifts, shift_index, velocity):
    columns, cells_x, cells_y, cells_z = source.shape
    shift_value = select_shifts(shifts, shift_index)
    reaction_top = reaction[None]
    backward, forward, centre = coefficients(velocity, 1.0)
    diagonal = centre + reaction_top + shift_value[:, None, None, None]

    iterate = multigrid_cycle(0, source, reaction_top, shift_value, velocity)
    residual = source - apply_stencil(face_halo(iterate), backward, forward, diagonal)
    local_squares = jnp.sum(residual * residual, axis=(1, 2, 3))
    squares = lax.psum(local_squares, ("gx", "gy"))
    total_cells = cells_x * cells_y * cells_z * lax.axis_size("gx") * lax.axis_size("gy")
    residual_rms = jnp.sqrt(squares / total_cells + EPSILON)
    return (iterate, residual, residual_rms)


def split_dot(values, matrix):
    high = values.astype(jnp.bfloat16)
    low = (values - high.astype(jnp.float32)).astype(jnp.bfloat16)
    return jnp.dot(high, matrix, preferred_element_type=jnp.float32) + jnp.dot(
        low, matrix, preferred_element_type=jnp.float32
    )


def sweep(planes, get, put):
    planes = list(planes)
    for first in range(0, len(planes), GROUP):
        group = planes[first : first + GROUP]
        values = [get(x) for x in group]
        for x, value in zip(group, values):
            put(x, value)


class Level:
    def __init__(self, index, ny, nz, rim, scalar_ref, f, r, w):
        self.ny, self.nz, self.rim = ny, nz, rim
        self.f, self.r, self.w = f, r, w
        spacing = 2.0**index
        scale_a = 1.0 / (spacing * spacing)
        inverse = 1.0 / spacing
        shift = scalar_ref[0, 0]
        speed = [scalar_ref[1 + d, 0] for d in range(3)]
        self.backward = [scale_a + jnp.maximum(v, 0.0) * inverse for v in speed]
        self.forward = [scale_a - jnp.minimum(v, 0.0) * inverse for v in speed]
        total = jnp.abs(speed[0]) + jnp.abs(speed[1]) + jnp.abs(speed[2])
        self.centre = 6.0 * scale_a + total * inverse + shift
        lane = lax.broadcasted_iota(jnp.int32, (1, LANES), 1)
        inside = lane < nz
        self.low_z = jnp.where((lane > 0) & inside, self.backward[2], 0.0)
        self.high_z = jnp.where(lane < nz - 1, self.forward[2], 0.0)

    def plane(self, v, x):
        return v[x + self.rim, pl.ds(8, self.ny), :]

    def put(self, v):
        def write(x, value):
            v[x + self.rim, pl.ds(8, self.ny), :] = value

        return write

    def along_z(self, middle):
        return self.low_z * pltpu.roll(middle, 1, 1) + self.high_z * pltpu.roll(middle, LANES - 1, 1)

    def neighbours(self, v, x, middle):
        at, ny = x + self.rim, self.ny
        along_x = self.backward[0] * v[at - 1, pl.ds(8, ny), :] + self.forward[0] * v[at + 1, pl.ds(8, ny), :]
        along_y = self.backward[1] * v[at, pl.ds(7, ny), :] + self.forward[1] * v[at, pl.ds(9, ny), :]
        return along_x + along_y + self.along_z(middle)

    def smoothed(self, v, x):
        middle = self.plane(v, x)
        pulled = self.f[x] + self.neighbours(v, x, middle)
        return (1.0 - DAMPING) * middle + self.w[x] * pulled

    def smooth(self, src, dst, planes):
        sweep(planes, lambda x: self.smoothed(src, x), self.put(dst))

    def defect(self, v, x):
        middle = self.plane(v, x)
        pulled = self.f[x] + self.neighbours(v, x, middle)
        return pulled - (self.r[x] + self.centre) * middle

    def pool_rows(self, value, rows):
        half, ny = self.ny // 2, self.ny
        rows[pl.ds(0, ny), :] = value
        return rows[pl.ds(0, half, stride=2), :] + rows[pl.ds(1, half, stride=2), :]

    def spread_rows(self, part, rows):
        half, ny = self.ny // 2, self.ny
        rows[pl.ds(0, half, stride=2), :] = part
        rows[pl.ds(1, half, stride=2), :] = part
        return rows[pl.ds(0, ny), :]

    def solve_in_registers(self, rhs, reaction):
        row = lax.broadcasted_iota(jnp.int32, (self.ny, 1), 0)
        low_y = jnp.where(row > 0, self.backward[1], 0.0)
        high_y = jnp.where(row < self.ny - 1, self.forward[1], 0.0)
        weight = [DAMPING / (r + self.centre) for r in reaction]
        v = [w * f for w, f in zip(weight, rhs)]
        for _ in range(COARSE_SWEEPS - 1):
            new = []
            for x, here in enumerate(v):
                along_y = low_y * pltpu.roll(here, 1, 0) + high_y * pltpu.roll(here, self.ny - 1, 0)
                pulled = rhs[x] + self.along_z(here) + along_y
                if x > 0:
                    pulled += self.backward[0] * v[x - 1]
                if x < len(v) - 1:
                    pulled += self.forward[0] * v[x + 1]
                new.append((1.0 - DAMPING) * here + weight[x] * pulled)
            v = new
        return jnp.concatenate(v, axis=0)


def zero_rows(v, ny):
    edge = jnp.zeros((v.shape[0], 8, LANES), jnp.float32)
    v[:, pl.ds(0, 8), :] = edge
    v[:, pl.ds(8 + ny, 8), :] = edge


def pool_matrix(offset):
    row = lax.broadcasted_iota(jnp.int32, (LANES, LANES), 0)
    col = lax.broadcasted_iota(jnp.int32, (LANES, LANES), 1)
    return jnp.where(row // 2 + offset == col, 0.125, 0.0).astype(jnp.bfloat16)


def spread_matrix():
    row = lax.broadcasted_iota(jnp.int32, (LANES, LANES), 0)
    col = lax.broadcasted_iota(jnp.int32, (LANES, LANES), 1)
    return jnp.where(col // 2 == row, 1.0, 0.0).astype(jnp.bfloat16)


def keep_kernel(place_ref, source_ref, out_ref):
    for n in range(out_ref.shape[0]):
        out_ref[n] = source_ref[2 * n + (place_ref[0] & 1)]


def merge_kernel(place_ref, shifts_ref, index_ref, velocity_ref, *refs):
    mine_ref, theirs_ref, reaction_ref, other_reaction_ref = refs[:4]
    out_refs, scalar_ref = refs[4:-1], refs[-1]
    chip, core = place_ref[0] // 2, place_ref[0] & 1
    by = mine_ref.shape[2]
    mine = pl.ds(pl.multiple_of(core * by, 8), by)
    theirs = pl.ds(pl.multiple_of((1 - core) * by, 8), by)
    for m, out_ref in enumerate(out_refs):
        target = jnp.bitwise_xor(chip, m)
        out_ref[0, :, mine, :] = mine_ref[target]
        out_ref[0, :, theirs, :] = theirs_ref[2 * target + core]
        out_ref[1, :, mine, :] = reaction_ref[...]
        out_ref[1, :, theirs, :] = other_reaction_ref[...]
    scalars = [shifts_ref[index_ref[place_ref[0]]]] + [velocity_ref[d] for d in range(3)]
    for n, scalar in enumerate(scalars):
        scalar_ref[pl.ds(n, 1), :] = jnp.full((1, LANES), scalar, jnp.float32)


def edge_kernel(chips_y, place_ref, *refs):
    blocks, edge_ref = refs[:-1], refs[-1]
    for m, block in enumerate(blocks):
        chip = jnp.bitwise_xor(place_ref[0] // 2, m)
        _, bx, size, _ = block.shape
        planes = pl.ds((chip // chips_y) * (bx - NEAR), NEAR)
        rows = pl.ds(pl.multiple_of(lax.rem(chip, chips_y) * size, 8), size)
        edge_ref[:, :, rows, :] = block[:, planes]


def arrange_kernel(chips_y, place_ref, *refs):
    blocks, (slab_ref, edge_ref) = refs[:-2], refs[-2:]
    chip = place_ref[0] // 2
    for m, block in enumerate(blocks):
        owner = jnp.bitwise_xor(chip, m)
        _, bx, size, _ = block.shape
        planes = pl.ds((owner // chips_y) * bx, bx)
        rows = pl.ds(pl.multiple_of(lax.rem(owner, chips_y) * size, 8), size)
        slab_ref[:, planes, rows, :] = block[...]
    edge_ref[...] = slab_ref[:, pl.ds((1 - chip // chips_y) * (SLAB - NEAR), NEAR)]


def pre_kernel(slabs, chips_y, place_ref, scalar_ref, *refs):
    pool_ref, pool_up_ref, slab_ref, first_ref, second_ref = refs[:5]
    f, r, w, v1, coarse_ref, first_out, second_out, v0, tmp, pooled = refs[5:]
    ny = f.shape[1]
    slab = place_ref[1]
    fine = Level(0, ny, LANES, 0, scalar_ref, f, r, w)
    zero_rows(v0, ny)
    zero_rows(v1, ny)
    after = HALO + SLAB
    even = 1 - (slab & 1)

    f[pl.ds(HALO, SLAB)], r[pl.ds(HALO, SLAB)] = slab_ref[0], slab_ref[1]
    x = place_ref[0] // 2 // chips_y
    for ref, above in ((first_ref, 1 - x), (second_ref, x)):
        planes = pl.ds((HALO - NEAR) + above * (SLAB + NEAR), NEAR)
        f[planes], r[planes] = ref[0], ref[1]

    inside = [jnp.where(slab > 0, DAMPING, 0.0)] * HALO
    inside += [DAMPING] * SLAB
    inside += [jnp.where(slab < slabs - 1, DAMPING, 0.0)] * HALO

    def put(x, weight):
        w[x] = weight
        v0[x, pl.ds(8, ny), :] = weight * f[x]

    known = range(HALO - NEAR, after + NEAR)
    sweep(known, lambda x: inside[x] / (r[x] + fine.centre), put)
    fine.smooth(v0, v1, known[1:-1])
    for ref, above in ((first_out, even), (second_out, 1 - even)):
        ref[...] = v1[pl.ds(HALO + 1 + above * (SLAB - HALO), NEAR), pl.ds(8, ny), :]
    half = ny // 2

    def coarsened(x):
        at = HALO + 2 * x
        return fine.defect(v1, at) + fine.defect(v1, at + 1), r[at] + r[at + 1]

    def put_pooled(x, pair):
        for n in range(2):
            pooled[n, pl.ds(x * half, half), :] = fine.pool_rows(pair[n], tmp.at[2 * x + n])

    sweep(range(SLAB // 2), coarsened, put_pooled)
    packed = split_dot(pooled[0], pool_ref[...]) + split_dot(pooled[1], pool_up_ref[...])
    coarse_ref[...] = packed.reshape(coarse_ref.shape)


def coarse_kernel(grid, place_ref, scalar_ref, *refs):
    slabs, nx, ny, nz = grid
    pool_ref, spread_ref = refs[:2]
    coarse, out_ref = refs[2 : 2 + slabs], refs[2 + slabs]
    f1, r1, w1, v1a, v1b, pooled, tmp = refs[3 + slabs :]
    pool, spread = pool_ref[...], spread_ref[...]
    slab = place_ref[1]
    rim = HALO // 2
    nx1, ny1, nx2, ny2 = nx // 2, ny // 2, nx // 4, ny // 4
    mid = Level(1, ny1, nz // 2, rim, scalar_ref, f1, r1, w1)
    deep = Level(2, ny2, nz // 4, 0, scalar_ref, None, None, None)
    for v in (v1a, v1b):
        zero_rows(v, ny1)
        blank = jnp.zeros((rim,) + v.shape[1:], jnp.float32)
        v[pl.ds(0, rim)] = blank
        v[pl.ds(rim + nx1, rim)] = blank

    lower = lax.broadcasted_iota(jnp.int32, (1, LANES), 1) < LANES // 2
    own = SLAB // 2
    for k in range(slabs):
        first = jnp.bitwise_xor(slab, k) * own
        both = coarse[k][...]
        f1[pl.ds(first, own)] = jnp.where(lower, both, 0.0)
        r1[pl.ds(first, own)] = jnp.where(lower, pltpu.roll(both, LANES // 2, 2), 0.0)

    def put_start(x, weight):
        w1[x] = weight
        v1a[x + rim, pl.ds(8, ny1), :] = weight * f1[x]

    sweep(range(nx1), lambda x: DAMPING / (r1[x] + mid.centre), put_start)
    mid.smooth(v1a, v1b, range(nx1))

    def coarsened(x):
        return mid.defect(v1b, 2 * x) + mid.defect(v1b, 2 * x + 1), r1[2 * x] + r1[2 * x + 1]

    rows2 = nx2 * ny2

    def put_pooled(x, pair):
        for n in range(2):
            value = mid.pool_rows(pair[n], tmp.at[2 * x + n])
            pooled[pl.ds(n * rows2 + x * ny2, ny2), :] = value

    sweep(range(nx2), coarsened, put_pooled)
    deeper = split_dot(pooled[pl.ds(0, 2 * rows2), :], pool)
    planes = [deeper[n * ny2 : (n + 1) * ny2] for n in range(2 * nx2)]
    values = deep.solve_in_registers(planes[:nx2], planes[nx2:])

    pooled[pl.ds(0, rows2), :] = split_dot(values, spread)

    def refined1(x):
        return mid.spread_rows(pooled[pl.ds(x * ny2, ny2), :], tmp.at[x])

    def put_refined1(x, value):
        for n in range(2):
            v1b[2 * x + n + rim, pl.ds(8, ny1), :] += value

    sweep(range(nx2), refined1, put_refined1)
    mid.smooth(v1b, v1a, range(nx1))
    mid.smooth(v1a, v1b, range(nx1))

    window = own + 2 * rim
    values = v1b[pl.ds(slab * own, window), pl.ds(8, ny1), :].reshape(window * ny1, LANES)
    out_ref[...] = split_dot(values, spread)


def post_kernel(by, place_ref, scalar_ref, *refs):
    f, r, w, v1, correction, first_ref, second_ref, kept_ref, sent_ref, va, vb, tmp = refs
    count, ny = f.shape[:2]
    fine = Level(0, ny, LANES, 0, scalar_ref, f, r, w)
    for v in (va, vb):
        zero_rows(v, ny)
    even, half = 1 - (place_ref[1] & 1), ny // 2
    window = correction.shape[0] // half
    for ref, above in ((first_ref, even), (second_ref, 1 - even)):
        va[pl.ds(1 + above * (SLAB + HALO), NEAR), pl.ds(8, ny), :] = ref[...]

    def refined(x):
        return fine.spread_rows(correction[pl.ds(x * half, half), :], tmp.at[x])

    def put_refined(x, value):
        for at in (2 * x, 2 * x + 1):
            if 0 < at < count - 1:
                known = HALO - NEAR < at < HALO + SLAB + NEAR - 1
                here = v1 if known else va
                va[at, pl.ds(8, ny), :] = here[at, pl.ds(8, ny), :] + value

    sweep(range(window), refined, put_refined)
    fine.smooth(va, vb, range(2, count - 2))
    fine.smooth(vb, va, range(3, count - 3))

    total = jnp.zeros((8, LANES), jnp.float32)
    for x in range(SLAB):
        rest = fine.defect(va, HALO + x)
        total = total + jnp.sum((rest * rest).reshape(ny // 8, 8, LANES), axis=0)
        tmp[x] = rest
    squares = jnp.full((8, LANES), jnp.sum(total), jnp.float32)

    core, area = place_ref[0] & 1, half * SLAB
    for ref, first in ((kept_ref, core * by), (sent_ref, (1 - core) * by)):
        for y in range(half // by):
            row = pl.multiple_of(2 * y * by + first, 8)
            for x in range(SLAB):
                to = x * half + y * by
                ref[pl.ds(to, by), :] = va[HALO + x, pl.ds(8 + row, by), :]
                ref[pl.ds(area + to, by), :] = tmp[x, pl.ds(row, by), :]
        ref[pl.ds(2 * area, 8), :] = squares


def merge_back_kernel(bx, by, chips_y, place_ref, kept_ref, got_ref, *out_refs):
    chip, core = place_ref[0] // 2, place_ref[0] & 1
    area, half = bx * by, chips_y * by
    for m, out_ref in enumerate(out_refs):
        target = jnp.bitwise_xor(chip, m)
        first = (target // chips_y) * bx * half + lax.rem(target, chips_y) * by
        for ref, column in ((kept_ref, core), (got_ref, 1 - core)):
            for n in range(2):
                for p in range(bx):
                    at = pl.multiple_of(first + (n * SLAB + p) * half, 8)
                    to = pl.multiple_of((2 * column + n) * area + p * by, 8)
                    out_ref[pl.ds(to, by), :] = ref[pl.ds(at, by), :]
            to = pl.multiple_of(4 * area + 8 * column, 8)
            out_ref[pl.ds(to, 8), :] = ref[pl.ds(2 * SLAB * half, 8), :]


def collect_kernel(place_ref, *refs):
    parts, (iterate_ref, residual_ref) = refs[:-2], refs[-2:]
    _, bx, by, _ = iterate_ref.shape
    area = bx * by
    for m, part in enumerate(parts):
        target = jnp.bitwise_xor(place_ref[0] // 2, m)
        for n in range(2):
            for k, ref in enumerate((iterate_ref, residual_ref)):
                rows = pl.ds((2 * n + k) * area, area)
                ref[2 * target + n] = part[rows, :].reshape(bx, by, LANES)


def squares_kernel(row, *refs):
    for m, part in enumerate(refs[:-1]):
        for n in range(2):
            refs[-1][pl.ds(2 * m + n, 1), :] = part[pl.ds(row + 8 * n, 1), :]


SMEM = pl.BlockSpec(memory_space=pltpu.SMEM)
VMEM = pl.BlockSpec(memory_space=pltpu.VMEM)


def local_kernel(kernel, name, scalars, arrays, outs, scratch=()):
    return pl.pallas_call(
        kernel,
        out_shape=[jax.ShapeDtypeStruct(shape, jnp.float32) for shape in outs],
        in_specs=[SMEM] * len(scalars) + [VMEM] * len(arrays),
        out_specs=[VMEM] * len(outs),
        scratch_shapes=[pltpu.VMEM(shape, jnp.float32) for shape in scratch],
        compiler_params=pltpu.CompilerParams(vmem_limit_bytes=VMEM_LIMIT),
        name=name,
    )(*scalars, *arrays)


def swap_in_plane(pieces, unit):
    devices = lax.axis_size("gx") * lax.axis_size("gy")
    moved = [pieces[0]]
    for k in range(1, len(pieces)):
        pairs = [(i, i ^ (k * unit)) for i in range(devices)]
        moved.append(lax.ppermute(pieces[k], ("gx", "gy"), pairs))
    return moved


def swap_slabs(piece, step, slabs):
    size = lax.axis_size("gx")
    moved = [piece]
    for k in range(1, slabs):
        pairs = [(i, i ^ (k * step)) for i in range(size)]
        moved.append(lax.ppermute(piece, "gx", pairs))
    return moved


def column_body(source, reaction, shifts, shift_index, velocity):
    columns, bx, by, nz = source.shape
    gx_size, gy_size = lax.axis_size("gx"), lax.axis_size("gy")
    nx, ny = bx * gx_size, by * gy_size
    step = columns // gy_size
    slabs = gx_size // step
    along, across = lax.axis_index("gx"), lax.axis_index("gy")
    column = lax.rem(along, step) * gy_size + across
    place = jnp.stack([column, along // step]).astype(jnp.int32)
    count = SLAB + 2 * HALO
    area = bx * by

    chips, chips_y = columns // 2, gy_size // 2
    cores = [(i, i ^ 1) for i in range(gy_size)]
    theirs = [lax.ppermute(source, "gy", cores), lax.ppermute(reaction, "gy", cores)]
    (mine,) = local_kernel(keep_kernel, "keep", (place,), (source,), [(chips, bx, by, nz)])
    *blocks, scalar_rows = local_kernel(
        merge_kernel,
        "merge",
        (place, shifts, shift_index, velocity),
        (mine, theirs[0], reaction, theirs[1]),
        [(2, bx, 2 * by, nz)] * chips + [(8, LANES)],
    )
    scalars = (place, scalar_rows)
    blocks = swap_in_plane(blocks, 2)

    edge = (2, NEAR, ny, nz)
    (own_edge,) = local_kernel(
        functools.partial(edge_kernel, chips_y), "edge", (place,), blocks[:chips_y], [edge]
    )
    slab, other_edge = local_kernel(
        functools.partial(arrange_kernel, chips_y),
        "arrange",
        (place,),
        blocks,
        [(2, SLAB, ny, nz), edge],
    )
    beside = []
    for n, piece in enumerate((own_edge, other_edge)):
        pairs = [(i, i + step if i % step != n else i - step) for i in range(gx_size)]
        pairs = [(i, j) for i, j in pairs if 0 <= j < gx_size]
        beside.append(lax.ppermute(piece, "gx", pairs))

    def exchange(pieces):
        got = []
        for n, piece in enumerate(pieces):
            pairs = [(i, i + step if i // step % 2 == n else i - step) for i in range(gx_size)]
            pairs = [(i, j) for i, j in pairs if 0 <= j < gx_size]
            got.append(lax.ppermute(piece, "gx", pairs))
        return got

    grid, rimmed = (count, ny, nz), (count, ny + 16, nz)
    f, r, w, v1, coarse, *beyond = local_kernel(
        functools.partial(pre_kernel, slabs, chips_y),
        "pre",
        scalars,
        (pool_matrix(0), pool_matrix(LANES // 2), slab, *beside),
        [grid, grid, grid, rimmed, (SLAB // 2, ny // 2, nz)] + [(NEAR, ny, nz)] * 2,
        [rimmed, (SLAB, ny, nz), (2, SLAB // 2 * ny // 2, nz)],
    )
    gathered = swap_slabs(coarse, step, slabs)

    coarse_grid = (nx // 2, ny // 2, nz)
    coarse_rimmed = (nx // 2 + HALO, ny // 2 + 16, nz)
    window = (SLAB // 2 + HALO) * ny // 2
    (correction,) = local_kernel(
        functools.partial(coarse_kernel, (slabs, nx, ny, nz)),
        "coarse",
        scalars,
        (pool_matrix(0), spread_matrix(), *gathered),
        [(window, nz)],
        [coarse_grid] * 3 + [coarse_rimmed] * 2 + [(nx // 4 * ny // 2, nz), (nx // 2, ny // 2, nz)],
    )
    result = (SLAB * ny + 8, nz)
    kept, sent = local_kernel(
        functools.partial(post_kernel, by),
        "post",
        scalars,
        (f, r, w, v1, correction, *exchange(beyond)),
        [result, result],
        [rimmed] * 2 + [(SLAB, ny, nz)],
    )

    parts = local_kernel(
        functools.partial(merge_back_kernel, bx, by, chips_y),
        "merge_back",
        (place,),
        (kept, lax.ppermute(sent, "gy", cores)),
        [(4 * area + 16, nz)] * chips,
    )
    parts = swap_in_plane(parts, 2)
    (squares,) = local_kernel(
        functools.partial(squares_kernel, 4 * area), "squares", (), parts, [(columns, nz)]
    )
    iterate, residual = local_kernel(
        collect_kernel, "collect", (place,), parts, [source.shape] * 2
    )
    total = sum(swap_slabs(squares, step, slabs))
    rms = jnp.sqrt(total[:, 0] / (nx * ny * nz) + EPSILON)
    slots = jnp.arange(columns, dtype=jnp.int32)
    mine = jnp.bitwise_xor(slots, column // 2 * 2)[:, None] == slots[None, :]
    residual_rms = jnp.sum(jnp.where(mine, rms[None, :], 0.0), axis=1)
    return iterate, residual, residual_rms


def power_of_two(n):
    return n > 0 and n & (n - 1) == 0


def column_plan_fits(columns, bx, by, nz, gx_size, gy_size):
    if columns % gy_size or gx_size % (columns // gy_size):
        return False
    step = columns // gy_size
    slabs, ny = gx_size // step, by * gy_size
    whole = power_of_two(columns) and power_of_two(step) and power_of_two(slabs)
    small = slabs * ny * nz <= 2**15
    paired = step == 2 and bx == HALO and gy_size % 2 == 0
    return whole and small and paired and bx * step == SLAB and nz == LANES and by % 16 == 0


def solution(mesh):
    gx_size, gy_size = mesh.shape["gx"], mesh.shape["gy"]

    def body(source, reaction, shifts, shift_index, velocity):
        fits = column_plan_fits(*source.shape, gx_size, gy_size)
        plan = column_body if fits else halo_body
        return plan(source, reaction, shifts, shift_index, velocity)

    return jax.shard_map(
        body,
        mesh=mesh,
        in_specs=(P(None, "gx", "gy", None), P("gx", "gy", None), P(), P(), P()),
        out_specs=(P(None, "gx", "gy", None), P(None, "gx", "gy", None), P()),
        check_vma=False,
    )
```

```python
import functools

import jax
import jax.numpy as jnp
from jax import lax
from jax.experimental import pallas as pl
from jax.experimental.pallas import tpu as pltpu
from jax.sharding import PartitionSpec as P

LEVELS = 3
COARSE_SWEEPS = 6

DAMPING = 0.8
EPSILON = 1e-06
VMEM_LIMIT = 32 * 1024 * 1024
LANES = 128
GROUP = 4
SLAB = 8
HALO = 4
NEAR = 2


def with_halo(x, sides, width):
    for axis, dim in sides:
        peers, length = (lax.axis_size(axis), x.shape[dim])
        up = [(i, (i + 1) % peers) for i in range(peers - 1)]
        down = [(j, i) for i, j in up]
        last = lax.slice_in_dim(x, length - width, length, axis=dim)
        leading = lax.slice_in_dim(x, 0, width, axis=dim)
        before = lax.ppermute(last, axis, up)
        after = lax.ppermute(leading, axis, down)
        x = jnp.concatenate([before, x, after], axis=dim)
    return x


def select_shifts(shifts, shift_index):
    columns = jnp.arange(shifts.shape[0], dtype=jnp.int32)
    picked = jnp.where(shift_index[:, None] == columns[None, :], shifts[None, :], 0.0)
    return jnp.sum(picked, axis=1)


def coefficients(velocity, spacing):
    scale_a = 1.0 / (spacing * spacing)
    backward = scale_a + jnp.maximum(velocity, 0.0) / spacing
    forward = scale_a - jnp.minimum(velocity, 0.0) / spacing
    centre = 6.0 * scale_a + jnp.sum(jnp.abs(velocity)) / spacing
    return (backward, forward, centre)


def apply_stencil(padded, backward, forward, diagonal):
    middle = padded[:, 1:-1, 1:-1, :]
    along_z = jnp.pad(middle, ((0, 0), (0, 0), (0, 0), (1, 1)))
    others = backward[0] * padded[:, :-2, 1:-1, :] + forward[0] * padded[:, 2:, 1:-1, :]
    others = others + backward[1] * padded[:, 1:-1, :-2, :] + forward[1] * padded[:, 1:-1, 2:, :]
    others = others + backward[2] * along_z[:, :, :, :-2] + forward[2] * along_z[:, :, :, 2:]
    return diagonal * middle - others


def face_halo(iterate):
    return with_halo(iterate, (("gx", 1), ("gy", 2)), 1)


def coarsen(values):
    count, size_x, size_y, size_z = values.shape
    blocks = values.reshape(count, size_x // 2, 2, size_y // 2, 2, size_z // 2, 2)
    return jnp.sum(blocks, axis=(2, 4, 6)) * 0.125


def refine(values):
    return jnp.repeat(jnp.repeat(jnp.repeat(values, 2, 1), 2, 2), 2, 3)


def coarsest_solve(rhs_field, backward, forward, diagonal):
    iterate = DAMPING * rhs_field / diagonal
    for repeat in range(COARSE_SWEEPS - 1):
        applied = apply_stencil(face_halo(iterate), backward, forward, diagonal)
        iterate = iterate + DAMPING * (rhs_field - applied) / diagonal
    return iterate


def multigrid_cycle(level_index, rhs_field, reaction_l, shift_value, velocity):
    backward, forward, centre = coefficients(velocity, 2.0**level_index)
    diagonal = centre + reaction_l + shift_value[:, None, None, None]
    if level_index == LEVELS - 1:
        return coarsest_solve(rhs_field, backward, forward, diagonal)

    def operate(iterate):
        return apply_stencil(face_halo(iterate), backward, forward, diagonal)

    def smooth_step(iterate):
        return iterate + DAMPING * (rhs_field - operate(iterate)) / diagonal

    iterate = DAMPING * rhs_field / diagonal
    iterate = smooth_step(iterate)
    defect = rhs_field - operate(iterate)
    correction = multigrid_cycle(
        level_index + 1, coarsen(defect), coarsen(reaction_l), shift_value, velocity
    )
    iterate = iterate + refine(correction)
    iterate = smooth_step(iterate)
    iterate = smooth_step(iterate)
    return iterate


def halo_body(source, reaction, shifts, shift_index, velocity):
    columns, cells_x, cells_y, cells_z = source.shape
    shift_value = select_shifts(shifts, shift_index)
    reaction_top = reaction[None]
    backward, forward, centre = coefficients(velocity, 1.0)
    diagonal = centre + reaction_top + shift_value[:, None, None, None]

    iterate = multigrid_cycle(0, source, reaction_top, shift_value, velocity)
    residual = source - apply_stencil(face_halo(iterate), backward, forward, diagonal)
    local_squares = jnp.sum(residual * residual, axis=(1, 2, 3))
    squares = lax.psum(local_squares, ("gx", "gy"))
    total_cells = cells_x * cells_y * cells_z * lax.axis_size("gx") * lax.axis_size("gy")
    residual_rms = jnp.sqrt(squares / total_cells + EPSILON)
    return (iterate, residual, residual_rms)


def split_dot(values, matrix):
    high = values.astype(jnp.bfloat16)
    low = (values - high.astype(jnp.float32)).astype(jnp.bfloat16)
    return jnp.dot(high, matrix, preferred_element_type=jnp.float32) + jnp.dot(
        low, matrix, preferred_element_type=jnp.float32
    )


def sweep(planes, get, put):
    planes = list(planes)
    for first in range(0, len(planes), GROUP):
        group = planes[first : first + GROUP]
        values = [get(x) for x in group]
        for x, value in zip(group, values):
            put(x, value)


class Level:
    def __init__(self, index, ny, nz, rim, scalar_ref, f, r, w):
        self.ny, self.nz, self.rim = ny, nz, rim
        self.f, self.r, self.w = f, r, w
        spacing = 2.0**index
        scale_a = 1.0 / (spacing * spacing)
        inverse = 1.0 / spacing
        shift = scalar_ref[0, 0]
        speed = [scalar_ref[1 + d, 0] for d in range(3)]
        self.backward = [scale_a + jnp.maximum(v, 0.0) * inverse for v in speed]
        self.forward = [scale_a - jnp.minimum(v, 0.0) * inverse for v in speed]
        total = jnp.abs(speed[0]) + jnp.abs(speed[1]) + jnp.abs(speed[2])
        self.centre = 6.0 * scale_a + total * inverse + shift
        lane = lax.broadcasted_iota(jnp.int32, (1, LANES), 1)
        inside = lane < nz
        self.low_z = jnp.where((lane > 0) & inside, self.backward[2], 0.0)
        self.high_z = jnp.where(lane < nz - 1, self.forward[2], 0.0)

    def plane(self, v, x):
        return v[x + self.rim, pl.ds(8, self.ny), :]

    def put(self, v):
        def write(x, value):
            v[x + self.rim, pl.ds(8, self.ny), :] = value

        return write

    def along_z(self, middle):
        return self.low_z * pltpu.roll(middle, 1, 1) + self.high_z * pltpu.roll(middle, LANES - 1, 1)

    def neighbours(self, v, x, middle):
        at, ny = x + self.rim, self.ny
        along_x = self.backward[0] * v[at - 1, pl.ds(8, ny), :] + self.forward[0] * v[at + 1, pl.ds(8, ny), :]
        along_y = self.backward[1] * v[at, pl.ds(7, ny), :] + self.forward[1] * v[at, pl.ds(9, ny), :]
        return along_x + along_y + self.along_z(middle)

    def smoothed(self, v, x):
        middle = self.plane(v, x)
        pulled = self.f[x] + self.neighbours(v, x, middle)
        return (1.0 - DAMPING) * middle + self.w[x] * pulled

    def smooth(self, src, dst, planes):
        sweep(planes, lambda x: self.smoothed(src, x), self.put(dst))

    def defect(self, v, x):
        middle = self.plane(v, x)
        pulled = self.f[x] + self.neighbours(v, x, middle)
        return pulled - (self.r[x] + self.centre) * middle

    def pool_rows(self, value, rows):
        half, ny = self.ny // 2, self.ny
        rows[pl.ds(0, ny), :] = value
        return rows[pl.ds(0, half, stride=2), :] + rows[pl.ds(1, half, stride=2), :]

    def spread_rows(self, part, rows):
        half, ny = self.ny // 2, self.ny
        rows[pl.ds(0, half, stride=2), :] = part
        rows[pl.ds(1, half, stride=2), :] = part
        return rows[pl.ds(0, ny), :]

    def solve_in_registers(self, rhs, reaction):
        row = lax.broadcasted_iota(jnp.int32, (self.ny, 1), 0)
        low_y = jnp.where(row > 0, self.backward[1], 0.0)
        high_y = jnp.where(row < self.ny - 1, self.forward[1], 0.0)
        weight = [DAMPING / (r + self.centre) for r in reaction]
        v = [w * f for w, f in zip(weight, rhs)]
        for _ in range(COARSE_SWEEPS - 1):
            new = []
            for x, here in enumerate(v):
                along_y = low_y * pltpu.roll(here, 1, 0) + high_y * pltpu.roll(here, self.ny - 1, 0)
                pulled = rhs[x] + self.along_z(here) + along_y
                if x > 0:
                    pulled += self.backward[0] * v[x - 1]
                if x < len(v) - 1:
                    pulled += self.forward[0] * v[x + 1]
                new.append((1.0 - DAMPING) * here + weight[x] * pulled)
            v = new
        return jnp.concatenate(v, axis=0)


def zero_rows(v, ny):
    edge = jnp.zeros((v.shape[0], 8, LANES), jnp.float32)
    v[:, pl.ds(0, 8), :] = edge
    v[:, pl.ds(8 + ny, 8), :] = edge


def pool_matrix(offset):
    row = lax.broadcasted_iota(jnp.int32, (LANES, LANES), 0)
    col = lax.broadcasted_iota(jnp.int32, (LANES, LANES), 1)
    return jnp.where(row // 2 + offset == col, 0.125, 0.0).astype(jnp.bfloat16)


def spread_matrix():
    row = lax.broadcasted_iota(jnp.int32, (LANES, LANES), 0)
    col = lax.broadcasted_iota(jnp.int32, (LANES, LANES), 1)
    return jnp.where(col // 2 == row, 1.0, 0.0).astype(jnp.bfloat16)


def keep_kernel(place_ref, source_ref, out_ref):
    for n in range(out_ref.shape[0]):
        out_ref[n] = source_ref[2 * n + (place_ref[0] & 1)]


def merge_kernel(place_ref, shifts_ref, index_ref, velocity_ref, *refs):
    mine_ref, theirs_ref, reaction_ref, other_reaction_ref = refs[:4]
    out_refs, scalar_ref = refs[4:-1], refs[-1]
    chip, core = place_ref[0] // 2, place_ref[0] & 1
    by = mine_ref.shape[2]
    mine = pl.ds(pl.multiple_of(core * by, 8), by)
    theirs = pl.ds(pl.multiple_of((1 - core) * by, 8), by)
    for m, out_ref in enumerate(out_refs):
        target = jnp.bitwise_xor(chip, m)
        out_ref[0, :, mine, :] = mine_ref[target]
        out_ref[0, :, theirs, :] = theirs_ref[2 * target + core]
        out_ref[1, :, mine, :] = reaction_ref[...]
        out_ref[1, :, theirs, :] = other_reaction_ref[...]
    scalars = [shifts_ref[index_ref[place_ref[0]]]] + [velocity_ref[d] for d in range(3)]
    for n, scalar in enumerate(scalars):
        scalar_ref[pl.ds(n, 1), :] = jnp.full((1, LANES), scalar, jnp.float32)


def half_kernel(chips_y, place_ref, *refs):
    blocks, half_ref = refs[:-1], refs[-1]
    for m, block in enumerate(blocks):
        size = block.shape[2]
        chip = jnp.bitwise_xor(place_ref[0] // 2, m)
        rows = pl.ds(pl.multiple_of(lax.rem(chip, chips_y) * size, 8), size)
        half_ref[:, :, rows, :] = block[...]


def arrange_kernel(chips_y, place_ref, *refs):
    blocks, (slab_ref, near_ref, far_ref) = refs[:-3], refs[-3:]
    chip = place_ref[0] // 2
    for m, block in enumerate(blocks):
        owner = jnp.bitwise_xor(chip, m)
        _, bx, size, _ = block.shape
        planes = pl.ds((owner // chips_y) * bx, bx)
        rows = pl.ds(pl.multiple_of(lax.rem(owner, chips_y) * size, 8), size)
        slab_ref[:, planes, rows, :] = block[...]
    other = 1 - chip // chips_y
    near_ref[...] = slab_ref[:, pl.ds(other * (SLAB - NEAR), NEAR)]
    far_ref[...] = slab_ref[:, pl.ds(NEAR + other * (SLAB - 3 * NEAR), NEAR)]


def beyond_kernel(slabs, chips_y, place_ref, scalar_ref, half_ref, near_ref, far_ref, *refs):
    out_refs, (f, r, w, v0) = refs[:2], refs[2:]
    ny, slab = f.shape[1], place_ref[1]
    x = place_ref[0] // 2 // chips_y
    fine = Level(0, ny, LANES, 0, scalar_ref, f, r, w)
    zero_rows(v0, ny)
    last = NEAR * (1 - x)
    sides = ((1 - x, ((half_ref, 0, HALO),)), (x, ((near_ref, last, NEAR), (far_ref, NEAR - last, NEAR))))
    for out_ref, (above, parts) in zip(out_refs, sides):
        for ref, first, size in parts:
            f[pl.ds(first, size)], r[pl.ds(first, size)] = ref[0], ref[1]
        beside = jnp.where(above == 1, slab < slabs - 1, slab > 0)
        inside = jnp.where(beside, DAMPING, 0.0)

        def put(at, weight):
            w[at] = weight
            v0[at, pl.ds(8, ny), :] = weight * f[at]

        sweep(range(HALO), lambda at: inside / (r[at] + fine.centre), put)
        for n in range(NEAR):
            out_ref[n] = fine.smoothed(v0, 1 + n)


def pre_kernel(slabs, chips_y, place_ref, scalar_ref, *refs):
    pool_ref, pool_up_ref, slab_ref, half_ref, near_ref = refs[:5]
    f, r, w, v1, coarse_ref, v0, tmp, pooled = refs[5:]
    ny = f.shape[1]
    slab = place_ref[1]
    fine = Level(0, ny, LANES, 0, scalar_ref, f, r, w)
    zero_rows(v0, ny)
    zero_rows(v1, ny)
    after = HALO + SLAB

    f[pl.ds(HALO, SLAB)], r[pl.ds(HALO, SLAB)] = slab_ref[0], slab_ref[1]
    x = place_ref[0] // 2 // chips_y
    for above, ref, first in ((1 - x, half_ref, x * NEAR), (x, near_ref, 0)):
        planes = pl.ds((HALO - NEAR) + above * (SLAB + NEAR), NEAR)
        f[planes], r[planes] = ref[0, pl.ds(first, NEAR)], ref[1, pl.ds(first, NEAR)]

    inside = [jnp.where(slab > 0, DAMPING, 0.0)] * HALO
    inside += [DAMPING] * SLAB
    inside += [jnp.where(slab < slabs - 1, DAMPING, 0.0)] * HALO

    def put(x, weight):
        w[x] = weight
        v0[x, pl.ds(8, ny), :] = weight * f[x]

    known = range(HALO - NEAR, after + NEAR)
    sweep(known, lambda x: inside[x] / (r[x] + fine.centre), put)
    fine.smooth(v0, v1, known[1:-1])
    half = ny // 2

    def coarsened(x):
        at = HALO + 2 * x
        return fine.defect(v1, at) + fine.defect(v1, at + 1), r[at] + r[at + 1]

    def put_pooled(x, pair):
        for n in range(2):
            pooled[n, pl.ds(x * half, half), :] = fine.pool_rows(pair[n], tmp.at[2 * x + n])

    sweep(range(SLAB // 2), coarsened, put_pooled)
    packed = split_dot(pooled[0], pool_ref[...]) + split_dot(pooled[1], pool_up_ref[...])
    coarse_ref[...] = packed.reshape(coarse_ref.shape)


def coarse_kernel(grid, place_ref, scalar_ref, *refs):
    slabs, nx, ny, nz = grid
    pool_ref, spread_ref = refs[:2]
    coarse, out_ref = refs[2 : 2 + slabs], refs[2 + slabs]
    f1, r1, w1, v1a, v1b, pooled, tmp = refs[3 + slabs :]
    pool, spread = pool_ref[...], spread_ref[...]
    slab = place_ref[1]
    rim = HALO // 2
    nx1, ny1, nx2, ny2 = nx // 2, ny // 2, nx // 4, ny // 4
    mid = Level(1, ny1, nz // 2, rim, scalar_ref, f1, r1, w1)
    deep = Level(2, ny2, nz // 4, 0, scalar_ref, None, None, None)
    for v in (v1a, v1b):
        zero_rows(v, ny1)
        blank = jnp.zeros((rim,) + v.shape[1:], jnp.float32)
        v[pl.ds(0, rim)] = blank
        v[pl.ds(rim + nx1, rim)] = blank

    lower = lax.broadcasted_iota(jnp.int32, (1, LANES), 1) < LANES // 2
    own = SLAB // 2
    for k in range(slabs):
        first = jnp.bitwise_xor(slab, k) * own
        both = coarse[k][...]
        f1[pl.ds(first, own)] = jnp.where(lower, both, 0.0)
        r1[pl.ds(first, own)] = jnp.where(lower, pltpu.roll(both, LANES // 2, 2), 0.0)

    def put_start(x, weight):
        w1[x] = weight
        v1a[x + rim, pl.ds(8, ny1), :] = weight * f1[x]

    sweep(range(nx1), lambda x: DAMPING / (r1[x] + mid.centre), put_start)
    mid.smooth(v1a, v1b, range(nx1))

    def coarsened(x):
        return mid.defect(v1b, 2 * x) + mid.defect(v1b, 2 * x + 1), r1[2 * x] + r1[2 * x + 1]

    rows2 = nx2 * ny2

    def put_pooled(x, pair):
        for n in range(2):
            value = mid.pool_rows(pair[n], tmp.at[2 * x + n])
            pooled[pl.ds(n * rows2 + x * ny2, ny2), :] = value

    sweep(range(nx2), coarsened, put_pooled)
    deeper = split_dot(pooled[pl.ds(0, 2 * rows2), :], pool)
    planes = [deeper[n * ny2 : (n + 1) * ny2] for n in range(2 * nx2)]
    values = deep.solve_in_registers(planes[:nx2], planes[nx2:])

    pooled[pl.ds(0, rows2), :] = split_dot(values, spread)

    def refined1(x):
        return mid.spread_rows(pooled[pl.ds(x * ny2, ny2), :], tmp.at[x])

    def put_refined1(x, value):
        for n in range(2):
            v1b[2 * x + n + rim, pl.ds(8, ny1), :] += value

    sweep(range(nx2), refined1, put_refined1)
    mid.smooth(v1b, v1a, range(nx1))
    mid.smooth(v1a, v1b, range(nx1))

    window = own + 2 * rim
    values = v1b[pl.ds(slab * own, window), pl.ds(8, ny1), :].reshape(window * ny1, LANES)
    out_ref[...] = split_dot(values, spread)


def post_kernel(by, chips_y, place_ref, scalar_ref, *refs):
    f, r, w, v1, correction, first_ref, second_ref, kept_ref, sent_ref, va, vb, tmp = refs
    count, ny = f.shape[:2]
    fine = Level(0, ny, LANES, 0, scalar_ref, f, r, w)
    for v in (va, vb):
        zero_rows(v, ny)
    x, half = place_ref[0] // 2 // chips_y, ny // 2
    window = correction.shape[0] // half
    for ref, above in ((first_ref, 1 - x), (second_ref, x)):
        va[pl.ds(1 + above * (SLAB + HALO), NEAR), pl.ds(8, ny), :] = ref[...]

    def refined(x):
        return fine.spread_rows(correction[pl.ds(x * half, half), :], tmp.at[x])

    def put_refined(x, value):
        for at in (2 * x, 2 * x + 1):
            if 0 < at < count - 1:
                known = HALO - NEAR < at < HALO + SLAB + NEAR - 1
                here = v1 if known else va
                va[at, pl.ds(8, ny), :] = here[at, pl.ds(8, ny), :] + value

    sweep(range(window), refined, put_refined)
    fine.smooth(va, vb, range(2, count - 2))
    fine.smooth(vb, va, range(3, count - 3))

    total = jnp.zeros((8, LANES), jnp.float32)
    for x in range(SLAB):
        rest = fine.defect(va, HALO + x)
        total = total + jnp.sum((rest * rest).reshape(ny // 8, 8, LANES), axis=0)
        tmp[x] = rest
    squares = jnp.full((8, LANES), jnp.sum(total), jnp.float32)

    core, area = place_ref[0] & 1, half * SLAB
    for ref, first in ((kept_ref, core * by), (sent_ref, (1 - core) * by)):
        for y in range(half // by):
            row = pl.multiple_of(2 * y * by + first, 8)
            for x in range(SLAB):
                to = x * half + y * by
                ref[pl.ds(to, by), :] = va[HALO + x, pl.ds(8 + row, by), :]
                ref[pl.ds(area + to, by), :] = tmp[x, pl.ds(row, by), :]
        ref[pl.ds(2 * area, 8), :] = squares


def merge_back_kernel(bx, by, chips_y, place_ref, kept_ref, got_ref, *out_refs):
    chip, core = place_ref[0] // 2, place_ref[0] & 1
    area, half = bx * by, chips_y * by
    for m, out_ref in enumerate(out_refs):
        target = jnp.bitwise_xor(chip, m)
        first = (target // chips_y) * bx * half + lax.rem(target, chips_y) * by
        for ref, column in ((kept_ref, core), (got_ref, 1 - core)):
            for n in range(2):
                for p in range(bx):
                    at = pl.multiple_of(first + (n * SLAB + p) * half, 8)
                    to = pl.multiple_of((2 * column + n) * area + p * by, 8)
                    out_ref[pl.ds(to, by), :] = ref[pl.ds(at, by), :]
            to = pl.multiple_of(4 * area + 8 * column, 8)
            out_ref[pl.ds(to, 8), :] = ref[pl.ds(2 * SLAB * half, 8), :]


def collect_kernel(place_ref, *refs):
    parts, (iterate_ref, residual_ref) = refs[:-2], refs[-2:]
    _, bx, by, _ = iterate_ref.shape
    area = bx * by
    for m, part in enumerate(parts):
        target = jnp.bitwise_xor(place_ref[0] // 2, m)
        for n in range(2):
            for k, ref in enumerate((iterate_ref, residual_ref)):
                rows = pl.ds((2 * n + k) * area, area)
                ref[2 * target + n] = part[rows, :].reshape(bx, by, LANES)


def squares_kernel(row, *refs):
    for m, part in enumerate(refs[:-1]):
        for n in range(2):
            refs[-1][pl.ds(2 * m + n, 1), :] = part[pl.ds(row + 8 * n, 1), :]


SMEM = pl.BlockSpec(memory_space=pltpu.SMEM)
VMEM = pl.BlockSpec(memory_space=pltpu.VMEM)


def local_kernel(kernel, name, scalars, arrays, outs, scratch=()):
    return pl.pallas_call(
        kernel,
        out_shape=[jax.ShapeDtypeStruct(shape, jnp.float32) for shape in outs],
        in_specs=[SMEM] * len(scalars) + [VMEM] * len(arrays),
        out_specs=[VMEM] * len(outs),
        scratch_shapes=[pltpu.VMEM(shape, jnp.float32) for shape in scratch],
        compiler_params=pltpu.CompilerParams(vmem_limit_bytes=VMEM_LIMIT),
        name=name,
    )(*scalars, *arrays)


def swap_in_plane(pieces, unit):
    devices = lax.axis_size("gx") * lax.axis_size("gy")
    moved = [pieces[0]]
    for k in range(1, len(pieces)):
        pairs = [(i, i ^ (k * unit)) for i in range(devices)]
        moved.append(lax.ppermute(pieces[k], ("gx", "gy"), pairs))
    return moved


def swap_slabs(piece, step, slabs):
    size = lax.axis_size("gx")
    moved = [piece]
    for k in range(1, slabs):
        pairs = [(i, i ^ (k * step)) for i in range(size)]
        moved.append(lax.ppermute(piece, "gx", pairs))
    return moved


def column_body(source, reaction, shifts, shift_index, velocity):
    columns, bx, by, nz = source.shape
    gx_size, gy_size = lax.axis_size("gx"), lax.axis_size("gy")
    nx, ny = bx * gx_size, by * gy_size
    step = columns // gy_size
    slabs = gx_size // step
    along, across = lax.axis_index("gx"), lax.axis_index("gy")
    column = lax.rem(along, step) * gy_size + across
    place = jnp.stack([column, along // step]).astype(jnp.int32)
    count = SLAB + 2 * HALO
    area = bx * by

    chips, chips_y = columns // 2, gy_size // 2
    cores = [(i, i ^ 1) for i in range(gy_size)]
    theirs = [lax.ppermute(source, "gy", cores), lax.ppermute(reaction, "gy", cores)]
    (mine,) = local_kernel(keep_kernel, "keep", (place,), (source,), [(chips, bx, by, nz)])
    *blocks, scalar_rows = local_kernel(
        merge_kernel,
        "merge",
        (place, shifts, shift_index, velocity),
        (mine, theirs[0], reaction, theirs[1]),
        [(2, bx, 2 * by, nz)] * chips + [(8, LANES)],
    )
    scalars = (place, scalar_rows)
    blocks = swap_in_plane(blocks, 2)

    edge = (2, NEAR, ny, nz)
    (own_half,) = local_kernel(
        functools.partial(half_kernel, chips_y),
        "half",
        (place,),
        blocks[:chips_y],
        [(2, HALO, ny, nz)],
    )
    slab, near, far = local_kernel(
        functools.partial(arrange_kernel, chips_y),
        "arrange",
        (place,),
        blocks,
        [(2, SLAB, ny, nz), edge, edge],
    )

    def send_beside(piece, up):
        pairs = [(i, i + step if i % step == up else i - step) for i in range(gx_size)]
        return lax.ppermute(piece, "gx", [(i, j) for i, j in pairs if 0 <= j < gx_size])

    beside = [send_beside(own_half, 1), send_beside(near, 0), send_beside(far, 0)]
    grid, rimmed = (count, ny, nz), (count, ny + 16, nz)
    f, r, w, v1, coarse = local_kernel(
        functools.partial(pre_kernel, slabs, chips_y),
        "pre",
        scalars,
        (pool_matrix(0), pool_matrix(LANES // 2), slab, *beside[:2]),
        [grid, grid, grid, rimmed, (SLAB // 2, ny // 2, nz)],
        [rimmed, (SLAB, ny, nz), (2, SLAB // 2 * ny // 2, nz)],
    )
    gathered = swap_slabs(coarse, step, slabs)
    beyond = local_kernel(
        functools.partial(beyond_kernel, slabs, chips_y),
        "beyond",
        scalars,
        beside,
        [(NEAR, ny, nz)] * 2,
        [(HALO, ny, nz)] * 3 + [(HALO, ny + 16, nz)],
    )

    coarse_grid = (nx // 2, ny // 2, nz)
    coarse_rimmed = (nx // 2 + HALO, ny // 2 + 16, nz)
    window = (SLAB // 2 + HALO) * ny // 2
    (correction,) = local_kernel(
        functools.partial(coarse_kernel, (slabs, nx, ny, nz)),
        "coarse",
        scalars,
        (pool_matrix(0), spread_matrix(), *gathered),
        [(window, nz)],
        [coarse_grid] * 3 + [coarse_rimmed] * 2 + [(nx // 4 * ny // 2, nz), (nx // 2, ny // 2, nz)],
    )
    result = (SLAB * ny + 8, nz)
    kept, sent = local_kernel(
        functools.partial(post_kernel, by, chips_y),
        "post",
        scalars,
        (f, r, w, v1, correction, *beyond),
        [result, result],
        [rimmed] * 2 + [(SLAB, ny, nz)],
    )

    parts = local_kernel(
        functools.partial(merge_back_kernel, bx, by, chips_y),
        "merge_back",
        (place,),
        (kept, lax.ppermute(sent, "gy", cores)),
        [(4 * area + 16, nz)] * chips,
    )
    parts = swap_in_plane(parts, 2)
    (squares,) = local_kernel(
        functools.partial(squares_kernel, 4 * area), "squares", (), parts, [(columns, nz)]
    )
    iterate, residual = local_kernel(
        collect_kernel, "collect", (place,), parts, [source.shape] * 2
    )
    total = sum(swap_slabs(squares, step, slabs))
    rms = jnp.sqrt(total[:, 0] / (nx * ny * nz) + EPSILON)
    slots = jnp.arange(columns, dtype=jnp.int32)
    mine = jnp.bitwise_xor(slots, column // 2 * 2)[:, None] == slots[None, :]
    residual_rms = jnp.sum(jnp.where(mine, rms[None, :], 0.0), axis=1)
    return iterate, residual, residual_rms


def power_of_two(n):
    return n > 0 and n & (n - 1) == 0


def column_plan_fits(columns, bx, by, nz, gx_size, gy_size):
    if columns % gy_size or gx_size % (columns // gy_size):
        return False
    step = columns // gy_size
    slabs, ny = gx_size // step, by * gy_size
    whole = power_of_two(columns) and power_of_two(step) and power_of_two(slabs)
    small = slabs * ny * nz <= 2**15
    paired = step == 2 and bx == HALO and gy_size % 2 == 0
    return whole and small and paired and bx * step == SLAB and nz == LANES and by % 16 == 0


def solution(mesh):
    gx_size, gy_size = mesh.shape["gx"], mesh.shape["gy"]

    def body(source, reaction, shifts, shift_index, velocity):
        fits = column_plan_fits(*source.shape, gx_size, gy_size)
        plan = column_body if fits else halo_body
        return plan(source, reaction, shifts, shift_index, velocity)

    return jax.shard_map(
        body,
        mesh=mesh,
        in_specs=(P(None, "gx", "gy", None), P("gx", "gy", None), P(), P(), P()),
        out_specs=(P(None, "gx", "gy", None), P(None, "gx", "gy", None), P()),
        check_vma=False,
    )
```

```python
import functools

import jax
import jax.numpy as jnp
from jax import lax
from jax.experimental import pallas as pl
from jax.experimental.pallas import tpu as pltpu
from jax.sharding import PartitionSpec as P

LEVELS = 3
COARSE_SWEEPS = 6

DAMPING = 0.8
EPSILON = 1e-06
VMEM_LIMIT = 32 * 1024 * 1024
LANES = 128
GROUP = 4
SLAB = 8
HALO = 4
NEAR = 2


def with_halo(x, sides, width):
    for axis, dim in sides:
        peers, length = (lax.axis_size(axis), x.shape[dim])
        up = [(i, (i + 1) % peers) for i in range(peers - 1)]
        down = [(j, i) for i, j in up]
        last = lax.slice_in_dim(x, length - width, length, axis=dim)
        leading = lax.slice_in_dim(x, 0, width, axis=dim)
        before = lax.ppermute(last, axis, up)
        after = lax.ppermute(leading, axis, down)
        x = jnp.concatenate([before, x, after], axis=dim)
    return x


def select_shifts(shifts, shift_index):
    columns = jnp.arange(shifts.shape[0], dtype=jnp.int32)
    picked = jnp.where(shift_index[:, None] == columns[None, :], shifts[None, :], 0.0)
    return jnp.sum(picked, axis=1)


def coefficients(velocity, spacing):
    scale_a = 1.0 / (spacing * spacing)
    backward = scale_a + jnp.maximum(velocity, 0.0) / spacing
    forward = scale_a - jnp.minimum(velocity, 0.0) / spacing
    centre = 6.0 * scale_a + jnp.sum(jnp.abs(velocity)) / spacing
    return (backward, forward, centre)


def apply_stencil(padded, backward, forward, diagonal):
    middle = padded[:, 1:-1, 1:-1, :]
    along_z = jnp.pad(middle, ((0, 0), (0, 0), (0, 0), (1, 1)))
    others = backward[0] * padded[:, :-2, 1:-1, :] + forward[0] * padded[:, 2:, 1:-1, :]
    others = others + backward[1] * padded[:, 1:-1, :-2, :] + forward[1] * padded[:, 1:-1, 2:, :]
    others = others + backward[2] * along_z[:, :, :, :-2] + forward[2] * along_z[:, :, :, 2:]
    return diagonal * middle - others


def face_halo(iterate):
    return with_halo(iterate, (("gx", 1), ("gy", 2)), 1)


def coarsen(values):
    count, size_x, size_y, size_z = values.shape
    blocks = values.reshape(count, size_x // 2, 2, size_y // 2, 2, size_z // 2, 2)
    return jnp.sum(blocks, axis=(2, 4, 6)) * 0.125


def refine(values):
    return jnp.repeat(jnp.repeat(jnp.repeat(values, 2, 1), 2, 2), 2, 3)


def coarsest_solve(rhs_field, backward, forward, diagonal):
    iterate = DAMPING * rhs_field / diagonal
    for repeat in range(COARSE_SWEEPS - 1):
        applied = apply_stencil(face_halo(iterate), backward, forward, diagonal)
        iterate = iterate + DAMPING * (rhs_field - applied) / diagonal
    return iterate


def multigrid_cycle(level_index, rhs_field, reaction_l, shift_value, velocity):
    backward, forward, centre = coefficients(velocity, 2.0**level_index)
    diagonal = centre + reaction_l + shift_value[:, None, None, None]
    if level_index == LEVELS - 1:
        return coarsest_solve(rhs_field, backward, forward, diagonal)

    def operate(iterate):
        return apply_stencil(face_halo(iterate), backward, forward, diagonal)

    def smooth_step(iterate):
        return iterate + DAMPING * (rhs_field - operate(iterate)) / diagonal

    iterate = DAMPING * rhs_field / diagonal
    iterate = smooth_step(iterate)
    defect = rhs_field - operate(iterate)
    correction = multigrid_cycle(
        level_index + 1, coarsen(defect), coarsen(reaction_l), shift_value, velocity
    )
    iterate = iterate + refine(correction)
    iterate = smooth_step(iterate)
    iterate = smooth_step(iterate)
    return iterate


def halo_body(source, reaction, shifts, shift_index, velocity):
    columns, cells_x, cells_y, cells_z = source.shape
    shift_value = select_shifts(shifts, shift_index)
    reaction_top = reaction[None]
    backward, forward, centre = coefficients(velocity, 1.0)
    diagonal = centre + reaction_top + shift_value[:, None, None, None]

    iterate = multigrid_cycle(0, source, reaction_top, shift_value, velocity)
    residual = source - apply_stencil(face_halo(iterate), backward, forward, diagonal)
    local_squares = jnp.sum(residual * residual, axis=(1, 2, 3))
    squares = lax.psum(local_squares, ("gx", "gy"))
    total_cells = cells_x * cells_y * cells_z * lax.axis_size("gx") * lax.axis_size("gy")
    residual_rms = jnp.sqrt(squares / total_cells + EPSILON)
    return (iterate, residual, residual_rms)


def split_dot(values, matrix):
    high = values.astype(jnp.bfloat16)
    low = (values - high.astype(jnp.float32)).astype(jnp.bfloat16)
    return jnp.dot(high, matrix, preferred_element_type=jnp.float32) + jnp.dot(
        low, matrix, preferred_element_type=jnp.float32
    )


def sweep(planes, get, put):
    planes = list(planes)
    for first in range(0, len(planes), GROUP):
        group = planes[first : first + GROUP]
        values = [get(x) for x in group]
        for x, value in zip(group, values):
            put(x, value)


class Level:
    def __init__(self, index, ny, nz, rim, scalar_ref, f, r, w):
        self.ny, self.nz, self.rim = ny, nz, rim
        self.f, self.r, self.w = f, r, w
        spacing = 2.0**index
        scale_a = 1.0 / (spacing * spacing)
        inverse = 1.0 / spacing
        shift = scalar_ref[0, 0]
        speed = [scalar_ref[1 + d, 0] for d in range(3)]
        self.backward = [scale_a + jnp.maximum(v, 0.0) * inverse for v in speed]
        self.forward = [scale_a - jnp.minimum(v, 0.0) * inverse for v in speed]
        total = jnp.abs(speed[0]) + jnp.abs(speed[1]) + jnp.abs(speed[2])
        self.centre = 6.0 * scale_a + total * inverse + shift
        lane = lax.broadcasted_iota(jnp.int32, (1, LANES), 1)
        inside = lane < nz
        self.low_z = jnp.where((lane > 0) & inside, self.backward[2], 0.0)
        self.high_z = jnp.where(lane < nz - 1, self.forward[2], 0.0)

    def plane(self, v, x):
        return v[x + self.rim, pl.ds(8, self.ny), :]

    def put(self, v):
        def write(x, value):
            v[x + self.rim, pl.ds(8, self.ny), :] = value

        return write

    def along_z(self, middle):
        return self.low_z * pltpu.roll(middle, 1, 1) + self.high_z * pltpu.roll(middle, LANES - 1, 1)

    def neighbours(self, v, x, middle):
        at, ny = x + self.rim, self.ny
        along_x = self.backward[0] * v[at - 1, pl.ds(8, ny), :] + self.forward[0] * v[at + 1, pl.ds(8, ny), :]
        along_y = self.backward[1] * v[at, pl.ds(7, ny), :] + self.forward[1] * v[at, pl.ds(9, ny), :]
        return along_x + along_y + self.along_z(middle)

    def smoothed(self, v, x):
        middle = self.plane(v, x)
        pulled = self.f[x] + self.neighbours(v, x, middle)
        return (1.0 - DAMPING) * middle + self.w[x] * pulled

    def smooth(self, src, dst, planes):
        sweep(planes, lambda x: self.smoothed(src, x), self.put(dst))

    def defect(self, v, x):
        middle = self.plane(v, x)
        pulled = self.f[x] + self.neighbours(v, x, middle)
        return pulled - (self.r[x] + self.centre) * middle

    def pool_rows(self, value, rows):
        half, ny = self.ny // 2, self.ny
        rows[pl.ds(0, ny), :] = value
        return rows[pl.ds(0, half, stride=2), :] + rows[pl.ds(1, half, stride=2), :]

    def spread_rows(self, part, rows):
        half, ny = self.ny // 2, self.ny
        rows[pl.ds(0, half, stride=2), :] = part
        rows[pl.ds(1, half, stride=2), :] = part
        return rows[pl.ds(0, ny), :]

    def solve_in_registers(self, rhs, reaction):
        row = lax.broadcasted_iota(jnp.int32, (self.ny, 1), 0)
        low_y = jnp.where(row > 0, self.backward[1], 0.0)
        high_y = jnp.where(row < self.ny - 1, self.forward[1], 0.0)
        weight = [DAMPING / (r + self.centre) for r in reaction]
        v = [w * f for w, f in zip(weight, rhs)]
        for _ in range(COARSE_SWEEPS - 1):
            new = []
            for x, here in enumerate(v):
                along_y = low_y * pltpu.roll(here, 1, 0) + high_y * pltpu.roll(here, self.ny - 1, 0)
                pulled = rhs[x] + self.along_z(here) + along_y
                if x > 0:
                    pulled += self.backward[0] * v[x - 1]
                if x < len(v) - 1:
                    pulled += self.forward[0] * v[x + 1]
                new.append((1.0 - DAMPING) * here + weight[x] * pulled)
            v = new
        return jnp.concatenate(v, axis=0)


def zero_rows(v, ny):
    edge = jnp.zeros((v.shape[0], 8, LANES), jnp.float32)
    v[:, pl.ds(0, 8), :] = edge
    v[:, pl.ds(8 + ny, 8), :] = edge


def pool_matrix(offset):
    row = lax.broadcasted_iota(jnp.int32, (LANES, LANES), 0)
    col = lax.broadcasted_iota(jnp.int32, (LANES, LANES), 1)
    return jnp.where(row // 2 + offset == col, 0.125, 0.0).astype(jnp.bfloat16)


def spread_matrix():
    row = lax.broadcasted_iota(jnp.int32, (LANES, LANES), 0)
    col = lax.broadcasted_iota(jnp.int32, (LANES, LANES), 1)
    return jnp.where(col // 2 == row, 1.0, 0.0).astype(jnp.bfloat16)


def keep_kernel(place_ref, source_ref, out_ref):
    for n in range(out_ref.shape[0]):
        out_ref[n] = source_ref[2 * n + (place_ref[0] & 1)]


def merge_kernel(place_ref, shifts_ref, index_ref, velocity_ref, *refs):
    mine_ref, theirs_ref, reaction_ref, other_reaction_ref = refs[:4]
    out_refs, scalar_ref = refs[4:-1], refs[-1]
    chip, core = place_ref[0] // 2, place_ref[0] & 1
    by = mine_ref.shape[2]
    mine = pl.ds(pl.multiple_of(core * by, 8), by)
    theirs = pl.ds(pl.multiple_of((1 - core) * by, 8), by)
    for m, out_ref in enumerate(out_refs):
        target = jnp.bitwise_xor(chip, m)
        out_ref[0, :, mine, :] = mine_ref[target]
        out_ref[0, :, theirs, :] = theirs_ref[2 * target + core]
        out_ref[1, :, mine, :] = reaction_ref[...]
        out_ref[1, :, theirs, :] = other_reaction_ref[...]
    scalars = [shifts_ref[index_ref[place_ref[0]]]] + [velocity_ref[d] for d in range(3)]
    for n, scalar in enumerate(scalars):
        scalar_ref[pl.ds(n, 1), :] = jnp.full((1, LANES), scalar, jnp.float32)


def edge_kernel(chips_y, place_ref, *refs):
    blocks, edge_ref = refs[:-1], refs[-1]
    for m, block in enumerate(blocks):
        chip = jnp.bitwise_xor(place_ref[0] // 2, m)
        _, bx, size, _ = block.shape
        planes = pl.ds((chip // chips_y) * (bx - NEAR), NEAR)
        rows = pl.ds(pl.multiple_of(lax.rem(chip, chips_y) * size, 8), size)
        edge_ref[:, :, rows, :] = block[:, planes]


def arrange_kernel(chips_y, place_ref, *refs):
    blocks, (slab_ref, edge_ref) = refs[:-2], refs[-2:]
    chip = place_ref[0] // 2
    for m, block in enumerate(blocks):
        owner = jnp.bitwise_xor(chip, m)
        _, bx, size, _ = block.shape
        planes = pl.ds((owner // chips_y) * bx, bx)
        rows = pl.ds(pl.multiple_of(lax.rem(owner, chips_y) * size, 8), size)
        slab_ref[:, planes, rows, :] = block[...]
    edge_ref[...] = slab_ref[:, pl.ds((1 - chip // chips_y) * (SLAB - NEAR), NEAR)]


def pre_kernel(slabs, chips_y, place_ref, scalar_ref, *refs):
    pool_ref, pool_up_ref, slab_ref, first_ref, second_ref = refs[:5]
    f, r, w, v1, coarse_ref, first_out, second_out, v0, tmp, pooled = refs[5:]
    ny = f.shape[1]
    slab = place_ref[1]
    fine = Level(0, ny, LANES, 0, scalar_ref, f, r, w)
    zero_rows(v0, ny)
    zero_rows(v1, ny)
    after = HALO + SLAB
    even = 1 - (slab & 1)

    f[pl.ds(HALO, SLAB)], r[pl.ds(HALO, SLAB)] = slab_ref[0], slab_ref[1]
    x = place_ref[0] // 2 // chips_y
    for ref, above in ((first_ref, 1 - x), (second_ref, x)):
        planes = pl.ds((HALO - NEAR) + above * (SLAB + NEAR), NEAR)
        f[planes], r[planes] = ref[0], ref[1]

    inside = [jnp.where(slab > 0, DAMPING, 0.0)] * HALO
    inside += [DAMPING] * SLAB
    inside += [jnp.where(slab < slabs - 1, DAMPING, 0.0)] * HALO

    def put(x, weight):
        w[x] = weight
        v0[x, pl.ds(8, ny), :] = weight * f[x]

    known = range(HALO - NEAR, after + NEAR)
    sweep(known, lambda x: inside[x] / (r[x] + fine.centre), put)
    fine.smooth(v0, v1, known[1:-1])
    for ref, above in ((first_out, even), (second_out, 1 - even)):
        ref[...] = v1[pl.ds(HALO + 1 + above * (SLAB - HALO), NEAR), pl.ds(8, ny), :]
    half = ny // 2

    def coarsened(x):
        at = HALO + 2 * x
        return fine.defect(v1, at) + fine.defect(v1, at + 1), r[at] + r[at + 1]

    def put_pooled(x, pair):
        for n in range(2):
            pooled[n, pl.ds(x * half, half), :] = fine.pool_rows(pair[n], tmp.at[2 * x + n])

    sweep(range(SLAB // 2), coarsened, put_pooled)
    packed = split_dot(pooled[0], pool_ref[...]) + split_dot(pooled[1], pool_up_ref[...])
    coarse_ref[...] = packed.reshape(coarse_ref.shape)


def coarse_kernel(grid, place_ref, scalar_ref, *refs):
    slabs, nx, ny, nz = grid
    pool_ref, spread_ref = refs[:2]
    coarse, out_ref = refs[2 : 2 + slabs], refs[2 + slabs]
    f1, r1, w1, v1a, v1b, pooled, tmp = refs[3 + slabs :]
    pool, spread = pool_ref[...], spread_ref[...]
    slab = place_ref[1]
    rim = HALO // 2
    nx1, ny1, nx2, ny2 = nx // 2, ny // 2, nx // 4, ny // 4
    mid = Level(1, ny1, nz // 2, rim, scalar_ref, f1, r1, w1)
    deep = Level(2, ny2, nz // 4, 0, scalar_ref, None, None, None)
    for v in (v1a, v1b):
        zero_rows(v, ny1)
        blank = jnp.zeros((rim,) + v.shape[1:], jnp.float32)
        v[pl.ds(0, rim)] = blank
        v[pl.ds(rim + nx1, rim)] = blank

    lower = lax.broadcasted_iota(jnp.int32, (1, LANES), 1) < LANES // 2
    own = SLAB // 2
    for k in range(slabs):
        first = jnp.bitwise_xor(slab, k) * own
        both = coarse[k][...]
        f1[pl.ds(first, own)] = jnp.where(lower, both, 0.0)
        r1[pl.ds(first, own)] = jnp.where(lower, pltpu.roll(both, LANES // 2, 2), 0.0)

    def put_start(x, weight):
        w1[x] = weight
        v1a[x + rim, pl.ds(8, ny1), :] = weight * f1[x]

    sweep(range(nx1), lambda x: DAMPING / (r1[x] + mid.centre), put_start)
    mid.smooth(v1a, v1b, range(nx1))

    def coarsened(x):
        return mid.defect(v1b, 2 * x) + mid.defect(v1b, 2 * x + 1), r1[2 * x] + r1[2 * x + 1]

    rows2 = nx2 * ny2

    def put_pooled(x, pair):
        for n in range(2):
            value = mid.pool_rows(pair[n], tmp.at[2 * x + n])
            pooled[pl.ds(n * rows2 + x * ny2, ny2), :] = value

    sweep(range(nx2), coarsened, put_pooled)
    deeper = split_dot(pooled[pl.ds(0, 2 * rows2), :], pool)
    planes = [deeper[n * ny2 : (n + 1) * ny2] for n in range(2 * nx2)]
    values = deep.solve_in_registers(planes[:nx2], planes[nx2:])

    pooled[pl.ds(0, rows2), :] = split_dot(values, spread)

    def refined1(x):
        return mid.spread_rows(pooled[pl.ds(x * ny2, ny2), :], tmp.at[x])

    def put_refined1(x, value):
        for n in range(2):
            v1b[2 * x + n + rim, pl.ds(8, ny1), :] += value

    sweep(range(nx2), refined1, put_refined1)
    mid.smooth(v1b, v1a, range(nx1))
    mid.smooth(v1a, v1b, range(nx1))

    window = own + 2 * rim
    values = v1b[pl.ds(slab * own, window), pl.ds(8, ny1), :].reshape(window * ny1, LANES)
    out_ref[...] = split_dot(values, spread)


def post_kernel(by, place_ref, scalar_ref, *refs):
    f, r, w, v1, correction, first_ref, second_ref, kept_ref, sent_ref, va, vb, tmp = refs
    count, ny = f.shape[:2]
    fine = Level(0, ny, LANES, 0, scalar_ref, f, r, w)
    for v in (va, vb):
        zero_rows(v, ny)
    even, half = 1 - (place_ref[1] & 1), ny // 2
    window = correction.shape[0] // half
    for ref, above in ((first_ref, even), (second_ref, 1 - even)):
        va[pl.ds(1 + above * (SLAB + HALO), NEAR), pl.ds(8, ny), :] = ref[...]

    def refined(x):
        return fine.spread_rows(correction[pl.ds(x * half, half), :], tmp.at[x])

    def put_refined(x, value):
        for at in (2 * x, 2 * x + 1):
            if 0 < at < count - 1:
                known = HALO - NEAR < at < HALO + SLAB + NEAR - 1
                here = v1 if known else va
                va[at, pl.ds(8, ny), :] = here[at, pl.ds(8, ny), :] + value

    sweep(range(window), refined, put_refined)
    fine.smooth(va, vb, range(2, count - 2))
    fine.smooth(vb, va, range(3, count - 3))

    total = jnp.zeros((8, LANES), jnp.float32)
    for x in range(SLAB):
        rest = fine.defect(va, HALO + x)
        total = total + jnp.sum((rest * rest).reshape(ny // 8, 8, LANES), axis=0)
        tmp[x] = rest
    squares = jnp.full((8, LANES), jnp.sum(total), jnp.float32)

    core, area = place_ref[0] & 1, half * SLAB
    for ref, first in ((kept_ref, core * by), (sent_ref, (1 - core) * by)):
        for y in range(half // by):
            row = pl.multiple_of(2 * y * by + first, 8)
            for x in range(SLAB):
                to = x * half + y * by
                ref[pl.ds(to, by), :] = va[HALO + x, pl.ds(8 + row, by), :]
                ref[pl.ds(area + to, by), :] = tmp[x, pl.ds(row, by), :]
        ref[pl.ds(2 * area, 8), :] = squares


def merge_back_kernel(bx, by, chips_y, place_ref, kept_ref, got_ref, *out_refs):
    chip, core = place_ref[0] // 2, place_ref[0] & 1
    area, half = bx * by, chips_y * by
    for m, out_ref in enumerate(out_refs):
        target = jnp.bitwise_xor(chip, m)
        first = (target // chips_y) * bx * half + lax.rem(target, chips_y) * by
        for ref, column in ((kept_ref, core), (got_ref, 1 - core)):
            for n in range(2):
                for p in range(bx):
                    at = pl.multiple_of(first + (n * SLAB + p) * half, 8)
                    to = pl.multiple_of((2 * column + n) * area + p * by, 8)
                    out_ref[pl.ds(to, by), :] = ref[pl.ds(at, by), :]
            to = pl.multiple_of(4 * area + 8 * column, 8)
            out_ref[pl.ds(to, 8), :] = ref[pl.ds(2 * SLAB * half, 8), :]


def collect_kernel(which, place_ref, *refs):
    parts, out_ref = refs[:-1], refs[-1]
    _, bx, by, _ = out_ref.shape
    area = bx * by
    for m, part in enumerate(parts):
        target = jnp.bitwise_xor(place_ref[0] // 2, m)
        for n in range(2):
            rows = pl.ds((2 * n + which) * area, area)
            out_ref[2 * target + n] = part[rows, :].reshape(bx, by, LANES)


def collect_first_kernel(place_ref, squares_ref, *refs):
    collect_kernel(0, place_ref, *refs[:-1])
    refs[-1][...] = squares_ref[...]


def squares_kernel(row, *refs):
    for m, part in enumerate(refs[:-1]):
        for n in range(2):
            refs[-1][pl.ds(2 * m + n, 1), :] = part[pl.ds(row + 8 * n, 1), :]


SMEM = pl.BlockSpec(memory_space=pltpu.SMEM)
VMEM = pl.BlockSpec(memory_space=pltpu.VMEM)


def local_kernel(kernel, name, scalars, arrays, outs, scratch=()):
    return pl.pallas_call(
        kernel,
        out_shape=[jax.ShapeDtypeStruct(shape, jnp.float32) for shape in outs],
        in_specs=[SMEM] * len(scalars) + [VMEM] * len(arrays),
        out_specs=[VMEM] * len(outs),
        scratch_shapes=[pltpu.VMEM(shape, jnp.float32) for shape in scratch],
        compiler_params=pltpu.CompilerParams(vmem_limit_bytes=VMEM_LIMIT),
        name=name,
    )(*scalars, *arrays)


def swap_in_plane(pieces, unit):
    devices = lax.axis_size("gx") * lax.axis_size("gy")
    moved = [pieces[0]]
    for k in range(1, len(pieces)):
        pairs = [(i, i ^ (k * unit)) for i in range(devices)]
        moved.append(lax.ppermute(pieces[k], ("gx", "gy"), pairs))
    return moved


def swap_slabs(piece, step, slabs):
    size = lax.axis_size("gx")
    moved = [piece]
    for k in range(1, slabs):
        pairs = [(i, i ^ (k * step)) for i in range(size)]
        moved.append(lax.ppermute(piece, "gx", pairs))
    return moved


def column_body(source, reaction, shifts, shift_index, velocity):
    columns, bx, by, nz = source.shape
    gx_size, gy_size = lax.axis_size("gx"), lax.axis_size("gy")
    nx, ny = bx * gx_size, by * gy_size
    step = columns // gy_size
    slabs = gx_size // step
    along, across = lax.axis_index("gx"), lax.axis_index("gy")
    column = lax.rem(along, step) * gy_size + across
    place = jnp.stack([column, along // step]).astype(jnp.int32)
    count = SLAB + 2 * HALO
    area = bx * by

    chips, chips_y = columns // 2, gy_size // 2
    cores = [(i, i ^ 1) for i in range(gy_size)]
    theirs = [lax.ppermute(source, "gy", cores), lax.ppermute(reaction, "gy", cores)]
    (mine,) = local_kernel(keep_kernel, "keep", (place,), (source,), [(chips, bx, by, nz)])
    *blocks, scalar_rows = local_kernel(
        merge_kernel,
        "merge",
        (place, shifts, shift_index, velocity),
        (mine, theirs[0], reaction, theirs[1]),
        [(2, bx, 2 * by, nz)] * chips + [(8, LANES)],
    )
    scalars = (place, scalar_rows)
    blocks = swap_in_plane(blocks, 2)

    edge = (2, NEAR, ny, nz)
    (own_edge,) = local_kernel(
        functools.partial(edge_kernel, chips_y), "edge", (place,), blocks[:chips_y], [edge]
    )
    slab, other_edge = local_kernel(
        functools.partial(arrange_kernel, chips_y),
        "arrange",
        (place,),
        blocks,
        [(2, SLAB, ny, nz), edge],
    )
    beside = []
    for n, piece in enumerate((own_edge, other_edge)):
        pairs = [(i, i + step if i % step != n else i - step) for i in range(gx_size)]
        pairs = [(i, j) for i, j in pairs if 0 <= j < gx_size]
        beside.append(lax.ppermute(piece, "gx", pairs))

    def exchange(pieces):
        got = []
        for n, piece in enumerate(pieces):
            pairs = [(i, i + step if i // step % 2 == n else i - step) for i in range(gx_size)]
            pairs = [(i, j) for i, j in pairs if 0 <= j < gx_size]
            got.append(lax.ppermute(piece, "gx", pairs))
        return got

    grid, rimmed = (count, ny, nz), (count, ny + 16, nz)
    f, r, w, v1, coarse, *beyond = local_kernel(
        functools.partial(pre_kernel, slabs, chips_y),
        "pre",
        scalars,
        (pool_matrix(0), pool_matrix(LANES // 2), slab, *beside),
        [grid, grid, grid, rimmed, (SLAB // 2, ny // 2, nz)] + [(NEAR, ny, nz)] * 2,
        [rimmed, (SLAB, ny, nz), (2, SLAB // 2 * ny // 2, nz)],
    )
    gathered = swap_slabs(coarse, step, slabs)

    coarse_grid = (nx // 2, ny // 2, nz)
    coarse_rimmed = (nx // 2 + HALO, ny // 2 + 16, nz)
    window = (SLAB // 2 + HALO) * ny // 2
    (correction,) = local_kernel(
        functools.partial(coarse_kernel, (slabs, nx, ny, nz)),
        "coarse",
        scalars,
        (pool_matrix(0), spread_matrix(), *gathered),
        [(window, nz)],
        [coarse_grid] * 3 + [coarse_rimmed] * 2 + [(nx // 4 * ny // 2, nz), (nx // 2, ny // 2, nz)],
    )
    result = (SLAB * ny + 8, nz)
    kept, sent = local_kernel(
        functools.partial(post_kernel, by),
        "post",
        scalars,
        (f, r, w, v1, correction, *exchange(beyond)),
        [result, result],
        [rimmed] * 2 + [(SLAB, ny, nz)],
    )

    parts = local_kernel(
        functools.partial(merge_back_kernel, bx, by, chips_y),
        "merge_back",
        (place,),
        (kept, lax.ppermute(sent, "gy", cores)),
        [(4 * area + 16, nz)] * chips,
    )
    parts = swap_in_plane(parts, 2)
    (squares,) = local_kernel(
        functools.partial(squares_kernel, 4 * area), "squares", (), parts, [(columns, nz)]
    )
    total, stride = squares, 1
    iterate, own = local_kernel(
        collect_first_kernel, "collect", (place,), (squares, *parts), [source.shape, squares.shape]
    )
    while stride < slabs:
        pairs = [(i, i ^ (stride * step)) for i in range(gx_size)]
        got = lax.ppermute(total, "gx", pairs)
        total = (own if stride == 1 else total) + got
        stride *= 2
    (residual,) = local_kernel(
        functools.partial(collect_kernel, 1), "collect", (place,), parts, [source.shape]
    )
    rms = jnp.sqrt(total[:, 0] / (nx * ny * nz) + EPSILON)
    slots = jnp.arange(columns, dtype=jnp.int32)
    mine = jnp.bitwise_xor(slots, column // 2 * 2)[:, None] == slots[None, :]
    residual_rms = jnp.sum(jnp.where(mine, rms[None, :], 0.0), axis=1)
    return iterate, residual, residual_rms


def power_of_two(n):
    return n > 0 and n & (n - 1) == 0


def column_plan_fits(columns, bx, by, nz, gx_size, gy_size):
    if columns % gy_size or gx_size % (columns // gy_size):
        return False
    step = columns // gy_size
    slabs, ny = gx_size // step, by * gy_size
    whole = power_of_two(columns) and power_of_two(step) and power_of_two(slabs)
    small = slabs * ny * nz <= 2**15
    paired = step == 2 and bx == HALO and gy_size % 2 == 0
    return whole and small and paired and bx * step == SLAB and nz == LANES and by % 16 == 0


def solution(mesh):
    gx_size, gy_size = mesh.shape["gx"], mesh.shape["gy"]

    def body(source, reaction, shifts, shift_index, velocity):
        fits = column_plan_fits(*source.shape, gx_size, gy_size)
        plan = column_body if fits else halo_body
        return plan(source, reaction, shifts, shift_index, velocity)

    return jax.shard_map(
        body,
        mesh=mesh,
        in_specs=(P(None, "gx", "gy", None), P("gx", "gy", None), P(), P(), P()),
        out_specs=(P(None, "gx", "gy", None), P(None, "gx", "gy", None), P()),
        check_vma=False,
    )
```

```python
import functools

import jax
import jax.numpy as jnp
from jax import lax
from jax.experimental import pallas as pl
from jax.experimental.pallas import tpu as pltpu
from jax.sharding import PartitionSpec as P

LEVELS = 3
COARSE_SWEEPS = 6

DAMPING = 0.8
EPSILON = 1e-06
VMEM_LIMIT = 32 * 1024 * 1024
LANES = 128
GROUP = 4
SLAB = 8
HALO = 4
NEAR = 2


def with_halo(x, sides, width):
    for axis, dim in sides:
        peers, length = (lax.axis_size(axis), x.shape[dim])
        up = [(i, (i + 1) % peers) for i in range(peers - 1)]
        down = [(j, i) for i, j in up]
        last = lax.slice_in_dim(x, length - width, length, axis=dim)
        leading = lax.slice_in_dim(x, 0, width, axis=dim)
        before = lax.ppermute(last, axis, up)
        after = lax.ppermute(leading, axis, down)
        x = jnp.concatenate([before, x, after], axis=dim)
    return x


def select_shifts(shifts, shift_index):
    columns = jnp.arange(shifts.shape[0], dtype=jnp.int32)
    picked = jnp.where(shift_index[:, None] == columns[None, :], shifts[None, :], 0.0)
    return jnp.sum(picked, axis=1)


def coefficients(velocity, spacing):
    scale_a = 1.0 / (spacing * spacing)
    backward = scale_a + jnp.maximum(velocity, 0.0) / spacing
    forward = scale_a - jnp.minimum(velocity, 0.0) / spacing
    centre = 6.0 * scale_a + jnp.sum(jnp.abs(velocity)) / spacing
    return (backward, forward, centre)


def apply_stencil(padded, backward, forward, diagonal):
    middle = padded[:, 1:-1, 1:-1, :]
    along_z = jnp.pad(middle, ((0, 0), (0, 0), (0, 0), (1, 1)))
    others = backward[0] * padded[:, :-2, 1:-1, :] + forward[0] * padded[:, 2:, 1:-1, :]
    others = others + backward[1] * padded[:, 1:-1, :-2, :] + forward[1] * padded[:, 1:-1, 2:, :]
    others = others + backward[2] * along_z[:, :, :, :-2] + forward[2] * along_z[:, :, :, 2:]
    return diagonal * middle - others


def face_halo(iterate):
    return with_halo(iterate, (("gx", 1), ("gy", 2)), 1)


def coarsen(values):
    count, size_x, size_y, size_z = values.shape
    blocks = values.reshape(count, size_x // 2, 2, size_y // 2, 2, size_z // 2, 2)
    return jnp.sum(blocks, axis=(2, 4, 6)) * 0.125


def refine(values):
    return jnp.repeat(jnp.repeat(jnp.repeat(values, 2, 1), 2, 2), 2, 3)


def coarsest_solve(rhs_field, backward, forward, diagonal):
    iterate = DAMPING * rhs_field / diagonal
    for repeat in range(COARSE_SWEEPS - 1):
        applied = apply_stencil(face_halo(iterate), backward, forward, diagonal)
        iterate = iterate + DAMPING * (rhs_field - applied) / diagonal
    return iterate


def multigrid_cycle(level_index, rhs_field, reaction_l, shift_value, velocity):
    backward, forward, centre = coefficients(velocity, 2.0**level_index)
    diagonal = centre + reaction_l + shift_value[:, None, None, None]
    if level_index == LEVELS - 1:
        return coarsest_solve(rhs_field, backward, forward, diagonal)

    def operate(iterate):
        return apply_stencil(face_halo(iterate), backward, forward, diagonal)

    def smooth_step(iterate):
        return iterate + DAMPING * (rhs_field - operate(iterate)) / diagonal

    iterate = DAMPING * rhs_field / diagonal
    iterate = smooth_step(iterate)
    defect = rhs_field - operate(iterate)
    correction = multigrid_cycle(
        level_index + 1, coarsen(defect), coarsen(reaction_l), shift_value, velocity
    )
    iterate = iterate + refine(correction)
    iterate = smooth_step(iterate)
    iterate = smooth_step(iterate)
    return iterate


def halo_body(source, reaction, shifts, shift_index, velocity):
    columns, cells_x, cells_y, cells_z = source.shape
    shift_value = select_shifts(shifts, shift_index)
    reaction_top = reaction[None]
    backward, forward, centre = coefficients(velocity, 1.0)
    diagonal = centre + reaction_top + shift_value[:, None, None, None]

    iterate = multigrid_cycle(0, source, reaction_top, shift_value, velocity)
    residual = source - apply_stencil(face_halo(iterate), backward, forward, diagonal)
    local_squares = jnp.sum(residual * residual, axis=(1, 2, 3))
    squares = lax.psum(local_squares, ("gx", "gy"))
    total_cells = cells_x * cells_y * cells_z * lax.axis_size("gx") * lax.axis_size("gy")
    residual_rms = jnp.sqrt(squares / total_cells + EPSILON)
    return (iterate, residual, residual_rms)


def split_dot(values, matrix):
    high = values.astype(jnp.bfloat16)
    low = (values - high.astype(jnp.float32)).astype(jnp.bfloat16)
    return jnp.dot(high, matrix, preferred_element_type=jnp.float32) + jnp.dot(
        low, matrix, preferred_element_type=jnp.float32
    )


def sweep(planes, get, put):
    planes = list(planes)
    for first in range(0, len(planes), GROUP):
        group = planes[first : first + GROUP]
        values = [get(x) for x in group]
        for x, value in zip(group, values):
            put(x, value)


class Grid:
    def __init__(self, ny):
        self.ny = ny

    def pool_rows(self, value, rows):
        half, ny = self.ny // 2, self.ny
        rows[pl.ds(0, ny), :] = value
        return rows[pl.ds(0, half, stride=2), :] + rows[pl.ds(1, half, stride=2), :]

    def spread_rows(self, part, rows):
        half, ny = self.ny // 2, self.ny
        rows[pl.ds(0, half, stride=2), :] = part
        rows[pl.ds(1, half, stride=2), :] = part
        return rows[pl.ds(0, ny), :]


class Level(Grid):
    def __init__(self, index, ny, nz, rim, scalar_ref, f, r, w):
        super().__init__(ny)
        self.nz, self.rim = nz, rim
        self.f, self.r, self.w = f, r, w
        spacing = 2.0**index
        scale_a = 1.0 / (spacing * spacing)
        inverse = 1.0 / spacing
        shift = scalar_ref[0, 0]
        speed = [scalar_ref[1 + d, 0] for d in range(3)]
        self.backward = [scale_a + jnp.maximum(v, 0.0) * inverse for v in speed]
        self.forward = [scale_a - jnp.minimum(v, 0.0) * inverse for v in speed]
        total = jnp.abs(speed[0]) + jnp.abs(speed[1]) + jnp.abs(speed[2])
        self.centre = 6.0 * scale_a + total * inverse + shift
        lane = lax.broadcasted_iota(jnp.int32, (1, LANES), 1)
        inside = lane < nz
        self.low_z = jnp.where((lane > 0) & inside, self.backward[2], 0.0)
        self.high_z = jnp.where(lane < nz - 1, self.forward[2], 0.0)

    def plane(self, v, x):
        return v[x + self.rim, pl.ds(8, self.ny), :]

    def put(self, v):
        def write(x, value):
            v[x + self.rim, pl.ds(8, self.ny), :] = value

        return write

    def along_z(self, middle):
        return self.low_z * pltpu.roll(middle, 1, 1) + self.high_z * pltpu.roll(middle, LANES - 1, 1)

    def neighbours(self, v, x, middle):
        at, ny = x + self.rim, self.ny
        along_x = self.backward[0] * v[at - 1, pl.ds(8, ny), :] + self.forward[0] * v[at + 1, pl.ds(8, ny), :]
        along_y = self.backward[1] * v[at, pl.ds(7, ny), :] + self.forward[1] * v[at, pl.ds(9, ny), :]
        return along_x + along_y + self.along_z(middle)

    def smoothed(self, v, x):
        middle = self.plane(v, x)
        pulled = self.f[x] + self.neighbours(v, x, middle)
        return (1.0 - DAMPING) * middle + self.w[x] * pulled

    def smooth(self, src, dst, planes):
        sweep(planes, lambda x: self.smoothed(src, x), self.put(dst))

    def defect(self, v, x):
        middle = self.plane(v, x)
        pulled = self.f[x] + self.neighbours(v, x, middle)
        return pulled - (self.r[x] + self.centre) * middle

    def solve_in_registers(self, rhs, reaction):
        row = lax.broadcasted_iota(jnp.int32, (self.ny, 1), 0)
        low_y = jnp.where(row > 0, self.backward[1], 0.0)
        high_y = jnp.where(row < self.ny - 1, self.forward[1], 0.0)
        weight = [DAMPING / (r + self.centre) for r in reaction]
        v = [w * f for w, f in zip(weight, rhs)]
        for _ in range(COARSE_SWEEPS - 1):
            new = []
            for x, here in enumerate(v):
                along_y = low_y * pltpu.roll(here, 1, 0) + high_y * pltpu.roll(here, self.ny - 1, 0)
                pulled = rhs[x] + self.along_z(here) + along_y
                if x > 0:
                    pulled += self.backward[0] * v[x - 1]
                if x < len(v) - 1:
                    pulled += self.forward[0] * v[x + 1]
                new.append((1.0 - DAMPING) * here + weight[x] * pulled)
            v = new
        return jnp.concatenate(v, axis=0)


def zero_rows(v, ny):
    edge = jnp.zeros((v.shape[0], 8, LANES), jnp.float32)
    v[:, pl.ds(0, 8), :] = edge
    v[:, pl.ds(8 + ny, 8), :] = edge


def pool_matrix(offset):
    row = lax.broadcasted_iota(jnp.int32, (LANES, LANES), 0)
    col = lax.broadcasted_iota(jnp.int32, (LANES, LANES), 1)
    return jnp.where(row // 2 + offset == col, 0.125, 0.0).astype(jnp.bfloat16)


def spread_matrix():
    row = lax.broadcasted_iota(jnp.int32, (LANES, LANES), 0)
    col = lax.broadcasted_iota(jnp.int32, (LANES, LANES), 1)
    return jnp.where(col // 2 == row, 1.0, 0.0).astype(jnp.bfloat16)


def keep_kernel(place_ref, source_ref, out_ref):
    for n in range(out_ref.shape[0]):
        out_ref[n] = source_ref[2 * n + (place_ref[0] & 1)]


def merge_kernel(place_ref, shifts_ref, index_ref, velocity_ref, *refs):
    mine_ref, theirs_ref, reaction_ref, other_reaction_ref = refs[:4]
    out_refs, scalar_ref = refs[4:-1], refs[-1]
    chip, core = place_ref[0] // 2, place_ref[0] & 1
    by = mine_ref.shape[2]
    mine = pl.ds(pl.multiple_of(core * by, 8), by)
    theirs = pl.ds(pl.multiple_of((1 - core) * by, 8), by)
    for m, out_ref in enumerate(out_refs):
        target = jnp.bitwise_xor(chip, m)
        out_ref[0, :, mine, :] = mine_ref[target]
        out_ref[0, :, theirs, :] = theirs_ref[2 * target + core]
        out_ref[1, :, mine, :] = reaction_ref[...]
        out_ref[1, :, theirs, :] = other_reaction_ref[...]
    scalars = [shifts_ref[index_ref[place_ref[0]]]] + [velocity_ref[d] for d in range(3)]
    for n, scalar in enumerate(scalars):
        scalar_ref[pl.ds(n, 1), :] = jnp.full((1, LANES), scalar, jnp.float32)


def half_kernel(chips_y, place_ref, *refs):
    blocks, half_ref = refs[:-1], refs[-1]
    for m, block in enumerate(blocks):
        size = block.shape[2]
        chip = jnp.bitwise_xor(place_ref[0] // 2, m)
        rows = pl.ds(pl.multiple_of(lax.rem(chip, chips_y) * size, 8), size)
        half_ref[:, :, rows, :] = block[...]


def arrange_kernel(chips_y, place_ref, *refs):
    blocks, (slab_ref, near_ref) = refs[:-2], refs[-2:]
    chip = place_ref[0] // 2
    for m, block in enumerate(blocks):
        owner = jnp.bitwise_xor(chip, m)
        _, bx, size, _ = block.shape
        planes = pl.ds((owner // chips_y) * bx, bx)
        rows = pl.ds(pl.multiple_of(lax.rem(owner, chips_y) * size, 8), size)
        slab_ref[:, planes, rows, :] = block[...]
    other = 1 - chip // chips_y
    near_ref[...] = slab_ref[:, pl.ds(other * (SLAB - NEAR), NEAR)]


def smooth_beyond(fine, inside, half_ref, v0):
    f, r, w, ny = fine.f, fine.r, fine.w, fine.ny
    f[...], r[...] = half_ref[0], half_ref[1]

    def put(at, weight):
        w[at] = weight
        v0[at, pl.ds(8, ny), :] = weight * f[at]

    sweep(range(HALO), lambda at: inside / (r[at] + fine.centre), put)
    return [fine.smoothed(v0, 1 + n) for n in range(NEAR)]


def pre_kernel(slabs, chips_y, place_ref, scalar_ref, *refs):
    pool_ref, pool_up_ref, slab_ref, half_ref, near_ref = refs[:5]
    f, r, w, v1, coarse_ref, beyond_ref, v0, tmp, pooled = refs[5:]
    ny = f.shape[1]
    slab = place_ref[1]
    fine = Level(0, ny, LANES, 0, scalar_ref, f, r, w)
    zero_rows(v0, ny)
    zero_rows(v1, ny)
    after = HALO + SLAB

    f[pl.ds(HALO, SLAB)], r[pl.ds(HALO, SLAB)] = slab_ref[0], slab_ref[1]
    x = place_ref[0] // 2 // chips_y
    for above, ref, first in ((1 - x, half_ref, x * NEAR), (x, near_ref, 0)):
        planes = pl.ds((HALO - NEAR) + above * (SLAB + NEAR), NEAR)
        f[planes], r[planes] = ref[0, pl.ds(first, NEAR)], ref[1, pl.ds(first, NEAR)]

    inside = [jnp.where(slab > 0, DAMPING, 0.0)] * HALO
    inside += [DAMPING] * SLAB
    inside += [jnp.where(slab < slabs - 1, DAMPING, 0.0)] * HALO

    def put(x, weight):
        w[x] = weight
        v0[x, pl.ds(8, ny), :] = weight * f[x]

    known = range(HALO - NEAR, after + NEAR)
    sweep(known, lambda x: inside[x] / (r[x] + fine.centre), put)
    fine.smooth(v0, v1, known[1:-1])
    half = ny // 2

    def coarsened(x):
        at = HALO + 2 * x
        return fine.defect(v1, at) + fine.defect(v1, at + 1), r[at] + r[at + 1]

    def put_pooled(x, pair):
        for n in range(2):
            pooled[n, pl.ds(x * half, half), :] = fine.pool_rows(pair[n], tmp.at[2 * x + n])

    sweep(range(SLAB // 2), coarsened, put_pooled)
    packed = split_dot(pooled[0], pool_ref[...]) + split_dot(pooled[1], pool_up_ref[...])
    coarse_ref[...] = packed.reshape(coarse_ref.shape)
    first = HALO + 1 + (1 - x) * (SLAB - HALO)
    beyond_ref[...] = v1[pl.ds(first, NEAR), pl.ds(8, ny), :]


def coarse_kernel(grid, place_ref, scalar_ref, *refs):
    slabs, nx, ny, nz = grid
    pool_ref, spread_ref = refs[:2]
    coarse, out_ref = refs[2 : 2 + slabs], refs[2 + slabs]
    f1, r1, w1, v1a, v1b, pooled, tmp = refs[3 + slabs :]
    pool, spread = pool_ref[...], spread_ref[...]
    slab = place_ref[1]
    rim = HALO // 2
    nx1, ny1, nx2, ny2 = nx // 2, ny // 2, nx // 4, ny // 4
    mid = Level(1, ny1, nz // 2, rim, scalar_ref, f1, r1, w1)
    deep = Level(2, ny2, nz // 4, 0, scalar_ref, None, None, None)
    for v in (v1a, v1b):
        zero_rows(v, ny1)
        blank = jnp.zeros((rim,) + v.shape[1:], jnp.float32)
        v[pl.ds(0, rim)] = blank
        v[pl.ds(rim + nx1, rim)] = blank

    lower = lax.broadcasted_iota(jnp.int32, (1, LANES), 1) < LANES // 2
    own = SLAB // 2
    for k in range(slabs):
        first = jnp.bitwise_xor(slab, k) * own
        both = coarse[k][...]
        f1[pl.ds(first, own)] = jnp.where(lower, both, 0.0)
        r1[pl.ds(first, own)] = jnp.where(lower, pltpu.roll(both, LANES // 2, 2), 0.0)

    def put_start(x, weight):
        w1[x] = weight
        v1a[x + rim, pl.ds(8, ny1), :] = weight * f1[x]

    sweep(range(nx1), lambda x: DAMPING / (r1[x] + mid.centre), put_start)
    mid.smooth(v1a, v1b, range(nx1))

    def coarsened(x):
        return mid.defect(v1b, 2 * x) + mid.defect(v1b, 2 * x + 1), r1[2 * x] + r1[2 * x + 1]

    rows2 = nx2 * ny2

    def put_pooled(x, pair):
        for n in range(2):
            value = mid.pool_rows(pair[n], tmp.at[2 * x + n])
            pooled[pl.ds(n * rows2 + x * ny2, ny2), :] = value

    sweep(range(nx2), coarsened, put_pooled)
    deeper = split_dot(pooled[pl.ds(0, 2 * rows2), :], pool)
    planes = [deeper[n * ny2 : (n + 1) * ny2] for n in range(2 * nx2)]
    values = deep.solve_in_registers(planes[:nx2], planes[nx2:])

    pooled[pl.ds(0, rows2), :] = split_dot(values, spread)

    def refined1(x):
        return mid.spread_rows(pooled[pl.ds(x * ny2, ny2), :], tmp.at[x])

    def put_refined1(x, value):
        for n in range(2):
            v1b[2 * x + n + rim, pl.ds(8, ny1), :] += value

    sweep(range(nx2), refined1, put_refined1)
    mid.smooth(v1b, v1a, range(nx1))
    mid.smooth(v1a, v1b, range(nx1))

    window = own + 2 * rim
    values = v1b[pl.ds(slab * own, window), pl.ds(8, ny1), :].reshape(window * ny1, LANES)
    out_ref[...] = split_dot(values, spread)


def post_kernel(slabs, by, chips_y, place_ref, scalar_ref, *refs):
    f, r, w, v1, correction, half_ref, beyond_ref = refs[:7]
    kept_ref, sent_ref, va, vb, tmp, f_side, r_side, w_side, v_side = refs[7:]
    count, ny = f.shape[:2]
    fine = Level(0, ny, LANES, 0, scalar_ref, f, r, w)
    for v in (va, vb):
        zero_rows(v, ny)
    x, half = place_ref[0] // 2 // chips_y, ny // 2
    window = correction.shape[0] // half
    side = Level(0, ny, LANES, 0, scalar_ref, f_side, r_side, w_side)
    zero_rows(v_side, ny)
    slab = place_ref[1]
    beside = jnp.where(x == 0, slab < slabs - 1, slab > 0)
    planes = smooth_beyond(side, jnp.where(beside, DAMPING, 0.0), half_ref, v_side)
    for n in range(NEAR):
        va[1 + (1 - x) * (SLAB + HALO) + n, pl.ds(8, ny), :] = planes[n]
        va[1 + x * (SLAB + HALO) + n, pl.ds(8, ny), :] = beyond_ref[n]

    def refined(x):
        return fine.spread_rows(correction[pl.ds(x * half, half), :], tmp.at[x])

    def put_refined(x, value):
        for at in (2 * x, 2 * x + 1):
            if 0 < at < count - 1:
                known = HALO - NEAR < at < HALO + SLAB + NEAR - 1
                here = v1 if known else va
                va[at, pl.ds(8, ny), :] = here[at, pl.ds(8, ny), :] + value

    sweep(range(window), refined, put_refined)
    fine.smooth(va, vb, range(2, count - 2))
    fine.smooth(vb, va, range(3, count - 3))

    total = jnp.zeros((8, LANES), jnp.float32)
    for x in range(SLAB):
        rest = fine.defect(va, HALO + x)
        total = total + jnp.sum((rest * rest).reshape(ny // 8, 8, LANES), axis=0)
        tmp[x] = rest
    squares = jnp.full((8, LANES), jnp.sum(total), jnp.float32)

    core, area = place_ref[0] & 1, half * SLAB
    for ref, first in ((kept_ref, core * by), (sent_ref, (1 - core) * by)):
        for y in range(half // by):
            row = pl.multiple_of(2 * y * by + first, 8)
            for x in range(SLAB):
                to = x * half + y * by
                ref[pl.ds(to, by), :] = va[HALO + x, pl.ds(8 + row, by), :]
                ref[pl.ds(area + to, by), :] = tmp[x, pl.ds(row, by), :]
        ref[pl.ds(2 * area, 8), :] = squares


def merge_back_kernel(bx, by, chips_y, place_ref, kept_ref, got_ref, *out_refs):
    chip, core = place_ref[0] // 2, place_ref[0] & 1
    area, half = bx * by, chips_y * by
    for m, out_ref in enumerate(out_refs):
        target = jnp.bitwise_xor(chip, m)
        first = (target // chips_y) * bx * half + lax.rem(target, chips_y) * by
        for ref, column in ((kept_ref, core), (got_ref, 1 - core)):
            for n in range(2):
                for p in range(bx):
                    at = pl.multiple_of(first + (n * SLAB + p) * half, 8)
                    to = pl.multiple_of((2 * column + n) * area + p * by, 8)
                    out_ref[pl.ds(to, by), :] = ref[pl.ds(at, by), :]
            to = pl.multiple_of(4 * area + 8 * column, 8)
            out_ref[pl.ds(to, 8), :] = ref[pl.ds(2 * SLAB * half, 8), :]


def collect_kernel(place_ref, *refs):
    parts, (iterate_ref, residual_ref) = refs[:-2], refs[-2:]
    _, bx, by, _ = iterate_ref.shape
    area = bx * by
    for m, part in enumerate(parts):
        target = jnp.bitwise_xor(place_ref[0] // 2, m)
        for n in range(2):
            for k, ref in enumerate((iterate_ref, residual_ref)):
                rows = pl.ds((2 * n + k) * area, area)
                ref[2 * target + n] = part[rows, :].reshape(bx, by, LANES)


def squares_kernel(row, *refs):
    for m, part in enumerate(refs[:-1]):
        for n in range(2):
            refs[-1][pl.ds(2 * m + n, 1), :] = part[pl.ds(row + 8 * n, 1), :]


SMEM = pl.BlockSpec(memory_space=pltpu.SMEM)
VMEM = pl.BlockSpec(memory_space=pltpu.VMEM)


def local_kernel(kernel, name, scalars, arrays, outs, scratch=()):
    return pl.pallas_call(
        kernel,
        out_shape=[jax.ShapeDtypeStruct(shape, jnp.float32) for shape in outs],
        in_specs=[SMEM] * len(scalars) + [VMEM] * len(arrays),
        out_specs=[VMEM] * len(outs),
        scratch_shapes=[pltpu.VMEM(shape, jnp.float32) for shape in scratch],
        compiler_params=pltpu.CompilerParams(vmem_limit_bytes=VMEM_LIMIT),
        name=name,
    )(*scalars, *arrays)


def swap_in_plane(pieces, unit):
    devices = lax.axis_size("gx") * lax.axis_size("gy")
    moved = [pieces[0]]
    for k in range(1, len(pieces)):
        pairs = [(i, i ^ (k * unit)) for i in range(devices)]
        moved.append(lax.ppermute(pieces[k], ("gx", "gy"), pairs))
    return moved


def swap_slabs(piece, step, slabs):
    size = lax.axis_size("gx")
    moved = [piece]
    for k in range(1, slabs):
        pairs = [(i, i ^ (k * step)) for i in range(size)]
        moved.append(lax.ppermute(piece, "gx", pairs))
    return moved


def column_body(source, reaction, shifts, shift_index, velocity):
    columns, bx, by, nz = source.shape
    gx_size, gy_size = lax.axis_size("gx"), lax.axis_size("gy")
    nx, ny = bx * gx_size, by * gy_size
    step = columns // gy_size
    slabs = gx_size // step
    along, across = lax.axis_index("gx"), lax.axis_index("gy")
    column = lax.rem(along, step) * gy_size + across
    place = jnp.stack([column, along // step]).astype(jnp.int32)
    count = SLAB + 2 * HALO
    area = bx * by

    chips, chips_y = columns // 2, gy_size // 2
    cores = [(i, i ^ 1) for i in range(gy_size)]
    theirs = [lax.ppermute(source, "gy", cores), lax.ppermute(reaction, "gy", cores)]
    (mine,) = local_kernel(keep_kernel, "keep", (place,), (source,), [(chips, bx, by, nz)])
    *blocks, scalar_rows = local_kernel(
        merge_kernel,
        "merge",
        (place, shifts, shift_index, velocity),
        (mine, theirs[0], reaction, theirs[1]),
        [(2, bx, 2 * by, nz)] * chips + [(8, LANES)],
    )
    scalars = (place, scalar_rows)
    blocks = swap_in_plane(blocks, 2)

    edge = (2, NEAR, ny, nz)
    (own_half,) = local_kernel(
        functools.partial(half_kernel, chips_y),
        "half",
        (place,),
        blocks[:chips_y],
        [(2, HALO, ny, nz)],
    )
    slab, near = local_kernel(
        functools.partial(arrange_kernel, chips_y),
        "arrange",
        (place,),
        blocks,
        [(2, SLAB, ny, nz), edge],
    )

    def send_beside(piece, up):
        pairs = [(i, i + step if i % step == up else i - step) for i in range(gx_size)]
        return lax.ppermute(piece, "gx", [(i, j) for i, j in pairs if 0 <= j < gx_size])

    beside = [send_beside(own_half, 1), send_beside(near, 0)]
    grid, rimmed = (count, ny, nz), (count, ny + 16, nz)
    f, r, w, v1, coarse, beyond = local_kernel(
        functools.partial(pre_kernel, slabs, chips_y),
        "pre",
        scalars,
        (pool_matrix(0), pool_matrix(LANES // 2), slab, *beside),
        [grid, grid, grid, rimmed, (SLAB // 2, ny // 2, nz), (NEAR, ny, nz)],
        [rimmed, (SLAB, ny, nz), (2, SLAB // 2 * ny // 2, nz)],
    )
    gathered = swap_slabs(coarse, step, slabs)

    coarse_grid = (nx // 2, ny // 2, nz)
    coarse_rimmed = (nx // 2 + HALO, ny // 2 + 16, nz)
    window = (SLAB // 2 + HALO) * ny // 2
    (correction,) = local_kernel(
        functools.partial(coarse_kernel, (slabs, nx, ny, nz)),
        "coarse",
        scalars,
        (pool_matrix(0), spread_matrix(), *gathered),
        [(window, nz)],
        [coarse_grid] * 3 + [coarse_rimmed] * 2 + [(nx // 4 * ny // 2, nz), (nx // 2, ny // 2, nz)],
    )
    result = (SLAB * ny + 8, nz)
    kept, sent = local_kernel(
        functools.partial(post_kernel, slabs, by, chips_y),
        "post",
        scalars,
        (f, r, w, v1, correction, beside[0], send_beside(beyond, 0)),
        [result, result],
        [rimmed] * 2 + [(SLAB, ny, nz)] + [(HALO, ny, nz)] * 3 + [(HALO, ny + 16, nz)],
    )

    parts = local_kernel(
        functools.partial(merge_back_kernel, bx, by, chips_y),
        "merge_back",
        (place,),
        (kept, lax.ppermute(sent, "gy", cores)),
        [(4 * area + 16, nz)] * chips,
    )
    parts = swap_in_plane(parts, 2)
    (squares,) = local_kernel(
        functools.partial(squares_kernel, 4 * area), "squares", (), parts, [(columns, nz)]
    )
    iterate, residual = local_kernel(
        collect_kernel, "collect", (place,), parts, [source.shape] * 2
    )
    total = sum(swap_slabs(squares, step, slabs))
    rms = jnp.sqrt(total[:, 0] / (nx * ny * nz) + EPSILON)
    slots = jnp.arange(columns, dtype=jnp.int32)
    mine = jnp.bitwise_xor(slots, column // 2 * 2)[:, None] == slots[None, :]
    residual_rms = jnp.sum(jnp.where(mine, rms[None, :], 0.0), axis=1)
    return iterate, residual, residual_rms


def power_of_two(n):
    return n > 0 and n & (n - 1) == 0


def column_plan_fits(columns, bx, by, nz, gx_size, gy_size):
    if columns % gy_size or gx_size % (columns // gy_size):
        return False
    step = columns // gy_size
    slabs, ny = gx_size // step, by * gy_size
    whole = power_of_two(columns) and power_of_two(step) and power_of_two(slabs)
    small = slabs * ny * nz <= 2**15
    paired = step == 2 and bx == HALO and gy_size % 2 == 0
    return whole and small and paired and bx * step == SLAB and nz == LANES and by % 16 == 0


def solution(mesh):
    gx_size, gy_size = mesh.shape["gx"], mesh.shape["gy"]

    def body(source, reaction, shifts, shift_index, velocity):
        fits = column_plan_fits(*source.shape, gx_size, gy_size)
        plan = column_body if fits else halo_body
        return plan(source, reaction, shifts, shift_index, velocity)

    return jax.shard_map(
        body,
        mesh=mesh,
        in_specs=(P(None, "gx", "gy", None), P("gx", "gy", None), P(), P(), P()),
        out_specs=(P(None, "gx", "gy", None), P(None, "gx", "gy", None), P()),
        check_vma=False,
    )
```

```python
import functools

import jax
import jax.numpy as jnp
from jax import lax
from jax.experimental import pallas as pl
from jax.experimental.pallas import tpu as pltpu
from jax.sharding import PartitionSpec as P

LEVELS = 3
COARSE_SWEEPS = 6

DAMPING = 0.8
EPSILON = 1e-06
VMEM_LIMIT = 32 * 1024 * 1024
LANES = 128
GROUP = 4
SLAB = 8
HALO = 4
NEAR = 2


def with_halo(x, sides, width):
    for axis, dim in sides:
        peers, length = (lax.axis_size(axis), x.shape[dim])
        up = [(i, (i + 1) % peers) for i in range(peers - 1)]
        down = [(j, i) for i, j in up]
        last = lax.slice_in_dim(x, length - width, length, axis=dim)
        leading = lax.slice_in_dim(x, 0, width, axis=dim)
        before = lax.ppermute(last, axis, up)
        after = lax.ppermute(leading, axis, down)
        x = jnp.concatenate([before, x, after], axis=dim)
    return x


def select_shifts(shifts, shift_index):
    columns = jnp.arange(shifts.shape[0], dtype=jnp.int32)
    picked = jnp.where(shift_index[:, None] == columns[None, :], shifts[None, :], 0.0)
    return jnp.sum(picked, axis=1)


def coefficients(velocity, spacing):
    scale_a = 1.0 / (spacing * spacing)
    backward = scale_a + jnp.maximum(velocity, 0.0) / spacing
    forward = scale_a - jnp.minimum(velocity, 0.0) / spacing
    centre = 6.0 * scale_a + jnp.sum(jnp.abs(velocity)) / spacing
    return (backward, forward, centre)


def apply_stencil(padded, backward, forward, diagonal):
    middle = padded[:, 1:-1, 1:-1, :]
    along_z = jnp.pad(middle, ((0, 0), (0, 0), (0, 0), (1, 1)))
    others = backward[0] * padded[:, :-2, 1:-1, :] + forward[0] * padded[:, 2:, 1:-1, :]
    others = others + backward[1] * padded[:, 1:-1, :-2, :] + forward[1] * padded[:, 1:-1, 2:, :]
    others = others + backward[2] * along_z[:, :, :, :-2] + forward[2] * along_z[:, :, :, 2:]
    return diagonal * middle - others


def face_halo(iterate):
    return with_halo(iterate, (("gx", 1), ("gy", 2)), 1)


def coarsen(values):
    count, size_x, size_y, size_z = values.shape
    blocks = values.reshape(count, size_x // 2, 2, size_y // 2, 2, size_z // 2, 2)
    return jnp.sum(blocks, axis=(2, 4, 6)) * 0.125


def refine(values):
    return jnp.repeat(jnp.repeat(jnp.repeat(values, 2, 1), 2, 2), 2, 3)


def coarsest_solve(rhs_field, backward, forward, diagonal):
    iterate = DAMPING * rhs_field / diagonal
    for repeat in range(COARSE_SWEEPS - 1):
        applied = apply_stencil(face_halo(iterate), backward, forward, diagonal)
        iterate = iterate + DAMPING * (rhs_field - applied) / diagonal
    return iterate


def multigrid_cycle(level_index, rhs_field, reaction_l, shift_value, velocity):
    backward, forward, centre = coefficients(velocity, 2.0**level_index)
    diagonal = centre + reaction_l + shift_value[:, None, None, None]
    if level_index == LEVELS - 1:
        return coarsest_solve(rhs_field, backward, forward, diagonal)

    def operate(iterate):
        return apply_stencil(face_halo(iterate), backward, forward, diagonal)

    def smooth_step(iterate):
        return iterate + DAMPING * (rhs_field - operate(iterate)) / diagonal

    iterate = DAMPING * rhs_field / diagonal
    iterate = smooth_step(iterate)
    defect = rhs_field - operate(iterate)
    correction = multigrid_cycle(
        level_index + 1, coarsen(defect), coarsen(reaction_l), shift_value, velocity
    )
    iterate = iterate + refine(correction)
    iterate = smooth_step(iterate)
    iterate = smooth_step(iterate)
    return iterate


def halo_body(source, reaction, shifts, shift_index, velocity):
    columns, cells_x, cells_y, cells_z = source.shape
    shift_value = select_shifts(shifts, shift_index)
    reaction_top = reaction[None]
    backward, forward, centre = coefficients(velocity, 1.0)
    diagonal = centre + reaction_top + shift_value[:, None, None, None]

    iterate = multigrid_cycle(0, source, reaction_top, shift_value, velocity)
    residual = source - apply_stencil(face_halo(iterate), backward, forward, diagonal)
    local_squares = jnp.sum(residual * residual, axis=(1, 2, 3))
    squares = lax.psum(local_squares, ("gx", "gy"))
    total_cells = cells_x * cells_y * cells_z * lax.axis_size("gx") * lax.axis_size("gy")
    residual_rms = jnp.sqrt(squares / total_cells + EPSILON)
    return (iterate, residual, residual_rms)


def split_dot(values, matrix):
    high = values.astype(jnp.bfloat16)
    low = (values - high.astype(jnp.float32)).astype(jnp.bfloat16)
    return jnp.dot(high, matrix, preferred_element_type=jnp.float32) + jnp.dot(
        low, matrix, preferred_element_type=jnp.float32
    )


def sweep(planes, get, put):
    planes = list(planes)
    for first in range(0, len(planes), GROUP):
        group = planes[first : first + GROUP]
        values = [get(x) for x in group]
        for x, value in zip(group, values):
            put(x, value)


class Grid:
    def __init__(self, ny):
        self.ny = ny

    def pool_rows(self, value, rows):
        half, ny = self.ny // 2, self.ny
        rows[pl.ds(0, ny), :] = value
        return rows[pl.ds(0, half, stride=2), :] + rows[pl.ds(1, half, stride=2), :]

    def spread_rows(self, part, rows):
        half, ny = self.ny // 2, self.ny
        rows[pl.ds(0, half, stride=2), :] = part
        rows[pl.ds(1, half, stride=2), :] = part
        return rows[pl.ds(0, ny), :]


class Level(Grid):
    def __init__(self, index, ny, nz, rim, scalars, f, r, w):
        super().__init__(ny)
        self.nz, self.rim = nz, rim
        self.f, self.r, self.w = f, r, w
        spacing = 2.0**index
        scale_a = 1.0 / (spacing * spacing)
        inverse = 1.0 / spacing
        shift, speed = scalars
        self.backward = [scale_a + jnp.maximum(v, 0.0) * inverse for v in speed]
        self.forward = [scale_a - jnp.minimum(v, 0.0) * inverse for v in speed]
        total = jnp.abs(speed[0]) + jnp.abs(speed[1]) + jnp.abs(speed[2])
        self.centre = 6.0 * scale_a + total * inverse + shift
        lane = lax.broadcasted_iota(jnp.int32, (1, LANES), 1)
        inside = lane < nz
        self.low_z = jnp.where((lane > 0) & inside, self.backward[2], 0.0)
        self.high_z = jnp.where(lane < nz - 1, self.forward[2], 0.0)

    def plane(self, v, x):
        return v[x + self.rim, pl.ds(8, self.ny), :]

    def put(self, v):
        def write(x, value):
            v[x + self.rim, pl.ds(8, self.ny), :] = value

        return write

    def along_z(self, middle):
        return self.low_z * pltpu.roll(middle, 1, 1) + self.high_z * pltpu.roll(middle, LANES - 1, 1)

    def neighbours(self, v, x, middle):
        at, ny = x + self.rim, self.ny
        along_x = self.backward[0] * v[at - 1, pl.ds(8, ny), :] + self.forward[0] * v[at + 1, pl.ds(8, ny), :]
        along_y = self.backward[1] * v[at, pl.ds(7, ny), :] + self.forward[1] * v[at, pl.ds(9, ny), :]
        return along_x + along_y + self.along_z(middle)

    def smoothed(self, v, x):
        middle = self.plane(v, x)
        pulled = self.f[x] + self.neighbours(v, x, middle)
        return (1.0 - DAMPING) * middle + self.w[x] * pulled

    def smooth(self, src, dst, planes):
        sweep(planes, lambda x: self.smoothed(src, x), self.put(dst))

    def defect(self, v, x):
        middle = self.plane(v, x)
        pulled = self.f[x] + self.neighbours(v, x, middle)
        return pulled - (self.r[x] + self.centre) * middle

    def solve_in_registers(self, rhs, reaction):
        row = lax.broadcasted_iota(jnp.int32, (self.ny, 1), 0)
        low_y = jnp.where(row > 0, self.backward[1], 0.0)
        high_y = jnp.where(row < self.ny - 1, self.forward[1], 0.0)
        weight = [DAMPING / (r + self.centre) for r in reaction]
        v = [w * f for w, f in zip(weight, rhs)]
        for _ in range(COARSE_SWEEPS - 1):
            new = []
            for x, here in enumerate(v):
                along_y = low_y * pltpu.roll(here, 1, 0) + high_y * pltpu.roll(here, self.ny - 1, 0)
                pulled = rhs[x] + self.along_z(here) + along_y
                if x > 0:
                    pulled += self.backward[0] * v[x - 1]
                if x < len(v) - 1:
                    pulled += self.forward[0] * v[x + 1]
                new.append((1.0 - DAMPING) * here + weight[x] * pulled)
            v = new
        return jnp.concatenate(v, axis=0)


def scalars_of(scalar_ref):
    return scalar_ref[0, 0], [scalar_ref[1 + d, 0] for d in range(3)]


def zero_rows(v, ny):
    edge = jnp.zeros((v.shape[0], 8, LANES), jnp.float32)
    v[:, pl.ds(0, 8), :] = edge
    v[:, pl.ds(8 + ny, 8), :] = edge


def pool_matrix(offset):
    row = lax.broadcasted_iota(jnp.int32, (LANES, LANES), 0)
    col = lax.broadcasted_iota(jnp.int32, (LANES, LANES), 1)
    return jnp.where(row // 2 + offset == col, 0.125, 0.0).astype(jnp.bfloat16)


def spread_matrix():
    row = lax.broadcasted_iota(jnp.int32, (LANES, LANES), 0)
    col = lax.broadcasted_iota(jnp.int32, (LANES, LANES), 1)
    return jnp.where(col // 2 == row, 1.0, 0.0).astype(jnp.bfloat16)


def keep_kernel(place_ref, source_ref, out_ref):
    for n in range(out_ref.shape[0]):
        out_ref[n] = source_ref[2 * n + (place_ref[0] & 1)]


def merge_kernel(place_ref, shifts_ref, index_ref, velocity_ref, *refs):
    mine_ref, theirs_ref, reaction_ref, other_reaction_ref = refs[:4]
    out_refs, scalar_ref = refs[4:-1], refs[-1]
    chip, core = place_ref[0] // 2, place_ref[0] & 1
    by = mine_ref.shape[2]
    mine = pl.ds(pl.multiple_of(core * by, 8), by)
    theirs = pl.ds(pl.multiple_of((1 - core) * by, 8), by)
    for m, out_ref in enumerate(out_refs):
        target = jnp.bitwise_xor(chip, m)
        out_ref[0, :, mine, :] = mine_ref[target]
        out_ref[0, :, theirs, :] = theirs_ref[2 * target + core]
        out_ref[1, :, mine, :] = reaction_ref[...]
        out_ref[1, :, theirs, :] = other_reaction_ref[...]
    scalars = [shifts_ref[index_ref[place_ref[0]]]] + [velocity_ref[d] for d in range(3)]
    for n, scalar in enumerate(scalars):
        scalar_ref[pl.ds(n, 1), :] = jnp.full((1, LANES), scalar, jnp.float32)


def half_kernel(chips_y, place_ref, *refs):
    blocks, half_ref = refs[:-1], refs[-1]
    for m, block in enumerate(blocks):
        size = block.shape[2]
        chip = jnp.bitwise_xor(place_ref[0] // 2, m)
        rows = pl.ds(pl.multiple_of(lax.rem(chip, chips_y) * size, 8), size)
        half_ref[:, :, rows, :] = block[...]


def arrange_kernel(chips_y, place_ref, *refs):
    blocks, (slab_ref, near_ref) = refs[:-2], refs[-2:]
    chip = place_ref[0] // 2
    for m, block in enumerate(blocks):
        owner = jnp.bitwise_xor(chip, m)
        _, bx, size, _ = block.shape
        planes = pl.ds((owner // chips_y) * bx, bx)
        rows = pl.ds(pl.multiple_of(lax.rem(owner, chips_y) * size, 8), size)
        slab_ref[:, planes, rows, :] = block[...]
    other = 1 - chip // chips_y
    near_ref[...] = slab_ref[:, pl.ds(other * (SLAB - NEAR), NEAR)]


def smooth_beyond(fine, inside, half_ref, v0):
    f, r, w, ny = fine.f, fine.r, fine.w, fine.ny
    f[...], r[...] = half_ref[0], half_ref[1]

    def put(at, weight):
        w[at] = weight
        v0[at, pl.ds(8, ny), :] = weight * f[at]

    sweep(range(HALO), lambda at: inside / (r[at] + fine.centre), put)
    return [fine.smoothed(v0, 1 + n) for n in range(NEAR)]


def pre_kernel(slabs, chips_y, place_ref, scalar_ref, *refs):
    pool_ref, pool_up_ref, slab_ref, half_ref, near_ref = refs[:5]
    f, r, w, v1, coarse_ref, beyond_ref, v0, tmp, pooled = refs[5:]
    ny = f.shape[1]
    slab = place_ref[1]
    fine = Level(0, ny, LANES, 0, scalars_of(scalar_ref), f, r, w)
    zero_rows(v0, ny)
    zero_rows(v1, ny)
    after = HALO + SLAB

    f[pl.ds(HALO, SLAB)], r[pl.ds(HALO, SLAB)] = slab_ref[0], slab_ref[1]
    x = place_ref[0] // 2 // chips_y
    for above, ref, first in ((1 - x, half_ref, x * NEAR), (x, near_ref, 0)):
        planes = pl.ds((HALO - NEAR) + above * (SLAB + NEAR), NEAR)
        f[planes], r[planes] = ref[0, pl.ds(first, NEAR)], ref[1, pl.ds(first, NEAR)]

    inside = [jnp.where(slab > 0, DAMPING, 0.0)] * HALO
    inside += [DAMPING] * SLAB
    inside += [jnp.where(slab < slabs - 1, DAMPING, 0.0)] * HALO

    def put(x, weight):
        w[x] = weight
        v0[x, pl.ds(8, ny), :] = weight * f[x]

    known = range(HALO - NEAR, after + NEAR)
    sweep(known, lambda x: inside[x] / (r[x] + fine.centre), put)
    fine.smooth(v0, v1, known[1:-1])
    half = ny // 2

    def coarsened(x):
        at = HALO + 2 * x
        return fine.defect(v1, at) + fine.defect(v1, at + 1), r[at] + r[at + 1]

    def put_pooled(x, pair):
        for n in range(2):
            pooled[n, pl.ds(x * half, half), :] = fine.pool_rows(pair[n], tmp.at[2 * x + n])

    sweep(range(SLAB // 2), coarsened, put_pooled)
    packed = split_dot(pooled[0], pool_ref[...]) + split_dot(pooled[1], pool_up_ref[...])
    coarse_ref[...] = packed.reshape(coarse_ref.shape)
    first = HALO + 1 + (1 - x) * (SLAB - HALO)
    beyond_ref[...] = v1[pl.ds(first, NEAR), pl.ds(8, ny), :]


def coarse_kernel(grid, place_ref, scalar_ref, *refs):
    slabs, nx, ny, nz = grid
    pool_ref, spread_ref = refs[:2]
    coarse, out_ref = refs[2 : 2 + slabs], refs[2 + slabs]
    f1, r1, w1, v1a, v1b, pooled, tmp = refs[3 + slabs :]
    pool, spread = pool_ref[...], spread_ref[...]
    slab = place_ref[1]
    rim = HALO // 2
    nx1, ny1, nx2, ny2 = nx // 2, ny // 2, nx // 4, ny // 4
    mid = Level(1, ny1, nz // 2, rim, scalars_of(scalar_ref), f1, r1, w1)
    deep = Level(2, ny2, nz // 4, 0, scalars_of(scalar_ref), None, None, None)
    for v in (v1a, v1b):
        zero_rows(v, ny1)
        blank = jnp.zeros((rim,) + v.shape[1:], jnp.float32)
        v[pl.ds(0, rim)] = blank
        v[pl.ds(rim + nx1, rim)] = blank

    lower = lax.broadcasted_iota(jnp.int32, (1, LANES), 1) < LANES // 2
    own = SLAB // 2
    for k in range(slabs):
        first = jnp.bitwise_xor(slab, k) * own
        both = coarse[k][...]
        f1[pl.ds(first, own)] = jnp.where(lower, both, 0.0)
        r1[pl.ds(first, own)] = jnp.where(lower, pltpu.roll(both, LANES // 2, 2), 0.0)

    def put_start(x, weight):
        w1[x] = weight
        v1a[x + rim, pl.ds(8, ny1), :] = weight * f1[x]

    sweep(range(nx1), lambda x: DAMPING / (r1[x] + mid.centre), put_start)
    mid.smooth(v1a, v1b, range(nx1))

    def coarsened(x):
        return mid.defect(v1b, 2 * x) + mid.defect(v1b, 2 * x + 1), r1[2 * x] + r1[2 * x + 1]

    rows2 = nx2 * ny2

    def put_pooled(x, pair):
        for n in range(2):
            value = mid.pool_rows(pair[n], tmp.at[2 * x + n])
            pooled[pl.ds(n * rows2 + x * ny2, ny2), :] = value

    sweep(range(nx2), coarsened, put_pooled)
    deeper = split_dot(pooled[pl.ds(0, 2 * rows2), :], pool)
    planes = [deeper[n * ny2 : (n + 1) * ny2] for n in range(2 * nx2)]
    values = deep.solve_in_registers(planes[:nx2], planes[nx2:])

    pooled[pl.ds(0, rows2), :] = split_dot(values, spread)

    def refined1(x):
        return mid.spread_rows(pooled[pl.ds(x * ny2, ny2), :], tmp.at[x])

    def put_refined1(x, value):
        for n in range(2):
            v1b[2 * x + n + rim, pl.ds(8, ny1), :] += value

    sweep(range(nx2), refined1, put_refined1)
    mid.smooth(v1b, v1a, range(nx1))
    mid.smooth(v1a, v1b, range(nx1))

    window = own + 2 * rim
    values = v1b[pl.ds(slab * own, window), pl.ds(8, ny1), :].reshape(window * ny1, LANES)
    out_ref[...] = split_dot(values, spread)


def post_kernel(slabs, by, chips_y, place_ref, scalar_ref, *refs):
    f, r, w, v1, correction, half_ref, beyond_ref = refs[:7]
    kept_ref, sent_ref, va, vb, tmp, f_side, r_side, w_side, v_side = refs[7:]
    count, ny = f.shape[:2]
    fine = Level(0, ny, LANES, 0, scalars_of(scalar_ref), f, r, w)
    for v in (va, vb):
        zero_rows(v, ny)
    x, half = place_ref[0] // 2 // chips_y, ny // 2
    window = correction.shape[0] // half
    side = Level(0, ny, LANES, 0, scalars_of(scalar_ref), f_side, r_side, w_side)
    zero_rows(v_side, ny)
    slab = place_ref[1]
    beside = jnp.where(x == 0, slab < slabs - 1, slab > 0)
    planes = smooth_beyond(side, jnp.where(beside, DAMPING, 0.0), half_ref, v_side)
    for n in range(NEAR):
        va[1 + (1 - x) * (SLAB + HALO) + n, pl.ds(8, ny), :] = planes[n]
        va[1 + x * (SLAB + HALO) + n, pl.ds(8, ny), :] = beyond_ref[n]

    def refined(x):
        return fine.spread_rows(correction[pl.ds(x * half, half), :], tmp.at[x])

    def put_refined(x, value):
        for at in (2 * x, 2 * x + 1):
            if 0 < at < count - 1:
                known = HALO - NEAR < at < HALO + SLAB + NEAR - 1
                here = v1 if known else va
                va[at, pl.ds(8, ny), :] = here[at, pl.ds(8, ny), :] + value

    sweep(range(window), refined, put_refined)
    fine.smooth(va, vb, range(2, count - 2))
    fine.smooth(vb, va, range(3, count - 3))

    total = jnp.zeros((8, LANES), jnp.float32)
    for x in range(SLAB):
        rest = fine.defect(va, HALO + x)
        total = total + jnp.sum((rest * rest).reshape(ny // 8, 8, LANES), axis=0)
        tmp[x] = rest
    squares = jnp.full((8, LANES), jnp.sum(total), jnp.float32)

    core, area = place_ref[0] & 1, half * SLAB
    for ref, first in ((kept_ref, core * by), (sent_ref, (1 - core) * by)):
        for y in range(half // by):
            row = pl.multiple_of(2 * y * by + first, 8)
            for x in range(SLAB):
                to = x * half + y * by
                ref[pl.ds(to, by), :] = va[HALO + x, pl.ds(8 + row, by), :]
                ref[pl.ds(area + to, by), :] = tmp[x, pl.ds(row, by), :]
        ref[pl.ds(2 * area, 8), :] = squares


def part_rows(bx, by):
    outer = bx * by
    edges = outer + 2 * by
    squares = edges + 2 * (bx - 2)
    return outer, edges, squares, (squares + 8) // 8 * 8


def merge_back_kernel(bx, by, chips_y, place_ref, kept_ref, got_ref, *out_refs):
    chip, core = place_ref[0] // 2, place_ref[0] & 1
    half = chips_y * by
    outer, edges, squares, size = part_rows(bx, by)
    for m, out_ref in enumerate(out_refs):
        target = jnp.bitwise_xor(chip, m)
        first = (target // chips_y) * bx * half + lax.rem(target, chips_y) * by
        for ref, column in ((kept_ref, core), (got_ref, 1 - core)):
            base = pl.multiple_of(column * size, 8)
            for p in range(bx):
                at = pl.multiple_of(first + p * half, 8)
                out_ref[pl.ds(base + p * by, by), :] = ref[pl.ds(at, by), :]
                at = pl.multiple_of(at + SLAB * half, 8)
                if p in (0, bx - 1):
                    out_ref[pl.ds(base + outer + (p > 0) * by, by), :] = ref[pl.ds(at, by), :]
                else:
                    rows = ref[pl.ds(at, by), :]
                    to = base + edges + 2 * (p - 1)
                    out_ref[pl.ds(to, 1), :] = rows[:1]
                    out_ref[pl.ds(to + 1, 1), :] = rows[by - 1 :]
            out_ref[pl.ds(base + squares, 1), :] = ref[pl.ds(2 * SLAB * half, 1), :]


def collect_kernel(place_ref, shifts_ref, index_ref, velocity_ref, source_ref, reaction_ref, *refs):
    parts, (iterate_ref, residual_ref) = refs[:-2], refs[-2:]
    _, bx, by, nz = iterate_ref.shape
    outer, edges, _, size = part_rows(bx, by)
    fine = Level(0, by, nz, 0, (0.0, [velocity_ref[d] for d in range(3)]), None, None, None)
    reaction = [reaction_ref[p] + fine.centre for p in range(1, bx - 1)]
    for m, part in enumerate(parts):
        target = jnp.bitwise_xor(place_ref[0] // 2, m)
        for n in range(2):
            base, column = n * size, 2 * target + n
            shift = shifts_ref[index_ref[column]]
            planes = [part[pl.ds(base + p * by, by), :] for p in range(bx)]
            for p in range(bx):
                iterate_ref[column, p] = planes[p]
            for p in (0, bx - 1):
                residual_ref[column, p] = part[pl.ds(base + outer + (p > 0) * by, by), :]
            for p in range(1, bx - 1):
                here = planes[p]
                pulled = source_ref[column, p] + fine.along_z(here)
                pulled += fine.backward[0] * planes[p - 1] + fine.forward[0] * planes[p + 1]
                pulled += fine.backward[1] * pltpu.roll(here, 1, 0) + fine.forward[1] * pltpu.roll(here, by - 1, 0)
                residual_ref[column, p] = pulled - (reaction[p - 1] + shift) * here
                at = base + edges + 2 * (p - 1)
                residual_ref[column, p, pl.ds(0, 1), :] = part[pl.ds(at, 1), :]
                residual_ref[column, p, pl.ds(by - 1, 1), :] = part[pl.ds(at + 1, 1), :]


def squares_kernel(bx, by, *refs):
    _, _, squares, size = part_rows(bx, by)
    for m, part in enumerate(refs[:-1]):
        for n in range(2):
            refs[-1][pl.ds(2 * m + n, 1), :] = part[pl.ds(n * size + squares, 1), :]


SMEM = pl.BlockSpec(memory_space=pltpu.SMEM)
VMEM = pl.BlockSpec(memory_space=pltpu.VMEM)


def local_kernel(kernel, name, scalars, arrays, outs, scratch=()):
    return pl.pallas_call(
        kernel,
        out_shape=[jax.ShapeDtypeStruct(shape, jnp.float32) for shape in outs],
        in_specs=[SMEM] * len(scalars) + [VMEM] * len(arrays),
        out_specs=[VMEM] * len(outs),
        scratch_shapes=[pltpu.VMEM(shape, jnp.float32) for shape in scratch],
        compiler_params=pltpu.CompilerParams(vmem_limit_bytes=VMEM_LIMIT),
        name=name,
    )(*scalars, *arrays)


def swap_in_plane(pieces, unit):
    devices = lax.axis_size("gx") * lax.axis_size("gy")
    moved = [pieces[0]]
    for k in range(1, len(pieces)):
        pairs = [(i, i ^ (k * unit)) for i in range(devices)]
        moved.append(lax.ppermute(pieces[k], ("gx", "gy"), pairs))
    return moved


def swap_slabs(piece, step, slabs):
    size = lax.axis_size("gx")
    moved = [piece]
    for k in range(1, slabs):
        pairs = [(i, i ^ (k * step)) for i in range(size)]
        moved.append(lax.ppermute(piece, "gx", pairs))
    return moved


def column_body(source, reaction, shifts, shift_index, velocity):
    columns, bx, by, nz = source.shape
    gx_size, gy_size = lax.axis_size("gx"), lax.axis_size("gy")
    nx, ny = bx * gx_size, by * gy_size
    step = columns // gy_size
    slabs = gx_size // step
    along, across = lax.axis_index("gx"), lax.axis_index("gy")
    column = lax.rem(along, step) * gy_size + across
    place = jnp.stack([column, along // step]).astype(jnp.int32)
    count = SLAB + 2 * HALO
    area = bx * by

    chips, chips_y = columns // 2, gy_size // 2
    cores = [(i, i ^ 1) for i in range(gy_size)]
    theirs = [lax.ppermute(source, "gy", cores), lax.ppermute(reaction, "gy", cores)]
    (mine,) = local_kernel(keep_kernel, "keep", (place,), (source,), [(chips, bx, by, nz)])
    *blocks, scalar_rows = local_kernel(
        merge_kernel,
        "merge",
        (place, shifts, shift_index, velocity),
        (mine, theirs[0], reaction, theirs[1]),
        [(2, bx, 2 * by, nz)] * chips + [(8, LANES)],
    )
    scalars = (place, scalar_rows)
    blocks = swap_in_plane(blocks, 2)

    edge = (2, NEAR, ny, nz)
    (own_half,) = local_kernel(
        functools.partial(half_kernel, chips_y),
        "half",
        (place,),
        blocks[:chips_y],
        [(2, HALO, ny, nz)],
    )
    slab, near = local_kernel(
        functools.partial(arrange_kernel, chips_y),
        "arrange",
        (place,),
        blocks,
        [(2, SLAB, ny, nz), edge],
    )

    def send_beside(piece, up):
        pairs = [(i, i + step if i % step == up else i - step) for i in range(gx_size)]
        return lax.ppermute(piece, "gx", [(i, j) for i, j in pairs if 0 <= j < gx_size])

    beside = [send_beside(own_half, 1), send_beside(near, 0)]
    grid, rimmed = (count, ny, nz), (count, ny + 16, nz)
    f, r, w, v1, coarse, beyond = local_kernel(
        functools.partial(pre_kernel, slabs, chips_y),
        "pre",
        scalars,
        (pool_matrix(0), pool_matrix(LANES // 2), slab, *beside),
        [grid, grid, grid, rimmed, (SLAB // 2, ny // 2, nz), (NEAR, ny, nz)],
        [rimmed, (SLAB, ny, nz), (2, SLAB // 2 * ny // 2, nz)],
    )
    gathered = swap_slabs(coarse, step, slabs)

    coarse_grid = (nx // 2, ny // 2, nz)
    coarse_rimmed = (nx // 2 + HALO, ny // 2 + 16, nz)
    window = (SLAB // 2 + HALO) * ny // 2
    (correction,) = local_kernel(
        functools.partial(coarse_kernel, (slabs, nx, ny, nz)),
        "coarse",
        scalars,
        (pool_matrix(0), spread_matrix(), *gathered),
        [(window, nz)],
        [coarse_grid] * 3 + [coarse_rimmed] * 2 + [(nx // 4 * ny // 2, nz), (nx // 2, ny // 2, nz)],
    )
    result = (SLAB * ny + 8, nz)
    kept, sent = local_kernel(
        functools.partial(post_kernel, slabs, by, chips_y),
        "post",
        scalars,
        (f, r, w, v1, correction, beside[0], send_beside(beyond, 0)),
        [result, result],
        [rimmed] * 2 + [(SLAB, ny, nz)] + [(HALO, ny, nz)] * 3 + [(HALO, ny + 16, nz)],
    )

    parts = local_kernel(
        functools.partial(merge_back_kernel, bx, by, chips_y),
        "merge_back",
        (place,),
        (kept, lax.ppermute(sent, "gy", cores)),
        [(2 * part_rows(bx, by)[3], nz)] * chips,
    )
    parts = swap_in_plane(parts, 2)
    (squares,) = local_kernel(
        functools.partial(squares_kernel, bx, by), "squares", (), parts, [(columns, nz)]
    )
    iterate, residual = local_kernel(
        collect_kernel,
        "collect",
        (place, shifts, shift_index, velocity),
        (source, reaction, *parts),
        [source.shape] * 2,
    )
    total = sum(swap_slabs(squares, step, slabs))
    rms = jnp.sqrt(total[:, 0] / (nx * ny * nz) + EPSILON)
    slots = jnp.arange(columns, dtype=jnp.int32)
    mine = jnp.bitwise_xor(slots, column // 2 * 2)[:, None] == slots[None, :]
    residual_rms = jnp.sum(jnp.where(mine, rms[None, :], 0.0), axis=1)
    return iterate, residual, residual_rms


def power_of_two(n):
    return n > 0 and n & (n - 1) == 0


def column_plan_fits(columns, bx, by, nz, gx_size, gy_size):
    if columns % gy_size or gx_size % (columns // gy_size):
        return False
    step = columns // gy_size
    slabs, ny = gx_size // step, by * gy_size
    whole = power_of_two(columns) and power_of_two(step) and power_of_two(slabs)
    small = slabs * ny * nz <= 2**15
    paired = step == 2 and bx == HALO and gy_size % 2 == 0
    return whole and small and paired and bx * step == SLAB and nz == LANES and by % 16 == 0


def solution(mesh):
    gx_size, gy_size = mesh.shape["gx"], mesh.shape["gy"]

    def body(source, reaction, shifts, shift_index, velocity):
        fits = column_plan_fits(*source.shape, gx_size, gy_size)
        plan = column_body if fits else halo_body
        return plan(source, reaction, shifts, shift_index, velocity)

    return jax.shard_map(
        body,
        mesh=mesh,
        in_specs=(P(None, "gx", "gy", None), P("gx", "gy", None), P(), P(), P()),
        out_specs=(P(None, "gx", "gy", None), P(None, "gx", "gy", None), P()),
        check_vma=False,
    )
```

```python
import functools

import jax
import jax.numpy as jnp
from jax import lax
from jax.experimental import pallas as pl
from jax.experimental.pallas import tpu as pltpu
from jax.sharding import PartitionSpec as P

LEVELS = 3
COARSE_SWEEPS = 6

DAMPING = 0.8
EPSILON = 1e-06
VMEM_LIMIT = 32 * 1024 * 1024
LANES = 128
GROUP = 4
SLAB = 8
HALO = 4
NEAR = 2


def with_halo(x, sides, width):
    for axis, dim in sides:
        peers, length = (lax.axis_size(axis), x.shape[dim])
        up = [(i, (i + 1) % peers) for i in range(peers - 1)]
        down = [(j, i) for i, j in up]
        last = lax.slice_in_dim(x, length - width, length, axis=dim)
        leading = lax.slice_in_dim(x, 0, width, axis=dim)
        before = lax.ppermute(last, axis, up)
        after = lax.ppermute(leading, axis, down)
        x = jnp.concatenate([before, x, after], axis=dim)
    return x


def select_shifts(shifts, shift_index):
    columns = jnp.arange(shifts.shape[0], dtype=jnp.int32)
    picked = jnp.where(shift_index[:, None] == columns[None, :], shifts[None, :], 0.0)
    return jnp.sum(picked, axis=1)


def coefficients(velocity, spacing):
    scale_a = 1.0 / (spacing * spacing)
    backward = scale_a + jnp.maximum(velocity, 0.0) / spacing
    forward = scale_a - jnp.minimum(velocity, 0.0) / spacing
    centre = 6.0 * scale_a + jnp.sum(jnp.abs(velocity)) / spacing
    return (backward, forward, centre)


def apply_stencil(padded, backward, forward, diagonal):
    middle = padded[:, 1:-1, 1:-1, :]
    along_z = jnp.pad(middle, ((0, 0), (0, 0), (0, 0), (1, 1)))
    others = backward[0] * padded[:, :-2, 1:-1, :] + forward[0] * padded[:, 2:, 1:-1, :]
    others = others + backward[1] * padded[:, 1:-1, :-2, :] + forward[1] * padded[:, 1:-1, 2:, :]
    others = others + backward[2] * along_z[:, :, :, :-2] + forward[2] * along_z[:, :, :, 2:]
    return diagonal * middle - others


def face_halo(iterate):
    return with_halo(iterate, (("gx", 1), ("gy", 2)), 1)


def coarsen(values):
    count, size_x, size_y, size_z = values.shape
    blocks = values.reshape(count, size_x // 2, 2, size_y // 2, 2, size_z // 2, 2)
    return jnp.sum(blocks, axis=(2, 4, 6)) * 0.125


def refine(values):
    return jnp.repeat(jnp.repeat(jnp.repeat(values, 2, 1), 2, 2), 2, 3)


def coarsest_solve(rhs_field, backward, forward, diagonal):
    iterate = DAMPING * rhs_field / diagonal
    for repeat in range(COARSE_SWEEPS - 1):
        applied = apply_stencil(face_halo(iterate), backward, forward, diagonal)
        iterate = iterate + DAMPING * (rhs_field - applied) / diagonal
    return iterate


def multigrid_cycle(level_index, rhs_field, reaction_l, shift_value, velocity):
    backward, forward, centre = coefficients(velocity, 2.0**level_index)
    diagonal = centre + reaction_l + shift_value[:, None, None, None]
    if level_index == LEVELS - 1:
        return coarsest_solve(rhs_field, backward, forward, diagonal)

    def operate(iterate):
        return apply_stencil(face_halo(iterate), backward, forward, diagonal)

    def smooth_step(iterate):
        return iterate + DAMPING * (rhs_field - operate(iterate)) / diagonal

    iterate = DAMPING * rhs_field / diagonal
    iterate = smooth_step(iterate)
    defect = rhs_field - operate(iterate)
    correction = multigrid_cycle(
        level_index + 1, coarsen(defect), coarsen(reaction_l), shift_value, velocity
    )
    iterate = iterate + refine(correction)
    iterate = smooth_step(iterate)
    iterate = smooth_step(iterate)
    return iterate


def halo_body(source, reaction, shifts, shift_index, velocity):
    columns, cells_x, cells_y, cells_z = source.shape
    shift_value = select_shifts(shifts, shift_index)
    reaction_top = reaction[None]
    backward, forward, centre = coefficients(velocity, 1.0)
    diagonal = centre + reaction_top + shift_value[:, None, None, None]

    iterate = multigrid_cycle(0, source, reaction_top, shift_value, velocity)
    residual = source - apply_stencil(face_halo(iterate), backward, forward, diagonal)
    local_squares = jnp.sum(residual * residual, axis=(1, 2, 3))
    squares = lax.psum(local_squares, ("gx", "gy"))
    total_cells = cells_x * cells_y * cells_z * lax.axis_size("gx") * lax.axis_size("gy")
    residual_rms = jnp.sqrt(squares / total_cells + EPSILON)
    return (iterate, residual, residual_rms)


def split_dot(values, matrix):
    high = values.astype(jnp.bfloat16)
    low = (values - high.astype(jnp.float32)).astype(jnp.bfloat16)
    return jnp.dot(high, matrix, preferred_element_type=jnp.float32) + jnp.dot(
        low, matrix, preferred_element_type=jnp.float32
    )


def sweep(planes, get, put):
    planes = list(planes)
    for first in range(0, len(planes), GROUP):
        group = planes[first : first + GROUP]
        values = [get(x) for x in group]
        for x, value in zip(group, values):
            put(x, value)


class Grid:
    def __init__(self, ny):
        self.ny = ny

    def pool_rows(self, value, rows):
        half, ny = self.ny // 2, self.ny
        rows[pl.ds(0, ny), :] = value
        return rows[pl.ds(0, half, stride=2), :] + rows[pl.ds(1, half, stride=2), :]

    def spread_rows(self, part, rows):
        half, ny = self.ny // 2, self.ny
        rows[pl.ds(0, half, stride=2), :] = part
        rows[pl.ds(1, half, stride=2), :] = part
        return rows[pl.ds(0, ny), :]


class Level(Grid):
    def __init__(self, index, ny, nz, rim, scalars, f, r, w):
        super().__init__(ny)
        self.nz, self.rim = nz, rim
        self.f, self.r, self.w = f, r, w
        spacing = 2.0**index
        scale_a = 1.0 / (spacing * spacing)
        inverse = 1.0 / spacing
        shift, speed = scalars
        self.backward = [scale_a + jnp.maximum(v, 0.0) * inverse for v in speed]
        self.forward = [scale_a - jnp.minimum(v, 0.0) * inverse for v in speed]
        total = jnp.abs(speed[0]) + jnp.abs(speed[1]) + jnp.abs(speed[2])
        self.centre = 6.0 * scale_a + total * inverse + shift
        lane = lax.broadcasted_iota(jnp.int32, (1, LANES), 1)
        inside = lane < nz
        self.low_z = jnp.where((lane > 0) & inside, self.backward[2], 0.0)
        self.high_z = jnp.where(lane < nz - 1, self.forward[2], 0.0)

    def plane(self, v, x):
        return v[x + self.rim, pl.ds(8, self.ny), :]

    def put(self, v):
        def write(x, value):
            v[x + self.rim, pl.ds(8, self.ny), :] = value

        return write

    def along_z(self, middle):
        return self.low_z * pltpu.roll(middle, 1, 1) + self.high_z * pltpu.roll(middle, LANES - 1, 1)

    def neighbours(self, v, x, middle):
        at, ny = x + self.rim, self.ny
        along_x = self.backward[0] * v[at - 1, pl.ds(8, ny), :] + self.forward[0] * v[at + 1, pl.ds(8, ny), :]
        along_y = self.backward[1] * v[at, pl.ds(7, ny), :] + self.forward[1] * v[at, pl.ds(9, ny), :]
        return along_x + along_y + self.along_z(middle)

    def smoothed(self, v, x):
        middle = self.plane(v, x)
        pulled = self.f[x] + self.neighbours(v, x, middle)
        return (1.0 - DAMPING) * middle + self.w[x] * pulled

    def smooth(self, src, dst, planes):
        sweep(planes, lambda x: self.smoothed(src, x), self.put(dst))

    def defect(self, v, x):
        middle = self.plane(v, x)
        pulled = self.f[x] + self.neighbours(v, x, middle)
        return pulled - (self.r[x] + self.centre) * middle

    def solve_in_registers(self, rhs, reaction):
        row = lax.broadcasted_iota(jnp.int32, (self.ny, 1), 0)
        low_y = jnp.where(row > 0, self.backward[1], 0.0)
        high_y = jnp.where(row < self.ny - 1, self.forward[1], 0.0)
        weight = [DAMPING / (r + self.centre) for r in reaction]
        v = [w * f for w, f in zip(weight, rhs)]
        for _ in range(COARSE_SWEEPS - 1):
            new = []
            for x, here in enumerate(v):
                along_y = low_y * pltpu.roll(here, 1, 0) + high_y * pltpu.roll(here, self.ny - 1, 0)
                pulled = rhs[x] + self.along_z(here) + along_y
                if x > 0:
                    pulled += self.backward[0] * v[x - 1]
                if x < len(v) - 1:
                    pulled += self.forward[0] * v[x + 1]
                new.append((1.0 - DAMPING) * here + weight[x] * pulled)
            v = new
        return jnp.concatenate(v, axis=0)


def scalars_of(scalar_ref):
    return scalar_ref[0, 0], [scalar_ref[1 + d, 0] for d in range(3)]


def zero_rows(v, ny):
    edge = jnp.zeros((v.shape[0], 8, LANES), jnp.float32)
    v[:, pl.ds(0, 8), :] = edge
    v[:, pl.ds(8 + ny, 8), :] = edge


def pool_matrix(offset):
    row = lax.broadcasted_iota(jnp.int32, (LANES, LANES), 0)
    col = lax.broadcasted_iota(jnp.int32, (LANES, LANES), 1)
    return jnp.where(row // 2 + offset == col, 0.125, 0.0).astype(jnp.bfloat16)


def spread_matrix():
    row = lax.broadcasted_iota(jnp.int32, (LANES, LANES), 0)
    col = lax.broadcasted_iota(jnp.int32, (LANES, LANES), 1)
    return jnp.where(col // 2 == row, 1.0, 0.0).astype(jnp.bfloat16)


def keep_kernel(place_ref, source_ref, out_ref):
    for n in range(out_ref.shape[0]):
        out_ref[n] = source_ref[2 * n + (place_ref[0] & 1)]


def merge_kernel(place_ref, shifts_ref, index_ref, velocity_ref, *refs):
    mine_ref, theirs_ref, reaction_ref, other_reaction_ref = refs[:4]
    out_refs, scalar_ref = refs[4:-1], refs[-1]
    chip, core = place_ref[0] // 2, place_ref[0] & 1
    by = mine_ref.shape[2]
    mine = pl.ds(pl.multiple_of(core * by, 8), by)
    theirs = pl.ds(pl.multiple_of((1 - core) * by, 8), by)
    for m, out_ref in enumerate(out_refs):
        target = jnp.bitwise_xor(chip, m)
        out_ref[0, :, mine, :] = mine_ref[target]
        out_ref[0, :, theirs, :] = theirs_ref[2 * target + core]
        out_ref[1, :, mine, :] = reaction_ref[...]
        out_ref[1, :, theirs, :] = other_reaction_ref[...]
    scalars = [shifts_ref[index_ref[place_ref[0]]]] + [velocity_ref[d] for d in range(3)]
    for n, scalar in enumerate(scalars):
        scalar_ref[pl.ds(n, 1), :] = jnp.full((1, LANES), scalar, jnp.float32)


def half_kernel(chips_y, place_ref, *refs):
    blocks, half_ref = refs[:-1], refs[-1]
    for m, block in enumerate(blocks):
        size = block.shape[2]
        chip = jnp.bitwise_xor(place_ref[0] // 2, m)
        rows = pl.ds(pl.multiple_of(lax.rem(chip, chips_y) * size, 8), size)
        half_ref[:, :, rows, :] = block[...]


def arrange_kernel(chips_y, place_ref, *refs):
    blocks, (slab_ref, near_ref) = refs[:-2], refs[-2:]
    chip = place_ref[0] // 2
    for m, block in enumerate(blocks):
        owner = jnp.bitwise_xor(chip, m)
        _, bx, size, _ = block.shape
        planes = pl.ds((owner // chips_y) * bx, bx)
        rows = pl.ds(pl.multiple_of(lax.rem(owner, chips_y) * size, 8), size)
        slab_ref[:, planes, rows, :] = block[...]
    other = 1 - chip // chips_y
    near_ref[...] = slab_ref[:, pl.ds(other * (SLAB - NEAR), NEAR)]


def beyond_kernel(slabs, chips_y, place_ref, scalar_ref, half_ref, out_ref, f, r, w, v0):
    ny, slab = f.shape[1], place_ref[1]
    x = place_ref[0] // 2 // chips_y
    fine = Level(0, ny, LANES, 0, scalars_of(scalar_ref), f, r, w)
    zero_rows(v0, ny)
    f[...], r[...] = half_ref[0], half_ref[1]
    beside = jnp.where(x == 0, slab < slabs - 1, slab > 0)
    inside = jnp.where(beside, DAMPING, 0.0)

    def put(at, weight):
        w[at] = weight
        v0[at, pl.ds(8, ny), :] = weight * f[at]

    sweep(range(HALO), lambda at: inside / (r[at] + fine.centre), put)
    for n in range(NEAR):
        out_ref[n] = fine.smoothed(v0, 1 + n)


def begin_kernel(scalar_ref, slab_ref, f, r, w, v0, v1):
    ny = f.shape[1]
    fine = Level(0, ny, LANES, 0, scalars_of(scalar_ref), f, r, w)
    zero_rows(v0, ny)
    zero_rows(v1, ny)
    own = range(HALO, HALO + SLAB)
    f[pl.ds(HALO, SLAB)], r[pl.ds(HALO, SLAB)] = slab_ref[0], slab_ref[1]

    def put(at, weight):
        w[at] = weight
        v0[at, pl.ds(8, ny), :] = weight * f[at]

    sweep(own, lambda at: DAMPING / (r[at] + fine.centre), put)
    fine.smooth(v0, v1, own[1:-1])


def pre_kernel(slabs, chips_y, place_ref, scalar_ref, *refs):
    half_ref, near_ref, pool_ref, pool_up_ref = refs[5:9]
    f, r, w, v0, v1, coarse_ref, beyond_ref, tmp, pooled = refs[9:]
    ny = f.shape[1]
    slab = place_ref[1]
    fine = Level(0, ny, LANES, 0, scalars_of(scalar_ref), f, r, w)
    after = HALO + SLAB

    x = place_ref[0] // 2 // chips_y
    for above, ref, first in ((1 - x, half_ref, x * NEAR), (x, near_ref, 0)):
        planes = pl.ds((HALO - NEAR) + above * (SLAB + NEAR), NEAR)
        f[planes], r[planes] = ref[0, pl.ds(first, NEAR)], ref[1, pl.ds(first, NEAR)]

    below = jnp.where(slab > 0, DAMPING, 0.0)
    above = jnp.where(slab < slabs - 1, DAMPING, 0.0)

    def put(at, weight):
        w[at] = weight
        v0[at, pl.ds(8, ny), :] = weight * f[at]

    beside = [*range(HALO - NEAR, HALO), *range(after, after + NEAR)]
    sweep(beside, lambda at: (below if at < HALO else above) / (r[at] + fine.centre), put)
    fine.smooth(v0, v1, (HALO - 1, HALO, after - 1, after))
    half = ny // 2

    def coarsened(x):
        at = HALO + 2 * x
        return fine.defect(v1, at) + fine.defect(v1, at + 1), r[at] + r[at + 1]

    def put_pooled(x, pair):
        for n in range(2):
            pooled[n, pl.ds(x * half, half), :] = fine.pool_rows(pair[n], tmp.at[2 * x + n])

    sweep(range(SLAB // 2), coarsened, put_pooled)
    packed = split_dot(pooled[0], pool_ref[...]) + split_dot(pooled[1], pool_up_ref[...])
    coarse_ref[...] = packed.reshape(coarse_ref.shape)
    first = HALO + 1 + (1 - x) * (SLAB - HALO)
    beyond_ref[...] = v1[pl.ds(first, NEAR), pl.ds(8, ny), :]


def coarse_kernel(grid, place_ref, scalar_ref, *refs):
    slabs, nx, ny, nz = grid
    pool_ref, spread_ref = refs[:2]
    coarse, out_ref = refs[2 : 2 + slabs], refs[2 + slabs]
    f1, r1, w1, v1a, v1b, pooled, tmp = refs[3 + slabs :]
    pool, spread = pool_ref[...], spread_ref[...]
    slab = place_ref[1]
    rim = HALO // 2
    nx1, ny1, nx2, ny2 = nx // 2, ny // 2, nx // 4, ny // 4
    mid = Level(1, ny1, nz // 2, rim, scalars_of(scalar_ref), f1, r1, w1)
    deep = Level(2, ny2, nz // 4, 0, scalars_of(scalar_ref), None, None, None)
    for v in (v1a, v1b):
        zero_rows(v, ny1)
        blank = jnp.zeros((rim,) + v.shape[1:], jnp.float32)
        v[pl.ds(0, rim)] = blank
        v[pl.ds(rim + nx1, rim)] = blank

    lower = lax.broadcasted_iota(jnp.int32, (1, LANES), 1) < LANES // 2
    own = SLAB // 2
    for k in range(slabs):
        first = jnp.bitwise_xor(slab, k) * own
        both = coarse[k][...]
        f1[pl.ds(first, own)] = jnp.where(lower, both, 0.0)
        r1[pl.ds(first, own)] = jnp.where(lower, pltpu.roll(both, LANES // 2, 2), 0.0)

    def put_start(x, weight):
        w1[x] = weight
        v1a[x + rim, pl.ds(8, ny1), :] = weight * f1[x]

    sweep(range(nx1), lambda x: DAMPING / (r1[x] + mid.centre), put_start)
    mid.smooth(v1a, v1b, range(nx1))

    def coarsened(x):
        return mid.defect(v1b, 2 * x) + mid.defect(v1b, 2 * x + 1), r1[2 * x] + r1[2 * x + 1]

    rows2 = nx2 * ny2

    def put_pooled(x, pair):
        for n in range(2):
            value = mid.pool_rows(pair[n], tmp.at[2 * x + n])
            pooled[pl.ds(n * rows2 + x * ny2, ny2), :] = value

    sweep(range(nx2), coarsened, put_pooled)
    deeper = split_dot(pooled[pl.ds(0, 2 * rows2), :], pool)
    planes = [deeper[n * ny2 : (n + 1) * ny2] for n in range(2 * nx2)]
    values = deep.solve_in_registers(planes[:nx2], planes[nx2:])

    pooled[pl.ds(0, rows2), :] = split_dot(values, spread)

    def refined1(x):
        return mid.spread_rows(pooled[pl.ds(x * ny2, ny2), :], tmp.at[x])

    def put_refined1(x, value):
        for n in range(2):
            v1b[2 * x + n + rim, pl.ds(8, ny1), :] += value

    sweep(range(nx2), refined1, put_refined1)
    mid.smooth(v1b, v1a, range(nx1))
    mid.smooth(v1a, v1b, range(nx1))

    window = own + 2 * rim
    values = v1b[pl.ds(slab * own, window), pl.ds(8, ny1), :].reshape(window * ny1, LANES)
    out_ref[...] = split_dot(values, spread)


def post_kernel(by, chips_y, place_ref, scalar_ref, *refs):
    f, r, w, v1, correction, first_ref, second_ref, kept_ref, sent_ref, va, vb, tmp = refs
    count, ny = f.shape[:2]
    fine = Level(0, ny, LANES, 0, scalars_of(scalar_ref), f, r, w)
    for v in (va, vb):
        zero_rows(v, ny)
    x, half = place_ref[0] // 2 // chips_y, ny // 2
    window = correction.shape[0] // half
    for ref, above in ((first_ref, 1 - x), (second_ref, x)):
        va[pl.ds(1 + above * (SLAB + HALO), NEAR), pl.ds(8, ny), :] = ref[...]

    def refined(x):
        return fine.spread_rows(correction[pl.ds(x * half, half), :], tmp.at[x])

    def put_refined(x, value):
        for at in (2 * x, 2 * x + 1):
            if 0 < at < count - 1:
                known = HALO - NEAR < at < HALO + SLAB + NEAR - 1
                here = v1 if known else va
                va[at, pl.ds(8, ny), :] = here[at, pl.ds(8, ny), :] + value

    sweep(range(window), refined, put_refined)
    fine.smooth(va, vb, range(2, count - 2))
    fine.smooth(vb, va, range(3, count - 3))

    total = jnp.zeros((8, LANES), jnp.float32)
    for x in range(SLAB):
        rest = fine.defect(va, HALO + x)
        total = total + jnp.sum((rest * rest).reshape(ny // 8, 8, LANES), axis=0)
        tmp[x] = rest
    squares = jnp.full((8, LANES), jnp.sum(total), jnp.float32)

    core, area = place_ref[0] & 1, half * SLAB
    for ref, first in ((kept_ref, core * by), (sent_ref, (1 - core) * by)):
        for y in range(half // by):
            row = pl.multiple_of(2 * y * by + first, 8)
            for x in range(SLAB):
                to = x * half + y * by
                ref[pl.ds(to, by), :] = va[HALO + x, pl.ds(8 + row, by), :]
                ref[pl.ds(area + to, by), :] = tmp[x, pl.ds(row, by), :]
        ref[pl.ds(2 * area, 8), :] = squares


def part_rows(bx, by):
    outer = bx * by
    edges = outer + 2 * by
    squares = edges + 2 * (bx - 2)
    return outer, edges, squares, (squares + 8) // 8 * 8


def merge_back_kernel(bx, by, chips_y, place_ref, kept_ref, got_ref, *out_refs):
    chip, core = place_ref[0] // 2, place_ref[0] & 1
    half = chips_y * by
    outer, edges, squares, size = part_rows(bx, by)
    for m, out_ref in enumerate(out_refs):
        target = jnp.bitwise_xor(chip, m)
        first = (target // chips_y) * bx * half + lax.rem(target, chips_y) * by
        for ref, column in ((kept_ref, core), (got_ref, 1 - core)):
            base = pl.multiple_of(column * size, 8)
            for p in range(bx):
                at = pl.multiple_of(first + p * half, 8)
                out_ref[pl.ds(base + p * by, by), :] = ref[pl.ds(at, by), :]
                at = pl.multiple_of(at + SLAB * half, 8)
                if p in (0, bx - 1):
                    out_ref[pl.ds(base + outer + (p > 0) * by, by), :] = ref[pl.ds(at, by), :]
                else:
                    rows = ref[pl.ds(at, by), :]
                    to = base + edges + 2 * (p - 1)
                    out_ref[pl.ds(to, 1), :] = rows[:1]
                    out_ref[pl.ds(to + 1, 1), :] = rows[by - 1 :]
            out_ref[pl.ds(base + squares, 1), :] = ref[pl.ds(2 * SLAB * half, 1), :]


def collect_kernel(place_ref, shifts_ref, index_ref, velocity_ref, source_ref, reaction_ref, *refs):
    parts, (iterate_ref, residual_ref) = refs[:-2], refs[-2:]
    _, bx, by, nz = iterate_ref.shape
    outer, edges, _, size = part_rows(bx, by)
    fine = Level(0, by, nz, 0, (0.0, [velocity_ref[d] for d in range(3)]), None, None, None)
    reaction = [reaction_ref[p] + fine.centre for p in range(1, bx - 1)]
    for m, part in enumerate(parts):
        target = jnp.bitwise_xor(place_ref[0] // 2, m)
        for n in range(2):
            base, column = n * size, 2 * target + n
            shift = shifts_ref[index_ref[column]]
            planes = [part[pl.ds(base + p * by, by), :] for p in range(bx)]
            for p in range(bx):
                iterate_ref[column, p] = planes[p]
            for p in (0, bx - 1):
                residual_ref[column, p] = part[pl.ds(base + outer + (p > 0) * by, by), :]
            for p in range(1, bx - 1):
                here = planes[p]
                pulled = source_ref[column, p] + fine.along_z(here)
                pulled += fine.backward[0] * planes[p - 1] + fine.forward[0] * planes[p + 1]
                pulled += fine.backward[1] * pltpu.roll(here, 1, 0) + fine.forward[1] * pltpu.roll(here, by - 1, 0)
                residual_ref[column, p] = pulled - (reaction[p - 1] + shift) * here
                at = base + edges + 2 * (p - 1)
                residual_ref[column, p, pl.ds(0, 1), :] = part[pl.ds(at, 1), :]
                residual_ref[column, p, pl.ds(by - 1, 1), :] = part[pl.ds(at + 1, 1), :]


def squares_kernel(bx, by, *refs):
    _, _, squares, size = part_rows(bx, by)
    for m, part in enumerate(refs[:-1]):
        for n in range(2):
            refs[-1][pl.ds(2 * m + n, 1), :] = part[pl.ds(n * size + squares, 1), :]


SMEM = pl.BlockSpec(memory_space=pltpu.SMEM)
VMEM = pl.BlockSpec(memory_space=pltpu.VMEM)


def local_kernel(kernel, name, scalars, arrays, outs, scratch=(), in_place=0):
    return pl.pallas_call(
        kernel,
        out_shape=[jax.ShapeDtypeStruct(shape, jnp.float32) for shape in outs],
        in_specs=[SMEM] * len(scalars) + [VMEM] * len(arrays),
        out_specs=[VMEM] * len(outs),
        scratch_shapes=[pltpu.VMEM(shape, jnp.float32) for shape in scratch],
        input_output_aliases={len(scalars) + n: n for n in range(in_place)},
        compiler_params=pltpu.CompilerParams(vmem_limit_bytes=VMEM_LIMIT),
        name=name,
    )(*scalars, *arrays)


def swap_in_plane(pieces, unit):
    devices = lax.axis_size("gx") * lax.axis_size("gy")
    moved = [pieces[0]]
    for k in range(1, len(pieces)):
        pairs = [(i, i ^ (k * unit)) for i in range(devices)]
        moved.append(lax.ppermute(pieces[k], ("gx", "gy"), pairs))
    return moved


def swap_slabs(piece, step, slabs):
    size = lax.axis_size("gx")
    moved = [piece]
    for k in range(1, slabs):
        pairs = [(i, i ^ (k * step)) for i in range(size)]
        moved.append(lax.ppermute(piece, "gx", pairs))
    return moved


def column_body(source, reaction, shifts, shift_index, velocity):
    columns, bx, by, nz = source.shape
    gx_size, gy_size = lax.axis_size("gx"), lax.axis_size("gy")
    nx, ny = bx * gx_size, by * gy_size
    step = columns // gy_size
    slabs = gx_size // step
    along, across = lax.axis_index("gx"), lax.axis_index("gy")
    column = lax.rem(along, step) * gy_size + across
    place = jnp.stack([column, along // step]).astype(jnp.int32)
    count = SLAB + 2 * HALO
    area = bx * by

    chips, chips_y = columns // 2, gy_size // 2
    cores = [(i, i ^ 1) for i in range(gy_size)]
    theirs = [lax.ppermute(source, "gy", cores), lax.ppermute(reaction, "gy", cores)]
    (mine,) = local_kernel(keep_kernel, "keep", (place,), (source,), [(chips, bx, by, nz)])
    *blocks, scalar_rows = local_kernel(
        merge_kernel,
        "merge",
        (place, shifts, shift_index, velocity),
        (mine, theirs[0], reaction, theirs[1]),
        [(2, bx, 2 * by, nz)] * chips + [(8, LANES)],
    )
    scalars = (place, scalar_rows)
    blocks = swap_in_plane(blocks, 2)

    edge = (2, NEAR, ny, nz)
    (own_half,) = local_kernel(
        functools.partial(half_kernel, chips_y),
        "half",
        (place,),
        blocks[:chips_y],
        [(2, HALO, ny, nz)],
    )
    slab, near = local_kernel(
        functools.partial(arrange_kernel, chips_y),
        "arrange",
        (place,),
        blocks,
        [(2, SLAB, ny, nz), edge],
    )

    def send_beside(piece, up):
        pairs = [(i, i + step if i % step == up else i - step) for i in range(gx_size)]
        return lax.ppermute(piece, "gx", [(i, j) for i, j in pairs if 0 <= j < gx_size])

    beside = [send_beside(own_half, 1), send_beside(near, 0)]
    grid, rimmed = (count, ny, nz), (count, ny + 16, nz)
    fields = [grid, grid, grid, rimmed, rimmed]
    fields_own = local_kernel(begin_kernel, "begin", (scalar_rows,), (slab,), fields)
    f, r, w, _, v1, coarse, beyond = local_kernel(
        functools.partial(pre_kernel, slabs, chips_y),
        "pre",
        scalars,
        (*fields_own, *beside, pool_matrix(0), pool_matrix(LANES // 2)),
        fields + [(SLAB // 2, ny // 2, nz), (NEAR, ny, nz)],
        [(SLAB, ny, nz), (2, SLAB // 2 * ny // 2, nz)],
        in_place=len(fields),
    )
    (own_beyond,) = local_kernel(
        functools.partial(beyond_kernel, slabs, chips_y),
        "beyond",
        scalars,
        beside[:1],
        [(NEAR, ny, nz)],
        [(HALO, ny, nz)] * 3 + [(HALO, ny + 16, nz)],
    )
    gathered = swap_slabs(coarse, step, slabs)

    coarse_grid = (nx // 2, ny // 2, nz)
    coarse_rimmed = (nx // 2 + HALO, ny // 2 + 16, nz)
    window = (SLAB // 2 + HALO) * ny // 2
    (correction,) = local_kernel(
        functools.partial(coarse_kernel, (slabs, nx, ny, nz)),
        "coarse",
        scalars,
        (pool_matrix(0), spread_matrix(), *gathered),
        [(window, nz)],
        [coarse_grid] * 3 + [coarse_rimmed] * 2 + [(nx // 4 * ny // 2, nz), (nx // 2, ny // 2, nz)],
    )
    result = (SLAB * ny + 8, nz)
    kept, sent = local_kernel(
        functools.partial(post_kernel, by, chips_y),
        "post",
        scalars,
        (f, r, w, v1, correction, own_beyond, send_beside(beyond, 0)),
        [result, result],
        [rimmed] * 2 + [(SLAB, ny, nz)],
    )

    parts = local_kernel(
        functools.partial(merge_back_kernel, bx, by, chips_y),
        "merge_back",
        (place,),
        (kept, lax.ppermute(sent, "gy", cores)),
        [(2 * part_rows(bx, by)[3], nz)] * chips,
    )
    parts = swap_in_plane(parts, 2)
    (squares,) = local_kernel(
        functools.partial(squares_kernel, bx, by), "squares", (), parts, [(columns, nz)]
    )
    iterate, residual = local_kernel(
        collect_kernel,
        "collect",
        (place, shifts, shift_index, velocity),
        (source, reaction, *parts),
        [source.shape] * 2,
    )
    total = sum(swap_slabs(squares, step, slabs))
    rms = jnp.sqrt(total[:, 0] / (nx * ny * nz) + EPSILON)
    slots = jnp.arange(columns, dtype=jnp.int32)
    mine = jnp.bitwise_xor(slots, column // 2 * 2)[:, None] == slots[None, :]
    residual_rms = jnp.sum(jnp.where(mine, rms[None, :], 0.0), axis=1)
    return iterate, residual, residual_rms


def power_of_two(n):
    return n > 0 and n & (n - 1) == 0


def column_plan_fits(columns, bx, by, nz, gx_size, gy_size):
    if columns % gy_size or gx_size % (columns // gy_size):
        return False
    step = columns // gy_size
    slabs, ny = gx_size // step, by * gy_size
    whole = power_of_two(columns) and power_of_two(step) and power_of_two(slabs)
    small = slabs * ny * nz <= 2**15
    paired = step == 2 and bx == HALO and gy_size % 2 == 0
    return whole and small and paired and bx * step == SLAB and nz == LANES and by % 16 == 0


def solution(mesh):
    gx_size, gy_size = mesh.shape["gx"], mesh.shape["gy"]

    def body(source, reaction, shifts, shift_index, velocity):
        fits = column_plan_fits(*source.shape, gx_size, gy_size)
        plan = column_body if fits else halo_body
        return plan(source, reaction, shifts, shift_index, velocity)

    return jax.shard_map(
        body,
        mesh=mesh,
        in_specs=(P(None, "gx", "gy", None), P("gx", "gy", None), P(), P(), P()),
        out_specs=(P(None, "gx", "gy", None), P(None, "gx", "gy", None), P()),
        check_vma=False,
    )
```

```python
import functools

import jax
import jax.numpy as jnp
from jax import lax
from jax.experimental import pallas as pl
from jax.experimental.pallas import tpu as pltpu
from jax.sharding import PartitionSpec as P

LEVELS = 3
COARSE_SWEEPS = 6

DAMPING = 0.8
EPSILON = 1e-06
VMEM_LIMIT = 32 * 1024 * 1024
LANES = 128
GROUP = 4
SLAB = 8
HALO = 4
NEAR = 2


def with_halo(x, sides, width):
    for axis, dim in sides:
        peers, length = (lax.axis_size(axis), x.shape[dim])
        up = [(i, (i + 1) % peers) for i in range(peers - 1)]
        down = [(j, i) for i, j in up]
        last = lax.slice_in_dim(x, length - width, length, axis=dim)
        leading = lax.slice_in_dim(x, 0, width, axis=dim)
        before = lax.ppermute(last, axis, up)
        after = lax.ppermute(leading, axis, down)
        x = jnp.concatenate([before, x, after], axis=dim)
    return x


def select_shifts(shifts, shift_index):
    columns = jnp.arange(shifts.shape[0], dtype=jnp.int32)
    picked = jnp.where(shift_index[:, None] == columns[None, :], shifts[None, :], 0.0)
    return jnp.sum(picked, axis=1)


def coefficients(velocity, spacing):
    scale_a = 1.0 / (spacing * spacing)
    backward = scale_a + jnp.maximum(velocity, 0.0) / spacing
    forward = scale_a - jnp.minimum(velocity, 0.0) / spacing
    centre = 6.0 * scale_a + jnp.sum(jnp.abs(velocity)) / spacing
    return (backward, forward, centre)


def apply_stencil(padded, backward, forward, diagonal):
    middle = padded[:, 1:-1, 1:-1, :]
    along_z = jnp.pad(middle, ((0, 0), (0, 0), (0, 0), (1, 1)))
    others = backward[0] * padded[:, :-2, 1:-1, :] + forward[0] * padded[:, 2:, 1:-1, :]
    others = others + backward[1] * padded[:, 1:-1, :-2, :] + forward[1] * padded[:, 1:-1, 2:, :]
    others = others + backward[2] * along_z[:, :, :, :-2] + forward[2] * along_z[:, :, :, 2:]
    return diagonal * middle - others


def face_halo(iterate):
    return with_halo(iterate, (("gx", 1), ("gy", 2)), 1)


def coarsen(values):
    count, size_x, size_y, size_z = values.shape
    blocks = values.reshape(count, size_x // 2, 2, size_y // 2, 2, size_z // 2, 2)
    return jnp.sum(blocks, axis=(2, 4, 6)) * 0.125


def refine(values):
    return jnp.repeat(jnp.repeat(jnp.repeat(values, 2, 1), 2, 2), 2, 3)


def coarsest_solve(rhs_field, backward, forward, diagonal):
    iterate = DAMPING * rhs_field / diagonal
    for repeat in range(COARSE_SWEEPS - 1):
        applied = apply_stencil(face_halo(iterate), backward, forward, diagonal)
        iterate = iterate + DAMPING * (rhs_field - applied) / diagonal
    return iterate


def multigrid_cycle(level_index, rhs_field, reaction_l, shift_value, velocity):
    backward, forward, centre = coefficients(velocity, 2.0**level_index)
    diagonal = centre + reaction_l + shift_value[:, None, None, None]
    if level_index == LEVELS - 1:
        return coarsest_solve(rhs_field, backward, forward, diagonal)

    def operate(iterate):
        return apply_stencil(face_halo(iterate), backward, forward, diagonal)

    def smooth_step(iterate):
        return iterate + DAMPING * (rhs_field - operate(iterate)) / diagonal

    iterate = DAMPING * rhs_field / diagonal
    iterate = smooth_step(iterate)
    defect = rhs_field - operate(iterate)
    correction = multigrid_cycle(
        level_index + 1, coarsen(defect), coarsen(reaction_l), shift_value, velocity
    )
    iterate = iterate + refine(correction)
    iterate = smooth_step(iterate)
    iterate = smooth_step(iterate)
    return iterate


def halo_body(source, reaction, shifts, shift_index, velocity):
    columns, cells_x, cells_y, cells_z = source.shape
    shift_value = select_shifts(shifts, shift_index)
    reaction_top = reaction[None]
    backward, forward, centre = coefficients(velocity, 1.0)
    diagonal = centre + reaction_top + shift_value[:, None, None, None]

    iterate = multigrid_cycle(0, source, reaction_top, shift_value, velocity)
    residual = source - apply_stencil(face_halo(iterate), backward, forward, diagonal)
    local_squares = jnp.sum(residual * residual, axis=(1, 2, 3))
    squares = lax.psum(local_squares, ("gx", "gy"))
    total_cells = cells_x * cells_y * cells_z * lax.axis_size("gx") * lax.axis_size("gy")
    residual_rms = jnp.sqrt(squares / total_cells + EPSILON)
    return (iterate, residual, residual_rms)


def split_dot(values, matrix):
    high = values.astype(jnp.bfloat16)
    low = (values - high.astype(jnp.float32)).astype(jnp.bfloat16)
    return jnp.dot(high, matrix, preferred_element_type=jnp.float32) + jnp.dot(
        low, matrix, preferred_element_type=jnp.float32
    )


def sweep(planes, get, put):
    planes = list(planes)
    for first in range(0, len(planes), GROUP):
        group = planes[first : first + GROUP]
        values = [get(x) for x in group]
        for x, value in zip(group, values):
            put(x, value)


class Grid:
    def __init__(self, ny):
        self.ny = ny

    def pool_rows(self, value, rows):
        half, ny = self.ny // 2, self.ny
        rows[pl.ds(0, ny), :] = value
        return rows[pl.ds(0, half, stride=2), :] + rows[pl.ds(1, half, stride=2), :]

    def spread_rows(self, part, rows):
        half, ny = self.ny // 2, self.ny
        rows[pl.ds(0, half, stride=2), :] = part
        rows[pl.ds(1, half, stride=2), :] = part
        return rows[pl.ds(0, ny), :]


class Level(Grid):
    def __init__(self, index, ny, nz, rim, scalars, f, r, w):
        super().__init__(ny)
        self.nz, self.rim = nz, rim
        self.f, self.r, self.w = f, r, w
        spacing = 2.0**index
        scale_a = 1.0 / (spacing * spacing)
        inverse = 1.0 / spacing
        shift, speed = scalars
        self.backward = [scale_a + jnp.maximum(v, 0.0) * inverse for v in speed]
        self.forward = [scale_a - jnp.minimum(v, 0.0) * inverse for v in speed]
        total = jnp.abs(speed[0]) + jnp.abs(speed[1]) + jnp.abs(speed[2])
        self.centre = 6.0 * scale_a + total * inverse + shift
        lane = lax.broadcasted_iota(jnp.int32, (1, LANES), 1)
        inside = lane < nz
        self.low_z = jnp.where((lane > 0) & inside, self.backward[2], 0.0)
        self.high_z = jnp.where(lane < nz - 1, self.forward[2], 0.0)

    def plane(self, v, x):
        return v[x + self.rim, pl.ds(8, self.ny), :]

    def put(self, v):
        def write(x, value):
            v[x + self.rim, pl.ds(8, self.ny), :] = value

        return write

    def along_z(self, middle):
        return self.low_z * pltpu.roll(middle, 1, 1) + self.high_z * pltpu.roll(middle, LANES - 1, 1)

    def neighbours(self, v, x, middle):
        at, ny = x + self.rim, self.ny
        along_x = self.backward[0] * v[at - 1, pl.ds(8, ny), :] + self.forward[0] * v[at + 1, pl.ds(8, ny), :]
        along_y = self.backward[1] * v[at, pl.ds(7, ny), :] + self.forward[1] * v[at, pl.ds(9, ny), :]
        return along_x + along_y + self.along_z(middle)

    def smoothed(self, v, x):
        middle = self.plane(v, x)
        pulled = self.f[x] + self.neighbours(v, x, middle)
        return (1.0 - DAMPING) * middle + self.w[x] * pulled

    def smooth(self, src, dst, planes):
        sweep(planes, lambda x: self.smoothed(src, x), self.put(dst))

    def defect(self, v, x):
        middle = self.plane(v, x)
        pulled = self.f[x] + self.neighbours(v, x, middle)
        return pulled - (self.r[x] + self.centre) * middle

    def solve_in_registers(self, rhs, reaction):
        row = lax.broadcasted_iota(jnp.int32, (self.ny, 1), 0)
        low_y = jnp.where(row > 0, self.backward[1], 0.0)
        high_y = jnp.where(row < self.ny - 1, self.forward[1], 0.0)
        weight = [DAMPING / (r + self.centre) for r in reaction]
        v = [w * f for w, f in zip(weight, rhs)]
        for _ in range(COARSE_SWEEPS - 1):
            new = []
            for x, here in enumerate(v):
                along_y = low_y * pltpu.roll(here, 1, 0) + high_y * pltpu.roll(here, self.ny - 1, 0)
                pulled = rhs[x] + self.along_z(here) + along_y
                if x > 0:
                    pulled += self.backward[0] * v[x - 1]
                if x < len(v) - 1:
                    pulled += self.forward[0] * v[x + 1]
                new.append((1.0 - DAMPING) * here + weight[x] * pulled)
            v = new
        return jnp.concatenate(v, axis=0)


def scalars_of(scalar_ref):
    return scalar_ref[0, 0], [scalar_ref[1 + d, 0] for d in range(3)]


def zero_rows(v, ny):
    edge = jnp.zeros((v.shape[0], 8, LANES), jnp.float32)
    v[:, pl.ds(0, 8), :] = edge
    v[:, pl.ds(8 + ny, 8), :] = edge


def pool_matrix(offset):
    row = lax.broadcasted_iota(jnp.int32, (LANES, LANES), 0)
    col = lax.broadcasted_iota(jnp.int32, (LANES, LANES), 1)
    return jnp.where(row // 2 + offset == col, 0.125, 0.0).astype(jnp.bfloat16)


def spread_matrix():
    row = lax.broadcasted_iota(jnp.int32, (LANES, LANES), 0)
    col = lax.broadcasted_iota(jnp.int32, (LANES, LANES), 1)
    return jnp.where(col // 2 == row, 1.0, 0.0).astype(jnp.bfloat16)


def step_of(k, count):
    return -k % count


def keep_kernel(place_ref, source_ref, out_ref):
    for n in range(out_ref.shape[0]):
        out_ref[n] = source_ref[2 * n + (place_ref[0] & 1)]


def merge_kernel(place_ref, shifts_ref, index_ref, velocity_ref, *refs):
    mine_ref, theirs_ref, reaction_ref, other_reaction_ref = refs[:4]
    out_refs, scalar_ref = refs[4:-1], refs[-1]
    chip, core = place_ref[0] // 2, place_ref[0] & 1
    by = mine_ref.shape[2]
    mine = pl.ds(pl.multiple_of(core * by, 8), by)
    theirs = pl.ds(pl.multiple_of((1 - core) * by, 8), by)
    for m, out_ref in enumerate(out_refs):
        target = jnp.bitwise_xor(chip, m)
        out_ref[0, :, mine, :] = mine_ref[target]
        out_ref[0, :, theirs, :] = theirs_ref[2 * target + core]
        out_ref[1, :, mine, :] = reaction_ref[...]
        out_ref[1, :, theirs, :] = other_reaction_ref[...]
    scalars = [shifts_ref[index_ref[place_ref[0]]]] + [velocity_ref[d] for d in range(3)]
    for n, scalar in enumerate(scalars):
        scalar_ref[pl.ds(n, 1), :] = jnp.full((1, LANES), scalar, jnp.float32)


def half_kernel(chips_y, place_ref, *refs):
    blocks, half_ref = refs[:-1], refs[-1]
    for m, block in enumerate(blocks):
        size = block.shape[2]
        chip = jnp.bitwise_xor(place_ref[0] // 2, m)
        rows = pl.ds(pl.multiple_of(lax.rem(chip, chips_y) * size, 8), size)
        half_ref[:, :, rows, :] = block[...]


def arrange_kernel(chips_y, place_ref, *refs):
    blocks, (slab_ref, near_ref) = refs[:-2], refs[-2:]
    chip = place_ref[0] // 2
    for m, block in enumerate(blocks):
        owner = jnp.bitwise_xor(chip, m)
        _, bx, size, _ = block.shape
        planes = pl.ds((owner // chips_y) * bx, bx)
        rows = pl.ds(pl.multiple_of(lax.rem(owner, chips_y) * size, 8), size)
        slab_ref[:, planes, rows, :] = block[...]
    other = 1 - chip // chips_y
    near_ref[...] = slab_ref[:, pl.ds(other * (SLAB - NEAR), NEAR)]


def beyond_kernel(slabs, chips_y, place_ref, scalar_ref, half_ref, out_ref, f, r, w, v0):
    ny, slab = f.shape[1], place_ref[1]
    x = place_ref[0] // 2 // chips_y
    fine = Level(0, ny, LANES, 0, scalars_of(scalar_ref), f, r, w)
    zero_rows(v0, ny)
    f[...], r[...] = half_ref[0], half_ref[1]
    beside = jnp.where(x == 0, slab < slabs - 1, slab > 0)
    inside = jnp.where(beside, DAMPING, 0.0)

    def put(at, weight):
        w[at] = weight
        v0[at, pl.ds(8, ny), :] = weight * f[at]

    sweep(range(HALO), lambda at: inside / (r[at] + fine.centre), put)
    for n in range(NEAR):
        out_ref[n] = fine.smoothed(v0, 1 + n)


def begin_kernel(scalar_ref, slab_ref, f, r, w, v0, v1):
    ny = f.shape[1]
    fine = Level(0, ny, LANES, 0, scalars_of(scalar_ref), f, r, w)
    zero_rows(v0, ny)
    zero_rows(v1, ny)
    own = range(HALO, HALO + SLAB)
    f[pl.ds(HALO, SLAB)], r[pl.ds(HALO, SLAB)] = slab_ref[0], slab_ref[1]

    def put(at, weight):
        w[at] = weight
        v0[at, pl.ds(8, ny), :] = weight * f[at]

    sweep(own, lambda at: DAMPING / (r[at] + fine.centre), put)
    fine.smooth(v0, v1, own[1:-1])


def pre_kernel(slabs, chips_y, place_ref, scalar_ref, *refs):
    half_ref, near_ref, pool_ref, pool_up_ref = refs[5:9]
    f, r, w, v0, v1, coarse_ref, beyond_ref, tmp, pooled = refs[9:]
    ny = f.shape[1]
    slab = place_ref[1]
    fine = Level(0, ny, LANES, 0, scalars_of(scalar_ref), f, r, w)
    after = HALO + SLAB

    x = place_ref[0] // 2 // chips_y
    for above, ref, first in ((1 - x, half_ref, x * NEAR), (x, near_ref, 0)):
        planes = pl.ds((HALO - NEAR) + above * (SLAB + NEAR), NEAR)
        f[planes], r[planes] = ref[0, pl.ds(first, NEAR)], ref[1, pl.ds(first, NEAR)]

    below = jnp.where(slab > 0, DAMPING, 0.0)
    above = jnp.where(slab < slabs - 1, DAMPING, 0.0)

    def put(at, weight):
        w[at] = weight
        v0[at, pl.ds(8, ny), :] = weight * f[at]

    beside = [*range(HALO - NEAR, HALO), *range(after, after + NEAR)]
    sweep(beside, lambda at: (below if at < HALO else above) / (r[at] + fine.centre), put)
    fine.smooth(v0, v1, (HALO - 1, HALO, after - 1, after))
    half = ny // 2

    def coarsened(x):
        at = HALO + 2 * x
        return fine.defect(v1, at) + fine.defect(v1, at + 1), r[at] + r[at + 1]

    def put_pooled(x, pair):
        for n in range(2):
            pooled[n, pl.ds(x * half, half), :] = fine.pool_rows(pair[n], tmp.at[2 * x + n])

    sweep(range(SLAB // 2), coarsened, put_pooled)
    packed = split_dot(pooled[0], pool_ref[...]) + split_dot(pooled[1], pool_up_ref[...])
    coarse_ref[...] = packed.reshape(coarse_ref.shape)
    first = HALO + 1 + (1 - x) * (SLAB - HALO)
    beyond_ref[...] = v1[pl.ds(first, NEAR), pl.ds(8, ny), :]


def coarse_kernel(grid, place_ref, scalar_ref, *refs):
    slabs, nx, ny, nz = grid
    pool_ref, spread_ref = refs[:2]
    coarse, out_ref = refs[2 : 2 + slabs], refs[2 + slabs]
    f1, r1, w1, v1a, v1b, pooled, tmp = refs[3 + slabs :]
    pool, spread = pool_ref[...], spread_ref[...]
    slab = place_ref[1]
    rim = HALO // 2
    nx1, ny1, nx2, ny2 = nx // 2, ny // 2, nx // 4, ny // 4
    mid = Level(1, ny1, nz // 2, rim, scalars_of(scalar_ref), f1, r1, w1)
    deep = Level(2, ny2, nz // 4, 0, scalars_of(scalar_ref), None, None, None)
    for v in (v1a, v1b):
        zero_rows(v, ny1)
        blank = jnp.zeros((rim,) + v.shape[1:], jnp.float32)
        v[pl.ds(0, rim)] = blank
        v[pl.ds(rim + nx1, rim)] = blank

    lower = lax.broadcasted_iota(jnp.int32, (1, LANES), 1) < LANES // 2
    own = SLAB // 2
    for k in range(slabs):
        first = jnp.bitwise_xor(slab, step_of(k, slabs)) * own
        both = coarse[k][...]
        f1[pl.ds(first, own)] = jnp.where(lower, both, 0.0)
        r1[pl.ds(first, own)] = jnp.where(lower, pltpu.roll(both, LANES // 2, 2), 0.0)

    def put_start(x, weight):
        w1[x] = weight
        v1a[x + rim, pl.ds(8, ny1), :] = weight * f1[x]

    sweep(range(nx1), lambda x: DAMPING / (r1[x] + mid.centre), put_start)
    mid.smooth(v1a, v1b, range(nx1))

    def coarsened(x):
        return mid.defect(v1b, 2 * x) + mid.defect(v1b, 2 * x + 1), r1[2 * x] + r1[2 * x + 1]

    rows2 = nx2 * ny2

    def put_pooled(x, pair):
        for n in range(2):
            value = mid.pool_rows(pair[n], tmp.at[2 * x + n])
            pooled[pl.ds(n * rows2 + x * ny2, ny2), :] = value

    sweep(range(nx2), coarsened, put_pooled)
    deeper = split_dot(pooled[pl.ds(0, 2 * rows2), :], pool)
    planes = [deeper[n * ny2 : (n + 1) * ny2] for n in range(2 * nx2)]
    values = deep.solve_in_registers(planes[:nx2], planes[nx2:])

    pooled[pl.ds(0, rows2), :] = split_dot(values, spread)

    def refined1(x):
        return mid.spread_rows(pooled[pl.ds(x * ny2, ny2), :], tmp.at[x])

    def put_refined1(x, value):
        for n in range(2):
            v1b[2 * x + n + rim, pl.ds(8, ny1), :] += value

    sweep(range(nx2), refined1, put_refined1)
    mid.smooth(v1b, v1a, range(nx1))
    mid.smooth(v1a, v1b, range(nx1))

    window = own + 2 * rim
    values = v1b[pl.ds(slab * own, window), pl.ds(8, ny1), :].reshape(window * ny1, LANES)
    out_ref[...] = split_dot(values, spread)


def post_kernel(by, chips_y, place_ref, scalar_ref, *refs):
    f, r, w, v1, correction, first_ref, second_ref, kept_ref, sent_ref, va, vb, tmp = refs
    count, ny = f.shape[:2]
    fine = Level(0, ny, LANES, 0, scalars_of(scalar_ref), f, r, w)
    for v in (va, vb):
        zero_rows(v, ny)
    x, half = place_ref[0] // 2 // chips_y, ny // 2
    window = correction.shape[0] // half
    for ref, above in ((first_ref, 1 - x), (second_ref, x)):
        va[pl.ds(1 + above * (SLAB + HALO), NEAR), pl.ds(8, ny), :] = ref[...]

    def refined(x):
        return fine.spread_rows(correction[pl.ds(x * half, half), :], tmp.at[x])

    def put_refined(x, value):
        for at in (2 * x, 2 * x + 1):
            if 0 < at < count - 1:
                known = HALO - NEAR < at < HALO + SLAB + NEAR - 1
                here = v1 if known else va
                va[at, pl.ds(8, ny), :] = here[at, pl.ds(8, ny), :] + value

    sweep(range(window), refined, put_refined)
    fine.smooth(va, vb, range(2, count - 2))
    fine.smooth(vb, va, range(3, count - 3))

    total = jnp.zeros((8, LANES), jnp.float32)
    for x in range(SLAB):
        rest = fine.defect(va, HALO + x)
        total = total + jnp.sum((rest * rest).reshape(ny // 8, 8, LANES), axis=0)
        tmp[x] = rest
    squares = jnp.full((8, LANES), jnp.sum(total), jnp.float32)

    core, area = place_ref[0] & 1, half * SLAB
    for ref, first in ((kept_ref, core * by), (sent_ref, (1 - core) * by)):
        for y in range(half // by):
            row = pl.multiple_of(2 * y * by + first, 8)
            for x in range(SLAB):
                to = x * half + y * by
                ref[pl.ds(to, by), :] = va[HALO + x, pl.ds(8 + row, by), :]
                ref[pl.ds(area + to, by), :] = tmp[x, pl.ds(row, by), :]
        ref[pl.ds(2 * area, 8), :] = squares


def part_rows(bx, by):
    outer = bx * by
    edges = outer + 2 * by
    squares = edges + 2 * (bx - 2)
    return outer, edges, squares, (squares + 8) // 8 * 8


def merge_back_kernel(bx, by, chips_y, place_ref, kept_ref, got_ref, *out_refs):
    chip, core = place_ref[0] // 2, place_ref[0] & 1
    half = chips_y * by
    outer, edges, squares, size = part_rows(bx, by)
    for m, out_ref in enumerate(out_refs):
        target = jnp.bitwise_xor(chip, m)
        first = (target // chips_y) * bx * half + lax.rem(target, chips_y) * by
        for ref, column in ((kept_ref, core), (got_ref, 1 - core)):
            base = pl.multiple_of(column * size, 8)
            for p in range(bx):
                at = pl.multiple_of(first + p * half, 8)
                out_ref[pl.ds(base + p * by, by), :] = ref[pl.ds(at, by), :]
                at = pl.multiple_of(at + SLAB * half, 8)
                if p in (0, bx - 1):
                    out_ref[pl.ds(base + outer + (p > 0) * by, by), :] = ref[pl.ds(at, by), :]
                else:
                    rows = ref[pl.ds(at, by), :]
                    to = base + edges + 2 * (p - 1)
                    out_ref[pl.ds(to, 1), :] = rows[:1]
                    out_ref[pl.ds(to + 1, 1), :] = rows[by - 1 :]
            out_ref[pl.ds(base + squares, 1), :] = ref[pl.ds(2 * SLAB * half, 1), :]


def collect_kernel(place_ref, shifts_ref, index_ref, velocity_ref, source_ref, reaction_ref, *refs):
    parts, (iterate_ref, residual_ref) = refs[:-2], refs[-2:]
    _, bx, by, nz = iterate_ref.shape
    outer, edges, _, size = part_rows(bx, by)
    fine = Level(0, by, nz, 0, (0.0, [velocity_ref[d] for d in range(3)]), None, None, None)
    reaction = [reaction_ref[p] + fine.centre for p in range(1, bx - 1)]
    for m, part in enumerate(parts):
        target = jnp.bitwise_xor(place_ref[0] // 2, m)
        for n in range(2):
            base, column = n * size, 2 * target + n
            shift = shifts_ref[index_ref[column]]
            planes = [part[pl.ds(base + p * by, by), :] for p in range(bx)]
            for p in range(bx):
                iterate_ref[column, p] = planes[p]
            for p in (0, bx - 1):
                residual_ref[column, p] = part[pl.ds(base + outer + (p > 0) * by, by), :]
            for p in range(1, bx - 1):
                here = planes[p]
                pulled = source_ref[column, p] + fine.along_z(here)
                pulled += fine.backward[0] * planes[p - 1] + fine.forward[0] * planes[p + 1]
                pulled += fine.backward[1] * pltpu.roll(here, 1, 0) + fine.forward[1] * pltpu.roll(here, by - 1, 0)
                residual_ref[column, p] = pulled - (reaction[p - 1] + shift) * here
                at = base + edges + 2 * (p - 1)
                residual_ref[column, p, pl.ds(0, 1), :] = part[pl.ds(at, 1), :]
                residual_ref[column, p, pl.ds(by - 1, 1), :] = part[pl.ds(at + 1, 1), :]


def squares_kernel(bx, by, *refs):
    _, _, squares, size = part_rows(bx, by)
    for m, part in enumerate(refs[:-1]):
        for n in range(2):
            refs[-1][pl.ds(2 * m + n, 1), :] = part[pl.ds(n * size + squares, 1), :]


SMEM = pl.BlockSpec(memory_space=pltpu.SMEM)
VMEM = pl.BlockSpec(memory_space=pltpu.VMEM)


def local_kernel(kernel, name, scalars, arrays, outs, scratch=(), in_place=0):
    return pl.pallas_call(
        kernel,
        out_shape=[jax.ShapeDtypeStruct(shape, jnp.float32) for shape in outs],
        in_specs=[SMEM] * len(scalars) + [VMEM] * len(arrays),
        out_specs=[VMEM] * len(outs),
        scratch_shapes=[pltpu.VMEM(shape, jnp.float32) for shape in scratch],
        input_output_aliases={len(scalars) + n: n for n in range(in_place)},
        compiler_params=pltpu.CompilerParams(vmem_limit_bytes=VMEM_LIMIT),
        name=name,
    )(*scalars, *arrays)


def swap_in_plane(pieces, unit):
    devices = lax.axis_size("gx") * lax.axis_size("gy")
    moved = [pieces[0]]
    for k in range(1, len(pieces)):
        pairs = [(i, i ^ (k * unit)) for i in range(devices)]
        moved.append(lax.ppermute(pieces[k], ("gx", "gy"), pairs))
    return moved


def swap_slabs(piece, step, slabs):
    size = lax.axis_size("gx")
    moved = [piece]
    for k in range(1, slabs):
        pairs = [(i, i ^ (step_of(k, slabs) * step)) for i in range(size)]
        moved.append(lax.ppermute(piece, "gx", pairs))
    return moved


def column_body(source, reaction, shifts, shift_index, velocity):
    columns, bx, by, nz = source.shape
    gx_size, gy_size = lax.axis_size("gx"), lax.axis_size("gy")
    nx, ny = bx * gx_size, by * gy_size
    step = columns // gy_size
    slabs = gx_size // step
    along, across = lax.axis_index("gx"), lax.axis_index("gy")
    column = lax.rem(along, step) * gy_size + across
    place = jnp.stack([column, along // step]).astype(jnp.int32)
    count = SLAB + 2 * HALO
    area = bx * by

    chips, chips_y = columns // 2, gy_size // 2
    cores = [(i, i ^ 1) for i in range(gy_size)]
    theirs = [lax.ppermute(source, "gy", cores), lax.ppermute(reaction, "gy", cores)]
    (mine,) = local_kernel(keep_kernel, "keep", (place,), (source,), [(chips, bx, by, nz)])
    *blocks, scalar_rows = local_kernel(
        merge_kernel,
        "merge",
        (place, shifts, shift_index, velocity),
        (mine, theirs[0], reaction, theirs[1]),
        [(2, bx, 2 * by, nz)] * chips + [(8, LANES)],
    )
    scalars = (place, scalar_rows)
    blocks = swap_in_plane(blocks, 2)

    edge = (2, NEAR, ny, nz)
    (own_half,) = local_kernel(
        functools.partial(half_kernel, chips_y),
        "half",
        (place,),
        blocks[:chips_y],
        [(2, HALO, ny, nz)],
    )
    slab, near = local_kernel(
        functools.partial(arrange_kernel, chips_y),
        "arrange",
        (place,),
        blocks,
        [(2, SLAB, ny, nz), edge],
    )

    def send_beside(piece, up):
        pairs = [(i, i + step if i % step == up else i - step) for i in range(gx_size)]
        return lax.ppermute(piece, "gx", [(i, j) for i, j in pairs if 0 <= j < gx_size])

    beside = [send_beside(own_half, 1), send_beside(near, 0)]
    grid, rimmed = (count, ny, nz), (count, ny + 16, nz)
    fields = [grid, grid, grid, rimmed, rimmed]
    fields_own = local_kernel(begin_kernel, "begin", (scalar_rows,), (slab,), fields)
    f, r, w, _, v1, coarse, beyond = local_kernel(
        functools.partial(pre_kernel, slabs, chips_y),
        "pre",
        scalars,
        (*fields_own, *beside, pool_matrix(0), pool_matrix(LANES // 2)),
        fields + [(SLAB // 2, ny // 2, nz), (NEAR, ny, nz)],
        [(SLAB, ny, nz), (2, SLAB // 2 * ny // 2, nz)],
        in_place=len(fields),
    )
    (own_beyond,) = local_kernel(
        functools.partial(beyond_kernel, slabs, chips_y),
        "beyond",
        scalars,
        beside[:1],
        [(NEAR, ny, nz)],
        [(HALO, ny, nz)] * 3 + [(HALO, ny + 16, nz)],
    )
    gathered = swap_slabs(coarse, step, slabs)

    coarse_grid = (nx // 2, ny // 2, nz)
    coarse_rimmed = (nx // 2 + HALO, ny // 2 + 16, nz)
    window = (SLAB // 2 + HALO) * ny // 2
    (correction,) = local_kernel(
        functools.partial(coarse_kernel, (slabs, nx, ny, nz)),
        "coarse",
        scalars,
        (pool_matrix(0), spread_matrix(), *gathered),
        [(window, nz)],
        [coarse_grid] * 3 + [coarse_rimmed] * 2 + [(nx // 4 * ny // 2, nz), (nx // 2, ny // 2, nz)],
    )
    result = (SLAB * ny + 8, nz)
    kept, sent = local_kernel(
        functools.partial(post_kernel, by, chips_y),
        "post",
        scalars,
        (f, r, w, v1, correction, own_beyond, send_beside(beyond, 0)),
        [result, result],
        [rimmed] * 2 + [(SLAB, ny, nz)],
    )

    parts = local_kernel(
        functools.partial(merge_back_kernel, bx, by, chips_y),
        "merge_back",
        (place,),
        (kept, lax.ppermute(sent, "gy", cores)),
        [(2 * part_rows(bx, by)[3], nz)] * chips,
    )
    parts = swap_in_plane(parts, 2)
    (squares,) = local_kernel(
        functools.partial(squares_kernel, bx, by), "squares", (), parts, [(columns, nz)]
    )
    iterate, residual = local_kernel(
        collect_kernel,
        "collect",
        (place, shifts, shift_index, velocity),
        (source, reaction, *parts),
        [source.shape] * 2,
    )
    total = sum(swap_slabs(squares, step, slabs))
    rms = jnp.sqrt(total[:, 0] / (nx * ny * nz) + EPSILON)
    slots = jnp.arange(columns, dtype=jnp.int32)
    mine = jnp.bitwise_xor(slots, column // 2 * 2)[:, None] == slots[None, :]
    residual_rms = jnp.sum(jnp.where(mine, rms[None, :], 0.0), axis=1)
    return iterate, residual, residual_rms


def power_of_two(n):
    return n > 0 and n & (n - 1) == 0


def column_plan_fits(columns, bx, by, nz, gx_size, gy_size):
    if columns % gy_size or gx_size % (columns // gy_size):
        return False
    step = columns // gy_size
    slabs, ny = gx_size // step, by * gy_size
    whole = power_of_two(columns) and power_of_two(step) and power_of_two(slabs)
    small = slabs * ny * nz <= 2**15
    paired = step == 2 and bx == HALO and gy_size % 2 == 0
    return whole and small and paired and bx * step == SLAB and nz == LANES and by % 16 == 0


def solution(mesh):
    gx_size, gy_size = mesh.shape["gx"], mesh.shape["gy"]

    def body(source, reaction, shifts, shift_index, velocity):
        fits = column_plan_fits(*source.shape, gx_size, gy_size)
        plan = column_body if fits else halo_body
        return plan(source, reaction, shifts, shift_index, velocity)

    return jax.shard_map(
        body,
        mesh=mesh,
        in_specs=(P(None, "gx", "gy", None), P("gx", "gy", None), P(), P(), P()),
        out_specs=(P(None, "gx", "gy", None), P(None, "gx", "gy", None), P()),
        check_vma=False,
    )
```

```python
import functools

import jax
import jax.numpy as jnp
from jax import lax
from jax.experimental import pallas as pl
from jax.experimental.pallas import tpu as pltpu
from jax.sharding import PartitionSpec as P

LEVELS = 3
COARSE_SWEEPS = 6

DAMPING = 0.8
EPSILON = 1e-06
VMEM_LIMIT = 32 * 1024 * 1024
LANES = 128
GROUP = 4
SLAB = 8
HALO = 4
NEAR = 2


def with_halo(x, sides, width):
    for axis, dim in sides:
        peers, length = (lax.axis_size(axis), x.shape[dim])
        up = [(i, (i + 1) % peers) for i in range(peers - 1)]
        down = [(j, i) for i, j in up]
        last = lax.slice_in_dim(x, length - width, length, axis=dim)
        leading = lax.slice_in_dim(x, 0, width, axis=dim)
        before = lax.ppermute(last, axis, up)
        after = lax.ppermute(leading, axis, down)
        x = jnp.concatenate([before, x, after], axis=dim)
    return x


def select_shifts(shifts, shift_index):
    columns = jnp.arange(shifts.shape[0], dtype=jnp.int32)
    picked = jnp.where(shift_index[:, None] == columns[None, :], shifts[None, :], 0.0)
    return jnp.sum(picked, axis=1)


def coefficients(velocity, spacing):
    scale_a = 1.0 / (spacing * spacing)
    backward = scale_a + jnp.maximum(velocity, 0.0) / spacing
    forward = scale_a - jnp.minimum(velocity, 0.0) / spacing
    centre = 6.0 * scale_a + jnp.sum(jnp.abs(velocity)) / spacing
    return (backward, forward, centre)


def apply_stencil(padded, backward, forward, diagonal):
    middle = padded[:, 1:-1, 1:-1, :]
    along_z = jnp.pad(middle, ((0, 0), (0, 0), (0, 0), (1, 1)))
    others = backward[0] * padded[:, :-2, 1:-1, :] + forward[0] * padded[:, 2:, 1:-1, :]
    others = others + backward[1] * padded[:, 1:-1, :-2, :] + forward[1] * padded[:, 1:-1, 2:, :]
    others = others + backward[2] * along_z[:, :, :, :-2] + forward[2] * along_z[:, :, :, 2:]
    return diagonal * middle - others


def face_halo(iterate):
    return with_halo(iterate, (("gx", 1), ("gy", 2)), 1)


def coarsen(values):
    count, size_x, size_y, size_z = values.shape
    blocks = values.reshape(count, size_x // 2, 2, size_y // 2, 2, size_z // 2, 2)
    return jnp.sum(blocks, axis=(2, 4, 6)) * 0.125


def refine(values):
    return jnp.repeat(jnp.repeat(jnp.repeat(values, 2, 1), 2, 2), 2, 3)


def coarsest_solve(rhs_field, backward, forward, diagonal):
    iterate = DAMPING * rhs_field / diagonal
    for repeat in range(COARSE_SWEEPS - 1):
        applied = apply_stencil(face_halo(iterate), backward, forward, diagonal)
        iterate = iterate + DAMPING * (rhs_field - applied) / diagonal
    return iterate


def multigrid_cycle(level_index, rhs_field, reaction_l, shift_value, velocity):
    backward, forward, centre = coefficients(velocity, 2.0**level_index)
    diagonal = centre + reaction_l + shift_value[:, None, None, None]
    if level_index == LEVELS - 1:
        return coarsest_solve(rhs_field, backward, forward, diagonal)

    def operate(iterate):
        return apply_stencil(face_halo(iterate), backward, forward, diagonal)

    def smooth_step(iterate):
        return iterate + DAMPING * (rhs_field - operate(iterate)) / diagonal

    iterate = DAMPING * rhs_field / diagonal
    iterate = smooth_step(iterate)
    defect = rhs_field - operate(iterate)
    correction = multigrid_cycle(
        level_index + 1, coarsen(defect), coarsen(reaction_l), shift_value, velocity
    )
    iterate = iterate + refine(correction)
    iterate = smooth_step(iterate)
    iterate = smooth_step(iterate)
    return iterate


def halo_body(source, reaction, shifts, shift_index, velocity):
    columns, cells_x, cells_y, cells_z = source.shape
    shift_value = select_shifts(shifts, shift_index)
    reaction_top = reaction[None]
    backward, forward, centre = coefficients(velocity, 1.0)
    diagonal = centre + reaction_top + shift_value[:, None, None, None]

    iterate = multigrid_cycle(0, source, reaction_top, shift_value, velocity)
    residual = source - apply_stencil(face_halo(iterate), backward, forward, diagonal)
    local_squares = jnp.sum(residual * residual, axis=(1, 2, 3))
    squares = lax.psum(local_squares, ("gx", "gy"))
    total_cells = cells_x * cells_y * cells_z * lax.axis_size("gx") * lax.axis_size("gy")
    residual_rms = jnp.sqrt(squares / total_cells + EPSILON)
    return (iterate, residual, residual_rms)


def split_dot(values, matrix):
    high = values.astype(jnp.bfloat16)
    low = (values - high.astype(jnp.float32)).astype(jnp.bfloat16)
    return jnp.dot(high, matrix, preferred_element_type=jnp.float32) + jnp.dot(
        low, matrix, preferred_element_type=jnp.float32
    )


def sweep(planes, get, put):
    planes = list(planes)
    for first in range(0, len(planes), GROUP):
        group = planes[first : first + GROUP]
        values = [get(x) for x in group]
        for x, value in zip(group, values):
            put(x, value)


class Grid:
    def __init__(self, ny):
        self.ny = ny

    def pool_rows(self, value, rows):
        half, ny = self.ny // 2, self.ny
        rows[pl.ds(0, ny), :] = value
        return rows[pl.ds(0, half, stride=2), :] + rows[pl.ds(1, half, stride=2), :]

    def spread_rows(self, part, rows):
        half, ny = self.ny // 2, self.ny
        rows[pl.ds(0, half, stride=2), :] = part
        rows[pl.ds(1, half, stride=2), :] = part
        return rows[pl.ds(0, ny), :]


class Level(Grid):
    def __init__(self, index, ny, nz, rim, scalars, f, r, w):
        super().__init__(ny)
        self.nz, self.rim = nz, rim
        self.f, self.r, self.w = f, r, w
        spacing = 2.0**index
        scale_a = 1.0 / (spacing * spacing)
        inverse = 1.0 / spacing
        shift, speed = scalars
        self.backward = [scale_a + jnp.maximum(v, 0.0) * inverse for v in speed]
        self.forward = [scale_a - jnp.minimum(v, 0.0) * inverse for v in speed]
        total = jnp.abs(speed[0]) + jnp.abs(speed[1]) + jnp.abs(speed[2])
        self.centre = 6.0 * scale_a + total * inverse + shift
        lane = lax.broadcasted_iota(jnp.int32, (1, LANES), 1)
        inside = lane < nz
        self.low_z = jnp.where((lane > 0) & inside, self.backward[2], 0.0)
        self.high_z = jnp.where(lane < nz - 1, self.forward[2], 0.0)

    def plane(self, v, x):
        return v[x + self.rim, pl.ds(8, self.ny), :]

    def put(self, v):
        def write(x, value):
            v[x + self.rim, pl.ds(8, self.ny), :] = value

        return write

    def along_z(self, middle):
        return self.low_z * pltpu.roll(middle, 1, 1) + self.high_z * pltpu.roll(middle, LANES - 1, 1)

    def neighbours(self, v, x, middle):
        at, ny = x + self.rim, self.ny
        along_x = self.backward[0] * v[at - 1, pl.ds(8, ny), :] + self.forward[0] * v[at + 1, pl.ds(8, ny), :]
        along_y = self.backward[1] * v[at, pl.ds(7, ny), :] + self.forward[1] * v[at, pl.ds(9, ny), :]
        return along_x + along_y + self.along_z(middle)

    def smoothed(self, v, x):
        middle = self.plane(v, x)
        pulled = self.f[x] + self.neighbours(v, x, middle)
        return (1.0 - DAMPING) * middle + self.w[x] * pulled

    def smooth(self, src, dst, planes):
        sweep(planes, lambda x: self.smoothed(src, x), self.put(dst))

    def defect(self, v, x):
        middle = self.plane(v, x)
        pulled = self.f[x] + self.neighbours(v, x, middle)
        return pulled - (self.r[x] + self.centre) * middle

    def solve_in_registers(self, rhs, reaction):
        row = lax.broadcasted_iota(jnp.int32, (self.ny, 1), 0)
        low_y = jnp.where(row > 0, self.backward[1], 0.0)
        high_y = jnp.where(row < self.ny - 1, self.forward[1], 0.0)
        weight = [DAMPING / (r + self.centre) for r in reaction]
        v = [w * f for w, f in zip(weight, rhs)]
        for _ in range(COARSE_SWEEPS - 1):
            new = []
            for x, here in enumerate(v):
                along_y = low_y * pltpu.roll(here, 1, 0) + high_y * pltpu.roll(here, self.ny - 1, 0)
                pulled = rhs[x] + self.along_z(here) + along_y
                if x > 0:
                    pulled += self.backward[0] * v[x - 1]
                if x < len(v) - 1:
                    pulled += self.forward[0] * v[x + 1]
                new.append((1.0 - DAMPING) * here + weight[x] * pulled)
            v = new
        return jnp.concatenate(v, axis=0)


def scalars_of(scalar_ref):
    return scalar_ref[0, 0], [scalar_ref[1 + d, 0] for d in range(3)]


def zero_rows(v, ny):
    edge = jnp.zeros((v.shape[0], 8, LANES), jnp.float32)
    v[:, pl.ds(0, 8), :] = edge
    v[:, pl.ds(8 + ny, 8), :] = edge


def pool_matrix(offset):
    row = lax.broadcasted_iota(jnp.int32, (LANES, LANES), 0)
    col = lax.broadcasted_iota(jnp.int32, (LANES, LANES), 1)
    return jnp.where(row // 2 + offset == col, 0.125, 0.0).astype(jnp.bfloat16)


def spread_matrix():
    row = lax.broadcasted_iota(jnp.int32, (LANES, LANES), 0)
    col = lax.broadcasted_iota(jnp.int32, (LANES, LANES), 1)
    return jnp.where(col // 2 == row, 1.0, 0.0).astype(jnp.bfloat16)


def step_of(k, count):
    return -k % count


def keep_kernel(place_ref, source_ref, out_ref):
    for n in range(out_ref.shape[0]):
        out_ref[n] = source_ref[2 * n + (place_ref[0] & 1)]


def merge_kernel(place_ref, shifts_ref, index_ref, velocity_ref, *refs):
    mine_ref, theirs_ref, reaction_ref, other_reaction_ref = refs[:4]
    out_refs, scalar_ref = refs[4:-1], refs[-1]
    chip, core = place_ref[0] // 2, place_ref[0] & 1
    by = mine_ref.shape[2]
    mine = pl.ds(pl.multiple_of(core * by, 8), by)
    theirs = pl.ds(pl.multiple_of((1 - core) * by, 8), by)
    for m, out_ref in enumerate(out_refs):
        target = jnp.bitwise_xor(chip, m)
        out_ref[0, :, mine, :] = mine_ref[target]
        out_ref[0, :, theirs, :] = theirs_ref[2 * target + core]
        out_ref[1, :, mine, :] = reaction_ref[...]
        out_ref[1, :, theirs, :] = other_reaction_ref[...]
    scalars = [shifts_ref[index_ref[place_ref[0]]]] + [velocity_ref[d] for d in range(3)]
    for n, scalar in enumerate(scalars):
        scalar_ref[pl.ds(n, 1), :] = jnp.full((1, LANES), scalar, jnp.float32)


def half_kernel(chips_y, place_ref, *refs):
    blocks, half_ref = refs[:-1], refs[-1]
    for m, block in enumerate(blocks):
        size = block.shape[2]
        chip = jnp.bitwise_xor(place_ref[0] // 2, m)
        rows = pl.ds(pl.multiple_of(lax.rem(chip, chips_y) * size, 8), size)
        half_ref[:, :, rows, :] = block[...]


def arrange_kernel(chips_y, place_ref, *refs):
    blocks, (slab_ref, near_ref) = refs[:-2], refs[-2:]
    chip = place_ref[0] // 2
    for m, block in enumerate(blocks):
        owner = jnp.bitwise_xor(chip, m)
        _, bx, size, _ = block.shape
        planes = pl.ds((owner // chips_y) * bx, bx)
        rows = pl.ds(pl.multiple_of(lax.rem(owner, chips_y) * size, 8), size)
        slab_ref[:, planes, rows, :] = block[...]
    other = 1 - chip // chips_y
    near_ref[...] = slab_ref[:, pl.ds(other * (SLAB - NEAR), NEAR)]


def beyond_kernel(slabs, chips_y, place_ref, scalar_ref, half_ref, out_ref, f, r, w, v0):
    ny, slab = f.shape[1], place_ref[1]
    x = place_ref[0] // 2 // chips_y
    fine = Level(0, ny, LANES, 0, scalars_of(scalar_ref), f, r, w)
    zero_rows(v0, ny)
    f[...], r[...] = half_ref[0], half_ref[1]
    beside = jnp.where(x == 0, slab < slabs - 1, slab > 0)
    inside = jnp.where(beside, DAMPING, 0.0)

    def put(at, weight):
        w[at] = weight
        v0[at, pl.ds(8, ny), :] = weight * f[at]

    sweep(range(HALO), lambda at: inside / (r[at] + fine.centre), put)
    for n in range(NEAR):
        out_ref[n] = fine.smoothed(v0, 1 + n)


def begin_kernel(scalar_ref, slab_ref, f, r, w, v0, v1):
    ny = f.shape[1]
    fine = Level(0, ny, LANES, 0, scalars_of(scalar_ref), f, r, w)
    zero_rows(v0, ny)
    zero_rows(v1, ny)
    own = range(HALO, HALO + SLAB)
    f[pl.ds(HALO, SLAB)], r[pl.ds(HALO, SLAB)] = slab_ref[0], slab_ref[1]

    def put(at, weight):
        w[at] = weight
        v0[at, pl.ds(8, ny), :] = weight * f[at]

    sweep(own, lambda at: DAMPING / (r[at] + fine.centre), put)
    fine.smooth(v0, v1, own[1:-1])


def pre_kernel(slabs, chips_y, place_ref, scalar_ref, *refs):
    half_ref, near_ref, pool_ref, pool_up_ref = refs[5:9]
    f, r, w, v0, v1, coarse_ref, beyond_ref, tmp, pooled = refs[9:]
    ny = f.shape[1]
    slab = place_ref[1]
    fine = Level(0, ny, LANES, 0, scalars_of(scalar_ref), f, r, w)
    after = HALO + SLAB

    x = place_ref[0] // 2 // chips_y
    for above, ref, first in ((1 - x, half_ref, x * NEAR), (x, near_ref, 0)):
        planes = pl.ds((HALO - NEAR) + above * (SLAB + NEAR), NEAR)
        f[planes], r[planes] = ref[0, pl.ds(first, NEAR)], ref[1, pl.ds(first, NEAR)]

    below = jnp.where(slab > 0, DAMPING, 0.0)
    above = jnp.where(slab < slabs - 1, DAMPING, 0.0)

    def put(at, weight):
        w[at] = weight
        v0[at, pl.ds(8, ny), :] = weight * f[at]

    beside = [*range(HALO - NEAR, HALO), *range(after, after + NEAR)]
    sweep(beside, lambda at: (below if at < HALO else above) / (r[at] + fine.centre), put)
    fine.smooth(v0, v1, (HALO - 1, HALO, after - 1, after))
    half = ny // 2

    def coarsened(x):
        at = HALO + 2 * x
        return fine.defect(v1, at) + fine.defect(v1, at + 1), r[at] + r[at + 1]

    def put_pooled(x, pair):
        for n in range(2):
            pooled[n, pl.ds(x * half, half), :] = fine.pool_rows(pair[n], tmp.at[2 * x + n])

    sweep(range(SLAB // 2), coarsened, put_pooled)
    packed = split_dot(pooled[0], pool_ref[...]) + split_dot(pooled[1], pool_up_ref[...])
    coarse_ref[...] = packed.reshape(coarse_ref.shape)
    first = HALO + 1 + (1 - x) * (SLAB - HALO)
    beyond_ref[...] = v1[pl.ds(first, NEAR), pl.ds(8, ny), :]


def coarse_kernel(grid, place_ref, scalar_ref, *refs):
    slabs, nx, ny, nz = grid
    pool_ref, spread_ref = refs[:2]
    coarse, out_ref = refs[2 : 2 + slabs], refs[2 + slabs]
    f1, r1, w1, v1a, v1b, pooled, tmp = refs[3 + slabs :]
    pool, spread = pool_ref[...], spread_ref[...]
    slab = place_ref[1]
    rim = HALO // 2
    nx1, ny1, nx2, ny2 = nx // 2, ny // 2, nx // 4, ny // 4
    mid = Level(1, ny1, nz // 2, rim, scalars_of(scalar_ref), f1, r1, w1)
    deep = Level(2, ny2, nz // 4, 0, scalars_of(scalar_ref), None, None, None)
    for v in (v1a, v1b):
        zero_rows(v, ny1)
        blank = jnp.zeros((rim,) + v.shape[1:], jnp.float32)
        v[pl.ds(0, rim)] = blank
        v[pl.ds(rim + nx1, rim)] = blank

    lower = lax.broadcasted_iota(jnp.int32, (1, LANES), 1) < LANES // 2
    own = SLAB // 2
    for k in range(slabs):
        first = jnp.bitwise_xor(slab, step_of(k, slabs)) * own
        both = coarse[k][...]
        f1[pl.ds(first, own)] = jnp.where(lower, both, 0.0)
        r1[pl.ds(first, own)] = jnp.where(lower, pltpu.roll(both, LANES // 2, 2), 0.0)

    def put_start(x, weight):
        w1[x] = weight
        v1a[x + rim, pl.ds(8, ny1), :] = weight * f1[x]

    sweep(range(nx1), lambda x: DAMPING / (r1[x] + mid.centre), put_start)
    mid.smooth(v1a, v1b, range(nx1))

    def coarsened(x):
        return mid.defect(v1b, 2 * x) + mid.defect(v1b, 2 * x + 1), r1[2 * x] + r1[2 * x + 1]

    rows2 = nx2 * ny2

    def put_pooled(x, pair):
        for n in range(2):
            value = mid.pool_rows(pair[n], tmp.at[2 * x + n])
            pooled[pl.ds(n * rows2 + x * ny2, ny2), :] = value

    sweep(range(nx2), coarsened, put_pooled)
    deeper = split_dot(pooled[pl.ds(0, 2 * rows2), :], pool)
    planes = [deeper[n * ny2 : (n + 1) * ny2] for n in range(2 * nx2)]
    values = deep.solve_in_registers(planes[:nx2], planes[nx2:])

    pooled[pl.ds(0, rows2), :] = split_dot(values, spread)

    def refined1(x):
        return mid.spread_rows(pooled[pl.ds(x * ny2, ny2), :], tmp.at[x])

    def put_refined1(x, value):
        for n in range(2):
            v1b[2 * x + n + rim, pl.ds(8, ny1), :] += value

    sweep(range(nx2), refined1, put_refined1)
    mid.smooth(v1b, v1a, range(nx1))
    mid.smooth(v1a, v1b, range(nx1))

    window = own + 2 * rim
    values = v1b[pl.ds(slab * own, window), pl.ds(8, ny1), :].reshape(window * ny1, LANES)
    out_ref[...] = split_dot(values, spread)


def post_kernel(by, chips_y, place_ref, scalar_ref, *refs):
    f, r, w, v1, correction, first_ref, second_ref, kept_ref, sent_ref, va, vb, tmp = refs
    count, ny = f.shape[:2]
    fine = Level(0, ny, LANES, 0, scalars_of(scalar_ref), f, r, w)
    for v in (va, vb):
        zero_rows(v, ny)
    x, half = place_ref[0] // 2 // chips_y, ny // 2
    window = correction.shape[0] // half
    for ref, above in ((first_ref, 1 - x), (second_ref, x)):
        va[pl.ds(1 + above * (SLAB + HALO), NEAR), pl.ds(8, ny), :] = ref[...]

    def refined(x):
        return fine.spread_rows(correction[pl.ds(x * half, half), :], tmp.at[x])

    def put_refined(x, value):
        for at in (2 * x, 2 * x + 1):
            if 0 < at < count - 1:
                known = HALO - NEAR < at < HALO + SLAB + NEAR - 1
                here = v1 if known else va
                va[at, pl.ds(8, ny), :] = here[at, pl.ds(8, ny), :] + value

    sweep(range(window), refined, put_refined)
    fine.smooth(va, vb, range(2, count - 2))
    fine.smooth(vb, va, range(3, count - 3))

    total = jnp.zeros((8, LANES), jnp.float32)
    for x in range(SLAB):
        rest = fine.defect(va, HALO + x)
        total = total + jnp.sum((rest * rest).reshape(ny // 8, 8, LANES), axis=0)
        tmp[x] = rest
    squares = jnp.full((8, LANES), jnp.sum(total), jnp.float32)

    core, area = place_ref[0] & 1, half * SLAB
    for ref, first in ((kept_ref, core * by), (sent_ref, (1 - core) * by)):
        for y in range(half // by):
            row = pl.multiple_of(2 * y * by + first, 8)
            for x in range(SLAB):
                to = x * half + y * by
                ref[pl.ds(to, by), :] = va[HALO + x, pl.ds(8 + row, by), :]
                ref[pl.ds(area + to, by), :] = tmp[x, pl.ds(row, by), :]
        ref[pl.ds(2 * area, 8), :] = squares


def part_rows(bx, by):
    outer = bx * by
    edges = outer + 2 * by
    squares = edges + 2 * (bx - 2)
    return outer, edges, squares, (squares + 8) // 8 * 8


def merge_back_kernel(bx, by, chips_y, place_ref, kept_ref, got_ref, *out_refs):
    chip, core = place_ref[0] // 2, place_ref[0] & 1
    half = chips_y * by
    outer, edges, squares, size = part_rows(bx, by)
    for m, out_ref in enumerate(out_refs):
        target = jnp.bitwise_xor(chip, m)
        first = (target // chips_y) * bx * half + lax.rem(target, chips_y) * by
        for ref, column in ((kept_ref, core), (got_ref, 1 - core)):
            base = pl.multiple_of(column * size, 8)
            for p in range(bx):
                at = pl.multiple_of(first + p * half, 8)
                out_ref[pl.ds(base + p * by, by), :] = ref[pl.ds(at, by), :]
                at = pl.multiple_of(at + SLAB * half, 8)
                if p in (0, bx - 1):
                    out_ref[pl.ds(base + outer + (p > 0) * by, by), :] = ref[pl.ds(at, by), :]
                else:
                    rows = ref[pl.ds(at, by), :]
                    to = base + edges + 2 * (p - 1)
                    out_ref[pl.ds(to, 1), :] = rows[:1]
                    out_ref[pl.ds(to + 1, 1), :] = rows[by - 1 :]
            out_ref[pl.ds(base + squares, 1), :] = ref[pl.ds(2 * SLAB * half, 1), :]


def collect_kernel(place_ref, shifts_ref, index_ref, velocity_ref, source_ref, reaction_ref, *refs):
    parts, (iterate_ref, residual_ref) = refs[:-2], refs[-2:]
    _, bx, by, nz = iterate_ref.shape
    outer, edges, _, size = part_rows(bx, by)
    fine = Level(0, by, nz, 0, (0.0, [velocity_ref[d] for d in range(3)]), None, None, None)
    reaction = [reaction_ref[p] + fine.centre for p in range(1, bx - 1)]
    for m, part in enumerate(parts):
        target = jnp.bitwise_xor(place_ref[0] // 2, m)
        for n in range(2):
            base, column = n * size, 2 * target + n
            shift = shifts_ref[index_ref[column]]
            planes = [part[pl.ds(base + p * by, by), :] for p in range(bx)]
            for p in range(bx):
                iterate_ref[column, p] = planes[p]
            for p in (0, bx - 1):
                residual_ref[column, p] = part[pl.ds(base + outer + (p > 0) * by, by), :]
            for p in range(1, bx - 1):
                here = planes[p]
                pulled = source_ref[column, p] + fine.along_z(here)
                pulled += fine.backward[0] * planes[p - 1] + fine.forward[0] * planes[p + 1]
                pulled += fine.backward[1] * pltpu.roll(here, 1, 0) + fine.forward[1] * pltpu.roll(here, by - 1, 0)
                residual_ref[column, p] = pulled - (reaction[p - 1] + shift) * here
                at = base + edges + 2 * (p - 1)
                residual_ref[column, p, pl.ds(0, 1), :] = part[pl.ds(at, 1), :]
                residual_ref[column, p, pl.ds(by - 1, 1), :] = part[pl.ds(at + 1, 1), :]


def squares_kernel(bx, by, place_ref, *refs):
    parts, out_ref = refs[:-1], refs[-1]
    _, _, squares, size = part_rows(bx, by)
    for m, part in enumerate(parts):
        target = jnp.bitwise_xor(place_ref[0] // 2, m)
        for n in range(2):
            out_ref[pl.ds(2 * target + n, 1), :] = part[pl.ds(n * size + squares, 1), :]


SMEM = pl.BlockSpec(memory_space=pltpu.SMEM)
VMEM = pl.BlockSpec(memory_space=pltpu.VMEM)


def local_kernel(kernel, name, scalars, arrays, outs, scratch=(), in_place=0):
    return pl.pallas_call(
        kernel,
        out_shape=[jax.ShapeDtypeStruct(shape, jnp.float32) for shape in outs],
        in_specs=[SMEM] * len(scalars) + [VMEM] * len(arrays),
        out_specs=[VMEM] * len(outs),
        scratch_shapes=[pltpu.VMEM(shape, jnp.float32) for shape in scratch],
        input_output_aliases={len(scalars) + n: n for n in range(in_place)},
        compiler_params=pltpu.CompilerParams(vmem_limit_bytes=VMEM_LIMIT),
        name=name,
    )(*scalars, *arrays)


def swap_in_plane(pieces, unit):
    devices = lax.axis_size("gx") * lax.axis_size("gy")
    moved = [pieces[0]]
    for k in range(1, len(pieces)):
        pairs = [(i, i ^ (k * unit)) for i in range(devices)]
        moved.append(lax.ppermute(pieces[k], ("gx", "gy"), pairs))
    return moved


def swap_slabs(piece, step, slabs):
    size = lax.axis_size("gx")
    moved = [piece]
    for k in range(1, slabs):
        pairs = [(i, i ^ (step_of(k, slabs) * step)) for i in range(size)]
        moved.append(lax.ppermute(piece, "gx", pairs))
    return moved


def column_body(source, reaction, shifts, shift_index, velocity):
    columns, bx, by, nz = source.shape
    gx_size, gy_size = lax.axis_size("gx"), lax.axis_size("gy")
    nx, ny = bx * gx_size, by * gy_size
    step = columns // gy_size
    slabs = gx_size // step
    along, across = lax.axis_index("gx"), lax.axis_index("gy")
    column = lax.rem(along, step) * gy_size + across
    place = jnp.stack([column, along // step]).astype(jnp.int32)
    count = SLAB + 2 * HALO
    area = bx * by

    chips, chips_y = columns // 2, gy_size // 2
    cores = [(i, i ^ 1) for i in range(gy_size)]
    theirs = [lax.ppermute(source, "gy", cores), lax.ppermute(reaction, "gy", cores)]
    (mine,) = local_kernel(keep_kernel, "keep", (place,), (source,), [(chips, bx, by, nz)])
    *blocks, scalar_rows = local_kernel(
        merge_kernel,
        "merge",
        (place, shifts, shift_index, velocity),
        (mine, theirs[0], reaction, theirs[1]),
        [(2, bx, 2 * by, nz)] * chips + [(8, LANES)],
    )
    scalars = (place, scalar_rows)
    blocks = swap_in_plane(blocks, 2)

    edge = (2, NEAR, ny, nz)
    (own_half,) = local_kernel(
        functools.partial(half_kernel, chips_y),
        "half",
        (place,),
        blocks[:chips_y],
        [(2, HALO, ny, nz)],
    )
    slab, near = local_kernel(
        functools.partial(arrange_kernel, chips_y),
        "arrange",
        (place,),
        blocks,
        [(2, SLAB, ny, nz), edge],
    )

    def send_beside(piece, up):
        pairs = [(i, i + step if i % step == up else i - step) for i in range(gx_size)]
        return lax.ppermute(piece, "gx", [(i, j) for i, j in pairs if 0 <= j < gx_size])

    beside = [send_beside(own_half, 1), send_beside(near, 0)]
    grid, rimmed = (count, ny, nz), (count, ny + 16, nz)
    fields = [grid, grid, grid, rimmed, rimmed]
    fields_own = local_kernel(begin_kernel, "begin", (scalar_rows,), (slab,), fields)
    f, r, w, _, v1, coarse, beyond = local_kernel(
        functools.partial(pre_kernel, slabs, chips_y),
        "pre",
        scalars,
        (*fields_own, *beside, pool_matrix(0), pool_matrix(LANES // 2)),
        fields + [(SLAB // 2, ny // 2, nz), (NEAR, ny, nz)],
        [(SLAB, ny, nz), (2, SLAB // 2 * ny // 2, nz)],
        in_place=len(fields),
    )
    (own_beyond,) = local_kernel(
        functools.partial(beyond_kernel, slabs, chips_y),
        "beyond",
        scalars,
        beside[:1],
        [(NEAR, ny, nz)],
        [(HALO, ny, nz)] * 3 + [(HALO, ny + 16, nz)],
    )
    gathered = swap_slabs(coarse, step, slabs)

    coarse_grid = (nx // 2, ny // 2, nz)
    coarse_rimmed = (nx // 2 + HALO, ny // 2 + 16, nz)
    window = (SLAB // 2 + HALO) * ny // 2
    (correction,) = local_kernel(
        functools.partial(coarse_kernel, (slabs, nx, ny, nz)),
        "coarse",
        scalars,
        (pool_matrix(0), spread_matrix(), *gathered),
        [(window, nz)],
        [coarse_grid] * 3 + [coarse_rimmed] * 2 + [(nx // 4 * ny // 2, nz), (nx // 2, ny // 2, nz)],
    )
    result = (SLAB * ny + 8, nz)
    kept, sent = local_kernel(
        functools.partial(post_kernel, by, chips_y),
        "post",
        scalars,
        (f, r, w, v1, correction, own_beyond, send_beside(beyond, 0)),
        [result, result],
        [rimmed] * 2 + [(SLAB, ny, nz)],
    )

    parts = local_kernel(
        functools.partial(merge_back_kernel, bx, by, chips_y),
        "merge_back",
        (place,),
        (kept, lax.ppermute(sent, "gy", cores)),
        [(2 * part_rows(bx, by)[3], nz)] * chips,
    )
    parts = swap_in_plane(parts, 2)
    (squares,) = local_kernel(
        functools.partial(squares_kernel, bx, by), "squares", (place,), parts, [(columns, nz)]
    )
    iterate, residual = local_kernel(
        collect_kernel,
        "collect",
        (place, shifts, shift_index, velocity),
        (source, reaction, *parts),
        [source.shape] * 2,
    )
    sums = swap_slabs(squares, step, slabs)
    sums = [*sums[1:], sums[0]]
    while len(sums) > 1:
        sums = [first + second for first, second in zip(sums[::2], sums[1::2])]
    (total,) = sums
    residual_rms = jnp.sqrt(total[:, 0] / (nx * ny * nz) + EPSILON)
    return iterate, residual, residual_rms


def power_of_two(n):
    return n > 0 and n & (n - 1) == 0


def column_plan_fits(columns, bx, by, nz, gx_size, gy_size):
    if columns % gy_size or gx_size % (columns // gy_size):
        return False
    step = columns // gy_size
    slabs, ny = gx_size // step, by * gy_size
    whole = power_of_two(columns) and power_of_two(step) and power_of_two(slabs)
    small = slabs * ny * nz <= 2**15
    paired = step == 2 and bx == HALO and gy_size % 2 == 0
    return whole and small and paired and bx * step == SLAB and nz == LANES and by % 16 == 0


def solution(mesh):
    gx_size, gy_size = mesh.shape["gx"], mesh.shape["gy"]

    def body(source, reaction, shifts, shift_index, velocity):
        fits = column_plan_fits(*source.shape, gx_size, gy_size)
        plan = column_body if fits else halo_body
        return plan(source, reaction, shifts, shift_index, velocity)

    return jax.shard_map(
        body,
        mesh=mesh,
        in_specs=(P(None, "gx", "gy", None), P("gx", "gy", None), P(), P(), P()),
        out_specs=(P(None, "gx", "gy", None), P(None, "gx", "gy", None), P()),
        check_vma=False,
    )
```

```python
import functools

import jax
import jax.numpy as jnp
from jax import lax
from jax.experimental import pallas as pl
from jax.experimental.pallas import tpu as pltpu
from jax.sharding import PartitionSpec as P

LEVELS = 3
COARSE_SWEEPS = 6

DAMPING = 0.8
EPSILON = 1e-06
VMEM_LIMIT = 32 * 1024 * 1024
LANES = 128
GROUP = 4
SLAB = 8
HALO = 4
NEAR = 2


def with_halo(x, sides, width):
    for axis, dim in sides:
        peers, length = (lax.axis_size(axis), x.shape[dim])
        up = [(i, (i + 1) % peers) for i in range(peers - 1)]
        down = [(j, i) for i, j in up]
        last = lax.slice_in_dim(x, length - width, length, axis=dim)
        leading = lax.slice_in_dim(x, 0, width, axis=dim)
        before = lax.ppermute(last, axis, up)
        after = lax.ppermute(leading, axis, down)
        x = jnp.concatenate([before, x, after], axis=dim)
    return x


def select_shifts(shifts, shift_index):
    columns = jnp.arange(shifts.shape[0], dtype=jnp.int32)
    picked = jnp.where(shift_index[:, None] == columns[None, :], shifts[None, :], 0.0)
    return jnp.sum(picked, axis=1)


def coefficients(velocity, spacing):
    scale_a = 1.0 / (spacing * spacing)
    backward = scale_a + jnp.maximum(velocity, 0.0) / spacing
    forward = scale_a - jnp.minimum(velocity, 0.0) / spacing
    centre = 6.0 * scale_a + jnp.sum(jnp.abs(velocity)) / spacing
    return (backward, forward, centre)


def apply_stencil(padded, backward, forward, diagonal):
    middle = padded[:, 1:-1, 1:-1, :]
    along_z = jnp.pad(middle, ((0, 0), (0, 0), (0, 0), (1, 1)))
    others = backward[0] * padded[:, :-2, 1:-1, :] + forward[0] * padded[:, 2:, 1:-1, :]
    others = others + backward[1] * padded[:, 1:-1, :-2, :] + forward[1] * padded[:, 1:-1, 2:, :]
    others = others + backward[2] * along_z[:, :, :, :-2] + forward[2] * along_z[:, :, :, 2:]
    return diagonal * middle - others


def face_halo(iterate):
    return with_halo(iterate, (("gx", 1), ("gy", 2)), 1)


def coarsen(values):
    count, size_x, size_y, size_z = values.shape
    blocks = values.reshape(count, size_x // 2, 2, size_y // 2, 2, size_z // 2, 2)
    return jnp.sum(blocks, axis=(2, 4, 6)) * 0.125


def refine(values):
    return jnp.repeat(jnp.repeat(jnp.repeat(values, 2, 1), 2, 2), 2, 3)


def coarsest_solve(rhs_field, backward, forward, diagonal):
    iterate = DAMPING * rhs_field / diagonal
    for repeat in range(COARSE_SWEEPS - 1):
        applied = apply_stencil(face_halo(iterate), backward, forward, diagonal)
        iterate = iterate + DAMPING * (rhs_field - applied) / diagonal
    return iterate


def multigrid_cycle(level_index, rhs_field, reaction_l, shift_value, velocity):
    backward, forward, centre = coefficients(velocity, 2.0**level_index)
    diagonal = centre + reaction_l + shift_value[:, None, None, None]
    if level_index == LEVELS - 1:
        return coarsest_solve(rhs_field, backward, forward, diagonal)

    def operate(iterate):
        return apply_stencil(face_halo(iterate), backward, forward, diagonal)

    def smooth_step(iterate):
        return iterate + DAMPING * (rhs_field - operate(iterate)) / diagonal

    iterate = DAMPING * rhs_field / diagonal
    iterate = smooth_step(iterate)
    defect = rhs_field - operate(iterate)
    correction = multigrid_cycle(
        level_index + 1, coarsen(defect), coarsen(reaction_l), shift_value, velocity
    )
    iterate = iterate + refine(correction)
    iterate = smooth_step(iterate)
    iterate = smooth_step(iterate)
    return iterate


def halo_body(source, reaction, shifts, shift_index, velocity):
    columns, cells_x, cells_y, cells_z = source.shape
    shift_value = select_shifts(shifts, shift_index)
    reaction_top = reaction[None]
    backward, forward, centre = coefficients(velocity, 1.0)
    diagonal = centre + reaction_top + shift_value[:, None, None, None]

    iterate = multigrid_cycle(0, source, reaction_top, shift_value, velocity)
    residual = source - apply_stencil(face_halo(iterate), backward, forward, diagonal)
    local_squares = jnp.sum(residual * residual, axis=(1, 2, 3))
    squares = lax.psum(local_squares, ("gx", "gy"))
    total_cells = cells_x * cells_y * cells_z * lax.axis_size("gx") * lax.axis_size("gy")
    residual_rms = jnp.sqrt(squares / total_cells + EPSILON)
    return (iterate, residual, residual_rms)


def split_dot(values, matrix):
    high = values.astype(jnp.bfloat16)
    low = (values - high.astype(jnp.float32)).astype(jnp.bfloat16)
    return jnp.dot(high, matrix, preferred_element_type=jnp.float32) + jnp.dot(
        low, matrix, preferred_element_type=jnp.float32
    )


def sweep(planes, get, put):
    planes = list(planes)
    for first in range(0, len(planes), GROUP):
        group = planes[first : first + GROUP]
        values = [get(x) for x in group]
        for x, value in zip(group, values):
            put(x, value)


class Grid:
    def __init__(self, ny):
        self.ny = ny

    def pool_rows(self, value, rows):
        half, ny = self.ny // 2, self.ny
        rows[pl.ds(0, ny), :] = value
        return rows[pl.ds(0, half, stride=2), :] + rows[pl.ds(1, half, stride=2), :]

    def spread_rows(self, part, rows):
        half, ny = self.ny // 2, self.ny
        rows[pl.ds(0, half, stride=2), :] = part
        rows[pl.ds(1, half, stride=2), :] = part
        return rows[pl.ds(0, ny), :]


class Level(Grid):
    def __init__(self, index, ny, nz, rim, scalars, f, r, w):
        super().__init__(ny)
        self.nz, self.rim = nz, rim
        self.f, self.r, self.w = f, r, w
        spacing = 2.0**index
        scale_a = 1.0 / (spacing * spacing)
        inverse = 1.0 / spacing
        shift, speed = scalars
        self.backward = [scale_a + jnp.maximum(v, 0.0) * inverse for v in speed]
        self.forward = [scale_a - jnp.minimum(v, 0.0) * inverse for v in speed]
        total = jnp.abs(speed[0]) + jnp.abs(speed[1]) + jnp.abs(speed[2])
        self.centre = 6.0 * scale_a + total * inverse + shift
        lane = lax.broadcasted_iota(jnp.int32, (1, LANES), 1)
        inside = lane < nz
        self.low_z = jnp.where((lane > 0) & inside, self.backward[2], 0.0)
        self.high_z = jnp.where(lane < nz - 1, self.forward[2], 0.0)

    def plane(self, v, x):
        return v[x + self.rim, pl.ds(8, self.ny), :]

    def put(self, v):
        def write(x, value):
            v[x + self.rim, pl.ds(8, self.ny), :] = value

        return write

    def along_z(self, middle):
        return self.low_z * pltpu.roll(middle, 1, 1) + self.high_z * pltpu.roll(middle, LANES - 1, 1)

    def neighbours(self, v, x, middle):
        at, ny = x + self.rim, self.ny
        along_x = self.backward[0] * v[at - 1, pl.ds(8, ny), :] + self.forward[0] * v[at + 1, pl.ds(8, ny), :]
        along_y = self.backward[1] * v[at, pl.ds(7, ny), :] + self.forward[1] * v[at, pl.ds(9, ny), :]
        return along_x + along_y + self.along_z(middle)

    def smoothed(self, v, x):
        middle = self.plane(v, x)
        pulled = self.f[x] + self.neighbours(v, x, middle)
        return (1.0 - DAMPING) * middle + self.w[x] * pulled

    def smooth(self, src, dst, planes):
        sweep(planes, lambda x: self.smoothed(src, x), self.put(dst))

    def defect(self, v, x):
        middle = self.plane(v, x)
        pulled = self.f[x] + self.neighbours(v, x, middle)
        return pulled - (self.r[x] + self.centre) * middle

    def solve_in_registers(self, rhs, reaction):
        row = lax.broadcasted_iota(jnp.int32, (self.ny, 1), 0)
        low_y = jnp.where(row > 0, self.backward[1], 0.0)
        high_y = jnp.where(row < self.ny - 1, self.forward[1], 0.0)
        weight = [DAMPING / (r + self.centre) for r in reaction]
        v = [w * f for w, f in zip(weight, rhs)]
        for _ in range(COARSE_SWEEPS - 1):
            new = []
            for x, here in enumerate(v):
                along_y = low_y * pltpu.roll(here, 1, 0) + high_y * pltpu.roll(here, self.ny - 1, 0)
                pulled = rhs[x] + self.along_z(here) + along_y
                if x > 0:
                    pulled += self.backward[0] * v[x - 1]
                if x < len(v) - 1:
                    pulled += self.forward[0] * v[x + 1]
                new.append((1.0 - DAMPING) * here + weight[x] * pulled)
            v = new
        return jnp.concatenate(v, axis=0)


def scalars_of(scalar_ref):
    return scalar_ref[pl.ds(0, 1), :], [scalar_ref[pl.ds(1 + d, 1), :] for d in range(3)]


def zero_rows(v, ny):
    edge = jnp.zeros((v.shape[0], 8, LANES), jnp.float32)
    v[:, pl.ds(0, 8), :] = edge
    v[:, pl.ds(8 + ny, 8), :] = edge


def pool_matrix(offset):
    row = lax.broadcasted_iota(jnp.int32, (LANES, LANES), 0)
    col = lax.broadcasted_iota(jnp.int32, (LANES, LANES), 1)
    return jnp.where(row // 2 + offset == col, 0.125, 0.0).astype(jnp.bfloat16)


def spread_matrix():
    row = lax.broadcasted_iota(jnp.int32, (LANES, LANES), 0)
    col = lax.broadcasted_iota(jnp.int32, (LANES, LANES), 1)
    return jnp.where(col // 2 == row, 1.0, 0.0).astype(jnp.bfloat16)


def step_of(k, count):
    return -k % count


def keep_kernel(place, source_ref, out_ref):
    for n in range(out_ref.shape[0]):
        out_ref[n] = source_ref[2 * n + (place[0] & 1)]


def scalars_kernel(place, shifts_ref, index_ref, velocity_ref, scalar_ref):
    scalars = [shifts_ref[index_ref[place[0]]]] + [velocity_ref[d] for d in range(3)]
    for n, scalar in enumerate(scalars):
        scalar_ref[pl.ds(n, 1), :] = jnp.full((1, LANES), scalar, jnp.float32)


def merge_kernel(place, mine_ref, theirs_ref, reaction_ref, other_reaction_ref, *out_refs):
    chip, core = place[0] // 2, place[0] & 1
    by = mine_ref.shape[2]
    mine = pl.ds(pl.multiple_of(core * by, 8), by)
    theirs = pl.ds(pl.multiple_of((1 - core) * by, 8), by)
    for m, out_ref in enumerate(out_refs):
        target = jnp.bitwise_xor(chip, m)
        out_ref[0, :, mine, :] = mine_ref[target]
        out_ref[0, :, theirs, :] = theirs_ref[2 * target + core]
        out_ref[1, :, mine, :] = reaction_ref[...]
        out_ref[1, :, theirs, :] = other_reaction_ref[...]


def half_kernel(chips_y, place, *refs):
    blocks, half_ref = refs[:-1], refs[-1]
    for m, block in enumerate(blocks):
        size = block.shape[2]
        chip = jnp.bitwise_xor(place[0] // 2, m)
        rows = pl.ds(pl.multiple_of(lax.rem(chip, chips_y) * size, 8), size)
        half_ref[:, :, rows, :] = block[...]


def arrange_kernel(chips_y, place, *refs):
    blocks, (slab_ref, near_ref) = refs[:-2], refs[-2:]
    chip = place[0] // 2
    for m, block in enumerate(blocks):
        owner = jnp.bitwise_xor(chip, m)
        _, bx, size, _ = block.shape
        planes = pl.ds((owner // chips_y) * bx, bx)
        rows = pl.ds(pl.multiple_of(lax.rem(owner, chips_y) * size, 8), size)
        slab_ref[:, planes, rows, :] = block[...]
    other = 1 - chip // chips_y
    near_ref[...] = slab_ref[:, pl.ds(other * (SLAB - NEAR), NEAR)]


def beyond_kernel(slabs, chips_y, place, scalar_ref, half_ref, out_ref, f, r, w, v0):
    ny, slab = f.shape[1], place[1]
    x = place[0] // 2 // chips_y
    fine = Level(0, ny, LANES, 0, scalars_of(scalar_ref), f, r, w)
    zero_rows(v0, ny)
    f[...], r[...] = half_ref[0], half_ref[1]
    beside = jnp.where(x == 0, slab < slabs - 1, slab > 0)
    inside = jnp.where(beside, DAMPING, 0.0)

    def put(at, weight):
        w[at] = weight
        v0[at, pl.ds(8, ny), :] = weight * f[at]

    sweep(range(HALO), lambda at: inside / (r[at] + fine.centre), put)
    for n in range(NEAR):
        out_ref[n] = fine.smoothed(v0, 1 + n)


def begin_kernel(_, scalar_ref, slab_ref, f, r, w, v0, v1):
    ny = f.shape[1]
    fine = Level(0, ny, LANES, 0, scalars_of(scalar_ref), f, r, w)
    zero_rows(v0, ny)
    zero_rows(v1, ny)
    own = range(HALO, HALO + SLAB)
    f[pl.ds(HALO, SLAB)], r[pl.ds(HALO, SLAB)] = slab_ref[0], slab_ref[1]

    def put(at, weight):
        w[at] = weight
        v0[at, pl.ds(8, ny), :] = weight * f[at]

    sweep(own, lambda at: DAMPING / (r[at] + fine.centre), put)
    fine.smooth(v0, v1, own[1:-1])


def pre_kernel(slabs, chips_y, place, scalar_ref, *refs):
    half_ref, near_ref, pool_ref, pool_up_ref = refs[5:9]
    f, r, w, v0, v1, coarse_ref, beyond_ref, tmp, pooled = refs[9:]
    ny = f.shape[1]
    slab = place[1]
    fine = Level(0, ny, LANES, 0, scalars_of(scalar_ref), f, r, w)
    after = HALO + SLAB

    x = place[0] // 2 // chips_y
    for above, ref, first in ((1 - x, half_ref, x * NEAR), (x, near_ref, 0)):
        planes = pl.ds((HALO - NEAR) + above * (SLAB + NEAR), NEAR)
        f[planes], r[planes] = ref[0, pl.ds(first, NEAR)], ref[1, pl.ds(first, NEAR)]

    below = jnp.where(slab > 0, DAMPING, 0.0)
    above = jnp.where(slab < slabs - 1, DAMPING, 0.0)

    def put(at, weight):
        w[at] = weight
        v0[at, pl.ds(8, ny), :] = weight * f[at]

    beside = [*range(HALO - NEAR, HALO), *range(after, after + NEAR)]
    sweep(beside, lambda at: (below if at < HALO else above) / (r[at] + fine.centre), put)
    fine.smooth(v0, v1, (HALO - 1, HALO, after - 1, after))
    half = ny // 2

    def coarsened(x):
        at = HALO + 2 * x
        return fine.defect(v1, at) + fine.defect(v1, at + 1), r[at] + r[at + 1]

    def put_pooled(x, pair):
        for n in range(2):
            pooled[n, pl.ds(x * half, half), :] = fine.pool_rows(pair[n], tmp.at[2 * x + n])

    sweep(range(SLAB // 2), coarsened, put_pooled)
    packed = split_dot(pooled[0], pool_ref[...]) + split_dot(pooled[1], pool_up_ref[...])
    coarse_ref[...] = packed.reshape(coarse_ref.shape)
    first = HALO + 1 + (1 - x) * (SLAB - HALO)
    beyond_ref[...] = v1[pl.ds(first, NEAR), pl.ds(8, ny), :]


def coarse_kernel(grid, place, scalar_ref, *refs):
    slabs, nx, ny, nz = grid
    pool_ref, spread_ref = refs[:2]
    coarse, out_ref = refs[2 : 2 + slabs], refs[2 + slabs]
    f1, r1, w1, v1a, v1b, pooled, tmp = refs[3 + slabs :]
    pool, spread = pool_ref[...], spread_ref[...]
    slab = place[1]
    rim = HALO // 2
    nx1, ny1, nx2, ny2 = nx // 2, ny // 2, nx // 4, ny // 4
    mid = Level(1, ny1, nz // 2, rim, scalars_of(scalar_ref), f1, r1, w1)
    deep = Level(2, ny2, nz // 4, 0, scalars_of(scalar_ref), None, None, None)
    for v in (v1a, v1b):
        zero_rows(v, ny1)
        blank = jnp.zeros((rim,) + v.shape[1:], jnp.float32)
        v[pl.ds(0, rim)] = blank
        v[pl.ds(rim + nx1, rim)] = blank

    lower = lax.broadcasted_iota(jnp.int32, (1, LANES), 1) < LANES // 2
    own = SLAB // 2
    for k in range(slabs):
        first = jnp.bitwise_xor(slab, step_of(k, slabs)) * own
        both = coarse[k][...]
        f1[pl.ds(first, own)] = jnp.where(lower, both, 0.0)
        r1[pl.ds(first, own)] = jnp.where(lower, pltpu.roll(both, LANES // 2, 2), 0.0)

    def put_start(x, weight):
        w1[x] = weight
        v1a[x + rim, pl.ds(8, ny1), :] = weight * f1[x]

    sweep(range(nx1), lambda x: DAMPING / (r1[x] + mid.centre), put_start)
    mid.smooth(v1a, v1b, range(nx1))

    def coarsened(x):
        return mid.defect(v1b, 2 * x) + mid.defect(v1b, 2 * x + 1), r1[2 * x] + r1[2 * x + 1]

    rows2 = nx2 * ny2

    def put_pooled(x, pair):
        for n in range(2):
            value = mid.pool_rows(pair[n], tmp.at[2 * x + n])
            pooled[pl.ds(n * rows2 + x * ny2, ny2), :] = value

    sweep(range(nx2), coarsened, put_pooled)
    deeper = split_dot(pooled[pl.ds(0, 2 * rows2), :], pool)
    planes = [deeper[n * ny2 : (n + 1) * ny2] for n in range(2 * nx2)]
    values = deep.solve_in_registers(planes[:nx2], planes[nx2:])

    pooled[pl.ds(0, rows2), :] = split_dot(values, spread)

    def refined1(x):
        return mid.spread_rows(pooled[pl.ds(x * ny2, ny2), :], tmp.at[x])

    def put_refined1(x, value):
        for n in range(2):
            v1b[2 * x + n + rim, pl.ds(8, ny1), :] += value

    sweep(range(nx2), refined1, put_refined1)
    mid.smooth(v1b, v1a, range(nx1))
    mid.smooth(v1a, v1b, range(nx1))

    window = own + 2 * rim
    values = v1b[pl.ds(slab * own, window), pl.ds(8, ny1), :].reshape(window * ny1, LANES)
    out_ref[...] = split_dot(values, spread)


def post_kernel(by, chips_y, place, scalar_ref, *refs):
    f, r, w, v1, correction, first_ref, second_ref, kept_ref, sent_ref, va, vb, tmp = refs
    count, ny = f.shape[:2]
    fine = Level(0, ny, LANES, 0, scalars_of(scalar_ref), f, r, w)
    for v in (va, vb):
        zero_rows(v, ny)
    x, half = place[0] // 2 // chips_y, ny // 2
    window = correction.shape[0] // half
    for ref, above in ((first_ref, 1 - x), (second_ref, x)):
        va[pl.ds(1 + above * (SLAB + HALO), NEAR), pl.ds(8, ny), :] = ref[...]

    def refined(x):
        return fine.spread_rows(correction[pl.ds(x * half, half), :], tmp.at[x])

    def put_refined(x, value):
        for at in (2 * x, 2 * x + 1):
            if 0 < at < count - 1:
                known = HALO - NEAR < at < HALO + SLAB + NEAR - 1
                here = v1 if known else va
                va[at, pl.ds(8, ny), :] = here[at, pl.ds(8, ny), :] + value

    sweep(range(window), refined, put_refined)
    fine.smooth(va, vb, range(2, count - 2))
    fine.smooth(vb, va, range(3, count - 3))

    total = jnp.zeros((8, LANES), jnp.float32)
    for x in range(SLAB):
        rest = fine.defect(va, HALO + x)
        total = total + jnp.sum((rest * rest).reshape(ny // 8, 8, LANES), axis=0)
        tmp[x] = rest
    squares = jnp.full((8, LANES), jnp.sum(total), jnp.float32)

    core, area = place[0] & 1, half * SLAB
    for ref, first in ((kept_ref, core * by), (sent_ref, (1 - core) * by)):
        for y in range(half // by):
            row = pl.multiple_of(2 * y * by + first, 8)
            for x in range(SLAB):
                to = x * half + y * by
                ref[pl.ds(to, by), :] = va[HALO + x, pl.ds(8 + row, by), :]
                ref[pl.ds(area + to, by), :] = tmp[x, pl.ds(row, by), :]
        ref[pl.ds(2 * area, 8), :] = squares


def part_rows(bx, by):
    outer = bx * by
    edges = outer + 2 * by
    squares = edges + 2 * (bx - 2)
    return outer, edges, squares, (squares + 8) // 8 * 8


def merge_back_kernel(bx, by, chips_y, place, kept_ref, got_ref, *out_refs):
    chip, core = place[0] // 2, place[0] & 1
    half = chips_y * by
    outer, edges, squares, size = part_rows(bx, by)
    for m, out_ref in enumerate(out_refs):
        target = jnp.bitwise_xor(chip, m)
        first = (target // chips_y) * bx * half + lax.rem(target, chips_y) * by
        for ref, column in ((kept_ref, core), (got_ref, 1 - core)):
            base = pl.multiple_of(column * size, 8)
            for p in range(bx):
                at = pl.multiple_of(first + p * half, 8)
                out_ref[pl.ds(base + p * by, by), :] = ref[pl.ds(at, by), :]
                at = pl.multiple_of(at + SLAB * half, 8)
                if p in (0, bx - 1):
                    out_ref[pl.ds(base + outer + (p > 0) * by, by), :] = ref[pl.ds(at, by), :]
                else:
                    rows = ref[pl.ds(at, by), :]
                    to = base + edges + 2 * (p - 1)
                    out_ref[pl.ds(to, 1), :] = rows[:1]
                    out_ref[pl.ds(to + 1, 1), :] = rows[by - 1 :]
            out_ref[pl.ds(base + squares, 1), :] = ref[pl.ds(2 * SLAB * half, 1), :]


def collect_kernel(place, shifts_ref, index_ref, velocity_ref, source_ref, reaction_ref, *refs):
    parts, (iterate_ref, residual_ref) = refs[:-2], refs[-2:]
    _, bx, by, nz = iterate_ref.shape
    outer, edges, _, size = part_rows(bx, by)
    fine = Level(0, by, nz, 0, (0.0, [velocity_ref[d] for d in range(3)]), None, None, None)
    reaction = [reaction_ref[p] + fine.centre for p in range(1, bx - 1)]
    for m, part in enumerate(parts):
        target = jnp.bitwise_xor(place[0] // 2, m)
        for n in range(2):
            base, column = n * size, 2 * target + n
            shift = shifts_ref[index_ref[column]]
            planes = [part[pl.ds(base + p * by, by), :] for p in range(bx)]
            for p in range(bx):
                iterate_ref[column, p] = planes[p]
            for p in (0, bx - 1):
                residual_ref[column, p] = part[pl.ds(base + outer + (p > 0) * by, by), :]
            for p in range(1, bx - 1):
                here = planes[p]
                pulled = source_ref[column, p] + fine.along_z(here)
                pulled += fine.backward[0] * planes[p - 1] + fine.forward[0] * planes[p + 1]
                pulled += fine.backward[1] * pltpu.roll(here, 1, 0) + fine.forward[1] * pltpu.roll(here, by - 1, 0)
                residual_ref[column, p] = pulled - (reaction[p - 1] + shift) * here
                at = base + edges + 2 * (p - 1)
                residual_ref[column, p, pl.ds(0, 1), :] = part[pl.ds(at, 1), :]
                residual_ref[column, p, pl.ds(by - 1, 1), :] = part[pl.ds(at + 1, 1), :]


def squares_kernel(bx, by, place, *refs):
    parts, out_ref = refs[:-1], refs[-1]
    _, _, squares, size = part_rows(bx, by)
    for m, part in enumerate(parts):
        target = jnp.bitwise_xor(place[0] // 2, m)
        for n in range(2):
            out_ref[pl.ds(2 * target + n, 1), :] = part[pl.ds(n * size + squares, 1), :]


SMEM = pl.BlockSpec(memory_space=pltpu.SMEM)
VMEM = pl.BlockSpec(memory_space=pltpu.VMEM)


def local_kernel(kernel, name, scalars, arrays, outs, scratch=(), in_place=()):
    gy_size = lax.axis_size("gy")
    step = SLAB // HALO

    def placed(*refs):
        along, across = lax.axis_index("gx"), lax.axis_index("gy")
        kernel((lax.rem(along, step) * gy_size + across, along // step), *refs)

    return pl.pallas_call(
        placed,
        out_shape=[jax.ShapeDtypeStruct(shape, jnp.float32) for shape in outs],
        in_specs=[SMEM] * len(scalars) + [VMEM] * len(arrays),
        out_specs=[VMEM] * len(outs),
        scratch_shapes=[pltpu.VMEM(shape, jnp.float32) for shape in scratch],
        input_output_aliases={len(scalars) + n: k for k, n in enumerate(in_place)},
        compiler_params=pltpu.CompilerParams(vmem_limit_bytes=VMEM_LIMIT),
        name=name,
    )(*scalars, *arrays)


def swap_in_plane(pieces, unit):
    devices = lax.axis_size("gx") * lax.axis_size("gy")
    moved = [pieces[0]]
    for k in range(1, len(pieces)):
        pairs = [(i, i ^ (k * unit)) for i in range(devices)]
        moved.append(lax.ppermute(pieces[k], ("gx", "gy"), pairs))
    return moved


def swap_slabs(piece, step, slabs):
    size = lax.axis_size("gx")
    moved = [piece]
    for k in range(1, slabs):
        pairs = [(i, i ^ (step_of(k, slabs) * step)) for i in range(size)]
        moved.append(lax.ppermute(piece, "gx", pairs))
    return moved


def column_body(source, reaction, shifts, shift_index, velocity):
    columns, bx, by, nz = source.shape
    gx_size, gy_size = lax.axis_size("gx"), lax.axis_size("gy")
    nx, ny = bx * gx_size, by * gy_size
    step = columns // gy_size
    slabs = gx_size // step
    count = SLAB + 2 * HALO
    area = bx * by

    chips, chips_y = columns // 2, gy_size // 2
    cores = [(i, i ^ 1) for i in range(gy_size)]
    theirs = [lax.ppermute(source, "gy", cores), lax.ppermute(reaction, "gy", cores)]
    (mine,) = local_kernel(keep_kernel, "keep", (), (source,), [(chips, bx, by, nz)])
    (scalar_rows,) = local_kernel(
        scalars_kernel, "scalars", (shifts, shift_index, velocity), (), [(8, LANES)]
    )
    blocks = local_kernel(
        merge_kernel,
        "merge",
        (),
        (mine, theirs[0], reaction, theirs[1]),
        [(2, bx, 2 * by, nz)] * chips,
    )
    blocks = swap_in_plane(blocks, 2)

    edge = (2, NEAR, ny, nz)
    (own_half,) = local_kernel(
        functools.partial(half_kernel, chips_y),
        "half",
        (),
        blocks[:chips_y],
        [(2, HALO, ny, nz)],
    )
    slab, near = local_kernel(
        functools.partial(arrange_kernel, chips_y),
        "arrange",
        (),
        blocks,
        [(2, SLAB, ny, nz), edge],
    )

    def send_beside(piece, up):
        pairs = [(i, i + step if i % step == up else i - step) for i in range(gx_size)]
        return lax.ppermute(piece, "gx", [(i, j) for i, j in pairs if 0 <= j < gx_size])

    beside = [send_beside(own_half, 1), send_beside(near, 0)]
    grid, rimmed = (count, ny, nz), (count, ny + 16, nz)
    fields = [grid, grid, grid, rimmed, rimmed]
    fields_own = local_kernel(begin_kernel, "begin", (), (scalar_rows, slab), fields)
    f, r, w, _, v1, coarse, beyond = local_kernel(
        functools.partial(pre_kernel, slabs, chips_y),
        "pre",
        (),
        (scalar_rows, *fields_own, *beside, pool_matrix(0), pool_matrix(LANES // 2)),
        fields + [(SLAB // 2, ny // 2, nz), (NEAR, ny, nz)],
        [(SLAB, ny, nz), (2, SLAB // 2 * ny // 2, nz)],
        in_place=range(1, 1 + len(fields)),
    )
    (own_beyond,) = local_kernel(
        functools.partial(beyond_kernel, slabs, chips_y),
        "beyond",
        (),
        (scalar_rows, beside[0]),
        [(NEAR, ny, nz)],
        [(HALO, ny, nz)] * 3 + [(HALO, ny + 16, nz)],
    )
    gathered = swap_slabs(coarse, step, slabs)

    coarse_grid = (nx // 2, ny // 2, nz)
    coarse_rimmed = (nx // 2 + HALO, ny // 2 + 16, nz)
    window = (SLAB // 2 + HALO) * ny // 2
    (correction,) = local_kernel(
        functools.partial(coarse_kernel, (slabs, nx, ny, nz)),
        "coarse",
        (),
        (scalar_rows, pool_matrix(0), spread_matrix(), *gathered),
        [(window, nz)],
        [coarse_grid] * 3 + [coarse_rimmed] * 2 + [(nx // 4 * ny // 2, nz), (nx // 2, ny // 2, nz)],
    )
    result = (SLAB * ny + 8, nz)
    kept, sent = local_kernel(
        functools.partial(post_kernel, by, chips_y),
        "post",
        (),
        (scalar_rows, f, r, w, v1, correction, own_beyond, send_beside(beyond, 0)),
        [result, result],
        [rimmed] * 2 + [(SLAB, ny, nz)],
    )

    parts = local_kernel(
        functools.partial(merge_back_kernel, bx, by, chips_y),
        "merge_back",
        (),
        (kept, lax.ppermute(sent, "gy", cores)),
        [(2 * part_rows(bx, by)[3], nz)] * chips,
    )
    parts = swap_in_plane(parts, 2)
    (squares,) = local_kernel(
        functools.partial(squares_kernel, bx, by), "squares", (), parts, [(columns, nz)]
    )
    iterate, residual = local_kernel(
        collect_kernel,
        "collect",
        (shifts, shift_index, velocity),
        (source, reaction, *parts),
        [source.shape] * 2,
    )
    sums = swap_slabs(squares, step, slabs)
    sums = [*sums[1:], sums[0]]
    while len(sums) > 1:
        sums = [first + second for first, second in zip(sums[::2], sums[1::2])]
    (total,) = sums
    residual_rms = jnp.sqrt(total[:, 0] / (nx * ny * nz) + EPSILON)
    return iterate, residual, residual_rms


def power_of_two(n):
    return n > 0 and n & (n - 1) == 0


def column_plan_fits(columns, bx, by, nz, gx_size, gy_size):
    if columns % gy_size or gx_size % (columns // gy_size):
        return False
    step = columns // gy_size
    slabs, ny = gx_size // step, by * gy_size
    whole = power_of_two(columns) and power_of_two(step) and power_of_two(slabs)
    small = slabs * ny * nz <= 2**15
    paired = step == 2 and bx == HALO and gy_size % 2 == 0
    return whole and small and paired and bx * step == SLAB and nz == LANES and by % 16 == 0


def solution(mesh):
    gx_size, gy_size = mesh.shape["gx"], mesh.shape["gy"]

    def body(source, reaction, shifts, shift_index, velocity):
        fits = column_plan_fits(*source.shape, gx_size, gy_size)
        plan = column_body if fits else halo_body
        return plan(source, reaction, shifts, shift_index, velocity)

    return jax.shard_map(
        body,
        mesh=mesh,
        in_specs=(P(None, "gx", "gy", None), P("gx", "gy", None), P(), P(), P()),
        out_specs=(P(None, "gx", "gy", None), P(None, "gx", "gy", None), P()),
        check_vma=False,
    )
```

```python
import functools

import jax
import jax.numpy as jnp
from jax import lax
from jax.experimental import pallas as pl
from jax.experimental.pallas import tpu as pltpu
from jax.sharding import PartitionSpec as P

LEVELS = 3
COARSE_SWEEPS = 6

DAMPING = 0.8
EPSILON = 1e-06
VMEM_LIMIT = 32 * 1024 * 1024
LANES = 128
GROUP = 4
SLAB = 8
HALO = 4
NEAR = 2


def with_halo(x, sides, width):
    for axis, dim in sides:
        peers, length = (lax.axis_size(axis), x.shape[dim])
        up = [(i, (i + 1) % peers) for i in range(peers - 1)]
        down = [(j, i) for i, j in up]
        last = lax.slice_in_dim(x, length - width, length, axis=dim)
        leading = lax.slice_in_dim(x, 0, width, axis=dim)
        before = lax.ppermute(last, axis, up)
        after = lax.ppermute(leading, axis, down)
        x = jnp.concatenate([before, x, after], axis=dim)
    return x


def select_shifts(shifts, shift_index):
    columns = jnp.arange(shifts.shape[0], dtype=jnp.int32)
    picked = jnp.where(shift_index[:, None] == columns[None, :], shifts[None, :], 0.0)
    return jnp.sum(picked, axis=1)


def coefficients(velocity, spacing):
    scale_a = 1.0 / (spacing * spacing)
    backward = scale_a + jnp.maximum(velocity, 0.0) / spacing
    forward = scale_a - jnp.minimum(velocity, 0.0) / spacing
    centre = 6.0 * scale_a + jnp.sum(jnp.abs(velocity)) / spacing
    return (backward, forward, centre)


def apply_stencil(padded, backward, forward, diagonal):
    middle = padded[:, 1:-1, 1:-1, :]
    along_z = jnp.pad(middle, ((0, 0), (0, 0), (0, 0), (1, 1)))
    others = backward[0] * padded[:, :-2, 1:-1, :] + forward[0] * padded[:, 2:, 1:-1, :]
    others = others + backward[1] * padded[:, 1:-1, :-2, :] + forward[1] * padded[:, 1:-1, 2:, :]
    others = others + backward[2] * along_z[:, :, :, :-2] + forward[2] * along_z[:, :, :, 2:]
    return diagonal * middle - others


def face_halo(iterate):
    return with_halo(iterate, (("gx", 1), ("gy", 2)), 1)


def coarsen(values):
    count, size_x, size_y, size_z = values.shape
    blocks = values.reshape(count, size_x // 2, 2, size_y // 2, 2, size_z // 2, 2)
    return jnp.sum(blocks, axis=(2, 4, 6)) * 0.125


def refine(values):
    return jnp.repeat(jnp.repeat(jnp.repeat(values, 2, 1), 2, 2), 2, 3)


def coarsest_solve(rhs_field, backward, forward, diagonal):
    iterate = DAMPING * rhs_field / diagonal
    for repeat in range(COARSE_SWEEPS - 1):
        applied = apply_stencil(face_halo(iterate), backward, forward, diagonal)
        iterate = iterate + DAMPING * (rhs_field - applied) / diagonal
    return iterate


def multigrid_cycle(level_index, rhs_field, reaction_l, shift_value, velocity):
    backward, forward, centre = coefficients(velocity, 2.0**level_index)
    diagonal = centre + reaction_l + shift_value[:, None, None, None]
    if level_index == LEVELS - 1:
        return coarsest_solve(rhs_field, backward, forward, diagonal)

    def operate(iterate):
        return apply_stencil(face_halo(iterate), backward, forward, diagonal)

    def smooth_step(iterate):
        return iterate + DAMPING * (rhs_field - operate(iterate)) / diagonal

    iterate = DAMPING * rhs_field / diagonal
    iterate = smooth_step(iterate)
    defect = rhs_field - operate(iterate)
    correction = multigrid_cycle(
        level_index + 1, coarsen(defect), coarsen(reaction_l), shift_value, velocity
    )
    iterate = iterate + refine(correction)
    iterate = smooth_step(iterate)
    iterate = smooth_step(iterate)
    return iterate


def halo_body(source, reaction, shifts, shift_index, velocity):
    columns, cells_x, cells_y, cells_z = source.shape
    shift_value = select_shifts(shifts, shift_index)
    reaction_top = reaction[None]
    backward, forward, centre = coefficients(velocity, 1.0)
    diagonal = centre + reaction_top + shift_value[:, None, None, None]

    iterate = multigrid_cycle(0, source, reaction_top, shift_value, velocity)
    residual = source - apply_stencil(face_halo(iterate), backward, forward, diagonal)
    local_squares = jnp.sum(residual * residual, axis=(1, 2, 3))
    squares = lax.psum(local_squares, ("gx", "gy"))
    total_cells = cells_x * cells_y * cells_z * lax.axis_size("gx") * lax.axis_size("gy")
    residual_rms = jnp.sqrt(squares / total_cells + EPSILON)
    return (iterate, residual, residual_rms)


def split_dot(values, matrix):
    high = values.astype(jnp.bfloat16)
    low = (values - high.astype(jnp.float32)).astype(jnp.bfloat16)
    return jnp.dot(high, matrix, preferred_element_type=jnp.float32) + jnp.dot(
        low, matrix, preferred_element_type=jnp.float32
    )


def sweep(planes, get, put):
    planes = list(planes)
    for first in range(0, len(planes), GROUP):
        group = planes[first : first + GROUP]
        values = [get(x) for x in group]
        for x, value in zip(group, values):
            put(x, value)


class Grid:
    def __init__(self, ny):
        self.ny = ny

    def pool_rows(self, value, rows):
        half, ny = self.ny // 2, self.ny
        rows[pl.ds(0, ny), :] = value
        return rows[pl.ds(0, half, stride=2), :] + rows[pl.ds(1, half, stride=2), :]

    def spread_rows(self, part, rows):
        half, ny = self.ny // 2, self.ny
        rows[pl.ds(0, half, stride=2), :] = part
        rows[pl.ds(1, half, stride=2), :] = part
        return rows[pl.ds(0, ny), :]


class Level(Grid):
    def __init__(self, index, ny, nz, rim, scalars, f, r, w):
        super().__init__(ny)
        self.nz, self.rim = nz, rim
        self.f, self.r, self.w = f, r, w
        spacing = 2.0**index
        scale_a = 1.0 / (spacing * spacing)
        inverse = 1.0 / spacing
        shift, speed = scalars
        self.backward = [scale_a + jnp.maximum(v, 0.0) * inverse for v in speed]
        self.forward = [scale_a - jnp.minimum(v, 0.0) * inverse for v in speed]
        total = jnp.abs(speed[0]) + jnp.abs(speed[1]) + jnp.abs(speed[2])
        self.centre = 6.0 * scale_a + total * inverse + shift
        lane = lax.broadcasted_iota(jnp.int32, (1, LANES), 1)
        inside = lane < nz
        self.low_z = jnp.where((lane > 0) & inside, self.backward[2], 0.0)
        self.high_z = jnp.where(lane < nz - 1, self.forward[2], 0.0)

    def plane(self, v, x):
        return v[x + self.rim, pl.ds(8, self.ny), :]

    def put(self, v):
        def write(x, value):
            v[x + self.rim, pl.ds(8, self.ny), :] = value

        return write

    def along_z(self, middle):
        return self.low_z * pltpu.roll(middle, 1, 1) + self.high_z * pltpu.roll(middle, LANES - 1, 1)

    def neighbours(self, v, x, middle):
        at, ny = x + self.rim, self.ny
        along_x = self.backward[0] * v[at - 1, pl.ds(8, ny), :] + self.forward[0] * v[at + 1, pl.ds(8, ny), :]
        along_y = self.backward[1] * v[at, pl.ds(7, ny), :] + self.forward[1] * v[at, pl.ds(9, ny), :]
        return along_x + along_y + self.along_z(middle)

    def smoothed(self, v, x):
        middle = self.plane(v, x)
        pulled = self.f[x] + self.neighbours(v, x, middle)
        return (1.0 - DAMPING) * middle + self.w[x] * pulled

    def smooth(self, src, dst, planes):
        sweep(planes, lambda x: self.smoothed(src, x), self.put(dst))

    def defect(self, v, x):
        middle = self.plane(v, x)
        pulled = self.f[x] + self.neighbours(v, x, middle)
        return pulled - (self.r[x] + self.centre) * middle

    def solve_in_registers(self, rhs, reaction):
        row = lax.broadcasted_iota(jnp.int32, (self.ny, 1), 0)
        low_y = jnp.where(row > 0, self.backward[1], 0.0)
        high_y = jnp.where(row < self.ny - 1, self.forward[1], 0.0)
        weight = [DAMPING / (r + self.centre) for r in reaction]
        v = [w * f for w, f in zip(weight, rhs)]
        for _ in range(COARSE_SWEEPS - 1):
            new = []
            for x, here in enumerate(v):
                along_y = low_y * pltpu.roll(here, 1, 0) + high_y * pltpu.roll(here, self.ny - 1, 0)
                pulled = rhs[x] + self.along_z(here) + along_y
                if x > 0:
                    pulled += self.backward[0] * v[x - 1]
                if x < len(v) - 1:
                    pulled += self.forward[0] * v[x + 1]
                new.append((1.0 - DAMPING) * here + weight[x] * pulled)
            v = new
        return jnp.concatenate(v, axis=0)


def scalars_of(scalar_ref):
    return scalar_ref[pl.ds(0, 1), :], [scalar_ref[pl.ds(1 + d, 1), :] for d in range(3)]


def zero_rows(v, ny):
    edge = jnp.zeros((v.shape[0], 8, LANES), jnp.float32)
    v[:, pl.ds(0, 8), :] = edge
    v[:, pl.ds(8 + ny, 8), :] = edge


def pool_matrix(offset):
    row = lax.broadcasted_iota(jnp.int32, (LANES, LANES), 0)
    col = lax.broadcasted_iota(jnp.int32, (LANES, LANES), 1)
    return jnp.where(row // 2 + offset == col, 0.125, 0.0).astype(jnp.bfloat16)


def spread_matrix():
    row = lax.broadcasted_iota(jnp.int32, (LANES, LANES), 0)
    col = lax.broadcasted_iota(jnp.int32, (LANES, LANES), 1)
    return jnp.where(col // 2 == row, 1.0, 0.0).astype(jnp.bfloat16)


def step_of(k, count):
    return -k % count


def keep_kernel(place, source_ref, out_ref):
    for n in range(out_ref.shape[0]):
        out_ref[n] = source_ref[2 * n + (place[0] & 1)]


def scalars_kernel(place, shifts_ref, index_ref, velocity_ref, scalar_ref):
    rows = {0: shifts_ref[index_ref[place[0]]]}
    rows.update({1 + d: velocity_ref[d] for d in range(3)})
    rows.update({8 + c: shifts_ref[index_ref[c]] for c in range(index_ref.shape[0])})
    for n, scalar in rows.items():
        scalar_ref[pl.ds(n, 1), :] = jnp.full((1, LANES), scalar, jnp.float32)


def merge_kernel(place, mine_ref, theirs_ref, reaction_ref, other_reaction_ref, *out_refs):
    chip, core = place[0] // 2, place[0] & 1
    by = mine_ref.shape[2]
    mine = pl.ds(pl.multiple_of(core * by, 8), by)
    theirs = pl.ds(pl.multiple_of((1 - core) * by, 8), by)
    for m, out_ref in enumerate(out_refs):
        target = jnp.bitwise_xor(chip, m)
        out_ref[0, :, mine, :] = mine_ref[target]
        out_ref[0, :, theirs, :] = theirs_ref[2 * target + core]
        out_ref[1, :, mine, :] = reaction_ref[...]
        out_ref[1, :, theirs, :] = other_reaction_ref[...]


def half_kernel(chips_y, place, *refs):
    blocks, half_ref = refs[:-1], refs[-1]
    for m, block in enumerate(blocks):
        size = block.shape[2]
        chip = jnp.bitwise_xor(place[0] // 2, m)
        rows = pl.ds(pl.multiple_of(lax.rem(chip, chips_y) * size, 8), size)
        half_ref[:, :, rows, :] = block[...]


def arrange_kernel(chips_y, place, *refs):
    blocks, (slab_ref, near_ref) = refs[:-2], refs[-2:]
    chip = place[0] // 2
    for m, block in enumerate(blocks):
        owner = jnp.bitwise_xor(chip, m)
        _, bx, size, _ = block.shape
        planes = pl.ds((owner // chips_y) * bx, bx)
        rows = pl.ds(pl.multiple_of(lax.rem(owner, chips_y) * size, 8), size)
        slab_ref[:, planes, rows, :] = block[...]
    other = 1 - chip // chips_y
    near_ref[...] = slab_ref[:, pl.ds(other * (SLAB - NEAR), NEAR)]


def beyond_kernel(slabs, chips_y, place, scalar_ref, half_ref, out_ref, f, r, w, v0):
    ny, slab = f.shape[1], place[1]
    x = place[0] // 2 // chips_y
    fine = Level(0, ny, LANES, 0, scalars_of(scalar_ref), f, r, w)
    zero_rows(v0, ny)
    f[...], r[...] = half_ref[0], half_ref[1]
    beside = jnp.where(x == 0, slab < slabs - 1, slab > 0)
    inside = jnp.where(beside, DAMPING, 0.0)

    def put(at, weight):
        w[at] = weight
        v0[at, pl.ds(8, ny), :] = weight * f[at]

    sweep(range(HALO), lambda at: inside / (r[at] + fine.centre), put)
    for n in range(NEAR):
        out_ref[n] = fine.smoothed(v0, 1 + n)


def begin_kernel(_, scalar_ref, slab_ref, f, r, w, v0, v1):
    ny = f.shape[1]
    fine = Level(0, ny, LANES, 0, scalars_of(scalar_ref), f, r, w)
    zero_rows(v0, ny)
    zero_rows(v1, ny)
    own = range(HALO, HALO + SLAB)
    f[pl.ds(HALO, SLAB)], r[pl.ds(HALO, SLAB)] = slab_ref[0], slab_ref[1]

    def put(at, weight):
        w[at] = weight
        v0[at, pl.ds(8, ny), :] = weight * f[at]

    sweep(own, lambda at: DAMPING / (r[at] + fine.centre), put)
    fine.smooth(v0, v1, own[1:-1])


def pre_kernel(slabs, chips_y, place, scalar_ref, *refs):
    half_ref, near_ref, pool_ref, pool_up_ref = refs[5:9]
    f, r, w, v0, v1, coarse_ref, beyond_ref, tmp, pooled = refs[9:]
    ny = f.shape[1]
    slab = place[1]
    fine = Level(0, ny, LANES, 0, scalars_of(scalar_ref), f, r, w)
    after = HALO + SLAB

    x = place[0] // 2 // chips_y
    for above, ref, first in ((1 - x, half_ref, x * NEAR), (x, near_ref, 0)):
        planes = pl.ds((HALO - NEAR) + above * (SLAB + NEAR), NEAR)
        f[planes], r[planes] = ref[0, pl.ds(first, NEAR)], ref[1, pl.ds(first, NEAR)]

    below = jnp.where(slab > 0, DAMPING, 0.0)
    above = jnp.where(slab < slabs - 1, DAMPING, 0.0)

    def put(at, weight):
        w[at] = weight
        v0[at, pl.ds(8, ny), :] = weight * f[at]

    beside = [*range(HALO - NEAR, HALO), *range(after, after + NEAR)]
    sweep(beside, lambda at: (below if at < HALO else above) / (r[at] + fine.centre), put)
    fine.smooth(v0, v1, (HALO - 1, HALO, after - 1, after))
    half = ny // 2

    def coarsened(x):
        at = HALO + 2 * x
        return fine.defect(v1, at) + fine.defect(v1, at + 1), r[at] + r[at + 1]

    def put_pooled(x, pair):
        for n in range(2):
            pooled[n, pl.ds(x * half, half), :] = fine.pool_rows(pair[n], tmp.at[2 * x + n])

    sweep(range(SLAB // 2), coarsened, put_pooled)
    packed = split_dot(pooled[0], pool_ref[...]) + split_dot(pooled[1], pool_up_ref[...])
    coarse_ref[...] = packed.reshape(coarse_ref.shape)
    first = HALO + 1 + (1 - x) * (SLAB - HALO)
    beyond_ref[...] = v1[pl.ds(first, NEAR), pl.ds(8, ny), :]


def coarse_kernel(grid, place, scalar_ref, *refs):
    slabs, nx, ny, nz = grid
    pool_ref, spread_ref = refs[:2]
    coarse, out_ref = refs[2 : 2 + slabs], refs[2 + slabs]
    f1, r1, w1, v1a, v1b, pooled, tmp = refs[3 + slabs :]
    pool, spread = pool_ref[...], spread_ref[...]
    slab = place[1]
    rim = HALO // 2
    nx1, ny1, nx2, ny2 = nx // 2, ny // 2, nx // 4, ny // 4
    mid = Level(1, ny1, nz // 2, rim, scalars_of(scalar_ref), f1, r1, w1)
    deep = Level(2, ny2, nz // 4, 0, scalars_of(scalar_ref), None, None, None)
    for v in (v1a, v1b):
        zero_rows(v, ny1)
        blank = jnp.zeros((rim,) + v.shape[1:], jnp.float32)
        v[pl.ds(0, rim)] = blank
        v[pl.ds(rim + nx1, rim)] = blank

    lower = lax.broadcasted_iota(jnp.int32, (1, LANES), 1) < LANES // 2
    own = SLAB // 2
    for k in range(slabs):
        first = jnp.bitwise_xor(slab, step_of(k, slabs)) * own
        both = coarse[k][...]
        f1[pl.ds(first, own)] = jnp.where(lower, both, 0.0)
        r1[pl.ds(first, own)] = jnp.where(lower, pltpu.roll(both, LANES // 2, 2), 0.0)

    def put_start(x, weight):
        w1[x] = weight
        v1a[x + rim, pl.ds(8, ny1), :] = weight * f1[x]

    sweep(range(nx1), lambda x: DAMPING / (r1[x] + mid.centre), put_start)
    mid.smooth(v1a, v1b, range(nx1))

    def coarsened(x):
        return mid.defect(v1b, 2 * x) + mid.defect(v1b, 2 * x + 1), r1[2 * x] + r1[2 * x + 1]

    rows2 = nx2 * ny2

    def put_pooled(x, pair):
        for n in range(2):
            value = mid.pool_rows(pair[n], tmp.at[2 * x + n])
            pooled[pl.ds(n * rows2 + x * ny2, ny2), :] = value

    sweep(range(nx2), coarsened, put_pooled)
    deeper = split_dot(pooled[pl.ds(0, 2 * rows2), :], pool)
    planes = [deeper[n * ny2 : (n + 1) * ny2] for n in range(2 * nx2)]
    values = deep.solve_in_registers(planes[:nx2], planes[nx2:])

    pooled[pl.ds(0, rows2), :] = split_dot(values, spread)

    def refined1(x):
        return mid.spread_rows(pooled[pl.ds(x * ny2, ny2), :], tmp.at[x])

    def put_refined1(x, value):
        for n in range(2):
            v1b[2 * x + n + rim, pl.ds(8, ny1), :] += value

    sweep(range(nx2), refined1, put_refined1)
    mid.smooth(v1b, v1a, range(nx1))
    mid.smooth(v1a, v1b, range(nx1))

    window = own + 2 * rim
    values = v1b[pl.ds(slab * own, window), pl.ds(8, ny1), :].reshape(window * ny1, LANES)
    out_ref[...] = split_dot(values, spread)


def post_kernel(by, chips_y, place, scalar_ref, *refs):
    f, r, w, v1, correction, first_ref, second_ref, kept_ref, sent_ref, va, vb, tmp = refs
    count, ny = f.shape[:2]
    fine = Level(0, ny, LANES, 0, scalars_of(scalar_ref), f, r, w)
    for v in (va, vb):
        zero_rows(v, ny)
    x, half = place[0] // 2 // chips_y, ny // 2
    window = correction.shape[0] // half
    for ref, above in ((first_ref, 1 - x), (second_ref, x)):
        va[pl.ds(1 + above * (SLAB + HALO), NEAR), pl.ds(8, ny), :] = ref[...]

    def refined(x):
        return fine.spread_rows(correction[pl.ds(x * half, half), :], tmp.at[x])

    def put_refined(x, value):
        for at in (2 * x, 2 * x + 1):
            if 0 < at < count - 1:
                known = HALO - NEAR < at < HALO + SLAB + NEAR - 1
                here = v1 if known else va
                va[at, pl.ds(8, ny), :] = here[at, pl.ds(8, ny), :] + value

    sweep(range(window), refined, put_refined)
    fine.smooth(va, vb, range(2, count - 2))
    fine.smooth(vb, va, range(3, count - 3))

    total = jnp.zeros((8, LANES), jnp.float32)
    for x in range(SLAB):
        rest = fine.defect(va, HALO + x)
        total = total + jnp.sum((rest * rest).reshape(ny // 8, 8, LANES), axis=0)
        tmp[x] = rest
    squares = jnp.full((8, LANES), jnp.sum(total), jnp.float32)

    core, area = place[0] & 1, half * SLAB
    for ref, first in ((kept_ref, core * by), (sent_ref, (1 - core) * by)):
        for y in range(half // by):
            row = pl.multiple_of(2 * y * by + first, 8)
            for x in range(SLAB):
                to = x * half + y * by
                ref[pl.ds(to, by), :] = va[HALO + x, pl.ds(8 + row, by), :]
                ref[pl.ds(area + to, by), :] = tmp[x, pl.ds(row, by), :]
        ref[pl.ds(2 * area, 8), :] = squares


def part_rows(bx, by):
    outer = bx * by
    edges = outer + 2 * by
    squares = edges + 2 * (bx - 2)
    return outer, edges, squares, (squares + 8) // 8 * 8


def merge_back_kernel(bx, by, chips_y, place, kept_ref, got_ref, *out_refs):
    chip, core = place[0] // 2, place[0] & 1
    half = chips_y * by
    outer, edges, squares, size = part_rows(bx, by)
    for m, out_ref in enumerate(out_refs):
        target = jnp.bitwise_xor(chip, m)
        first = (target // chips_y) * bx * half + lax.rem(target, chips_y) * by
        for ref, column in ((kept_ref, core), (got_ref, 1 - core)):
            base = pl.multiple_of(column * size, 8)
            for p in range(bx):
                at = pl.multiple_of(first + p * half, 8)
                out_ref[pl.ds(base + p * by, by), :] = ref[pl.ds(at, by), :]
                at = pl.multiple_of(at + SLAB * half, 8)
                if p in (0, bx - 1):
                    out_ref[pl.ds(base + outer + (p > 0) * by, by), :] = ref[pl.ds(at, by), :]
                else:
                    rows = ref[pl.ds(at, by), :]
                    to = base + edges + 2 * (p - 1)
                    out_ref[pl.ds(to, 1), :] = rows[:1]
                    out_ref[pl.ds(to + 1, 1), :] = rows[by - 1 :]
            out_ref[pl.ds(base + squares, 1), :] = ref[pl.ds(2 * SLAB * half, 1), :]


def collect_kernel(place, scalar_ref, source_ref, reaction_ref, *refs):
    parts, (iterate_ref, residual_ref) = refs[:-2], refs[-2:]
    _, bx, by, nz = iterate_ref.shape
    outer, edges, _, size = part_rows(bx, by)
    _, speed = scalars_of(scalar_ref)
    fine = Level(0, by, nz, 0, (0.0, speed), None, None, None)
    reaction = [reaction_ref[p] + fine.centre for p in range(1, bx - 1)]
    for m, part in enumerate(parts):
        target = jnp.bitwise_xor(place[0] // 2, m)
        for n in range(2):
            base, column = n * size, 2 * target + n
            shift = scalar_ref[pl.ds(8 + column, 1), :]
            planes = [part[pl.ds(base + p * by, by), :] for p in range(bx)]
            for p in range(bx):
                iterate_ref[column, p] = planes[p]
            for p in (0, bx - 1):
                residual_ref[column, p] = part[pl.ds(base + outer + (p > 0) * by, by), :]
            for p in range(1, bx - 1):
                here = planes[p]
                pulled = source_ref[column, p] + fine.along_z(here)
                pulled += fine.backward[0] * planes[p - 1] + fine.forward[0] * planes[p + 1]
                pulled += fine.backward[1] * pltpu.roll(here, 1, 0) + fine.forward[1] * pltpu.roll(here, by - 1, 0)
                residual_ref[column, p] = pulled - (reaction[p - 1] + shift) * here
                at = base + edges + 2 * (p - 1)
                residual_ref[column, p, pl.ds(0, 1), :] = part[pl.ds(at, 1), :]
                residual_ref[column, p, pl.ds(by - 1, 1), :] = part[pl.ds(at + 1, 1), :]


def squares_kernel(bx, by, place, *refs):
    parts, out_ref = refs[:-1], refs[-1]
    _, _, squares, size = part_rows(bx, by)
    lane = lax.broadcasted_iota(jnp.int32, (1, LANES), 1)
    row = jnp.zeros((1, LANES), jnp.float32)
    for m, part in enumerate(parts):
        target = jnp.bitwise_xor(place[0] // 2, m)
        for n in range(2):
            row = jnp.where(lane == 2 * target + n, part[pl.ds(n * size + squares, 1), :], row)
    out_ref[...] = row


SMEM = pl.BlockSpec(memory_space=pltpu.SMEM)
VMEM = pl.BlockSpec(memory_space=pltpu.VMEM)


def local_kernel(kernel, name, scalars, arrays, outs, scratch=(), in_place=()):
    gy_size = lax.axis_size("gy")
    step = SLAB // HALO

    def placed(*refs):
        along, across = lax.axis_index("gx"), lax.axis_index("gy")
        kernel((lax.rem(along, step) * gy_size + across, along // step), *refs)

    return pl.pallas_call(
        placed,
        out_shape=[jax.ShapeDtypeStruct(shape, jnp.float32) for shape in outs],
        in_specs=[SMEM] * len(scalars) + [VMEM] * len(arrays),
        out_specs=[VMEM] * len(outs),
        scratch_shapes=[pltpu.VMEM(shape, jnp.float32) for shape in scratch],
        input_output_aliases={len(scalars) + n: k for k, n in enumerate(in_place)},
        compiler_params=pltpu.CompilerParams(vmem_limit_bytes=VMEM_LIMIT),
        name=name,
    )(*scalars, *arrays)


def swap_in_plane(pieces, unit):
    devices = lax.axis_size("gx") * lax.axis_size("gy")
    moved = [pieces[0]]
    for k in range(1, len(pieces)):
        pairs = [(i, i ^ (k * unit)) for i in range(devices)]
        moved.append(lax.ppermute(pieces[k], ("gx", "gy"), pairs))
    return moved


def swap_slabs(piece, step, slabs):
    size = lax.axis_size("gx")
    moved = [piece]
    for k in range(1, slabs):
        pairs = [(i, i ^ (step_of(k, slabs) * step)) for i in range(size)]
        moved.append(lax.ppermute(piece, "gx", pairs))
    return moved


def column_body(source, reaction, shifts, shift_index, velocity):
    columns, bx, by, nz = source.shape
    gx_size, gy_size = lax.axis_size("gx"), lax.axis_size("gy")
    nx, ny = bx * gx_size, by * gy_size
    step = columns // gy_size
    slabs = gx_size // step
    count = SLAB + 2 * HALO
    area = bx * by

    chips, chips_y = columns // 2, gy_size // 2
    cores = [(i, i ^ 1) for i in range(gy_size)]
    theirs = [lax.ppermute(source, "gy", cores), lax.ppermute(reaction, "gy", cores)]
    (mine,) = local_kernel(keep_kernel, "keep", (), (source,), [(chips, bx, by, nz)])
    (scalar_rows,) = local_kernel(
        scalars_kernel, "scalars", (shifts, shift_index, velocity), (), [(8 + columns, LANES)]
    )
    blocks = local_kernel(
        merge_kernel,
        "merge",
        (),
        (mine, theirs[0], reaction, theirs[1]),
        [(2, bx, 2 * by, nz)] * chips,
    )
    blocks = swap_in_plane(blocks, 2)

    edge = (2, NEAR, ny, nz)
    (own_half,) = local_kernel(
        functools.partial(half_kernel, chips_y),
        "half",
        (),
        blocks[:chips_y],
        [(2, HALO, ny, nz)],
    )
    slab, near = local_kernel(
        functools.partial(arrange_kernel, chips_y),
        "arrange",
        (),
        blocks,
        [(2, SLAB, ny, nz), edge],
    )

    def send_beside(piece, up):
        pairs = [(i, i + step if i % step == up else i - step) for i in range(gx_size)]
        return lax.ppermute(piece, "gx", [(i, j) for i, j in pairs if 0 <= j < gx_size])

    beside = [send_beside(own_half, 1), send_beside(near, 0)]
    grid, rimmed = (count, ny, nz), (count, ny + 16, nz)
    fields = [grid, grid, grid, rimmed, rimmed]
    fields_own = local_kernel(begin_kernel, "begin", (), (scalar_rows, slab), fields)
    f, r, w, _, v1, coarse, beyond = local_kernel(
        functools.partial(pre_kernel, slabs, chips_y),
        "pre",
        (),
        (scalar_rows, *fields_own, *beside, pool_matrix(0), pool_matrix(LANES // 2)),
        fields + [(SLAB // 2, ny // 2, nz), (NEAR, ny, nz)],
        [(SLAB, ny, nz), (2, SLAB // 2 * ny // 2, nz)],
        in_place=range(1, 1 + len(fields)),
    )
    (own_beyond,) = local_kernel(
        functools.partial(beyond_kernel, slabs, chips_y),
        "beyond",
        (),
        (scalar_rows, beside[0]),
        [(NEAR, ny, nz)],
        [(HALO, ny, nz)] * 3 + [(HALO, ny + 16, nz)],
    )
    gathered = swap_slabs(coarse, step, slabs)

    coarse_grid = (nx // 2, ny // 2, nz)
    coarse_rimmed = (nx // 2 + HALO, ny // 2 + 16, nz)
    window = (SLAB // 2 + HALO) * ny // 2
    (correction,) = local_kernel(
        functools.partial(coarse_kernel, (slabs, nx, ny, nz)),
        "coarse",
        (),
        (scalar_rows, pool_matrix(0), spread_matrix(), *gathered),
        [(window, nz)],
        [coarse_grid] * 3 + [coarse_rimmed] * 2 + [(nx // 4 * ny // 2, nz), (nx // 2, ny // 2, nz)],
    )
    result = (SLAB * ny + 8, nz)
    kept, sent = local_kernel(
        functools.partial(post_kernel, by, chips_y),
        "post",
        (),
        (scalar_rows, f, r, w, v1, correction, own_beyond, send_beside(beyond, 0)),
        [result, result],
        [rimmed] * 2 + [(SLAB, ny, nz)],
    )

    parts = local_kernel(
        functools.partial(merge_back_kernel, bx, by, chips_y),
        "merge_back",
        (),
        (kept, lax.ppermute(sent, "gy", cores)),
        [(2 * part_rows(bx, by)[3], nz)] * chips,
    )
    parts = swap_in_plane(parts, 2)
    (squares,) = local_kernel(
        functools.partial(squares_kernel, bx, by), "squares", (), parts, [(1, nz)]
    )
    iterate, residual = local_kernel(
        collect_kernel,
        "collect",
        (),
        (scalar_rows, source, reaction, *parts),
        [source.shape] * 2,
    )
    sums = swap_slabs(squares, step, slabs)
    sums = [*sums[1:], sums[0]]
    while len(sums) > 1:
        sums = [first + second for first, second in zip(sums[::2], sums[1::2])]
    (total,) = sums
    residual_rms = jnp.sqrt(total[0, :columns] / (nx * ny * nz) + EPSILON)
    return iterate, residual, residual_rms


def power_of_two(n):
    return n > 0 and n & (n - 1) == 0


def column_plan_fits(columns, bx, by, nz, gx_size, gy_size):
    if columns % gy_size or gx_size % (columns // gy_size):
        return False
    step = columns // gy_size
    slabs, ny = gx_size // step, by * gy_size
    whole = power_of_two(columns) and power_of_two(step) and power_of_two(slabs)
    small = slabs * ny * nz <= 2**15
    paired = step == 2 and bx == HALO and gy_size % 2 == 0
    return whole and small and paired and bx * step == SLAB and nz == LANES and by % 16 == 0


def solution(mesh):
    gx_size, gy_size = mesh.shape["gx"], mesh.shape["gy"]

    def body(source, reaction, shifts, shift_index, velocity):
        fits = column_plan_fits(*source.shape, gx_size, gy_size)
        plan = column_body if fits else halo_body
        return plan(source, reaction, shifts, shift_index, velocity)

    return jax.shard_map(
        body,
        mesh=mesh,
        in_specs=(P(None, "gx", "gy", None), P("gx", "gy", None), P(), P(), P()),
        out_specs=(P(None, "gx", "gy", None), P(None, "gx", "gy", None), P()),
        check_vma=False,
    )
```

```python
import functools

import jax
import jax.numpy as jnp
from jax import lax
from jax.experimental import pallas as pl
from jax.experimental.pallas import tpu as pltpu
from jax.sharding import PartitionSpec as P

LEVELS = 3
COARSE_SWEEPS = 6

DAMPING = 0.8
EPSILON = 1e-06
VMEM_LIMIT = 32 * 1024 * 1024
LANES = 128
GROUP = 4
SLAB = 8
HALO = 4
NEAR = 2


def with_halo(x, sides, width):
    for axis, dim in sides:
        peers, length = (lax.axis_size(axis), x.shape[dim])
        up = [(i, (i + 1) % peers) for i in range(peers - 1)]
        down = [(j, i) for i, j in up]
        last = lax.slice_in_dim(x, length - width, length, axis=dim)
        leading = lax.slice_in_dim(x, 0, width, axis=dim)
        before = lax.ppermute(last, axis, up)
        after = lax.ppermute(leading, axis, down)
        x = jnp.concatenate([before, x, after], axis=dim)
    return x


def select_shifts(shifts, shift_index):
    columns = jnp.arange(shifts.shape[0], dtype=jnp.int32)
    picked = jnp.where(shift_index[:, None] == columns[None, :], shifts[None, :], 0.0)
    return jnp.sum(picked, axis=1)


def coefficients(velocity, spacing):
    scale_a = 1.0 / (spacing * spacing)
    backward = scale_a + jnp.maximum(velocity, 0.0) / spacing
    forward = scale_a - jnp.minimum(velocity, 0.0) / spacing
    centre = 6.0 * scale_a + jnp.sum(jnp.abs(velocity)) / spacing
    return (backward, forward, centre)


def apply_stencil(padded, backward, forward, diagonal):
    middle = padded[:, 1:-1, 1:-1, :]
    along_z = jnp.pad(middle, ((0, 0), (0, 0), (0, 0), (1, 1)))
    others = backward[0] * padded[:, :-2, 1:-1, :] + forward[0] * padded[:, 2:, 1:-1, :]
    others = others + backward[1] * padded[:, 1:-1, :-2, :] + forward[1] * padded[:, 1:-1, 2:, :]
    others = others + backward[2] * along_z[:, :, :, :-2] + forward[2] * along_z[:, :, :, 2:]
    return diagonal * middle - others


def face_halo(iterate):
    return with_halo(iterate, (("gx", 1), ("gy", 2)), 1)


def coarsen(values):
    count, size_x, size_y, size_z = values.shape
    blocks = values.reshape(count, size_x // 2, 2, size_y // 2, 2, size_z // 2, 2)
    return jnp.sum(blocks, axis=(2, 4, 6)) * 0.125


def refine(values):
    return jnp.repeat(jnp.repeat(jnp.repeat(values, 2, 1), 2, 2), 2, 3)


def coarsest_solve(rhs_field, backward, forward, diagonal):
    iterate = DAMPING * rhs_field / diagonal
    for repeat in range(COARSE_SWEEPS - 1):
        applied = apply_stencil(face_halo(iterate), backward, forward, diagonal)
        iterate = iterate + DAMPING * (rhs_field - applied) / diagonal
    return iterate


def multigrid_cycle(level_index, rhs_field, reaction_l, shift_value, velocity):
    backward, forward, centre = coefficients(velocity, 2.0**level_index)
    diagonal = centre + reaction_l + shift_value[:, None, None, None]
    if level_index == LEVELS - 1:
        return coarsest_solve(rhs_field, backward, forward, diagonal)

    def operate(iterate):
        return apply_stencil(face_halo(iterate), backward, forward, diagonal)

    def smooth_step(iterate):
        return iterate + DAMPING * (rhs_field - operate(iterate)) / diagonal

    iterate = DAMPING * rhs_field / diagonal
    iterate = smooth_step(iterate)
    defect = rhs_field - operate(iterate)
    correction = multigrid_cycle(
        level_index + 1, coarsen(defect), coarsen(reaction_l), shift_value, velocity
    )
    iterate = iterate + refine(correction)
    iterate = smooth_step(iterate)
    iterate = smooth_step(iterate)
    return iterate


def halo_body(source, reaction, shifts, shift_index, velocity):
    columns, cells_x, cells_y, cells_z = source.shape
    shift_value = select_shifts(shifts, shift_index)
    reaction_top = reaction[None]
    backward, forward, centre = coefficients(velocity, 1.0)
    diagonal = centre + reaction_top + shift_value[:, None, None, None]

    iterate = multigrid_cycle(0, source, reaction_top, shift_value, velocity)
    residual = source - apply_stencil(face_halo(iterate), backward, forward, diagonal)
    local_squares = jnp.sum(residual * residual, axis=(1, 2, 3))
    squares = lax.psum(local_squares, ("gx", "gy"))
    total_cells = cells_x * cells_y * cells_z * lax.axis_size("gx") * lax.axis_size("gy")
    residual_rms = jnp.sqrt(squares / total_cells + EPSILON)
    return (iterate, residual, residual_rms)


def split_dot(values, matrix):
    high = values.astype(jnp.bfloat16)
    low = (values - high.astype(jnp.float32)).astype(jnp.bfloat16)
    return jnp.dot(high, matrix, preferred_element_type=jnp.float32) + jnp.dot(
        low, matrix, preferred_element_type=jnp.float32
    )


def sweep(planes, get, put, size=GROUP):
    planes = list(planes)
    for first in range(0, len(planes), size):
        group = planes[first : first + size]
        values = [get(x) for x in group]
        for x, value in zip(group, values):
            put(x, value)


class Grid:
    def __init__(self, ny):
        self.ny = ny

    def pool_rows(self, value, rows):
        half, ny = self.ny // 2, self.ny
        rows[pl.ds(0, ny), :] = value
        return rows[pl.ds(0, half, stride=2), :] + rows[pl.ds(1, half, stride=2), :]

    def spread_rows(self, part, rows):
        half, ny = self.ny // 2, self.ny
        rows[pl.ds(0, half, stride=2), :] = part
        rows[pl.ds(1, half, stride=2), :] = part
        return rows[pl.ds(0, ny), :]


class Level(Grid):
    def __init__(self, index, ny, nz, rim, scalars, f, r, w):
        super().__init__(ny)
        self.nz, self.rim = nz, rim
        self.f, self.r, self.w = f, r, w
        spacing = 2.0**index
        scale_a = 1.0 / (spacing * spacing)
        inverse = 1.0 / spacing
        shift, speed = scalars
        self.backward = [scale_a + jnp.maximum(v, 0.0) * inverse for v in speed]
        self.forward = [scale_a - jnp.minimum(v, 0.0) * inverse for v in speed]
        total = jnp.abs(speed[0]) + jnp.abs(speed[1]) + jnp.abs(speed[2])
        self.centre = 6.0 * scale_a + total * inverse + shift
        lane = lax.broadcasted_iota(jnp.int32, (1, LANES), 1)
        inside = lane < nz
        self.low_z = jnp.where((lane > 0) & inside, self.backward[2], 0.0)
        self.high_z = jnp.where(lane < nz - 1, self.forward[2], 0.0)

    def plane(self, v, x):
        return v[x + self.rim, pl.ds(8, self.ny), :]

    def put(self, v):
        def write(x, value):
            v[x + self.rim, pl.ds(8, self.ny), :] = value

        return write

    def along_z(self, middle):
        return self.low_z * pltpu.roll(middle, 1, 1) + self.high_z * pltpu.roll(middle, LANES - 1, 1)

    def neighbours(self, v, x, middle):
        at, ny = x + self.rim, self.ny
        along_x = self.backward[0] * v[at - 1, pl.ds(8, ny), :] + self.forward[0] * v[at + 1, pl.ds(8, ny), :]
        along_y = self.backward[1] * v[at, pl.ds(7, ny), :] + self.forward[1] * v[at, pl.ds(9, ny), :]
        return along_x + along_y + self.along_z(middle)

    def smoothed(self, v, x):
        middle = self.plane(v, x)
        pulled = self.f[x] + self.neighbours(v, x, middle)
        return (1.0 - DAMPING) * middle + self.w[x] * pulled

    def smooth(self, src, dst, planes):
        sweep(planes, lambda x: self.smoothed(src, x), self.put(dst), GROUP * 64 // self.ny)

    def defect(self, v, x):
        middle = self.plane(v, x)
        pulled = self.f[x] + self.neighbours(v, x, middle)
        return pulled - (self.r[x] + self.centre) * middle

    def solve_in_registers(self, rhs, reaction):
        row = lax.broadcasted_iota(jnp.int32, (self.ny, 1), 0)
        low_y = jnp.where(row > 0, self.backward[1], 0.0)
        high_y = jnp.where(row < self.ny - 1, self.forward[1], 0.0)
        weight = [DAMPING / (r + self.centre) for r in reaction]
        v = [w * f for w, f in zip(weight, rhs)]
        for _ in range(COARSE_SWEEPS - 1):
            new = []
            for x, here in enumerate(v):
                along_y = low_y * pltpu.roll(here, 1, 0) + high_y * pltpu.roll(here, self.ny - 1, 0)
                pulled = rhs[x] + self.along_z(here) + along_y
                if x > 0:
                    pulled += self.backward[0] * v[x - 1]
                if x < len(v) - 1:
                    pulled += self.forward[0] * v[x + 1]
                new.append((1.0 - DAMPING) * here + weight[x] * pulled)
            v = new
        return jnp.concatenate(v, axis=0)


def scalars_of(scalar_ref):
    return scalar_ref[pl.ds(0, 1), :], [scalar_ref[pl.ds(1 + d, 1), :] for d in range(3)]


def zero_rows(v, ny):
    edge = jnp.zeros((v.shape[0], 8, LANES), jnp.float32)
    v[:, pl.ds(0, 8), :] = edge
    v[:, pl.ds(8 + ny, 8), :] = edge


def pool_matrix(offset):
    row = lax.broadcasted_iota(jnp.int32, (LANES, LANES), 0)
    col = lax.broadcasted_iota(jnp.int32, (LANES, LANES), 1)
    return jnp.where(row // 2 + offset == col, 0.125, 0.0).astype(jnp.bfloat16)


def spread_matrix():
    row = lax.broadcasted_iota(jnp.int32, (LANES, LANES), 0)
    col = lax.broadcasted_iota(jnp.int32, (LANES, LANES), 1)
    return jnp.where(col // 2 == row, 1.0, 0.0).astype(jnp.bfloat16)


def step_of(k, count):
    return -k % count


def keep_kernel(place, source_ref, reaction_ref, out_ref, kept_ref):
    kept_ref[...] = reaction_ref[...]
    for n in range(out_ref.shape[0]):
        out_ref[n] = source_ref[2 * n + (place[0] & 1)]


def scalars_kernel(place, shifts_ref, index_ref, velocity_ref, scalar_ref):
    rows = {0: shifts_ref[index_ref[place[0]]]}
    rows.update({1 + d: velocity_ref[d] for d in range(3)})
    rows.update({8 + c: shifts_ref[index_ref[c]] for c in range(index_ref.shape[0])})
    for n, scalar in rows.items():
        scalar_ref[pl.ds(n, 1), :] = jnp.full((1, LANES), scalar, jnp.float32)


def merge_kernel(place, mine_ref, theirs_ref, reaction_ref, other_reaction_ref, *out_refs):
    chip, core = place[0] // 2, place[0] & 1
    by = mine_ref.shape[2]
    mine = pl.ds(pl.multiple_of(core * by, 8), by)
    theirs = pl.ds(pl.multiple_of((1 - core) * by, 8), by)
    for m, out_ref in enumerate(out_refs):
        target = jnp.bitwise_xor(chip, m)
        out_ref[0, :, mine, :] = mine_ref[target]
        out_ref[0, :, theirs, :] = theirs_ref[2 * target + core]
        out_ref[1, :, mine, :] = reaction_ref[...]
        out_ref[1, :, theirs, :] = other_reaction_ref[...]


def half_kernel(chips_y, place, *refs):
    blocks, half_ref = refs[:-1], refs[-1]
    for m, block in enumerate(blocks):
        size = block.shape[2]
        chip = jnp.bitwise_xor(place[0] // 2, m)
        rows = pl.ds(pl.multiple_of(lax.rem(chip, chips_y) * size, 8), size)
        half_ref[:, :, rows, :] = block[...]


def arrange_kernel(chips_y, place, *refs):
    blocks, (slab_ref, near_ref) = refs[:-2], refs[-2:]
    chip = place[0] // 2
    for m, block in enumerate(blocks):
        owner = jnp.bitwise_xor(chip, m)
        _, bx, size, _ = block.shape
        planes = pl.ds((owner // chips_y) * bx, bx)
        rows = pl.ds(pl.multiple_of(lax.rem(owner, chips_y) * size, 8), size)
        slab_ref[:, planes, rows, :] = block[...]
    other = 1 - chip // chips_y
    near_ref[...] = slab_ref[:, pl.ds(other * (SLAB - NEAR), NEAR)]


def beyond_kernel(slabs, chips_y, place, scalar_ref, half_ref, out_ref, f, r, w, v0):
    ny, slab = f.shape[1], place[1]
    x = place[0] // 2 // chips_y
    fine = Level(0, ny, LANES, 0, scalars_of(scalar_ref), f, r, w)
    zero_rows(v0, ny)
    f[...], r[...] = half_ref[0], half_ref[1]
    beside = jnp.where(x == 0, slab < slabs - 1, slab > 0)
    inside = jnp.where(beside, DAMPING, 0.0)

    def put(at, weight):
        w[at] = weight
        v0[at, pl.ds(8, ny), :] = weight * f[at]

    sweep(range(HALO), lambda at: inside / (r[at] + fine.centre), put)
    for n in range(NEAR):
        out_ref[n] = fine.smoothed(v0, 1 + n)


def begin_kernel(_, scalar_ref, slab_ref, f, r, w, v0, v1):
    ny = f.shape[1]
    fine = Level(0, ny, LANES, 0, scalars_of(scalar_ref), f, r, w)
    zero_rows(v0, ny)
    zero_rows(v1, ny)
    own = range(HALO, HALO + SLAB)
    f[pl.ds(HALO, SLAB)], r[pl.ds(HALO, SLAB)] = slab_ref[0], slab_ref[1]

    def put(at, weight):
        w[at] = weight
        v0[at, pl.ds(8, ny), :] = weight * f[at]

    sweep(own, lambda at: DAMPING / (r[at] + fine.centre), put)
    fine.smooth(v0, v1, own[1:-1])


def pre_kernel(slabs, chips_y, place, scalar_ref, *refs):
    half_ref, near_ref, pool_ref, pool_up_ref = refs[5:9]
    f, r, w, v0, v1, coarse_ref, beyond_ref, tmp, pooled = refs[9:]
    ny = f.shape[1]
    slab = place[1]
    fine = Level(0, ny, LANES, 0, scalars_of(scalar_ref), f, r, w)
    after = HALO + SLAB

    x = place[0] // 2 // chips_y
    for above, ref, first in ((1 - x, half_ref, x * NEAR), (x, near_ref, 0)):
        planes = pl.ds((HALO - NEAR) + above * (SLAB + NEAR), NEAR)
        f[planes], r[planes] = ref[0, pl.ds(first, NEAR)], ref[1, pl.ds(first, NEAR)]

    below = jnp.where(slab > 0, DAMPING, 0.0)
    above = jnp.where(slab < slabs - 1, DAMPING, 0.0)

    def put(at, weight):
        w[at] = weight
        v0[at, pl.ds(8, ny), :] = weight * f[at]

    beside = [*range(HALO - NEAR, HALO), *range(after, after + NEAR)]
    sweep(beside, lambda at: (below if at < HALO else above) / (r[at] + fine.centre), put)
    fine.smooth(v0, v1, (HALO - 1, HALO, after - 1, after))
    half = ny // 2

    def coarsened(x):
        at = HALO + 2 * x
        return fine.defect(v1, at) + fine.defect(v1, at + 1), r[at] + r[at + 1]

    def put_pooled(x, pair):
        for n in range(2):
            pooled[n, pl.ds(x * half, half), :] = fine.pool_rows(pair[n], tmp.at[2 * x + n])

    sweep(range(SLAB // 2), coarsened, put_pooled)
    packed = split_dot(pooled[0], pool_ref[...]) + split_dot(pooled[1], pool_up_ref[...])
    coarse_ref[...] = packed.reshape(coarse_ref.shape)
    first = HALO + 1 + (1 - x) * (SLAB - HALO)
    beyond_ref[...] = v1[pl.ds(first, NEAR), pl.ds(8, ny), :]


def coarse_kernel(grid, place, scalar_ref, *refs):
    slabs, nx, ny, nz = grid
    pool_ref, spread_ref = refs[:2]
    coarse, out_ref = refs[2 : 2 + slabs], refs[2 + slabs]
    f1, r1, w1, v1a, v1b, pooled, tmp = refs[3 + slabs :]
    pool, spread = pool_ref[...], spread_ref[...]
    slab = place[1]
    rim = HALO // 2
    nx1, ny1, nx2, ny2 = nx // 2, ny // 2, nx // 4, ny // 4
    mid = Level(1, ny1, nz // 2, rim, scalars_of(scalar_ref), f1, r1, w1)
    deep = Level(2, ny2, nz // 4, 0, scalars_of(scalar_ref), None, None, None)
    for v in (v1a, v1b):
        zero_rows(v, ny1)
        blank = jnp.zeros((rim,) + v.shape[1:], jnp.float32)
        v[pl.ds(0, rim)] = blank
        v[pl.ds(rim + nx1, rim)] = blank

    lower = lax.broadcasted_iota(jnp.int32, (1, LANES), 1) < LANES // 2
    own = SLAB // 2
    for k in range(slabs):
        first = jnp.bitwise_xor(slab, step_of(k, slabs)) * own
        both = coarse[k][...]
        f1[pl.ds(first, own)] = jnp.where(lower, both, 0.0)
        r1[pl.ds(first, own)] = jnp.where(lower, pltpu.roll(both, LANES // 2, 2), 0.0)

    def put_start(x, weight):
        w1[x] = weight
        v1a[x + rim, pl.ds(8, ny1), :] = weight * f1[x]

    sweep(range(nx1), lambda x: DAMPING / (r1[x] + mid.centre), put_start, 2 * GROUP)
    mid.smooth(v1a, v1b, range(nx1))

    def coarsened(x):
        return mid.defect(v1b, 2 * x) + mid.defect(v1b, 2 * x + 1), r1[2 * x] + r1[2 * x + 1]

    rows2 = nx2 * ny2

    def put_pooled(x, pair):
        for n in range(2):
            value = mid.pool_rows(pair[n], tmp.at[2 * x + n])
            pooled[pl.ds(n * rows2 + x * ny2, ny2), :] = value

    sweep(range(nx2), coarsened, put_pooled)
    deeper = split_dot(pooled[pl.ds(0, 2 * rows2), :], pool)
    planes = [deeper[n * ny2 : (n + 1) * ny2] for n in range(2 * nx2)]
    values = deep.solve_in_registers(planes[:nx2], planes[nx2:])

    pooled[pl.ds(0, rows2), :] = split_dot(values, spread)

    def refined1(x):
        return mid.spread_rows(pooled[pl.ds(x * ny2, ny2), :], tmp.at[x])

    def put_refined1(x, value):
        for n in range(2):
            v1b[2 * x + n + rim, pl.ds(8, ny1), :] += value

    sweep(range(nx2), refined1, put_refined1)
    mid.smooth(v1b, v1a, range(nx1))
    mid.smooth(v1a, v1b, range(nx1))

    window = own + 2 * rim
    values = v1b[pl.ds(slab * own, window), pl.ds(8, ny1), :].reshape(window * ny1, LANES)
    out_ref[...] = split_dot(values, spread)


def post_kernel(by, chips_y, place, scalar_ref, *refs):
    f, r, w, v1, correction, first_ref, second_ref, kept_ref, sent_ref, va, vb, tmp = refs
    count, ny = f.shape[:2]
    fine = Level(0, ny, LANES, 0, scalars_of(scalar_ref), f, r, w)
    for v in (va, vb):
        zero_rows(v, ny)
    x, half = place[0] // 2 // chips_y, ny // 2
    window = correction.shape[0] // half
    for ref, above in ((first_ref, 1 - x), (second_ref, x)):
        va[pl.ds(1 + above * (SLAB + HALO), NEAR), pl.ds(8, ny), :] = ref[...]

    def refined(x):
        return fine.spread_rows(correction[pl.ds(x * half, half), :], tmp.at[x])

    def put_refined(x, value):
        for at in (2 * x, 2 * x + 1):
            if 0 < at < count - 1:
                known = HALO - NEAR < at < HALO + SLAB + NEAR - 1
                here = v1 if known else va
                va[at, pl.ds(8, ny), :] = here[at, pl.ds(8, ny), :] + value

    sweep(range(window), refined, put_refined)
    fine.smooth(va, vb, range(2, count - 2))
    fine.smooth(vb, va, range(3, count - 3))

    total = jnp.zeros((8, LANES), jnp.float32)
    for x in range(SLAB):
        rest = fine.defect(va, HALO + x)
        total = total + jnp.sum((rest * rest).reshape(ny // 8, 8, LANES), axis=0)
        tmp[x] = rest
    squares = jnp.full((8, LANES), jnp.sum(total), jnp.float32)

    core, area = place[0] & 1, half * SLAB
    for ref, first in ((kept_ref, core * by), (sent_ref, (1 - core) * by)):
        for y in range(half // by):
            row = pl.multiple_of(2 * y * by + first, 8)
            for x in range(SLAB):
                to = x * half + y * by
                ref[pl.ds(to, by), :] = va[HALO + x, pl.ds(8 + row, by), :]
                ref[pl.ds(area + to, by), :] = tmp[x, pl.ds(row, by), :]
        ref[pl.ds(2 * area, 8), :] = squares


def part_rows(bx, by):
    outer = bx * by
    edges = outer + 2 * by
    squares = edges + 2 * (bx - 2)
    return outer, edges, squares, (squares + 8) // 8 * 8


def merge_back_kernel(bx, by, chips_y, place, kept_ref, got_ref, *out_refs):
    chip, core = place[0] // 2, place[0] & 1
    half = chips_y * by
    outer, edges, squares, size = part_rows(bx, by)
    for m, out_ref in enumerate(out_refs):
        target = jnp.bitwise_xor(chip, m)
        first = (target // chips_y) * bx * half + lax.rem(target, chips_y) * by
        for ref, column in ((kept_ref, core), (got_ref, 1 - core)):
            base = pl.multiple_of(column * size, 8)
            for p in range(bx):
                at = pl.multiple_of(first + p * half, 8)
                out_ref[pl.ds(base + p * by, by), :] = ref[pl.ds(at, by), :]
                at = pl.multiple_of(at + SLAB * half, 8)
                if p in (0, bx - 1):
                    out_ref[pl.ds(base + outer + (p > 0) * by, by), :] = ref[pl.ds(at, by), :]
                else:
                    rows = ref[pl.ds(at, by), :]
                    to = base + edges + 2 * (p - 1)
                    out_ref[pl.ds(to, 1), :] = rows[:1]
                    out_ref[pl.ds(to + 1, 1), :] = rows[by - 1 :]
            out_ref[pl.ds(base + squares, 1), :] = ref[pl.ds(2 * SLAB * half, 1), :]


def collect_kernel(place, scalar_ref, source_ref, reaction_ref, *refs):
    parts, (iterate_ref, residual_ref) = refs[:-2], refs[-2:]
    _, bx, by, nz = iterate_ref.shape
    outer, edges, _, size = part_rows(bx, by)
    _, speed = scalars_of(scalar_ref)
    fine = Level(0, by, nz, 0, (0.0, speed), None, None, None)
    reaction = [reaction_ref[p] + fine.centre for p in range(1, bx - 1)]
    for m, part in enumerate(parts):
        target = jnp.bitwise_xor(place[0] // 2, m)
        for n in range(2):
            base, column = n * size, 2 * target + n
            shift = scalar_ref[pl.ds(8 + column, 1), :]
            planes = [part[pl.ds(base + p * by, by), :] for p in range(bx)]
            for p in range(bx):
                iterate_ref[column, p] = planes[p]
            for p in (0, bx - 1):
                residual_ref[column, p] = part[pl.ds(base + outer + (p > 0) * by, by), :]
            for p in range(1, bx - 1):
                here = planes[p]
                pulled = source_ref[column, p] + fine.along_z(here)
                pulled += fine.backward[0] * planes[p - 1] + fine.forward[0] * planes[p + 1]
                pulled += fine.backward[1] * pltpu.roll(here, 1, 0) + fine.forward[1] * pltpu.roll(here, by - 1, 0)
                residual_ref[column, p] = pulled - (reaction[p - 1] + shift) * here
                at = base + edges + 2 * (p - 1)
                residual_ref[column, p, pl.ds(0, 1), :] = part[pl.ds(at, 1), :]
                residual_ref[column, p, pl.ds(by - 1, 1), :] = part[pl.ds(at + 1, 1), :]


def squares_kernel(bx, by, place, *refs):
    parts, out_ref = refs[:-1], refs[-1]
    _, _, squares, size = part_rows(bx, by)
    lane = lax.broadcasted_iota(jnp.int32, (1, LANES), 1)
    row = jnp.zeros((1, LANES), jnp.float32)
    for m, part in enumerate(parts):
        target = jnp.bitwise_xor(place[0] // 2, m)
        for n in range(2):
            row = jnp.where(lane == 2 * target + n, part[pl.ds(n * size + squares, 1), :], row)
    out_ref[...] = row


SMEM = pl.BlockSpec(memory_space=pltpu.SMEM)
VMEM = pl.BlockSpec(memory_space=pltpu.VMEM)


def local_kernel(kernel, name, scalars, arrays, outs, scratch=(), in_place=()):
    gy_size = lax.axis_size("gy")
    step = SLAB // HALO

    def placed(*refs):
        along, across = lax.axis_index("gx"), lax.axis_index("gy")
        kernel((lax.rem(along, step) * gy_size + across, along // step), *refs)

    return pl.pallas_call(
        placed,
        out_shape=[jax.ShapeDtypeStruct(shape, jnp.float32) for shape in outs],
        in_specs=[SMEM] * len(scalars) + [VMEM] * len(arrays),
        out_specs=[VMEM] * len(outs),
        scratch_shapes=[pltpu.VMEM(shape, jnp.float32) for shape in scratch],
        input_output_aliases={len(scalars) + n: k for k, n in enumerate(in_place)},
        compiler_params=pltpu.CompilerParams(vmem_limit_bytes=VMEM_LIMIT),
        name=name,
    )(*scalars, *arrays)


def swap_in_plane(pieces, unit):
    devices = lax.axis_size("gx") * lax.axis_size("gy")
    moved = [pieces[0]]
    for k in range(1, len(pieces)):
        pairs = [(i, i ^ (k * unit)) for i in range(devices)]
        moved.append(lax.ppermute(pieces[k], ("gx", "gy"), pairs))
    return moved


def swap_slabs(piece, step, slabs):
    size = lax.axis_size("gx")
    moved = [piece]
    for k in range(1, slabs):
        pairs = [(i, i ^ (step_of(k, slabs) * step)) for i in range(size)]
        moved.append(lax.ppermute(piece, "gx", pairs))
    return moved


def column_body(source, reaction, shifts, shift_index, velocity):
    columns, bx, by, nz = source.shape
    gx_size, gy_size = lax.axis_size("gx"), lax.axis_size("gy")
    nx, ny = bx * gx_size, by * gy_size
    step = columns // gy_size
    slabs = gx_size // step
    count = SLAB + 2 * HALO
    area = bx * by

    chips, chips_y = columns // 2, gy_size // 2
    cores = [(i, i ^ 1) for i in range(gy_size)]
    theirs = [lax.ppermute(source, "gy", cores), lax.ppermute(reaction, "gy", cores)]
    mine, kept = local_kernel(
        keep_kernel, "keep", (), (source, reaction), [(chips, bx, by, nz), reaction.shape]
    )
    (scalar_rows,) = local_kernel(
        scalars_kernel, "scalars", (shifts, shift_index, velocity), (), [(8 + columns, LANES)]
    )
    blocks = local_kernel(
        merge_kernel,
        "merge",
        (),
        (mine, theirs[0], kept, theirs[1]),
        [(2, bx, 2 * by, nz)] * chips,
    )
    blocks = swap_in_plane(blocks, 2)

    edge = (2, NEAR, ny, nz)
    (own_half,) = local_kernel(
        functools.partial(half_kernel, chips_y),
        "half",
        (),
        blocks[:chips_y],
        [(2, HALO, ny, nz)],
    )
    slab, near = local_kernel(
        functools.partial(arrange_kernel, chips_y),
        "arrange",
        (),
        blocks,
        [(2, SLAB, ny, nz), edge],
    )

    def send_beside(piece, up):
        pairs = [(i, i + step if i % step == up else i - step) for i in range(gx_size)]
        return lax.ppermute(piece, "gx", [(i, j) for i, j in pairs if 0 <= j < gx_size])

    beside = [send_beside(own_half, 1), send_beside(near, 0)]
    grid, rimmed = (count, ny, nz), (count, ny + 16, nz)
    fields = [grid, grid, grid, rimmed, rimmed]
    fields_own = local_kernel(begin_kernel, "begin", (), (scalar_rows, slab), fields)
    f, r, w, _, v1, coarse, beyond = local_kernel(
        functools.partial(pre_kernel, slabs, chips_y),
        "pre",
        (),
        (scalar_rows, *fields_own, *beside, pool_matrix(0), pool_matrix(LANES // 2)),
        fields + [(SLAB // 2, ny // 2, nz), (NEAR, ny, nz)],
        [(SLAB, ny, nz), (2, SLAB // 2 * ny // 2, nz)],
        in_place=range(1, 1 + len(fields)),
    )
    (own_beyond,) = local_kernel(
        functools.partial(beyond_kernel, slabs, chips_y),
        "beyond",
        (),
        (scalar_rows, beside[0]),
        [(NEAR, ny, nz)],
        [(HALO, ny, nz)] * 3 + [(HALO, ny + 16, nz)],
    )
    gathered = swap_slabs(coarse, step, slabs)

    coarse_grid = (nx // 2, ny // 2, nz)
    coarse_rimmed = (nx // 2 + HALO, ny // 2 + 16, nz)
    window = (SLAB // 2 + HALO) * ny // 2
    (correction,) = local_kernel(
        functools.partial(coarse_kernel, (slabs, nx, ny, nz)),
        "coarse",
        (),
        (scalar_rows, pool_matrix(0), spread_matrix(), *gathered),
        [(window, nz)],
        [coarse_grid] * 3 + [coarse_rimmed] * 2 + [(nx // 4 * ny // 2, nz), (nx // 2, ny // 2, nz)],
    )
    result = (SLAB * ny + 8, nz)
    kept, sent = local_kernel(
        functools.partial(post_kernel, by, chips_y),
        "post",
        (),
        (scalar_rows, f, r, w, v1, correction, own_beyond, send_beside(beyond, 0)),
        [result, result],
        [rimmed] * 2 + [(SLAB, ny, nz)],
    )

    parts = local_kernel(
        functools.partial(merge_back_kernel, bx, by, chips_y),
        "merge_back",
        (),
        (kept, lax.ppermute(sent, "gy", cores)),
        [(2 * part_rows(bx, by)[3], nz)] * chips,
    )
    parts = swap_in_plane(parts, 2)
    (squares,) = local_kernel(
        functools.partial(squares_kernel, bx, by), "squares", (), parts, [(1, nz)]
    )
    iterate, residual = local_kernel(
        collect_kernel,
        "collect",
        (),
        (scalar_rows, source, reaction, *parts),
        [source.shape] * 2,
    )
    sums = swap_slabs(squares, step, slabs)
    sums = [*sums[1:], sums[0]]
    while len(sums) > 1:
        sums = [first + second for first, second in zip(sums[::2], sums[1::2])]
    (total,) = sums
    residual_rms = jnp.sqrt(total[0, :columns] / (nx * ny * nz) + EPSILON)
    return iterate, residual, residual_rms


def power_of_two(n):
    return n > 0 and n & (n - 1) == 0


def column_plan_fits(columns, bx, by, nz, gx_size, gy_size):
    if columns % gy_size or gx_size % (columns // gy_size):
        return False
    step = columns // gy_size
    slabs, ny = gx_size // step, by * gy_size
    whole = power_of_two(columns) and power_of_two(step) and power_of_two(slabs)
    small = slabs * ny * nz <= 2**15
    paired = step == 2 and bx == HALO and gy_size % 2 == 0
    return whole and small and paired and bx * step == SLAB and nz == LANES and by % 16 == 0


def solution(mesh):
    gx_size, gy_size = mesh.shape["gx"], mesh.shape["gy"]

    def body(source, reaction, shifts, shift_index, velocity):
        fits = column_plan_fits(*source.shape, gx_size, gy_size)
        plan = column_body if fits else halo_body
        return plan(source, reaction, shifts, shift_index, velocity)

    return jax.shard_map(
        body,
        mesh=mesh,
        in_specs=(P(None, "gx", "gy", None), P("gx", "gy", None), P(), P(), P()),
        out_specs=(P(None, "gx", "gy", None), P(None, "gx", "gy", None), P()),
        check_vma=False,
    )
```

```python
import functools

import jax
import jax.numpy as jnp
from jax import lax
from jax.experimental import pallas as pl
from jax.experimental.pallas import tpu as pltpu
from jax.sharding import PartitionSpec as P

LEVELS = 3
COARSE_SWEEPS = 6

DAMPING = 0.8
EPSILON = 1e-06
VMEM_LIMIT = 32 * 1024 * 1024
LANES = 128
GROUP = 4
SLAB = 8
HALO = 4
NEAR = 2


def with_halo(x, sides, width):
    for axis, dim in sides:
        peers, length = (lax.axis_size(axis), x.shape[dim])
        up = [(i, (i + 1) % peers) for i in range(peers - 1)]
        down = [(j, i) for i, j in up]
        last = lax.slice_in_dim(x, length - width, length, axis=dim)
        leading = lax.slice_in_dim(x, 0, width, axis=dim)
        before = lax.ppermute(last, axis, up)
        after = lax.ppermute(leading, axis, down)
        x = jnp.concatenate([before, x, after], axis=dim)
    return x


def select_shifts(shifts, shift_index):
    columns = jnp.arange(shifts.shape[0], dtype=jnp.int32)
    picked = jnp.where(shift_index[:, None] == columns[None, :], shifts[None, :], 0.0)
    return jnp.sum(picked, axis=1)


def coefficients(velocity, spacing):
    scale_a = 1.0 / (spacing * spacing)
    backward = scale_a + jnp.maximum(velocity, 0.0) / spacing
    forward = scale_a - jnp.minimum(velocity, 0.0) / spacing
    centre = 6.0 * scale_a + jnp.sum(jnp.abs(velocity)) / spacing
    return (backward, forward, centre)


def apply_stencil(padded, backward, forward, diagonal):
    middle = padded[:, 1:-1, 1:-1, :]
    along_z = jnp.pad(middle, ((0, 0), (0, 0), (0, 0), (1, 1)))
    others = backward[0] * padded[:, :-2, 1:-1, :] + forward[0] * padded[:, 2:, 1:-1, :]
    others = others + backward[1] * padded[:, 1:-1, :-2, :] + forward[1] * padded[:, 1:-1, 2:, :]
    others = others + backward[2] * along_z[:, :, :, :-2] + forward[2] * along_z[:, :, :, 2:]
    return diagonal * middle - others


def face_halo(iterate):
    return with_halo(iterate, (("gx", 1), ("gy", 2)), 1)


def coarsen(values):
    count, size_x, size_y, size_z = values.shape
    blocks = values.reshape(count, size_x // 2, 2, size_y // 2, 2, size_z // 2, 2)
    return jnp.sum(blocks, axis=(2, 4, 6)) * 0.125


def refine(values):
    return jnp.repeat(jnp.repeat(jnp.repeat(values, 2, 1), 2, 2), 2, 3)


def coarsest_solve(rhs_field, backward, forward, diagonal):
    iterate = DAMPING * rhs_field / diagonal
    for repeat in range(COARSE_SWEEPS - 1):
        applied = apply_stencil(face_halo(iterate), backward, forward, diagonal)
        iterate = iterate + DAMPING * (rhs_field - applied) / diagonal
    return iterate


def multigrid_cycle(level_index, rhs_field, reaction_l, shift_value, velocity):
    backward, forward, centre = coefficients(velocity, 2.0**level_index)
    diagonal = centre + reaction_l + shift_value[:, None, None, None]
    if level_index == LEVELS - 1:
        return coarsest_solve(rhs_field, backward, forward, diagonal)

    def operate(iterate):
        return apply_stencil(face_halo(iterate), backward, forward, diagonal)

    def smooth_step(iterate):
        return iterate + DAMPING * (rhs_field - operate(iterate)) / diagonal

    iterate = DAMPING * rhs_field / diagonal
    iterate = smooth_step(iterate)
    defect = rhs_field - operate(iterate)
    correction = multigrid_cycle(
        level_index + 1, coarsen(defect), coarsen(reaction_l), shift_value, velocity
    )
    iterate = iterate + refine(correction)
    iterate = smooth_step(iterate)
    iterate = smooth_step(iterate)
    return iterate


def halo_body(source, reaction, shifts, shift_index, velocity):
    columns, cells_x, cells_y, cells_z = source.shape
    shift_value = select_shifts(shifts, shift_index)
    reaction_top = reaction[None]
    backward, forward, centre = coefficients(velocity, 1.0)
    diagonal = centre + reaction_top + shift_value[:, None, None, None]

    iterate = multigrid_cycle(0, source, reaction_top, shift_value, velocity)
    residual = source - apply_stencil(face_halo(iterate), backward, forward, diagonal)
    local_squares = jnp.sum(residual * residual, axis=(1, 2, 3))
    squares = lax.psum(local_squares, ("gx", "gy"))
    total_cells = cells_x * cells_y * cells_z * lax.axis_size("gx") * lax.axis_size("gy")
    residual_rms = jnp.sqrt(squares / total_cells + EPSILON)
    return (iterate, residual, residual_rms)


def split_dot(values, matrix):
    high = values.astype(jnp.bfloat16)
    low = (values - high.astype(jnp.float32)).astype(jnp.bfloat16)
    return jnp.dot(high, matrix, preferred_element_type=jnp.float32) + jnp.dot(
        low, matrix, preferred_element_type=jnp.float32
    )


def sweep(planes, get, put, size=GROUP):
    planes = list(planes)
    for first in range(0, len(planes), size):
        group = planes[first : first + size]
        values = [get(x) for x in group]
        for x, value in zip(group, values):
            put(x, value)


class Grid:
    def __init__(self, ny):
        self.ny = ny

    def pool_rows(self, value, rows):
        half, ny = self.ny // 2, self.ny
        rows[pl.ds(0, ny), :] = value
        return rows[pl.ds(0, half, stride=2), :] + rows[pl.ds(1, half, stride=2), :]

    def spread_rows(self, part, rows):
        half, ny = self.ny // 2, self.ny
        rows[pl.ds(0, half, stride=2), :] = part
        rows[pl.ds(1, half, stride=2), :] = part
        return rows[pl.ds(0, ny), :]


class Level(Grid):
    def __init__(self, index, ny, nz, rim, scalars, f, r, w):
        super().__init__(ny)
        self.nz, self.rim = nz, rim
        self.f, self.r, self.w = f, r, w
        spacing = 2.0**index
        scale_a = 1.0 / (spacing * spacing)
        inverse = 1.0 / spacing
        shift, speed = scalars
        self.backward = [scale_a + jnp.maximum(v, 0.0) * inverse for v in speed]
        self.forward = [scale_a - jnp.minimum(v, 0.0) * inverse for v in speed]
        total = jnp.abs(speed[0]) + jnp.abs(speed[1]) + jnp.abs(speed[2])
        self.centre = 6.0 * scale_a + total * inverse + shift
        lane = lax.broadcasted_iota(jnp.int32, (1, LANES), 1)
        inside = lane < nz
        self.low_z = jnp.where((lane > 0) & inside, self.backward[2], 0.0)
        self.high_z = jnp.where(lane < nz - 1, self.forward[2], 0.0)

    def plane(self, v, x):
        return v[x + self.rim, pl.ds(8, self.ny), :]

    def put(self, v):
        def write(x, value):
            v[x + self.rim, pl.ds(8, self.ny), :] = value

        return write

    def along_z(self, middle):
        return self.low_z * pltpu.roll(middle, 1, 1) + self.high_z * pltpu.roll(middle, LANES - 1, 1)

    def neighbours(self, v, x, middle):
        at, ny = x + self.rim, self.ny
        along_x = self.backward[0] * v[at - 1, pl.ds(8, ny), :] + self.forward[0] * v[at + 1, pl.ds(8, ny), :]
        along_y = self.backward[1] * v[at, pl.ds(7, ny), :] + self.forward[1] * v[at, pl.ds(9, ny), :]
        return along_x + along_y + self.along_z(middle)

    def smoothed(self, v, x):
        middle = self.plane(v, x)
        pulled = self.f[x] + self.neighbours(v, x, middle)
        return (1.0 - DAMPING) * middle + self.w[x] * pulled

    def smooth(self, src, dst, planes):
        sweep(planes, lambda x: self.smoothed(src, x), self.put(dst), GROUP * 64 // self.ny)

    def defect(self, v, x):
        middle = self.plane(v, x)
        pulled = self.f[x] + self.neighbours(v, x, middle)
        return pulled - (self.r[x] + self.centre) * middle

    def solve_in_registers(self, rhs, reaction):
        row = lax.broadcasted_iota(jnp.int32, (self.ny, 1), 0)
        low_y = jnp.where(row > 0, self.backward[1], 0.0)
        high_y = jnp.where(row < self.ny - 1, self.forward[1], 0.0)
        weight = [DAMPING / (r + self.centre) for r in reaction]
        v = [w * f for w, f in zip(weight, rhs)]
        for _ in range(COARSE_SWEEPS - 1):
            new = []
            for x, here in enumerate(v):
                along_y = low_y * pltpu.roll(here, 1, 0) + high_y * pltpu.roll(here, self.ny - 1, 0)
                pulled = rhs[x] + self.along_z(here) + along_y
                if x > 0:
                    pulled += self.backward[0] * v[x - 1]
                if x < len(v) - 1:
                    pulled += self.forward[0] * v[x + 1]
                new.append((1.0 - DAMPING) * here + weight[x] * pulled)
            v = new
        return jnp.concatenate(v, axis=0)


def scalars_of(scalar_ref):
    return scalar_ref[pl.ds(0, 1), :], [scalar_ref[pl.ds(1 + d, 1), :] for d in range(3)]


def zero_rows(v, ny):
    edge = jnp.zeros((v.shape[0], 8, LANES), jnp.float32)
    v[:, pl.ds(0, 8), :] = edge
    v[:, pl.ds(8 + ny, 8), :] = edge


def pool_matrix(offset):
    row = lax.broadcasted_iota(jnp.int32, (LANES, LANES), 0)
    col = lax.broadcasted_iota(jnp.int32, (LANES, LANES), 1)
    return jnp.where(row // 2 + offset == col, 0.125, 0.0).astype(jnp.bfloat16)


def spread_matrix():
    row = lax.broadcasted_iota(jnp.int32, (LANES, LANES), 0)
    col = lax.broadcasted_iota(jnp.int32, (LANES, LANES), 1)
    return jnp.where(col // 2 == row, 1.0, 0.0).astype(jnp.bfloat16)


def step_of(k, count):
    return -k % count


def scalars_kernel(place, shifts_ref, index_ref, velocity_ref, scalar_ref):
    rows = {0: shifts_ref[index_ref[place[0]]]}
    rows.update({1 + d: velocity_ref[d] for d in range(3)})
    rows.update({8 + c: shifts_ref[index_ref[c]] for c in range(index_ref.shape[0])})
    for n, scalar in rows.items():
        scalar_ref[pl.ds(n, 1), :] = jnp.full((1, LANES), scalar, jnp.float32)


def merge_kernel(place, mine_ref, theirs_ref, other_reaction_ref, *out_refs):
    chip, core = place[0] // 2, place[0] & 1
    columns, by = theirs_ref.shape[0], theirs_ref.shape[2]
    mine = pl.ds(pl.multiple_of(core * by, 8), by)
    theirs = pl.ds(pl.multiple_of((1 - core) * by, 8), by)
    for m, out_ref in enumerate(out_refs):
        column = 2 * jnp.bitwise_xor(chip, m) + core
        out_ref[0, :, mine, :] = mine_ref[column]
        out_ref[0, :, theirs, :] = theirs_ref[column]
        out_ref[1, :, mine, :] = mine_ref[columns]
        out_ref[1, :, theirs, :] = other_reaction_ref[...]


def half_kernel(chips_y, place, *refs):
    blocks, half_ref = refs[:-1], refs[-1]
    for m, block in enumerate(blocks):
        size = block.shape[2]
        chip = jnp.bitwise_xor(place[0] // 2, m)
        rows = pl.ds(pl.multiple_of(lax.rem(chip, chips_y) * size, 8), size)
        half_ref[:, :, rows, :] = block[...]


def arrange_kernel(chips_y, place, *refs):
    blocks, (slab_ref, near_ref) = refs[:-2], refs[-2:]
    chip = place[0] // 2
    for m, block in enumerate(blocks):
        owner = jnp.bitwise_xor(chip, m)
        _, bx, size, _ = block.shape
        planes = pl.ds((owner // chips_y) * bx, bx)
        rows = pl.ds(pl.multiple_of(lax.rem(owner, chips_y) * size, 8), size)
        slab_ref[:, planes, rows, :] = block[...]
    other = 1 - chip // chips_y
    near_ref[...] = slab_ref[:, pl.ds(other * (SLAB - NEAR), NEAR)]


def beyond_kernel(slabs, chips_y, place, scalar_ref, half_ref, out_ref, f, r, w, v0):
    ny, slab = f.shape[1], place[1]
    x = place[0] // 2 // chips_y
    fine = Level(0, ny, LANES, 0, scalars_of(scalar_ref), f, r, w)
    zero_rows(v0, ny)
    f[...], r[...] = half_ref[0], half_ref[1]
    beside = jnp.where(x == 0, slab < slabs - 1, slab > 0)
    inside = jnp.where(beside, DAMPING, 0.0)

    def put(at, weight):
        w[at] = weight
        v0[at, pl.ds(8, ny), :] = weight * f[at]

    sweep(range(HALO), lambda at: inside / (r[at] + fine.centre), put)
    for n in range(NEAR):
        out_ref[n] = fine.smoothed(v0, 1 + n)


def begin_kernel(_, scalar_ref, slab_ref, f, r, w, v0, v1):
    ny = f.shape[1]
    fine = Level(0, ny, LANES, 0, scalars_of(scalar_ref), f, r, w)
    zero_rows(v0, ny)
    zero_rows(v1, ny)
    own = range(HALO, HALO + SLAB)
    f[pl.ds(HALO, SLAB)], r[pl.ds(HALO, SLAB)] = slab_ref[0], slab_ref[1]

    def put(at, weight):
        w[at] = weight
        v0[at, pl.ds(8, ny), :] = weight * f[at]

    sweep(own, lambda at: DAMPING / (r[at] + fine.centre), put)
    fine.smooth(v0, v1, own[1:-1])


def pre_kernel(slabs, chips_y, place, scalar_ref, *refs):
    half_ref, near_ref, pool_ref, pool_up_ref = refs[5:9]
    f, r, w, v0, v1, coarse_ref, beyond_ref, tmp, pooled = refs[9:]
    ny = f.shape[1]
    slab = place[1]
    fine = Level(0, ny, LANES, 0, scalars_of(scalar_ref), f, r, w)
    after = HALO + SLAB

    x = place[0] // 2 // chips_y
    for above, ref, first in ((1 - x, half_ref, x * NEAR), (x, near_ref, 0)):
        planes = pl.ds((HALO - NEAR) + above * (SLAB + NEAR), NEAR)
        f[planes], r[planes] = ref[0, pl.ds(first, NEAR)], ref[1, pl.ds(first, NEAR)]

    below = jnp.where(slab > 0, DAMPING, 0.0)
    above = jnp.where(slab < slabs - 1, DAMPING, 0.0)

    def put(at, weight):
        w[at] = weight
        v0[at, pl.ds(8, ny), :] = weight * f[at]

    beside = [*range(HALO - NEAR, HALO), *range(after, after + NEAR)]
    sweep(beside, lambda at: (below if at < HALO else above) / (r[at] + fine.centre), put)
    fine.smooth(v0, v1, (HALO - 1, HALO, after - 1, after))
    half = ny // 2

    def coarsened(x):
        at = HALO + 2 * x
        return fine.defect(v1, at) + fine.defect(v1, at + 1), r[at] + r[at + 1]

    def put_pooled(x, pair):
        for n in range(2):
            pooled[n, pl.ds(x * half, half), :] = fine.pool_rows(pair[n], tmp.at[2 * x + n])

    sweep(range(SLAB // 2), coarsened, put_pooled)
    packed = split_dot(pooled[0], pool_ref[...]) + split_dot(pooled[1], pool_up_ref[...])
    coarse_ref[...] = packed.reshape(coarse_ref.shape)
    first = HALO + 1 + (1 - x) * (SLAB - HALO)
    beyond_ref[...] = v1[pl.ds(first, NEAR), pl.ds(8, ny), :]


def coarse_kernel(grid, place, scalar_ref, *refs):
    slabs, nx, ny, nz = grid
    pool_ref, spread_ref = refs[:2]
    coarse, out_ref = refs[2 : 2 + slabs], refs[2 + slabs]
    f1, r1, w1, v1a, v1b, pooled, tmp = refs[3 + slabs :]
    pool, spread = pool_ref[...], spread_ref[...]
    slab = place[1]
    rim = HALO // 2
    nx1, ny1, nx2, ny2 = nx // 2, ny // 2, nx // 4, ny // 4
    mid = Level(1, ny1, nz // 2, rim, scalars_of(scalar_ref), f1, r1, w1)
    deep = Level(2, ny2, nz // 4, 0, scalars_of(scalar_ref), None, None, None)
    for v in (v1a, v1b):
        zero_rows(v, ny1)
        blank = jnp.zeros((rim,) + v.shape[1:], jnp.float32)
        v[pl.ds(0, rim)] = blank
        v[pl.ds(rim + nx1, rim)] = blank

    lower = lax.broadcasted_iota(jnp.int32, (1, LANES), 1) < LANES // 2
    own = SLAB // 2
    for k in range(slabs):
        first = jnp.bitwise_xor(slab, step_of(k, slabs)) * own
        both = coarse[k][...]
        f1[pl.ds(first, own)] = jnp.where(lower, both, 0.0)
        r1[pl.ds(first, own)] = jnp.where(lower, pltpu.roll(both, LANES // 2, 2), 0.0)

    def put_start(x, weight):
        w1[x] = weight
        v1a[x + rim, pl.ds(8, ny1), :] = weight * f1[x]

    sweep(range(nx1), lambda x: DAMPING / (r1[x] + mid.centre), put_start, 2 * GROUP)
    mid.smooth(v1a, v1b, range(nx1))

    def coarsened(x):
        return mid.defect(v1b, 2 * x) + mid.defect(v1b, 2 * x + 1), r1[2 * x] + r1[2 * x + 1]

    rows2 = nx2 * ny2

    def put_pooled(x, pair):
        for n in range(2):
            value = mid.pool_rows(pair[n], tmp.at[2 * x + n])
            pooled[pl.ds(n * rows2 + x * ny2, ny2), :] = value

    sweep(range(nx2), coarsened, put_pooled)
    deeper = split_dot(pooled[pl.ds(0, 2 * rows2), :], pool)
    planes = [deeper[n * ny2 : (n + 1) * ny2] for n in range(2 * nx2)]
    values = deep.solve_in_registers(planes[:nx2], planes[nx2:])

    pooled[pl.ds(0, rows2), :] = split_dot(values, spread)

    def refined1(x):
        return mid.spread_rows(pooled[pl.ds(x * ny2, ny2), :], tmp.at[x])

    def put_refined1(x, value):
        for n in range(2):
            v1b[2 * x + n + rim, pl.ds(8, ny1), :] += value

    sweep(range(nx2), refined1, put_refined1)
    mid.smooth(v1b, v1a, range(nx1))
    mid.smooth(v1a, v1b, range(nx1))

    window = own + 2 * rim
    values = v1b[pl.ds(slab * own, window), pl.ds(8, ny1), :].reshape(window * ny1, LANES)
    out_ref[...] = split_dot(values, spread)


def post_kernel(by, chips_y, place, scalar_ref, *refs):
    f, r, w, v1, correction, first_ref, second_ref, kept_ref, sent_ref, va, vb, tmp = refs
    count, ny = f.shape[:2]
    fine = Level(0, ny, LANES, 0, scalars_of(scalar_ref), f, r, w)
    for v in (va, vb):
        zero_rows(v, ny)
    x, half = place[0] // 2 // chips_y, ny // 2
    window = correction.shape[0] // half
    for ref, above in ((first_ref, 1 - x), (second_ref, x)):
        va[pl.ds(1 + above * (SLAB + HALO), NEAR), pl.ds(8, ny), :] = ref[...]

    def refined(x):
        return fine.spread_rows(correction[pl.ds(x * half, half), :], tmp.at[x])

    def put_refined(x, value):
        for at in (2 * x, 2 * x + 1):
            if 0 < at < count - 1:
                known = HALO - NEAR < at < HALO + SLAB + NEAR - 1
                here = v1 if known else va
                va[at, pl.ds(8, ny), :] = here[at, pl.ds(8, ny), :] + value

    sweep(range(window), refined, put_refined)
    fine.smooth(va, vb, range(2, count - 2))
    fine.smooth(vb, va, range(3, count - 3))

    total = jnp.zeros((8, LANES), jnp.float32)
    for x in range(SLAB):
        rest = fine.defect(va, HALO + x)
        total = total + jnp.sum((rest * rest).reshape(ny // 8, 8, LANES), axis=0)
        tmp[x] = rest
    squares = jnp.full((8, LANES), jnp.sum(total), jnp.float32)

    core, area = place[0] & 1, half * SLAB
    for ref, first in ((kept_ref, core * by), (sent_ref, (1 - core) * by)):
        for y in range(half // by):
            row = pl.multiple_of(2 * y * by + first, 8)
            for x in range(SLAB):
                to = x * half + y * by
                ref[pl.ds(to, by), :] = va[HALO + x, pl.ds(8 + row, by), :]
                ref[pl.ds(area + to, by), :] = tmp[x, pl.ds(row, by), :]
        ref[pl.ds(2 * area, 8), :] = squares


def part_rows(bx, by):
    outer = bx * by
    edges = outer + 2 * by
    squares = edges + 2 * (bx - 2)
    return outer, edges, squares, (squares + 8) // 8 * 8


def merge_back_kernel(bx, by, chips_y, place, kept_ref, got_ref, *out_refs):
    chip, core = place[0] // 2, place[0] & 1
    half = chips_y * by
    outer, edges, squares, size = part_rows(bx, by)
    for m, out_ref in enumerate(out_refs):
        target = jnp.bitwise_xor(chip, m)
        first = (target // chips_y) * bx * half + lax.rem(target, chips_y) * by
        for ref, column in ((kept_ref, core), (got_ref, 1 - core)):
            base = pl.multiple_of(column * size, 8)
            for p in range(bx):
                at = pl.multiple_of(first + p * half, 8)
                out_ref[pl.ds(base + p * by, by), :] = ref[pl.ds(at, by), :]
                at = pl.multiple_of(at + SLAB * half, 8)
                if p in (0, bx - 1):
                    out_ref[pl.ds(base + outer + (p > 0) * by, by), :] = ref[pl.ds(at, by), :]
                else:
                    rows = ref[pl.ds(at, by), :]
                    to = base + edges + 2 * (p - 1)
                    out_ref[pl.ds(to, 1), :] = rows[:1]
                    out_ref[pl.ds(to + 1, 1), :] = rows[by - 1 :]
            out_ref[pl.ds(base + squares, 1), :] = ref[pl.ds(2 * SLAB * half, 1), :]


def collect_kernel(place, scalar_ref, source_ref, reaction_ref, *refs):
    parts, (iterate_ref, residual_ref) = refs[:-2], refs[-2:]
    _, bx, by, nz = iterate_ref.shape
    outer, edges, _, size = part_rows(bx, by)
    _, speed = scalars_of(scalar_ref)
    fine = Level(0, by, nz, 0, (0.0, speed), None, None, None)
    reaction = [reaction_ref[p] + fine.centre for p in range(1, bx - 1)]
    for m, part in enumerate(parts):
        target = jnp.bitwise_xor(place[0] // 2, m)
        for n in range(2):
            base, column = n * size, 2 * target + n
            shift = scalar_ref[pl.ds(8 + column, 1), :]
            planes = [part[pl.ds(base + p * by, by), :] for p in range(bx)]
            for p in range(bx):
                iterate_ref[column, p] = planes[p]
            for p in (0, bx - 1):
                residual_ref[column, p] = part[pl.ds(base + outer + (p > 0) * by, by), :]
            for p in range(1, bx - 1):
                here = planes[p]
                pulled = source_ref[column, p] + fine.along_z(here)
                pulled += fine.backward[0] * planes[p - 1] + fine.forward[0] * planes[p + 1]
                pulled += fine.backward[1] * pltpu.roll(here, 1, 0) + fine.forward[1] * pltpu.roll(here, by - 1, 0)
                residual_ref[column, p] = pulled - (reaction[p - 1] + shift) * here
                at = base + edges + 2 * (p - 1)
                residual_ref[column, p, pl.ds(0, 1), :] = part[pl.ds(at, 1), :]
                residual_ref[column, p, pl.ds(by - 1, 1), :] = part[pl.ds(at + 1, 1), :]


def squares_kernel(bx, by, place, *refs):
    parts, out_ref = refs[:-1], refs[-1]
    _, _, squares, size = part_rows(bx, by)
    lane = lax.broadcasted_iota(jnp.int32, (1, LANES), 1)
    row = jnp.zeros((1, LANES), jnp.float32)
    for m, part in enumerate(parts):
        target = jnp.bitwise_xor(place[0] // 2, m)
        for n in range(2):
            row = jnp.where(lane == 2 * target + n, part[pl.ds(n * size + squares, 1), :], row)
    out_ref[...] = row


SMEM = pl.BlockSpec(memory_space=pltpu.SMEM)
VMEM = pl.BlockSpec(memory_space=pltpu.VMEM)


def local_kernel(kernel, name, scalars, arrays, outs, scratch=(), in_place=()):
    gy_size = lax.axis_size("gy")
    step = SLAB // HALO

    def placed(*refs):
        along, across = lax.axis_index("gx"), lax.axis_index("gy")
        kernel((lax.rem(along, step) * gy_size + across, along // step), *refs)

    return pl.pallas_call(
        placed,
        out_shape=[jax.ShapeDtypeStruct(shape, jnp.float32) for shape in outs],
        in_specs=[SMEM] * len(scalars) + [VMEM] * len(arrays),
        out_specs=[VMEM] * len(outs),
        scratch_shapes=[pltpu.VMEM(shape, jnp.float32) for shape in scratch],
        input_output_aliases={len(scalars) + n: k for k, n in enumerate(in_place)},
        compiler_params=pltpu.CompilerParams(vmem_limit_bytes=VMEM_LIMIT),
        name=name,
    )(*scalars, *arrays)


def swap_in_plane(pieces, unit):
    devices = lax.axis_size("gx") * lax.axis_size("gy")
    moved = [pieces[0]]
    for k in range(1, len(pieces)):
        pairs = [(i, i ^ (k * unit)) for i in range(devices)]
        moved.append(lax.ppermute(pieces[k], ("gx", "gy"), pairs))
    return moved


def swap_slabs(piece, step, slabs):
    size = lax.axis_size("gx")
    moved = [piece]
    for k in range(1, slabs):
        pairs = [(i, i ^ (step_of(k, slabs) * step)) for i in range(size)]
        moved.append(lax.ppermute(piece, "gx", pairs))
    return moved


def column_body(source, reaction, shifts, shift_index, velocity):
    columns, bx, by, nz = source.shape
    gx_size, gy_size = lax.axis_size("gx"), lax.axis_size("gy")
    nx, ny = bx * gx_size, by * gy_size
    step = columns // gy_size
    slabs = gx_size // step
    count = SLAB + 2 * HALO
    area = bx * by

    chips, chips_y = columns // 2, gy_size // 2
    cores = [(i, i ^ 1) for i in range(gy_size)]
    theirs = [lax.ppermute(source, "gy", cores), lax.ppermute(reaction, "gy", cores)]
    mine = jnp.concatenate([source, reaction[None]])
    (scalar_rows,) = local_kernel(
        scalars_kernel, "scalars", (shifts, shift_index, velocity), (), [(8 + columns, LANES)]
    )
    blocks = local_kernel(
        merge_kernel,
        "merge",
        (),
        (mine, *theirs),
        [(2, bx, 2 * by, nz)] * chips,
    )
    blocks = swap_in_plane(blocks, 2)

    edge = (2, NEAR, ny, nz)
    (own_half,) = local_kernel(
        functools.partial(half_kernel, chips_y),
        "half",
        (),
        blocks[:chips_y],
        [(2, HALO, ny, nz)],
    )
    slab, near = local_kernel(
        functools.partial(arrange_kernel, chips_y),
        "arrange",
        (),
        blocks,
        [(2, SLAB, ny, nz), edge],
    )

    def send_beside(piece, up):
        pairs = [(i, i + step if i % step == up else i - step) for i in range(gx_size)]
        return lax.ppermute(piece, "gx", [(i, j) for i, j in pairs if 0 <= j < gx_size])

    beside = [send_beside(own_half, 1), send_beside(near, 0)]
    grid, rimmed = (count, ny, nz), (count, ny + 16, nz)
    fields = [grid, grid, grid, rimmed, rimmed]
    fields_own = local_kernel(begin_kernel, "begin", (), (scalar_rows, slab), fields)
    f, r, w, _, v1, coarse, beyond = local_kernel(
        functools.partial(pre_kernel, slabs, chips_y),
        "pre",
        (),
        (scalar_rows, *fields_own, *beside, pool_matrix(0), pool_matrix(LANES // 2)),
        fields + [(SLAB // 2, ny // 2, nz), (NEAR, ny, nz)],
        [(SLAB, ny, nz), (2, SLAB // 2 * ny // 2, nz)],
        in_place=range(1, 1 + len(fields)),
    )
    (own_beyond,) = local_kernel(
        functools.partial(beyond_kernel, slabs, chips_y),
        "beyond",
        (),
        (scalar_rows, beside[0]),
        [(NEAR, ny, nz)],
        [(HALO, ny, nz)] * 3 + [(HALO, ny + 16, nz)],
    )
    gathered = swap_slabs(coarse, step, slabs)

    coarse_grid = (nx // 2, ny // 2, nz)
    coarse_rimmed = (nx // 2 + HALO, ny // 2 + 16, nz)
    window = (SLAB // 2 + HALO) * ny // 2
    (correction,) = local_kernel(
        functools.partial(coarse_kernel, (slabs, nx, ny, nz)),
        "coarse",
        (),
        (scalar_rows, pool_matrix(0), spread_matrix(), *gathered),
        [(window, nz)],
        [coarse_grid] * 3 + [coarse_rimmed] * 2 + [(nx // 4 * ny // 2, nz), (nx // 2, ny // 2, nz)],
    )
    result = (SLAB * ny + 8, nz)
    kept, sent = local_kernel(
        functools.partial(post_kernel, by, chips_y),
        "post",
        (),
        (scalar_rows, f, r, w, v1, correction, own_beyond, send_beside(beyond, 0)),
        [result, result],
        [rimmed] * 2 + [(SLAB, ny, nz)],
    )

    parts = local_kernel(
        functools.partial(merge_back_kernel, bx, by, chips_y),
        "merge_back",
        (),
        (kept, lax.ppermute(sent, "gy", cores)),
        [(2 * part_rows(bx, by)[3], nz)] * chips,
    )
    parts = swap_in_plane(parts, 2)
    (squares,) = local_kernel(
        functools.partial(squares_kernel, bx, by), "squares", (), parts, [(1, nz)]
    )
    iterate, residual = local_kernel(
        collect_kernel,
        "collect",
        (),
        (scalar_rows, source, reaction, *parts),
        [source.shape] * 2,
    )
    sums = swap_slabs(squares, step, slabs)
    sums = [*sums[1:], sums[0]]
    while len(sums) > 1:
        sums = [first + second for first, second in zip(sums[::2], sums[1::2])]
    (total,) = sums
    residual_rms = jnp.sqrt(total[0, :columns] / (nx * ny * nz) + EPSILON)
    return iterate, residual, residual_rms


def power_of_two(n):
    return n > 0 and n & (n - 1) == 0


def column_plan_fits(columns, bx, by, nz, gx_size, gy_size):
    if columns % gy_size or gx_size % (columns // gy_size):
        return False
    step = columns // gy_size
    slabs, ny = gx_size // step, by * gy_size
    whole = power_of_two(columns) and power_of_two(step) and power_of_two(slabs)
    small = slabs * ny * nz <= 2**15
    paired = step == 2 and bx == HALO and gy_size % 2 == 0
    return whole and small and paired and bx * step == SLAB and nz == LANES and by % 16 == 0


def solution(mesh):
    gx_size, gy_size = mesh.shape["gx"], mesh.shape["gy"]

    def body(source, reaction, shifts, shift_index, velocity):
        fits = column_plan_fits(*source.shape, gx_size, gy_size)
        plan = column_body if fits else halo_body
        return plan(source, reaction, shifts, shift_index, velocity)

    return jax.shard_map(
        body,
        mesh=mesh,
        in_specs=(P(None, "gx", "gy", None), P("gx", "gy", None), P(), P(), P()),
        out_specs=(P(None, "gx", "gy", None), P(None, "gx", "gy", None), P()),
        check_vma=False,
    )
```

```python
import functools

import jax
import jax.numpy as jnp
from jax import lax
from jax.experimental import pallas as pl
from jax.experimental.pallas import tpu as pltpu
from jax.sharding import PartitionSpec as P

LEVELS = 3
COARSE_SWEEPS = 6

DAMPING = 0.8
EPSILON = 1e-06
VMEM_LIMIT = 32 * 1024 * 1024
LANES = 128
GROUP = 4
SLAB = 8
HALO = 4
NEAR = 2


def with_halo(x, sides, width):
    for axis, dim in sides:
        peers, length = (lax.axis_size(axis), x.shape[dim])
        up = [(i, (i + 1) % peers) for i in range(peers - 1)]
        down = [(j, i) for i, j in up]
        last = lax.slice_in_dim(x, length - width, length, axis=dim)
        leading = lax.slice_in_dim(x, 0, width, axis=dim)
        before = lax.ppermute(last, axis, up)
        after = lax.ppermute(leading, axis, down)
        x = jnp.concatenate([before, x, after], axis=dim)
    return x


def select_shifts(shifts, shift_index):
    columns = jnp.arange(shifts.shape[0], dtype=jnp.int32)
    picked = jnp.where(shift_index[:, None] == columns[None, :], shifts[None, :], 0.0)
    return jnp.sum(picked, axis=1)


def coefficients(velocity, spacing):
    scale_a = 1.0 / (spacing * spacing)
    backward = scale_a + jnp.maximum(velocity, 0.0) / spacing
    forward = scale_a - jnp.minimum(velocity, 0.0) / spacing
    centre = 6.0 * scale_a + jnp.sum(jnp.abs(velocity)) / spacing
    return (backward, forward, centre)


def apply_stencil(padded, backward, forward, diagonal):
    middle = padded[:, 1:-1, 1:-1, :]
    along_z = jnp.pad(middle, ((0, 0), (0, 0), (0, 0), (1, 1)))
    others = backward[0] * padded[:, :-2, 1:-1, :] + forward[0] * padded[:, 2:, 1:-1, :]
    others = others + backward[1] * padded[:, 1:-1, :-2, :] + forward[1] * padded[:, 1:-1, 2:, :]
    others = others + backward[2] * along_z[:, :, :, :-2] + forward[2] * along_z[:, :, :, 2:]
    return diagonal * middle - others


def face_halo(iterate):
    return with_halo(iterate, (("gx", 1), ("gy", 2)), 1)


def coarsen(values):
    count, size_x, size_y, size_z = values.shape
    blocks = values.reshape(count, size_x // 2, 2, size_y // 2, 2, size_z // 2, 2)
    return jnp.sum(blocks, axis=(2, 4, 6)) * 0.125


def refine(values):
    return jnp.repeat(jnp.repeat(jnp.repeat(values, 2, 1), 2, 2), 2, 3)


def coarsest_solve(rhs_field, backward, forward, diagonal):
    iterate = DAMPING * rhs_field / diagonal
    for repeat in range(COARSE_SWEEPS - 1):
        applied = apply_stencil(face_halo(iterate), backward, forward, diagonal)
        iterate = iterate + DAMPING * (rhs_field - applied) / diagonal
    return iterate


def multigrid_cycle(level_index, rhs_field, reaction_l, shift_value, velocity):
    backward, forward, centre = coefficients(velocity, 2.0**level_index)
    diagonal = centre + reaction_l + shift_value[:, None, None, None]
    if level_index == LEVELS - 1:
        return coarsest_solve(rhs_field, backward, forward, diagonal)

    def operate(iterate):
        return apply_stencil(face_halo(iterate), backward, forward, diagonal)

    def smooth_step(iterate):
        return iterate + DAMPING * (rhs_field - operate(iterate)) / diagonal

    iterate = DAMPING * rhs_field / diagonal
    iterate = smooth_step(iterate)
    defect = rhs_field - operate(iterate)
    correction = multigrid_cycle(
        level_index + 1, coarsen(defect), coarsen(reaction_l), shift_value, velocity
    )
    iterate = iterate + refine(correction)
    iterate = smooth_step(iterate)
    iterate = smooth_step(iterate)
    return iterate


def halo_body(source, reaction, shifts, shift_index, velocity):
    columns, cells_x, cells_y, cells_z = source.shape
    shift_value = select_shifts(shifts, shift_index)
    reaction_top = reaction[None]
    backward, forward, centre = coefficients(velocity, 1.0)
    diagonal = centre + reaction_top + shift_value[:, None, None, None]

    iterate = multigrid_cycle(0, source, reaction_top, shift_value, velocity)
    residual = source - apply_stencil(face_halo(iterate), backward, forward, diagonal)
    local_squares = jnp.sum(residual * residual, axis=(1, 2, 3))
    squares = lax.psum(local_squares, ("gx", "gy"))
    total_cells = cells_x * cells_y * cells_z * lax.axis_size("gx") * lax.axis_size("gy")
    residual_rms = jnp.sqrt(squares / total_cells + EPSILON)
    return (iterate, residual, residual_rms)


def split_dot(values, matrix):
    high = values.astype(jnp.bfloat16)
    low = (values - high.astype(jnp.float32)).astype(jnp.bfloat16)
    return jnp.dot(high, matrix, preferred_element_type=jnp.float32) + jnp.dot(
        low, matrix, preferred_element_type=jnp.float32
    )


def sweep(planes, get, put, size=GROUP):
    planes = list(planes)
    for first in range(0, len(planes), size):
        group = planes[first : first + size]
        values = [get(x) for x in group]
        for x, value in zip(group, values):
            put(x, value)


class Grid:
    def __init__(self, ny):
        self.ny = ny

    def pool_rows(self, value, rows):
        half, ny = self.ny // 2, self.ny
        rows[pl.ds(0, ny), :] = value
        return rows[pl.ds(0, half, stride=2), :] + rows[pl.ds(1, half, stride=2), :]

    def spread_rows(self, part, rows):
        half, ny = self.ny // 2, self.ny
        rows[pl.ds(0, half, stride=2), :] = part
        rows[pl.ds(1, half, stride=2), :] = part
        return rows[pl.ds(0, ny), :]


class Level(Grid):
    def __init__(self, index, ny, nz, rim, scalars, f, r, w):
        super().__init__(ny)
        self.nz, self.rim = nz, rim
        self.f, self.r, self.w = f, r, w
        spacing = 2.0**index
        scale_a = 1.0 / (spacing * spacing)
        inverse = 1.0 / spacing
        shift, speed = scalars
        self.backward = [scale_a + jnp.maximum(v, 0.0) * inverse for v in speed]
        self.forward = [scale_a - jnp.minimum(v, 0.0) * inverse for v in speed]
        total = jnp.abs(speed[0]) + jnp.abs(speed[1]) + jnp.abs(speed[2])
        self.centre = 6.0 * scale_a + total * inverse + shift
        lane = lax.broadcasted_iota(jnp.int32, (1, LANES), 1)
        inside = lane < nz
        self.low_z = jnp.where((lane > 0) & inside, self.backward[2], 0.0)
        self.high_z = jnp.where(lane < nz - 1, self.forward[2], 0.0)

    def plane(self, v, x):
        return v[x + self.rim, pl.ds(8, self.ny), :]

    def put(self, v):
        def write(x, value):
            v[x + self.rim, pl.ds(8, self.ny), :] = value

        return write

    def along_z(self, middle):
        return self.low_z * pltpu.roll(middle, 1, 1) + self.high_z * pltpu.roll(middle, LANES - 1, 1)

    def neighbours(self, v, x, middle):
        at, ny = x + self.rim, self.ny
        along_x = self.backward[0] * v[at - 1, pl.ds(8, ny), :] + self.forward[0] * v[at + 1, pl.ds(8, ny), :]
        along_y = self.backward[1] * v[at, pl.ds(7, ny), :] + self.forward[1] * v[at, pl.ds(9, ny), :]
        return along_x + along_y + self.along_z(middle)

    def smoothed(self, v, x):
        middle = self.plane(v, x)
        pulled = self.f[x] + self.neighbours(v, x, middle)
        return (1.0 - DAMPING) * middle + self.w[x] * pulled

    def smooth(self, src, dst, planes):
        sweep(planes, lambda x: self.smoothed(src, x), self.put(dst), GROUP * 64 // self.ny)

    def defect(self, v, x):
        middle = self.plane(v, x)
        pulled = self.f[x] + self.neighbours(v, x, middle)
        return pulled - (self.r[x] + self.centre) * middle

    def solve_in_registers(self, rhs, reaction):
        row = lax.broadcasted_iota(jnp.int32, (self.ny, 1), 0)
        low_y = jnp.where(row > 0, self.backward[1], 0.0)
        high_y = jnp.where(row < self.ny - 1, self.forward[1], 0.0)
        weight = [DAMPING / (r + self.centre) for r in reaction]
        v = [w * f for w, f in zip(weight, rhs)]
        for _ in range(COARSE_SWEEPS - 1):
            new = []
            for x, here in enumerate(v):
                along_y = low_y * pltpu.roll(here, 1, 0) + high_y * pltpu.roll(here, self.ny - 1, 0)
                pulled = rhs[x] + self.along_z(here) + along_y
                if x > 0:
                    pulled += self.backward[0] * v[x - 1]
                if x < len(v) - 1:
                    pulled += self.forward[0] * v[x + 1]
                new.append((1.0 - DAMPING) * here + weight[x] * pulled)
            v = new
        return jnp.concatenate(v, axis=0)


def scalars_of(scalar_ref):
    return scalar_ref[pl.ds(0, 1), :], [scalar_ref[pl.ds(1 + d, 1), :] for d in range(3)]


def zero_rows(v, ny):
    edge = jnp.zeros((v.shape[0], 8, LANES), jnp.float32)
    v[:, pl.ds(0, 8), :] = edge
    v[:, pl.ds(8 + ny, 8), :] = edge


def pool_matrix(offset):
    row = lax.broadcasted_iota(jnp.int32, (LANES, LANES), 0)
    col = lax.broadcasted_iota(jnp.int32, (LANES, LANES), 1)
    return jnp.where(row // 2 + offset == col, 0.125, 0.0).astype(jnp.bfloat16)


def spread_matrix():
    row = lax.broadcasted_iota(jnp.int32, (LANES, LANES), 0)
    col = lax.broadcasted_iota(jnp.int32, (LANES, LANES), 1)
    return jnp.where(col // 2 == row, 1.0, 0.0).astype(jnp.bfloat16)


def step_of(k, count):
    return -k % count


def scalars_kernel(place, shifts_ref, index_ref, velocity_ref, scalar_ref):
    rows = {0: shifts_ref[index_ref[place[0]]]}
    rows.update({1 + d: velocity_ref[d] for d in range(3)})
    rows.update({8 + c: shifts_ref[index_ref[c]] for c in range(index_ref.shape[0])})
    for n, scalar in rows.items():
        scalar_ref[pl.ds(n, 1), :] = jnp.full((1, LANES), scalar, jnp.float32)


def merge_kernel(place, mine_ref, theirs_ref, other_reaction_ref, *out_refs):
    chip, core = place[0] // 2, place[0] & 1
    columns, by = theirs_ref.shape[0], theirs_ref.shape[2]
    mine = pl.ds(pl.multiple_of(core * by, 8), by)
    theirs = pl.ds(pl.multiple_of((1 - core) * by, 8), by)
    for m, out_ref in enumerate(out_refs):
        column = 2 * jnp.bitwise_xor(chip, m) + core
        out_ref[0, :, mine, :] = mine_ref[column]
        out_ref[0, :, theirs, :] = theirs_ref[column]
        out_ref[1, :, mine, :] = mine_ref[columns]
        out_ref[1, :, theirs, :] = other_reaction_ref[...]


def half_kernel(chips_y, place, *refs):
    blocks, half_ref = refs[:-1], refs[-1]
    for m, block in enumerate(blocks):
        size = block.shape[2]
        chip = jnp.bitwise_xor(place[0] // 2, m)
        rows = pl.ds(pl.multiple_of(lax.rem(chip, chips_y) * size, 8), size)
        half_ref[:, :, rows, :] = block[...]


def arrange_kernel(chips_y, place, *refs):
    blocks, (slab_ref, near_ref, far_ref) = refs[:-3], refs[-3:]
    chip = place[0] // 2
    for m, block in enumerate(blocks):
        owner = jnp.bitwise_xor(chip, m)
        _, bx, size, _ = block.shape
        planes = pl.ds((owner // chips_y) * bx, bx)
        rows = pl.ds(pl.multiple_of(lax.rem(owner, chips_y) * size, 8), size)
        slab_ref[:, planes, rows, :] = block[...]
    other = 1 - chip // chips_y
    near_ref[...] = slab_ref[:, pl.ds(other * (SLAB - NEAR), NEAR)]
    far_ref[...] = slab_ref[:, pl.ds(NEAR + other * (SLAB - 3 * NEAR), NEAR)]


def beyond_kernel(slabs, chips_y, place, scalar_ref, half_ref, near_ref, far_ref, *refs):
    out_refs, (f, r, w, v0) = refs[:2], refs[2:]
    ny, slab = f.shape[1], place[1]
    x = place[0] // 2 // chips_y
    fine = Level(0, ny, LANES, 0, scalars_of(scalar_ref), f, r, w)
    zero_rows(v0, ny)
    last = NEAR * (1 - x)
    sides = ((1 - x, ((half_ref, 0, HALO),)), (x, ((near_ref, last, NEAR), (far_ref, NEAR - last, NEAR))))
    for out_ref, (above, parts) in zip(out_refs, sides):
        for ref, first, size in parts:
            f[pl.ds(first, size)], r[pl.ds(first, size)] = ref[0], ref[1]
        beside = jnp.where(above == 1, slab < slabs - 1, slab > 0)
        inside = jnp.where(beside, DAMPING, 0.0)

        def put(at, weight):
            w[at] = weight
            v0[at, pl.ds(8, ny), :] = weight * f[at]

        sweep(range(HALO), lambda at: inside / (r[at] + fine.centre), put)
        for n in range(NEAR):
            out_ref[n] = fine.smoothed(v0, 1 + n)


def begin_kernel(_, scalar_ref, slab_ref, f, r, w, v0, v1):
    ny = f.shape[1]
    fine = Level(0, ny, LANES, 0, scalars_of(scalar_ref), f, r, w)
    zero_rows(v0, ny)
    zero_rows(v1, ny)
    own = range(HALO, HALO + SLAB)
    f[pl.ds(HALO, SLAB)], r[pl.ds(HALO, SLAB)] = slab_ref[0], slab_ref[1]

    def put(at, weight):
        w[at] = weight
        v0[at, pl.ds(8, ny), :] = weight * f[at]

    sweep(own, lambda at: DAMPING / (r[at] + fine.centre), put)
    fine.smooth(v0, v1, own[1:-1])


def pre_kernel(slabs, chips_y, place, scalar_ref, *refs):
    half_ref, near_ref, pool_ref, pool_up_ref = refs[5:9]
    f, r, w, v0, v1, coarse_ref, tmp, pooled = refs[9:]
    ny = f.shape[1]
    slab = place[1]
    fine = Level(0, ny, LANES, 0, scalars_of(scalar_ref), f, r, w)
    after = HALO + SLAB

    x = place[0] // 2 // chips_y
    for above, ref, first in ((1 - x, half_ref, x * NEAR), (x, near_ref, 0)):
        planes = pl.ds((HALO - NEAR) + above * (SLAB + NEAR), NEAR)
        f[planes], r[planes] = ref[0, pl.ds(first, NEAR)], ref[1, pl.ds(first, NEAR)]

    below = jnp.where(slab > 0, DAMPING, 0.0)
    above = jnp.where(slab < slabs - 1, DAMPING, 0.0)

    def put(at, weight):
        w[at] = weight
        v0[at, pl.ds(8, ny), :] = weight * f[at]

    beside = [*range(HALO - NEAR, HALO), *range(after, after + NEAR)]
    sweep(beside, lambda at: (below if at < HALO else above) / (r[at] + fine.centre), put)
    fine.smooth(v0, v1, (HALO - 1, HALO, after - 1, after))
    half = ny // 2

    def coarsened(x):
        at = HALO + 2 * x
        return fine.defect(v1, at) + fine.defect(v1, at + 1), r[at] + r[at + 1]

    def put_pooled(x, pair):
        for n in range(2):
            pooled[n, pl.ds(x * half, half), :] = fine.pool_rows(pair[n], tmp.at[2 * x + n])

    sweep(range(SLAB // 2), coarsened, put_pooled)
    packed = split_dot(pooled[0], pool_ref[...]) + split_dot(pooled[1], pool_up_ref[...])
    coarse_ref[...] = packed.reshape(coarse_ref.shape)


def coarse_kernel(grid, place, scalar_ref, *refs):
    slabs, nx, ny, nz = grid
    pool_ref, spread_ref = refs[:2]
    coarse, out_ref = refs[2 : 2 + slabs], refs[2 + slabs]
    f1, r1, w1, v1a, v1b, pooled, tmp = refs[3 + slabs :]
    pool, spread = pool_ref[...], spread_ref[...]
    slab = place[1]
    rim = HALO // 2
    nx1, ny1, nx2, ny2 = nx // 2, ny // 2, nx // 4, ny // 4
    mid = Level(1, ny1, nz // 2, rim, scalars_of(scalar_ref), f1, r1, w1)
    deep = Level(2, ny2, nz // 4, 0, scalars_of(scalar_ref), None, None, None)
    for v in (v1a, v1b):
        zero_rows(v, ny1)
        blank = jnp.zeros((rim,) + v.shape[1:], jnp.float32)
        v[pl.ds(0, rim)] = blank
        v[pl.ds(rim + nx1, rim)] = blank

    lower = lax.broadcasted_iota(jnp.int32, (1, LANES), 1) < LANES // 2
    own = SLAB // 2
    for k in range(slabs):
        first = jnp.bitwise_xor(slab, step_of(k, slabs)) * own
        both = coarse[k][...]
        f1[pl.ds(first, own)] = jnp.where(lower, both, 0.0)
        r1[pl.ds(first, own)] = jnp.where(lower, pltpu.roll(both, LANES // 2, 2), 0.0)

    def put_start(x, weight):
        w1[x] = weight
        v1a[x + rim, pl.ds(8, ny1), :] = weight * f1[x]

    sweep(range(nx1), lambda x: DAMPING / (r1[x] + mid.centre), put_start, 2 * GROUP)
    mid.smooth(v1a, v1b, range(nx1))

    def coarsened(x):
        return mid.defect(v1b, 2 * x) + mid.defect(v1b, 2 * x + 1), r1[2 * x] + r1[2 * x + 1]

    rows2 = nx2 * ny2

    def put_pooled(x, pair):
        for n in range(2):
            value = mid.pool_rows(pair[n], tmp.at[2 * x + n])
            pooled[pl.ds(n * rows2 + x * ny2, ny2), :] = value

    sweep(range(nx2), coarsened, put_pooled)
    deeper = split_dot(pooled[pl.ds(0, 2 * rows2), :], pool)
    planes = [deeper[n * ny2 : (n + 1) * ny2] for n in range(2 * nx2)]
    values = deep.solve_in_registers(planes[:nx2], planes[nx2:])

    pooled[pl.ds(0, rows2), :] = split_dot(values, spread)

    def refined1(x):
        return mid.spread_rows(pooled[pl.ds(x * ny2, ny2), :], tmp.at[x])

    def put_refined1(x, value):
        for n in range(2):
            v1b[2 * x + n + rim, pl.ds(8, ny1), :] += value

    sweep(range(nx2), refined1, put_refined1)
    mid.smooth(v1b, v1a, range(nx1))
    mid.smooth(v1a, v1b, range(nx1))

    window = own + 2 * rim
    values = v1b[pl.ds(slab * own, window), pl.ds(8, ny1), :].reshape(window * ny1, LANES)
    out_ref[...] = split_dot(values, spread)


def post_kernel(by, chips_y, place, scalar_ref, *refs):
    f, r, w, v1, correction, first_ref, second_ref, kept_ref, sent_ref, va, vb, tmp = refs
    count, ny = f.shape[:2]
    fine = Level(0, ny, LANES, 0, scalars_of(scalar_ref), f, r, w)
    for v in (va, vb):
        zero_rows(v, ny)
    x, half = place[0] // 2 // chips_y, ny // 2
    window = correction.shape[0] // half
    for ref, above in ((first_ref, 1 - x), (second_ref, x)):
        va[pl.ds(1 + above * (SLAB + HALO), NEAR), pl.ds(8, ny), :] = ref[...]

    def refined(x):
        return fine.spread_rows(correction[pl.ds(x * half, half), :], tmp.at[x])

    def put_refined(x, value):
        for at in (2 * x, 2 * x + 1):
            if 0 < at < count - 1:
                known = HALO - NEAR < at < HALO + SLAB + NEAR - 1
                here = v1 if known else va
                va[at, pl.ds(8, ny), :] = here[at, pl.ds(8, ny), :] + value

    sweep(range(window), refined, put_refined)
    fine.smooth(va, vb, range(2, count - 2))
    fine.smooth(vb, va, range(3, count - 3))

    total = jnp.zeros((8, LANES), jnp.float32)
    for x in range(SLAB):
        rest = fine.defect(va, HALO + x)
        total = total + jnp.sum((rest * rest).reshape(ny // 8, 8, LANES), axis=0)
        tmp[x] = rest
    squares = jnp.full((8, LANES), jnp.sum(total), jnp.float32)

    core, area = place[0] & 1, half * SLAB
    for ref, first in ((kept_ref, core * by), (sent_ref, (1 - core) * by)):
        for y in range(half // by):
            row = pl.multiple_of(2 * y * by + first, 8)
            for x in range(SLAB):
                to = x * half + y * by
                ref[pl.ds(to, by), :] = va[HALO + x, pl.ds(8 + row, by), :]
                ref[pl.ds(area + to, by), :] = tmp[x, pl.ds(row, by), :]
        ref[pl.ds(2 * area, 8), :] = squares


def part_rows(bx, by):
    outer = bx * by
    edges = outer + 2 * by
    squares = edges + 2 * (bx - 2)
    return outer, edges, squares, (squares + 8) // 8 * 8


def merge_back_kernel(bx, by, chips_y, place, kept_ref, got_ref, *out_refs):
    chip, core = place[0] // 2, place[0] & 1
    half = chips_y * by
    outer, edges, squares, size = part_rows(bx, by)
    for m, out_ref in enumerate(out_refs):
        target = jnp.bitwise_xor(chip, m)
        first = (target // chips_y) * bx * half + lax.rem(target, chips_y) * by
        for ref, column in ((kept_ref, core), (got_ref, 1 - core)):
            base = pl.multiple_of(column * size, 8)
            for p in range(bx):
                at = pl.multiple_of(first + p * half, 8)
                out_ref[pl.ds(base + p * by, by), :] = ref[pl.ds(at, by), :]
                at = pl.multiple_of(at + SLAB * half, 8)
                if p in (0, bx - 1):
                    out_ref[pl.ds(base + outer + (p > 0) * by, by), :] = ref[pl.ds(at, by), :]
                else:
                    rows = ref[pl.ds(at, by), :]
                    to = base + edges + 2 * (p - 1)
                    out_ref[pl.ds(to, 1), :] = rows[:1]
                    out_ref[pl.ds(to + 1, 1), :] = rows[by - 1 :]
            out_ref[pl.ds(base + squares, 1), :] = ref[pl.ds(2 * SLAB * half, 1), :]


def collect_kernel(place, scalar_ref, source_ref, reaction_ref, *refs):
    parts, (iterate_ref, residual_ref) = refs[:-2], refs[-2:]
    _, bx, by, nz = iterate_ref.shape
    outer, edges, _, size = part_rows(bx, by)
    _, speed = scalars_of(scalar_ref)
    fine = Level(0, by, nz, 0, (0.0, speed), None, None, None)
    reaction = [reaction_ref[p] + fine.centre for p in range(1, bx - 1)]
    for m, part in enumerate(parts):
        target = jnp.bitwise_xor(place[0] // 2, m)
        for n in range(2):
            base, column = n * size, 2 * target + n
            shift = scalar_ref[pl.ds(8 + column, 1), :]
            planes = [part[pl.ds(base + p * by, by), :] for p in range(bx)]
            for p in range(bx):
                iterate_ref[column, p] = planes[p]
            for p in (0, bx - 1):
                residual_ref[column, p] = part[pl.ds(base + outer + (p > 0) * by, by), :]
            for p in range(1, bx - 1):
                here = planes[p]
                pulled = source_ref[column, p] + fine.along_z(here)
                pulled += fine.backward[0] * planes[p - 1] + fine.forward[0] * planes[p + 1]
                pulled += fine.backward[1] * pltpu.roll(here, 1, 0) + fine.forward[1] * pltpu.roll(here, by - 1, 0)
                residual_ref[column, p] = pulled - (reaction[p - 1] + shift) * here
                at = base + edges + 2 * (p - 1)
                residual_ref[column, p, pl.ds(0, 1), :] = part[pl.ds(at, 1), :]
                residual_ref[column, p, pl.ds(by - 1, 1), :] = part[pl.ds(at + 1, 1), :]


def squares_kernel(bx, by, place, *refs):
    parts, out_ref = refs[:-1], refs[-1]
    _, _, squares, size = part_rows(bx, by)
    lane = lax.broadcasted_iota(jnp.int32, (1, LANES), 1)
    row = jnp.zeros((1, LANES), jnp.float32)
    for m, part in enumerate(parts):
        target = jnp.bitwise_xor(place[0] // 2, m)
        for n in range(2):
            row = jnp.where(lane == 2 * target + n, part[pl.ds(n * size + squares, 1), :], row)
    out_ref[...] = row


SMEM = pl.BlockSpec(memory_space=pltpu.SMEM)
VMEM = pl.BlockSpec(memory_space=pltpu.VMEM)


def local_kernel(kernel, name, scalars, arrays, outs, scratch=(), in_place=()):
    gy_size = lax.axis_size("gy")
    step = SLAB // HALO

    def placed(*refs):
        along, across = lax.axis_index("gx"), lax.axis_index("gy")
        kernel((lax.rem(along, step) * gy_size + across, along // step), *refs)

    return pl.pallas_call(
        placed,
        out_shape=[jax.ShapeDtypeStruct(shape, jnp.float32) for shape in outs],
        in_specs=[SMEM] * len(scalars) + [VMEM] * len(arrays),
        out_specs=[VMEM] * len(outs),
        scratch_shapes=[pltpu.VMEM(shape, jnp.float32) for shape in scratch],
        input_output_aliases={len(scalars) + n: k for k, n in enumerate(in_place)},
        compiler_params=pltpu.CompilerParams(vmem_limit_bytes=VMEM_LIMIT),
        name=name,
    )(*scalars, *arrays)


def swap_in_plane(pieces, unit):
    devices = lax.axis_size("gx") * lax.axis_size("gy")
    moved = [pieces[0]]
    for k in range(1, len(pieces)):
        pairs = [(i, i ^ (k * unit)) for i in range(devices)]
        moved.append(lax.ppermute(pieces[k], ("gx", "gy"), pairs))
    return moved


def swap_slabs(piece, step, slabs):
    size = lax.axis_size("gx")
    moved = [piece]
    for k in range(1, slabs):
        pairs = [(i, i ^ (step_of(k, slabs) * step)) for i in range(size)]
        moved.append(lax.ppermute(piece, "gx", pairs))
    return moved


def column_body(source, reaction, shifts, shift_index, velocity):
    columns, bx, by, nz = source.shape
    gx_size, gy_size = lax.axis_size("gx"), lax.axis_size("gy")
    nx, ny = bx * gx_size, by * gy_size
    step = columns // gy_size
    slabs = gx_size // step
    count = SLAB + 2 * HALO
    area = bx * by

    chips, chips_y = columns // 2, gy_size // 2
    cores = [(i, i ^ 1) for i in range(gy_size)]
    theirs = [lax.ppermute(source, "gy", cores), lax.ppermute(reaction, "gy", cores)]
    mine = jnp.concatenate([source, reaction[None]])
    (scalar_rows,) = local_kernel(
        scalars_kernel, "scalars", (shifts, shift_index, velocity), (), [(8 + columns, LANES)]
    )
    blocks = local_kernel(
        merge_kernel,
        "merge",
        (),
        (mine, *theirs),
        [(2, bx, 2 * by, nz)] * chips,
    )
    blocks = swap_in_plane(blocks, 2)

    edge = (2, NEAR, ny, nz)
    (own_half,) = local_kernel(
        functools.partial(half_kernel, chips_y),
        "half",
        (),
        blocks[:chips_y],
        [(2, HALO, ny, nz)],
    )
    slab, near, far = local_kernel(
        functools.partial(arrange_kernel, chips_y),
        "arrange",
        (),
        blocks,
        [(2, SLAB, ny, nz), edge, edge],
    )

    def send_beside(piece, up):
        pairs = [(i, i + step if i % step == up else i - step) for i in range(gx_size)]
        return lax.ppermute(piece, "gx", [(i, j) for i, j in pairs if 0 <= j < gx_size])

    beside = [send_beside(own_half, 1), send_beside(near, 0), send_beside(far, 0)]
    grid, rimmed = (count, ny, nz), (count, ny + 16, nz)
    fields = [grid, grid, grid, rimmed, rimmed]
    fields_own = local_kernel(begin_kernel, "begin", (), (scalar_rows, slab), fields)
    f, r, w, _, v1, coarse = local_kernel(
        functools.partial(pre_kernel, slabs, chips_y),
        "pre",
        (),
        (scalar_rows, *fields_own, *beside[:2], pool_matrix(0), pool_matrix(LANES // 2)),
        fields + [(SLAB // 2, ny // 2, nz)],
        [(SLAB, ny, nz), (2, SLAB // 2 * ny // 2, nz)],
        in_place=range(1, 1 + len(fields)),
    )
    beyond = local_kernel(
        functools.partial(beyond_kernel, slabs, chips_y),
        "beyond",
        (),
        (scalar_rows, *beside),
        [(NEAR, ny, nz)] * 2,
        [(HALO, ny, nz)] * 3 + [(HALO, ny + 16, nz)],
    )
    gathered = swap_slabs(coarse, step, slabs)

    coarse_grid = (nx // 2, ny // 2, nz)
    coarse_rimmed = (nx // 2 + HALO, ny // 2 + 16, nz)
    window = (SLAB // 2 + HALO) * ny // 2
    (correction,) = local_kernel(
        functools.partial(coarse_kernel, (slabs, nx, ny, nz)),
        "coarse",
        (),
        (scalar_rows, pool_matrix(0), spread_matrix(), *gathered),
        [(window, nz)],
        [coarse_grid] * 3 + [coarse_rimmed] * 2 + [(nx // 4 * ny // 2, nz), (nx // 2, ny // 2, nz)],
    )
    result = (SLAB * ny + 8, nz)
    kept, sent = local_kernel(
        functools.partial(post_kernel, by, chips_y),
        "post",
        (),
        (scalar_rows, f, r, w, v1, correction, *beyond),
        [result, result],
        [rimmed] * 2 + [(SLAB, ny, nz)],
    )

    parts = local_kernel(
        functools.partial(merge_back_kernel, bx, by, chips_y),
        "merge_back",
        (),
        (kept, lax.ppermute(sent, "gy", cores)),
        [(2 * part_rows(bx, by)[3], nz)] * chips,
    )
    parts = swap_in_plane(parts, 2)
    (squares,) = local_kernel(
        functools.partial(squares_kernel, bx, by), "squares", (), parts, [(1, nz)]
    )
    iterate, residual = local_kernel(
        collect_kernel,
        "collect",
        (),
        (scalar_rows, source, reaction, *parts),
        [source.shape] * 2,
    )
    sums = swap_slabs(squares, step, slabs)
    sums = [*sums[1:], sums[0]]
    while len(sums) > 1:
        sums = [first + second for first, second in zip(sums[::2], sums[1::2])]
    (total,) = sums
    residual_rms = jnp.sqrt(total[0, :columns] / (nx * ny * nz) + EPSILON)
    return iterate, residual, residual_rms


def power_of_two(n):
    return n > 0 and n & (n - 1) == 0


def column_plan_fits(columns, bx, by, nz, gx_size, gy_size):
    if columns % gy_size or gx_size % (columns // gy_size):
        return False
    step = columns // gy_size
    slabs, ny = gx_size // step, by * gy_size
    whole = power_of_two(columns) and power_of_two(step) and power_of_two(slabs)
    small = slabs * ny * nz <= 2**15
    paired = step == 2 and bx == HALO and gy_size % 2 == 0
    return whole and small and paired and bx * step == SLAB and nz == LANES and by % 16 == 0


def solution(mesh):
    gx_size, gy_size = mesh.shape["gx"], mesh.shape["gy"]

    def body(source, reaction, shifts, shift_index, velocity):
        fits = column_plan_fits(*source.shape, gx_size, gy_size)
        plan = column_body if fits else halo_body
        return plan(source, reaction, shifts, shift_index, velocity)

    return jax.shard_map(
        body,
        mesh=mesh,
        in_specs=(P(None, "gx", "gy", None), P("gx", "gy", None), P(), P(), P()),
        out_specs=(P(None, "gx", "gy", None), P(None, "gx", "gy", None), P()),
        check_vma=False,
    )
```

```python
import functools

import jax
import jax.numpy as jnp
from jax import lax
from jax.experimental import pallas as pl
from jax.experimental.pallas import tpu as pltpu
from jax.sharding import PartitionSpec as P

LEVELS = 3
COARSE_SWEEPS = 6

DAMPING = 0.8
EPSILON = 1e-06
VMEM_LIMIT = 32 * 1024 * 1024
LANES = 128
GROUP = 4
SLAB = 8
HALO = 4
NEAR = 2


def with_halo(x, sides, width):
    for axis, dim in sides:
        peers, length = (lax.axis_size(axis), x.shape[dim])
        up = [(i, (i + 1) % peers) for i in range(peers - 1)]
        down = [(j, i) for i, j in up]
        last = lax.slice_in_dim(x, length - width, length, axis=dim)
        leading = lax.slice_in_dim(x, 0, width, axis=dim)
        before = lax.ppermute(last, axis, up)
        after = lax.ppermute(leading, axis, down)
        x = jnp.concatenate([before, x, after], axis=dim)
    return x


def select_shifts(shifts, shift_index):
    columns = jnp.arange(shifts.shape[0], dtype=jnp.int32)
    picked = jnp.where(shift_index[:, None] == columns[None, :], shifts[None, :], 0.0)
    return jnp.sum(picked, axis=1)


def coefficients(velocity, spacing):
    scale_a = 1.0 / (spacing * spacing)
    backward = scale_a + jnp.maximum(velocity, 0.0) / spacing
    forward = scale_a - jnp.minimum(velocity, 0.0) / spacing
    centre = 6.0 * scale_a + jnp.sum(jnp.abs(velocity)) / spacing
    return (backward, forward, centre)


def apply_stencil(padded, backward, forward, diagonal):
    middle = padded[:, 1:-1, 1:-1, :]
    along_z = jnp.pad(middle, ((0, 0), (0, 0), (0, 0), (1, 1)))
    others = backward[0] * padded[:, :-2, 1:-1, :] + forward[0] * padded[:, 2:, 1:-1, :]
    others = others + backward[1] * padded[:, 1:-1, :-2, :] + forward[1] * padded[:, 1:-1, 2:, :]
    others = others + backward[2] * along_z[:, :, :, :-2] + forward[2] * along_z[:, :, :, 2:]
    return diagonal * middle - others


def face_halo(iterate):
    return with_halo(iterate, (("gx", 1), ("gy", 2)), 1)


def coarsen(values):
    count, size_x, size_y, size_z = values.shape
    blocks = values.reshape(count, size_x // 2, 2, size_y // 2, 2, size_z // 2, 2)
    return jnp.sum(blocks, axis=(2, 4, 6)) * 0.125


def refine(values):
    return jnp.repeat(jnp.repeat(jnp.repeat(values, 2, 1), 2, 2), 2, 3)


def coarsest_solve(rhs_field, backward, forward, diagonal):
    iterate = DAMPING * rhs_field / diagonal
    for repeat in range(COARSE_SWEEPS - 1):
        applied = apply_stencil(face_halo(iterate), backward, forward, diagonal)
        iterate = iterate + DAMPING * (rhs_field - applied) / diagonal
    return iterate


def multigrid_cycle(level_index, rhs_field, reaction_l, shift_value, velocity):
    backward, forward, centre = coefficients(velocity, 2.0**level_index)
    diagonal = centre + reaction_l + shift_value[:, None, None, None]
    if level_index == LEVELS - 1:
        return coarsest_solve(rhs_field, backward, forward, diagonal)

    def operate(iterate):
        return apply_stencil(face_halo(iterate), backward, forward, diagonal)

    def smooth_step(iterate):
        return iterate + DAMPING * (rhs_field - operate(iterate)) / diagonal

    iterate = DAMPING * rhs_field / diagonal
    iterate = smooth_step(iterate)
    defect = rhs_field - operate(iterate)
    correction = multigrid_cycle(
        level_index + 1, coarsen(defect), coarsen(reaction_l), shift_value, velocity
    )
    iterate = iterate + refine(correction)
    iterate = smooth_step(iterate)
    iterate = smooth_step(iterate)
    return iterate


def halo_body(source, reaction, shifts, shift_index, velocity):
    columns, cells_x, cells_y, cells_z = source.shape
    shift_value = select_shifts(shifts, shift_index)
    reaction_top = reaction[None]
    backward, forward, centre = coefficients(velocity, 1.0)
    diagonal = centre + reaction_top + shift_value[:, None, None, None]

    iterate = multigrid_cycle(0, source, reaction_top, shift_value, velocity)
    residual = source - apply_stencil(face_halo(iterate), backward, forward, diagonal)
    local_squares = jnp.sum(residual * residual, axis=(1, 2, 3))
    squares = lax.psum(local_squares, ("gx", "gy"))
    total_cells = cells_x * cells_y * cells_z * lax.axis_size("gx") * lax.axis_size("gy")
    residual_rms = jnp.sqrt(squares / total_cells + EPSILON)
    return (iterate, residual, residual_rms)


def split_dot(values, matrix):
    high = values.astype(jnp.bfloat16)
    low = (values - high.astype(jnp.float32)).astype(jnp.bfloat16)
    return jnp.dot(high, matrix, preferred_element_type=jnp.float32) + jnp.dot(
        low, matrix, preferred_element_type=jnp.float32
    )


def sweep(planes, get, put, size=GROUP):
    planes = list(planes)
    for first in range(0, len(planes), size):
        group = planes[first : first + size]
        values = [get(x) for x in group]
        for x, value in zip(group, values):
            put(x, value)


class Grid:
    def __init__(self, ny):
        self.ny = ny

    def pool_rows(self, value, rows):
        half, ny = self.ny // 2, self.ny
        rows[pl.ds(0, ny), :] = value
        return rows[pl.ds(0, half, stride=2), :] + rows[pl.ds(1, half, stride=2), :]

    def spread_rows(self, part, rows):
        half, ny = self.ny // 2, self.ny
        rows[pl.ds(0, half, stride=2), :] = part
        rows[pl.ds(1, half, stride=2), :] = part
        return rows[pl.ds(0, ny), :]


class Level(Grid):
    def __init__(self, index, ny, nz, rim, scalars, f, r, w):
        super().__init__(ny)
        self.nz, self.rim = nz, rim
        self.f, self.r, self.w = f, r, w
        spacing = 2.0**index
        scale_a = 1.0 / (spacing * spacing)
        inverse = 1.0 / spacing
        shift, speed = scalars
        self.backward = [scale_a + jnp.maximum(v, 0.0) * inverse for v in speed]
        self.forward = [scale_a - jnp.minimum(v, 0.0) * inverse for v in speed]
        total = jnp.abs(speed[0]) + jnp.abs(speed[1]) + jnp.abs(speed[2])
        self.centre = 6.0 * scale_a + total * inverse + shift
        lane = lax.broadcasted_iota(jnp.int32, (1, LANES), 1)
        inside = lane < nz
        self.low_z = jnp.where((lane > 0) & inside, self.backward[2], 0.0)
        self.high_z = jnp.where(lane < nz - 1, self.forward[2], 0.0)

    def plane(self, v, x):
        return v[x + self.rim, pl.ds(8, self.ny), :]

    def put(self, v):
        def write(x, value):
            v[x + self.rim, pl.ds(8, self.ny), :] = value

        return write

    def along_z(self, middle):
        return self.low_z * pltpu.roll(middle, 1, 1) + self.high_z * pltpu.roll(middle, LANES - 1, 1)

    def neighbours(self, v, x, middle):
        at, ny = x + self.rim, self.ny
        along_x = self.backward[0] * v[at - 1, pl.ds(8, ny), :] + self.forward[0] * v[at + 1, pl.ds(8, ny), :]
        along_y = self.backward[1] * v[at, pl.ds(7, ny), :] + self.forward[1] * v[at, pl.ds(9, ny), :]
        return along_x + along_y + self.along_z(middle)

    def smoothed(self, v, x):
        middle = self.plane(v, x)
        pulled = self.f[x] + self.neighbours(v, x, middle)
        return (1.0 - DAMPING) * middle + self.w[x] * pulled

    def smooth(self, src, dst, planes):
        sweep(planes, lambda x: self.smoothed(src, x), self.put(dst), GROUP * 64 // self.ny)

    def defect(self, v, x):
        middle = self.plane(v, x)
        pulled = self.f[x] + self.neighbours(v, x, middle)
        return pulled - (self.r[x] + self.centre) * middle

    def solve_in_registers(self, rhs, reaction):
        row = lax.broadcasted_iota(jnp.int32, (self.ny, 1), 0)
        low_y = jnp.where(row > 0, self.backward[1], 0.0)
        high_y = jnp.where(row < self.ny - 1, self.forward[1], 0.0)
        weight = [DAMPING / (r + self.centre) for r in reaction]
        v = [w * f for w, f in zip(weight, rhs)]
        for _ in range(COARSE_SWEEPS - 1):
            new = []
            for x, here in enumerate(v):
                along_y = low_y * pltpu.roll(here, 1, 0) + high_y * pltpu.roll(here, self.ny - 1, 0)
                pulled = rhs[x] + self.along_z(here) + along_y
                if x > 0:
                    pulled += self.backward[0] * v[x - 1]
                if x < len(v) - 1:
                    pulled += self.forward[0] * v[x + 1]
                new.append((1.0 - DAMPING) * here + weight[x] * pulled)
            v = new
        return jnp.concatenate(v, axis=0)


def scalars_of(scalar_ref):
    return scalar_ref[pl.ds(0, 1), :], [scalar_ref[pl.ds(1 + d, 1), :] for d in range(3)]


def zero_rows(v, ny):
    edge = jnp.zeros((v.shape[0], 8, LANES), jnp.float32)
    v[:, pl.ds(0, 8), :] = edge
    v[:, pl.ds(8 + ny, 8), :] = edge


def pool_matrix(offset):
    row = lax.broadcasted_iota(jnp.int32, (LANES, LANES), 0)
    col = lax.broadcasted_iota(jnp.int32, (LANES, LANES), 1)
    return jnp.where(row // 2 + offset == col, 0.125, 0.0).astype(jnp.bfloat16)


def spread_matrix():
    row = lax.broadcasted_iota(jnp.int32, (LANES, LANES), 0)
    col = lax.broadcasted_iota(jnp.int32, (LANES, LANES), 1)
    return jnp.where(col // 2 == row, 1.0, 0.0).astype(jnp.bfloat16)


def step_of(k, count):
    return -k % count


def scalars_kernel(place, shifts_ref, index_ref, velocity_ref, scalar_ref):
    rows = {0: shifts_ref[index_ref[place[0]]]}
    rows.update({1 + d: velocity_ref[d] for d in range(3)})
    rows.update({8 + c: shifts_ref[index_ref[c]] for c in range(index_ref.shape[0])})
    for n, scalar in rows.items():
        scalar_ref[pl.ds(n, 1), :] = jnp.full((1, LANES), scalar, jnp.float32)


def merge_kernel(place, mine_ref, theirs_ref, other_reaction_ref, *out_refs):
    chip, core = place[0] // 2, place[0] & 1
    columns, by = theirs_ref.shape[0], theirs_ref.shape[2]
    mine = pl.ds(pl.multiple_of(core * by, 8), by)
    theirs = pl.ds(pl.multiple_of((1 - core) * by, 8), by)
    for m, out_ref in enumerate(out_refs):
        column = 2 * jnp.bitwise_xor(chip, m) + core
        out_ref[0, :, mine, :] = mine_ref[column]
        out_ref[0, :, theirs, :] = theirs_ref[column]
        out_ref[1, :, mine, :] = mine_ref[columns]
        out_ref[1, :, theirs, :] = other_reaction_ref[...]


def half_kernel(chips_y, place, *refs):
    blocks, half_ref = refs[:-1], refs[-1]
    for m, block in enumerate(blocks):
        size = block.shape[2]
        chip = jnp.bitwise_xor(place[0] // 2, m)
        rows = pl.ds(pl.multiple_of(lax.rem(chip, chips_y) * size, 8), size)
        half_ref[:, :, rows, :] = block[...]


def arrange_kernel(chips_y, place, *refs):
    blocks, (slab_ref, near_ref) = refs[:-2], refs[-2:]
    chip = place[0] // 2
    for m, block in enumerate(blocks):
        owner = jnp.bitwise_xor(chip, m)
        _, bx, size, _ = block.shape
        planes = pl.ds((owner // chips_y) * bx, bx)
        rows = pl.ds(pl.multiple_of(lax.rem(owner, chips_y) * size, 8), size)
        slab_ref[:, planes, rows, :] = block[...]
    other = 1 - chip // chips_y
    near_ref[...] = slab_ref[:, pl.ds(other * (SLAB - NEAR), NEAR)]


def beyond_kernel(slabs, chips_y, place, scalar_ref, half_ref, out_ref, f, r, w, v0):
    ny, slab = f.shape[1], place[1]
    x = place[0] // 2 // chips_y
    fine = Level(0, ny, LANES, 0, scalars_of(scalar_ref), f, r, w)
    zero_rows(v0, ny)
    f[...], r[...] = half_ref[0], half_ref[1]
    beside = jnp.where(x == 0, slab < slabs - 1, slab > 0)
    inside = jnp.where(beside, DAMPING, 0.0)

    def put(at, weight):
        w[at] = weight
        v0[at, pl.ds(8, ny), :] = weight * f[at]

    sweep(range(HALO), lambda at: inside / (r[at] + fine.centre), put)
    for n in range(NEAR):
        out_ref[n] = fine.smoothed(v0, 1 + n)


def begin_kernel(_, scalar_ref, slab_ref, f, r, w, v0, v1):
    ny = f.shape[1]
    fine = Level(0, ny, LANES, 0, scalars_of(scalar_ref), f, r, w)
    zero_rows(v0, ny)
    zero_rows(v1, ny)
    own = range(HALO, HALO + SLAB)
    f[pl.ds(HALO, SLAB)], r[pl.ds(HALO, SLAB)] = slab_ref[0], slab_ref[1]

    def put(at, weight):
        w[at] = weight
        v0[at, pl.ds(8, ny), :] = weight * f[at]

    sweep(own, lambda at: DAMPING / (r[at] + fine.centre), put)
    fine.smooth(v0, v1, own[1:-1])


def pre_kernel(slabs, chips_y, place, scalar_ref, *refs):
    half_ref, near_ref, pool_ref, pool_up_ref = refs[5:9]
    f, r, w, v0, v1, coarse_ref, beyond_ref, tmp, pooled = refs[9:]
    ny = f.shape[1]
    slab = place[1]
    fine = Level(0, ny, LANES, 0, scalars_of(scalar_ref), f, r, w)
    after = HALO + SLAB

    x = place[0] // 2 // chips_y
    for above, ref, first in ((1 - x, half_ref, x * NEAR), (x, near_ref, 0)):
        planes = pl.ds((HALO - NEAR) + above * (SLAB + NEAR), NEAR)
        f[planes], r[planes] = ref[0, pl.ds(first, NEAR)], ref[1, pl.ds(first, NEAR)]

    below = jnp.where(slab > 0, DAMPING, 0.0)
    above = jnp.where(slab < slabs - 1, DAMPING, 0.0)

    def put(at, weight):
        w[at] = weight
        v0[at, pl.ds(8, ny), :] = weight * f[at]

    beside = [*range(HALO - NEAR, HALO), *range(after, after + NEAR)]
    sweep(beside, lambda at: (below if at < HALO else above) / (r[at] + fine.centre), put)
    fine.smooth(v0, v1, (HALO - 1, HALO, after - 1, after))
    half = ny // 2

    def coarsened(x):
        at = HALO + 2 * x
        return fine.defect(v1, at) + fine.defect(v1, at + 1), r[at] + r[at + 1]

    def put_pooled(x, pair):
        for n in range(2):
            pooled[n, pl.ds(x * half, half), :] = fine.pool_rows(pair[n], tmp.at[2 * x + n])

    sweep(range(SLAB // 2), coarsened, put_pooled)
    packed = split_dot(pooled[0], pool_ref[...]) + split_dot(pooled[1], pool_up_ref[...])
    coarse_ref[...] = packed.reshape(coarse_ref.shape)
    first = HALO + 1 + (1 - x) * (SLAB - HALO)
    beyond_ref[...] = v1[pl.ds(first, NEAR), pl.ds(8, ny), :]


def coarse_kernel(grid, place, scalar_ref, *refs):
    slabs, nx, ny, nz = grid
    pool_ref, spread_ref = refs[:2]
    coarse, out_ref = refs[2 : 2 + slabs], refs[2 + slabs]
    f1, r1, w1, v1a, v1b, pooled, tmp = refs[3 + slabs :]
    pool, spread = pool_ref[...], spread_ref[...]
    slab = place[1]
    rim = HALO // 2
    nx1, ny1, nx2, ny2 = nx // 2, ny // 2, nx // 4, ny // 4
    mid = Level(1, ny1, nz // 2, rim, scalars_of(scalar_ref), f1, r1, w1)
    deep = Level(2, ny2, nz // 4, 0, scalars_of(scalar_ref), None, None, None)
    for v in (v1a, v1b):
        zero_rows(v, ny1)
        blank = jnp.zeros((rim,) + v.shape[1:], jnp.float32)
        v[pl.ds(0, rim)] = blank
        v[pl.ds(rim + nx1, rim)] = blank

    lower = lax.broadcasted_iota(jnp.int32, (1, LANES), 1) < LANES // 2
    own = SLAB // 2
    for k in range(slabs):
        first = jnp.bitwise_xor(slab, step_of(k, slabs)) * own
        both = coarse[k][...]
        f1[pl.ds(first, own)] = jnp.where(lower, both, 0.0)
        r1[pl.ds(first, own)] = jnp.where(lower, pltpu.roll(both, LANES // 2, 2), 0.0)

    def put_start(x, weight):
        w1[x] = weight
        v1a[x + rim, pl.ds(8, ny1), :] = weight * f1[x]

    sweep(range(nx1), lambda x: DAMPING / (r1[x] + mid.centre), put_start, 2 * GROUP)
    mid.smooth(v1a, v1b, range(nx1))

    def coarsened(x):
        return mid.defect(v1b, 2 * x) + mid.defect(v1b, 2 * x + 1), r1[2 * x] + r1[2 * x + 1]

    rows2 = nx2 * ny2

    def put_pooled(x, pair):
        for n in range(2):
            value = mid.pool_rows(pair[n], tmp.at[2 * x + n])
            pooled[pl.ds(n * rows2 + x * ny2, ny2), :] = value

    sweep(range(nx2), coarsened, put_pooled)
    deeper = split_dot(pooled[pl.ds(0, 2 * rows2), :], pool)
    planes = [deeper[n * ny2 : (n + 1) * ny2] for n in range(2 * nx2)]
    values = deep.solve_in_registers(planes[:nx2], planes[nx2:])

    pooled[pl.ds(0, rows2), :] = split_dot(values, spread)

    def refined1(x):
        return mid.spread_rows(pooled[pl.ds(x * ny2, ny2), :], tmp.at[x])

    def put_refined1(x, value):
        for n in range(2):
            v1b[2 * x + n + rim, pl.ds(8, ny1), :] += value

    sweep(range(nx2), refined1, put_refined1)
    mid.smooth(v1b, v1a, range(nx1))
    mid.smooth(v1a, v1b, range(nx1))

    window = own + 2 * rim
    values = v1b[pl.ds(slab * own, window), pl.ds(8, ny1), :].reshape(window * ny1, LANES)
    out_ref[...] = split_dot(values, spread)


def post_kernel(by, chips_y, place, scalar_ref, *refs):
    f, r, w, v1, correction, first_ref, second_ref, kept_ref, sent_ref, va, vb, tmp = refs
    count, ny = f.shape[:2]
    fine = Level(0, ny, LANES, 0, scalars_of(scalar_ref), f, r, w)
    for v in (va, vb):
        zero_rows(v, ny)
    x, half = place[0] // 2 // chips_y, ny // 2
    window = correction.shape[0] // half
    for ref, above in ((first_ref, 1 - x), (second_ref, x)):
        va[pl.ds(1 + above * (SLAB + HALO), NEAR), pl.ds(8, ny), :] = ref[...]

    def refined(x):
        return fine.spread_rows(correction[pl.ds(x * half, half), :], tmp.at[x])

    def put_refined(x, value):
        for at in (2 * x, 2 * x + 1):
            if 0 < at < count - 1:
                known = HALO - NEAR < at < HALO + SLAB + NEAR - 1
                here = v1 if known else va
                va[at, pl.ds(8, ny), :] = here[at, pl.ds(8, ny), :] + value

    sweep(range(window), refined, put_refined)
    fine.smooth(va, vb, range(2, count - 2))
    fine.smooth(vb, va, range(3, count - 3))

    total = jnp.zeros((8, LANES), jnp.float32)
    for x in range(SLAB):
        rest = fine.defect(va, HALO + x)
        total = total + jnp.sum((rest * rest).reshape(ny // 8, 8, LANES), axis=0)
        tmp[x] = rest
    squares = jnp.full((8, LANES), jnp.sum(total), jnp.float32)

    core, area = place[0] & 1, half * SLAB
    for ref, first in ((kept_ref, core * by), (sent_ref, (1 - core) * by)):
        for y in range(half // by):
            row = pl.multiple_of(2 * y * by + first, 8)
            for x in range(SLAB):
                to = x * half + y * by
                ref[pl.ds(to, by), :] = va[HALO + x, pl.ds(8 + row, by), :]
                ref[pl.ds(area + to, by), :] = tmp[x, pl.ds(row, by), :]
        ref[pl.ds(2 * area, 8), :] = squares


def part_rows(bx, by):
    outer = bx * by
    edges = outer + 2 * by
    squares = edges + 2 * (bx - 2)
    return outer, edges, squares, (squares + 8) // 8 * 8


def merge_back_kernel(bx, by, chips_y, place, kept_ref, got_ref, *out_refs):
    chip, core = place[0] // 2, place[0] & 1
    half = chips_y * by
    outer, edges, squares, size = part_rows(bx, by)
    for m, out_ref in enumerate(out_refs):
        target = jnp.bitwise_xor(chip, m)
        first = (target // chips_y) * bx * half + lax.rem(target, chips_y) * by
        for ref, column in ((kept_ref, core), (got_ref, 1 - core)):
            base = pl.multiple_of(column * size, 8)
            for p in range(bx):
                at = pl.multiple_of(first + p * half, 8)
                out_ref[pl.ds(base + p * by, by), :] = ref[pl.ds(at, by), :]
                at = pl.multiple_of(at + SLAB * half, 8)
                if p in (0, bx - 1):
                    out_ref[pl.ds(base + outer + (p > 0) * by, by), :] = ref[pl.ds(at, by), :]
                else:
                    rows = ref[pl.ds(at, by), :]
                    to = base + edges + 2 * (p - 1)
                    out_ref[pl.ds(to, 1), :] = rows[:1]
                    out_ref[pl.ds(to + 1, 1), :] = rows[by - 1 :]
            out_ref[pl.ds(base + squares, 1), :] = ref[pl.ds(2 * SLAB * half, 1), :]


def collect_kernel(place, scalar_ref, source_ref, reaction_ref, *refs):
    parts, (iterate_ref, residual_ref) = refs[:-2], refs[-2:]
    _, bx, by, nz = iterate_ref.shape
    outer, edges, _, size = part_rows(bx, by)
    _, speed = scalars_of(scalar_ref)
    fine = Level(0, by, nz, 0, (0.0, speed), None, None, None)
    reaction = [reaction_ref[p] + fine.centre for p in range(1, bx - 1)]
    for m, part in enumerate(parts):
        target = jnp.bitwise_xor(place[0] // 2, step_of(m, len(parts)))
        for n in range(2):
            base, column = n * size, 2 * target + n
            shift = scalar_ref[pl.ds(8 + column, 1), :]
            planes = [part[pl.ds(base + p * by, by), :] for p in range(bx)]
            for p in range(bx):
                iterate_ref[column, p] = planes[p]
            for p in (0, bx - 1):
                residual_ref[column, p] = part[pl.ds(base + outer + (p > 0) * by, by), :]
            for p in range(1, bx - 1):
                here = planes[p]
                pulled = source_ref[column, p] + fine.along_z(here)
                pulled += fine.backward[0] * planes[p - 1] + fine.forward[0] * planes[p + 1]
                pulled += fine.backward[1] * pltpu.roll(here, 1, 0) + fine.forward[1] * pltpu.roll(here, by - 1, 0)
                residual_ref[column, p] = pulled - (reaction[p - 1] + shift) * here
                at = base + edges + 2 * (p - 1)
                residual_ref[column, p, pl.ds(0, 1), :] = part[pl.ds(at, 1), :]
                residual_ref[column, p, pl.ds(by - 1, 1), :] = part[pl.ds(at + 1, 1), :]


def squares_kernel(bx, by, place, *refs):
    parts, out_ref = refs[:-1], refs[-1]
    _, _, squares, size = part_rows(bx, by)
    lane = lax.broadcasted_iota(jnp.int32, (1, LANES), 1)
    row = jnp.zeros((1, LANES), jnp.float32)
    for m, part in enumerate(parts):
        target = jnp.bitwise_xor(place[0] // 2, step_of(m, len(parts)))
        for n in range(2):
            row = jnp.where(lane == 2 * target + n, part[pl.ds(n * size + squares, 1), :], row)
    out_ref[...] = row


SMEM = pl.BlockSpec(memory_space=pltpu.SMEM)
VMEM = pl.BlockSpec(memory_space=pltpu.VMEM)


def local_kernel(kernel, name, scalars, arrays, outs, scratch=(), in_place=()):
    gy_size = lax.axis_size("gy")
    step = SLAB // HALO

    def placed(*refs):
        along, across = lax.axis_index("gx"), lax.axis_index("gy")
        kernel((lax.rem(along, step) * gy_size + across, along // step), *refs)

    return pl.pallas_call(
        placed,
        out_shape=[jax.ShapeDtypeStruct(shape, jnp.float32) for shape in outs],
        in_specs=[SMEM] * len(scalars) + [VMEM] * len(arrays),
        out_specs=[VMEM] * len(outs),
        scratch_shapes=[pltpu.VMEM(shape, jnp.float32) for shape in scratch],
        input_output_aliases={len(scalars) + n: k for k, n in enumerate(in_place)},
        compiler_params=pltpu.CompilerParams(vmem_limit_bytes=VMEM_LIMIT),
        name=name,
    )(*scalars, *arrays)


def swap_in_plane(pieces, unit):
    devices = lax.axis_size("gx") * lax.axis_size("gy")
    moved = [pieces[0]]
    for k in range(1, len(pieces)):
        pairs = [(i, i ^ (k * unit)) for i in range(devices)]
        moved.append(lax.ppermute(pieces[k], ("gx", "gy"), pairs))
    return moved


def swap_slabs(piece, step, slabs):
    size = lax.axis_size("gx")
    moved = [piece]
    for k in range(1, slabs):
        pairs = [(i, i ^ (step_of(k, slabs) * step)) for i in range(size)]
        moved.append(lax.ppermute(piece, "gx", pairs))
    return moved


def column_body(source, reaction, shifts, shift_index, velocity):
    columns, bx, by, nz = source.shape
    gx_size, gy_size = lax.axis_size("gx"), lax.axis_size("gy")
    nx, ny = bx * gx_size, by * gy_size
    step = columns // gy_size
    slabs = gx_size // step
    count = SLAB + 2 * HALO
    area = bx * by

    chips, chips_y = columns // 2, gy_size // 2
    cores = [(i, i ^ 1) for i in range(gy_size)]
    theirs = [lax.ppermute(source, "gy", cores), lax.ppermute(reaction, "gy", cores)]
    mine = jnp.concatenate([source, reaction[None]])
    (scalar_rows,) = local_kernel(
        scalars_kernel, "scalars", (shifts, shift_index, velocity), (), [(8 + columns, LANES)]
    )
    blocks = local_kernel(
        merge_kernel,
        "merge",
        (),
        (mine, *theirs),
        [(2, bx, 2 * by, nz)] * chips,
    )
    blocks = swap_in_plane(blocks, 2)

    edge = (2, NEAR, ny, nz)
    (own_half,) = local_kernel(
        functools.partial(half_kernel, chips_y),
        "half",
        (),
        blocks[:chips_y],
        [(2, HALO, ny, nz)],
    )
    slab, near = local_kernel(
        functools.partial(arrange_kernel, chips_y),
        "arrange",
        (),
        blocks,
        [(2, SLAB, ny, nz), edge],
    )

    def send_beside(piece, up):
        pairs = [(i, i + step if i % step == up else i - step) for i in range(gx_size)]
        return lax.ppermute(piece, "gx", [(i, j) for i, j in pairs if 0 <= j < gx_size])

    beside = [send_beside(own_half, 1), send_beside(near, 0)]
    grid, rimmed = (count, ny, nz), (count, ny + 16, nz)
    fields = [grid, grid, grid, rimmed, rimmed]
    fields_own = local_kernel(begin_kernel, "begin", (), (scalar_rows, slab), fields)
    f, r, w, _, v1, coarse, beyond = local_kernel(
        functools.partial(pre_kernel, slabs, chips_y),
        "pre",
        (),
        (scalar_rows, *fields_own, *beside, pool_matrix(0), pool_matrix(LANES // 2)),
        fields + [(SLAB // 2, ny // 2, nz), (NEAR, ny, nz)],
        [(SLAB, ny, nz), (2, SLAB // 2 * ny // 2, nz)],
        in_place=range(1, 1 + len(fields)),
    )
    (own_beyond,) = local_kernel(
        functools.partial(beyond_kernel, slabs, chips_y),
        "beyond",
        (),
        (scalar_rows, beside[0]),
        [(NEAR, ny, nz)],
        [(HALO, ny, nz)] * 3 + [(HALO, ny + 16, nz)],
    )
    gathered = swap_slabs(coarse, step, slabs)

    coarse_grid = (nx // 2, ny // 2, nz)
    coarse_rimmed = (nx // 2 + HALO, ny // 2 + 16, nz)
    window = (SLAB // 2 + HALO) * ny // 2
    (correction,) = local_kernel(
        functools.partial(coarse_kernel, (slabs, nx, ny, nz)),
        "coarse",
        (),
        (scalar_rows, pool_matrix(0), spread_matrix(), *gathered),
        [(window, nz)],
        [coarse_grid] * 3 + [coarse_rimmed] * 2 + [(nx // 4 * ny // 2, nz), (nx // 2, ny // 2, nz)],
    )
    result = (SLAB * ny + 8, nz)
    kept, sent = local_kernel(
        functools.partial(post_kernel, by, chips_y),
        "post",
        (),
        (scalar_rows, f, r, w, v1, correction, own_beyond, send_beside(beyond, 0)),
        [result, result],
        [rimmed] * 2 + [(SLAB, ny, nz)],
    )

    parts = local_kernel(
        functools.partial(merge_back_kernel, bx, by, chips_y),
        "merge_back",
        (),
        (kept, lax.ppermute(sent, "gy", cores)),
        [(2 * part_rows(bx, by)[3], nz)] * chips,
    )
    parts = swap_in_plane(parts, 2)
    parts = [parts[step_of(k, chips)] for k in range(chips)]
    (squares,) = local_kernel(
        functools.partial(squares_kernel, bx, by), "squares", (), parts, [(1, nz)]
    )
    iterate, residual = local_kernel(
        collect_kernel,
        "collect",
        (),
        (scalar_rows, source, reaction, *parts),
        [source.shape] * 2,
    )
    sums = swap_slabs(squares, step, slabs)
    sums = [*sums[1:], sums[0]]
    while len(sums) > 1:
        sums = [first + second for first, second in zip(sums[::2], sums[1::2])]
    (total,) = sums
    residual_rms = jnp.sqrt(total[0, :columns] / (nx * ny * nz) + EPSILON)
    return iterate, residual, residual_rms


def power_of_two(n):
    return n > 0 and n & (n - 1) == 0


def column_plan_fits(columns, bx, by, nz, gx_size, gy_size):
    if columns % gy_size or gx_size % (columns // gy_size):
        return False
    step = columns // gy_size
    slabs, ny = gx_size // step, by * gy_size
    whole = power_of_two(columns) and power_of_two(step) and power_of_two(slabs)
    small = slabs * ny * nz <= 2**15
    paired = step == 2 and bx == HALO and gy_size % 2 == 0
    return whole and small and paired and bx * step == SLAB and nz == LANES and by % 16 == 0


def solution(mesh):
    gx_size, gy_size = mesh.shape["gx"], mesh.shape["gy"]

    def body(source, reaction, shifts, shift_index, velocity):
        fits = column_plan_fits(*source.shape, gx_size, gy_size)
        plan = column_body if fits else halo_body
        return plan(source, reaction, shifts, shift_index, velocity)

    return jax.shard_map(
        body,
        mesh=mesh,
        in_specs=(P(None, "gx", "gy", None), P("gx", "gy", None), P(), P(), P()),
        out_specs=(P(None, "gx", "gy", None), P(None, "gx", "gy", None), P()),
        check_vma=False,
    )
```

```python
import functools

import jax
import jax.numpy as jnp
from jax import lax
from jax.experimental import pallas as pl
from jax.experimental.pallas import tpu as pltpu
from jax.sharding import PartitionSpec as P

LEVELS = 3
COARSE_SWEEPS = 6

DAMPING = 0.8
EPSILON = 1e-06
VMEM_LIMIT = 32 * 1024 * 1024
LANES = 128
GROUP = 4
SLAB = 8
HALO = 4
NEAR = 2


def with_halo(x, sides, width):
    for axis, dim in sides:
        peers, length = (lax.axis_size(axis), x.shape[dim])
        up = [(i, (i + 1) % peers) for i in range(peers - 1)]
        down = [(j, i) for i, j in up]
        last = lax.slice_in_dim(x, length - width, length, axis=dim)
        leading = lax.slice_in_dim(x, 0, width, axis=dim)
        before = lax.ppermute(last, axis, up)
        after = lax.ppermute(leading, axis, down)
        x = jnp.concatenate([before, x, after], axis=dim)
    return x


def select_shifts(shifts, shift_index):
    columns = jnp.arange(shifts.shape[0], dtype=jnp.int32)
    picked = jnp.where(shift_index[:, None] == columns[None, :], shifts[None, :], 0.0)
    return jnp.sum(picked, axis=1)


def coefficients(velocity, spacing):
    scale_a = 1.0 / (spacing * spacing)
    backward = scale_a + jnp.maximum(velocity, 0.0) / spacing
    forward = scale_a - jnp.minimum(velocity, 0.0) / spacing
    centre = 6.0 * scale_a + jnp.sum(jnp.abs(velocity)) / spacing
    return (backward, forward, centre)


def apply_stencil(padded, backward, forward, diagonal):
    middle = padded[:, 1:-1, 1:-1, :]
    along_z = jnp.pad(middle, ((0, 0), (0, 0), (0, 0), (1, 1)))
    others = backward[0] * padded[:, :-2, 1:-1, :] + forward[0] * padded[:, 2:, 1:-1, :]
    others = others + backward[1] * padded[:, 1:-1, :-2, :] + forward[1] * padded[:, 1:-1, 2:, :]
    others = others + backward[2] * along_z[:, :, :, :-2] + forward[2] * along_z[:, :, :, 2:]
    return diagonal * middle - others


def face_halo(iterate):
    return with_halo(iterate, (("gx", 1), ("gy", 2)), 1)


def coarsen(values):
    count, size_x, size_y, size_z = values.shape
    blocks = values.reshape(count, size_x // 2, 2, size_y // 2, 2, size_z // 2, 2)
    return jnp.sum(blocks, axis=(2, 4, 6)) * 0.125


def refine(values):
    return jnp.repeat(jnp.repeat(jnp.repeat(values, 2, 1), 2, 2), 2, 3)


def coarsest_solve(rhs_field, backward, forward, diagonal):
    iterate = DAMPING * rhs_field / diagonal
    for repeat in range(COARSE_SWEEPS - 1):
        applied = apply_stencil(face_halo(iterate), backward, forward, diagonal)
        iterate = iterate + DAMPING * (rhs_field - applied) / diagonal
    return iterate


def multigrid_cycle(level_index, rhs_field, reaction_l, shift_value, velocity):
    backward, forward, centre = coefficients(velocity, 2.0**level_index)
    diagonal = centre + reaction_l + shift_value[:, None, None, None]
    if level_index == LEVELS - 1:
        return coarsest_solve(rhs_field, backward, forward, diagonal)

    def operate(iterate):
        return apply_stencil(face_halo(iterate), backward, forward, diagonal)

    def smooth_step(iterate):
        return iterate + DAMPING * (rhs_field - operate(iterate)) / diagonal

    iterate = DAMPING * rhs_field / diagonal
    iterate = smooth_step(iterate)
    defect = rhs_field - operate(iterate)
    correction = multigrid_cycle(
        level_index + 1, coarsen(defect), coarsen(reaction_l), shift_value, velocity
    )
    iterate = iterate + refine(correction)
    iterate = smooth_step(iterate)
    iterate = smooth_step(iterate)
    return iterate


def halo_body(source, reaction, shifts, shift_index, velocity):
    columns, cells_x, cells_y, cells_z = source.shape
    shift_value = select_shifts(shifts, shift_index)
    reaction_top = reaction[None]
    backward, forward, centre = coefficients(velocity, 1.0)
    diagonal = centre + reaction_top + shift_value[:, None, None, None]

    iterate = multigrid_cycle(0, source, reaction_top, shift_value, velocity)
    residual = source - apply_stencil(face_halo(iterate), backward, forward, diagonal)
    local_squares = jnp.sum(residual * residual, axis=(1, 2, 3))
    squares = lax.psum(local_squares, ("gx", "gy"))
    total_cells = cells_x * cells_y * cells_z * lax.axis_size("gx") * lax.axis_size("gy")
    residual_rms = jnp.sqrt(squares / total_cells + EPSILON)
    return (iterate, residual, residual_rms)


def split_dot(values, matrix):
    high = values.astype(jnp.bfloat16)
    low = (values - high.astype(jnp.float32)).astype(jnp.bfloat16)
    return jnp.dot(high, matrix, preferred_element_type=jnp.float32) + jnp.dot(
        low, matrix, preferred_element_type=jnp.float32
    )


def sweep(planes, get, put, size=GROUP):
    planes = list(planes)
    for first in range(0, len(planes), size):
        group = planes[first : first + size]
        values = [get(x) for x in group]
        for x, value in zip(group, values):
            put(x, value)


class Grid:
    def __init__(self, ny):
        self.ny = ny

    def pool_rows(self, value, rows):
        half, ny = self.ny // 2, self.ny
        rows[pl.ds(0, ny), :] = value
        return rows[pl.ds(0, half, stride=2), :] + rows[pl.ds(1, half, stride=2), :]

    def spread_rows(self, part, rows):
        half, ny = self.ny // 2, self.ny
        rows[pl.ds(0, half, stride=2), :] = part
        rows[pl.ds(1, half, stride=2), :] = part
        return rows[pl.ds(0, ny), :]


class Level(Grid):
    def __init__(self, index, ny, nz, rim, scalars, f, r, w):
        super().__init__(ny)
        self.nz, self.rim = nz, rim
        self.f, self.r, self.w = f, r, w
        spacing = 2.0**index
        scale_a = 1.0 / (spacing * spacing)
        inverse = 1.0 / spacing
        shift, speed = scalars
        self.backward = [scale_a + jnp.maximum(v, 0.0) * inverse for v in speed]
        self.forward = [scale_a - jnp.minimum(v, 0.0) * inverse for v in speed]
        total = jnp.abs(speed[0]) + jnp.abs(speed[1]) + jnp.abs(speed[2])
        self.centre = 6.0 * scale_a + total * inverse + shift
        lane = lax.broadcasted_iota(jnp.int32, (1, LANES), 1)
        inside = lane < nz
        self.low_z = jnp.where((lane > 0) & inside, self.backward[2], 0.0)
        self.high_z = jnp.where(lane < nz - 1, self.forward[2], 0.0)

    def plane(self, v, x):
        return v[x + self.rim, pl.ds(8, self.ny), :]

    def put(self, v):
        def write(x, value):
            v[x + self.rim, pl.ds(8, self.ny), :] = value

        return write

    def along_z(self, middle):
        return self.low_z * pltpu.roll(middle, 1, 1) + self.high_z * pltpu.roll(middle, LANES - 1, 1)

    def neighbours(self, v, x, middle):
        at, ny = x + self.rim, self.ny
        along_x = self.backward[0] * v[at - 1, pl.ds(8, ny), :] + self.forward[0] * v[at + 1, pl.ds(8, ny), :]
        along_y = self.backward[1] * v[at, pl.ds(7, ny), :] + self.forward[1] * v[at, pl.ds(9, ny), :]
        return along_x + along_y + self.along_z(middle)

    def smoothed(self, v, x):
        middle = self.plane(v, x)
        pulled = self.f[x] + self.neighbours(v, x, middle)
        return (1.0 - DAMPING) * middle + self.w[x] * pulled

    def smooth(self, src, dst, planes):
        sweep(planes, lambda x: self.smoothed(src, x), self.put(dst), GROUP * 64 // self.ny)

    def defect(self, v, x):
        middle = self.plane(v, x)
        pulled = self.f[x] + self.neighbours(v, x, middle)
        return pulled - (self.r[x] + self.centre) * middle

    def solve_in_registers(self, rhs, reaction):
        row = lax.broadcasted_iota(jnp.int32, (self.ny, 1), 0)
        low_y = jnp.where(row > 0, self.backward[1], 0.0)
        high_y = jnp.where(row < self.ny - 1, self.forward[1], 0.0)
        weight = [DAMPING / (r + self.centre) for r in reaction]
        v = [w * f for w, f in zip(weight, rhs)]
        for _ in range(COARSE_SWEEPS - 1):
            new = []
            for x, here in enumerate(v):
                along_y = low_y * pltpu.roll(here, 1, 0) + high_y * pltpu.roll(here, self.ny - 1, 0)
                pulled = rhs[x] + self.along_z(here) + along_y
                if x > 0:
                    pulled += self.backward[0] * v[x - 1]
                if x < len(v) - 1:
                    pulled += self.forward[0] * v[x + 1]
                new.append((1.0 - DAMPING) * here + weight[x] * pulled)
            v = new
        return jnp.concatenate(v, axis=0)


def scalars_of(scalar_ref):
    return scalar_ref[pl.ds(0, 1), :], [scalar_ref[pl.ds(1 + d, 1), :] for d in range(3)]


def zero_rows(v, ny):
    edge = jnp.zeros((v.shape[0], 8, LANES), jnp.float32)
    v[:, pl.ds(0, 8), :] = edge
    v[:, pl.ds(8 + ny, 8), :] = edge


def pool_matrix(offset):
    row = lax.broadcasted_iota(jnp.int32, (LANES, LANES), 0)
    col = lax.broadcasted_iota(jnp.int32, (LANES, LANES), 1)
    return jnp.where(row // 2 + offset == col, 0.125, 0.0).astype(jnp.bfloat16)


def spread_matrix():
    row = lax.broadcasted_iota(jnp.int32, (LANES, LANES), 0)
    col = lax.broadcasted_iota(jnp.int32, (LANES, LANES), 1)
    return jnp.where(col // 2 == row, 1.0, 0.0).astype(jnp.bfloat16)


def step_of(k, count):
    return -k % count


def scalars_kernel(place, shifts_ref, index_ref, velocity_ref, scalar_ref):
    rows = {0: shifts_ref[index_ref[place[0]]]}
    rows.update({1 + d: velocity_ref[d] for d in range(3)})
    rows.update({8 + c: shifts_ref[index_ref[c]] for c in range(index_ref.shape[0])})
    for n, scalar in rows.items():
        scalar_ref[pl.ds(n, 1), :] = jnp.full((1, LANES), scalar, jnp.float32)


def merge_kernel(place, mine_ref, theirs_ref, other_reaction_ref, *out_refs):
    chip, core = place[0] // 2, place[0] & 1
    columns, by = theirs_ref.shape[0], theirs_ref.shape[2]
    mine = pl.ds(pl.multiple_of(core * by, 8), by)
    theirs = pl.ds(pl.multiple_of((1 - core) * by, 8), by)
    for m, out_ref in enumerate(out_refs):
        column = 2 * jnp.bitwise_xor(chip, m) + core
        out_ref[0, :, mine, :] = mine_ref[column]
        out_ref[0, :, theirs, :] = theirs_ref[column]
        out_ref[1, :, mine, :] = mine_ref[columns]
        out_ref[1, :, theirs, :] = other_reaction_ref[...]


def half_kernel(chips_y, place, *refs):
    blocks, half_ref = refs[:-1], refs[-1]
    for m, block in enumerate(blocks):
        size = block.shape[2]
        chip = jnp.bitwise_xor(place[0] // 2, m)
        rows = pl.ds(pl.multiple_of(lax.rem(chip, chips_y) * size, 8), size)
        half_ref[:, :, rows, :] = block[...]


def arrange_kernel(chips_y, place, *refs):
    blocks, (slab_ref, near_ref) = refs[:-2], refs[-2:]
    chip = place[0] // 2
    for m, block in enumerate(blocks):
        owner = jnp.bitwise_xor(chip, m ^ (m >> 1))
        _, bx, size, _ = block.shape
        planes = pl.ds((owner // chips_y) * bx, bx)
        rows = pl.ds(pl.multiple_of(lax.rem(owner, chips_y) * size, 8), size)
        slab_ref[:, planes, rows, :] = block[...]
    other = 1 - chip // chips_y
    near_ref[...] = slab_ref[:, pl.ds(other * (SLAB - NEAR), NEAR)]


def beyond_kernel(slabs, chips_y, place, scalar_ref, half_ref, out_ref, f, r, w, v0):
    ny, slab = f.shape[1], place[1]
    x = place[0] // 2 // chips_y
    fine = Level(0, ny, LANES, 0, scalars_of(scalar_ref), f, r, w)
    zero_rows(v0, ny)
    f[...], r[...] = half_ref[0], half_ref[1]
    beside = jnp.where(x == 0, slab < slabs - 1, slab > 0)
    inside = jnp.where(beside, DAMPING, 0.0)

    def put(at, weight):
        w[at] = weight
        v0[at, pl.ds(8, ny), :] = weight * f[at]

    sweep(range(HALO), lambda at: inside / (r[at] + fine.centre), put)
    for n in range(NEAR):
        out_ref[n] = fine.smoothed(v0, 1 + n)


def begin_kernel(_, scalar_ref, slab_ref, f, r, w, v0, v1):
    ny = f.shape[1]
    fine = Level(0, ny, LANES, 0, scalars_of(scalar_ref), f, r, w)
    zero_rows(v0, ny)
    zero_rows(v1, ny)
    own = range(HALO, HALO + SLAB)
    f[pl.ds(HALO, SLAB)], r[pl.ds(HALO, SLAB)] = slab_ref[0], slab_ref[1]

    def put(at, weight):
        w[at] = weight
        v0[at, pl.ds(8, ny), :] = weight * f[at]

    sweep(own, lambda at: DAMPING / (r[at] + fine.centre), put)
    fine.smooth(v0, v1, own[1:-1])


def pre_kernel(slabs, chips_y, place, scalar_ref, *refs):
    half_ref, near_ref, pool_ref, pool_up_ref = refs[5:9]
    f, r, w, v0, v1, coarse_ref, beyond_ref, tmp, pooled = refs[9:]
    ny = f.shape[1]
    slab = place[1]
    fine = Level(0, ny, LANES, 0, scalars_of(scalar_ref), f, r, w)
    after = HALO + SLAB

    x = place[0] // 2 // chips_y
    for above, ref, first in ((1 - x, half_ref, x * NEAR), (x, near_ref, 0)):
        planes = pl.ds((HALO - NEAR) + above * (SLAB + NEAR), NEAR)
        f[planes], r[planes] = ref[0, pl.ds(first, NEAR)], ref[1, pl.ds(first, NEAR)]

    below = jnp.where(slab > 0, DAMPING, 0.0)
    above = jnp.where(slab < slabs - 1, DAMPING, 0.0)

    def put(at, weight):
        w[at] = weight
        v0[at, pl.ds(8, ny), :] = weight * f[at]

    beside = [*range(HALO - NEAR, HALO), *range(after, after + NEAR)]
    sweep(beside, lambda at: (below if at < HALO else above) / (r[at] + fine.centre), put)
    fine.smooth(v0, v1, (HALO - 1, HALO, after - 1, after))
    half = ny // 2

    def coarsened(x):
        at = HALO + 2 * x
        return fine.defect(v1, at) + fine.defect(v1, at + 1), r[at] + r[at + 1]

    def put_pooled(x, pair):
        for n in range(2):
            pooled[n, pl.ds(x * half, half), :] = fine.pool_rows(pair[n], tmp.at[2 * x + n])

    sweep(range(SLAB // 2), coarsened, put_pooled)
    packed = split_dot(pooled[0], pool_ref[...]) + split_dot(pooled[1], pool_up_ref[...])
    coarse_ref[...] = packed.reshape(coarse_ref.shape)
    first = HALO + 1 + (1 - x) * (SLAB - HALO)
    beyond_ref[...] = v1[pl.ds(first, NEAR), pl.ds(8, ny), :]


def coarse_kernel(grid, place, scalar_ref, *refs):
    slabs, nx, ny, nz = grid
    pool_ref, spread_ref = refs[:2]
    coarse, out_ref = refs[2 : 2 + slabs], refs[2 + slabs]
    f1, r1, w1, v1a, v1b, pooled, tmp = refs[3 + slabs :]
    pool, spread = pool_ref[...], spread_ref[...]
    slab = place[1]
    rim = HALO // 2
    nx1, ny1, nx2, ny2 = nx // 2, ny // 2, nx // 4, ny // 4
    mid = Level(1, ny1, nz // 2, rim, scalars_of(scalar_ref), f1, r1, w1)
    deep = Level(2, ny2, nz // 4, 0, scalars_of(scalar_ref), None, None, None)
    for v in (v1a, v1b):
        zero_rows(v, ny1)
        blank = jnp.zeros((rim,) + v.shape[1:], jnp.float32)
        v[pl.ds(0, rim)] = blank
        v[pl.ds(rim + nx1, rim)] = blank

    lower = lax.broadcasted_iota(jnp.int32, (1, LANES), 1) < LANES // 2
    own = SLAB // 2
    for k in range(slabs):
        first = jnp.bitwise_xor(slab, step_of(k, slabs)) * own
        both = coarse[k][...]
        f1[pl.ds(first, own)] = jnp.where(lower, both, 0.0)
        r1[pl.ds(first, own)] = jnp.where(lower, pltpu.roll(both, LANES // 2, 2), 0.0)

    def put_start(x, weight):
        w1[x] = weight
        v1a[x + rim, pl.ds(8, ny1), :] = weight * f1[x]

    sweep(range(nx1), lambda x: DAMPING / (r1[x] + mid.centre), put_start, 2 * GROUP)
    mid.smooth(v1a, v1b, range(nx1))

    def coarsened(x):
        return mid.defect(v1b, 2 * x) + mid.defect(v1b, 2 * x + 1), r1[2 * x] + r1[2 * x + 1]

    rows2 = nx2 * ny2

    def put_pooled(x, pair):
        for n in range(2):
            value = mid.pool_rows(pair[n], tmp.at[2 * x + n])
            pooled[pl.ds(n * rows2 + x * ny2, ny2), :] = value

    sweep(range(nx2), coarsened, put_pooled)
    deeper = split_dot(pooled[pl.ds(0, 2 * rows2), :], pool)
    planes = [deeper[n * ny2 : (n + 1) * ny2] for n in range(2 * nx2)]
    values = deep.solve_in_registers(planes[:nx2], planes[nx2:])

    pooled[pl.ds(0, rows2), :] = split_dot(values, spread)

    def refined1(x):
        return mid.spread_rows(pooled[pl.ds(x * ny2, ny2), :], tmp.at[x])

    def put_refined1(x, value):
        for n in range(2):
            v1b[2 * x + n + rim, pl.ds(8, ny1), :] += value

    sweep(range(nx2), refined1, put_refined1)
    mid.smooth(v1b, v1a, range(nx1))
    mid.smooth(v1a, v1b, range(nx1))

    window = own + 2 * rim
    values = v1b[pl.ds(slab * own, window), pl.ds(8, ny1), :].reshape(window * ny1, LANES)
    out_ref[...] = split_dot(values, spread)


def post_kernel(by, chips_y, place, scalar_ref, *refs):
    f, r, w, v1, correction, first_ref, second_ref, kept_ref, sent_ref, va, vb, tmp = refs
    count, ny = f.shape[:2]
    fine = Level(0, ny, LANES, 0, scalars_of(scalar_ref), f, r, w)
    for v in (va, vb):
        zero_rows(v, ny)
    x, half = place[0] // 2 // chips_y, ny // 2
    window = correction.shape[0] // half
    for ref, above in ((first_ref, 1 - x), (second_ref, x)):
        va[pl.ds(1 + above * (SLAB + HALO), NEAR), pl.ds(8, ny), :] = ref[...]

    def refined(x):
        return fine.spread_rows(correction[pl.ds(x * half, half), :], tmp.at[x])

    def put_refined(x, value):
        for at in (2 * x, 2 * x + 1):
            if 0 < at < count - 1:
                known = HALO - NEAR < at < HALO + SLAB + NEAR - 1
                here = v1 if known else va
                va[at, pl.ds(8, ny), :] = here[at, pl.ds(8, ny), :] + value

    sweep(range(window), refined, put_refined)
    fine.smooth(va, vb, range(2, count - 2))
    fine.smooth(vb, va, range(3, count - 3))

    total = jnp.zeros((8, LANES), jnp.float32)
    for x in range(SLAB):
        rest = fine.defect(va, HALO + x)
        total = total + jnp.sum((rest * rest).reshape(ny // 8, 8, LANES), axis=0)
        tmp[x] = rest
    squares = jnp.full((8, LANES), jnp.sum(total), jnp.float32)

    core, area = place[0] & 1, half * SLAB
    for ref, first in ((kept_ref, core * by), (sent_ref, (1 - core) * by)):
        for y in range(half // by):
            row = pl.multiple_of(2 * y * by + first, 8)
            for x in range(SLAB):
                to = x * half + y * by
                ref[pl.ds(to, by), :] = va[HALO + x, pl.ds(8 + row, by), :]
                ref[pl.ds(area + to, by), :] = tmp[x, pl.ds(row, by), :]
        ref[pl.ds(2 * area, 8), :] = squares


def part_rows(bx, by):
    outer = bx * by
    edges = outer + 2 * by
    squares = edges + 2 * (bx - 2)
    return outer, edges, squares, (squares + 8) // 8 * 8


def merge_back_kernel(bx, by, chips_y, place, kept_ref, got_ref, *out_refs):
    chip, core = place[0] // 2, place[0] & 1
    half = chips_y * by
    outer, edges, squares, size = part_rows(bx, by)
    for m, out_ref in enumerate(out_refs):
        target = jnp.bitwise_xor(chip, m)
        first = (target // chips_y) * bx * half + lax.rem(target, chips_y) * by
        for ref, column in ((kept_ref, core), (got_ref, 1 - core)):
            base = pl.multiple_of(column * size, 8)
            for p in range(bx):
                at = pl.multiple_of(first + p * half, 8)
                out_ref[pl.ds(base + p * by, by), :] = ref[pl.ds(at, by), :]
                at = pl.multiple_of(at + SLAB * half, 8)
                if p in (0, bx - 1):
                    out_ref[pl.ds(base + outer + (p > 0) * by, by), :] = ref[pl.ds(at, by), :]
                else:
                    rows = ref[pl.ds(at, by), :]
                    to = base + edges + 2 * (p - 1)
                    out_ref[pl.ds(to, 1), :] = rows[:1]
                    out_ref[pl.ds(to + 1, 1), :] = rows[by - 1 :]
            out_ref[pl.ds(base + squares, 1), :] = ref[pl.ds(2 * SLAB * half, 1), :]


def collect_kernel(place, scalar_ref, source_ref, reaction_ref, *refs):
    parts, (iterate_ref, residual_ref) = refs[:-2], refs[-2:]
    _, bx, by, nz = iterate_ref.shape
    outer, edges, _, size = part_rows(bx, by)
    _, speed = scalars_of(scalar_ref)
    fine = Level(0, by, nz, 0, (0.0, speed), None, None, None)
    reaction = [reaction_ref[p] + fine.centre for p in range(1, bx - 1)]
    for m, part in enumerate(parts):
        target = jnp.bitwise_xor(place[0] // 2, step_of(m, len(parts)))
        for n in range(2):
            base, column = n * size, 2 * target + n
            shift = scalar_ref[pl.ds(8 + column, 1), :]
            planes = [part[pl.ds(base + p * by, by), :] for p in range(bx)]
            for p in range(bx):
                iterate_ref[column, p] = planes[p]
            for p in (0, bx - 1):
                residual_ref[column, p] = part[pl.ds(base + outer + (p > 0) * by, by), :]
            for p in range(1, bx - 1):
                here = planes[p]
                pulled = source_ref[column, p] + fine.along_z(here)
                pulled += fine.backward[0] * planes[p - 1] + fine.forward[0] * planes[p + 1]
                pulled += fine.backward[1] * pltpu.roll(here, 1, 0) + fine.forward[1] * pltpu.roll(here, by - 1, 0)
                residual_ref[column, p] = pulled - (reaction[p - 1] + shift) * here
                at = base + edges + 2 * (p - 1)
                residual_ref[column, p, pl.ds(0, 1), :] = part[pl.ds(at, 1), :]
                residual_ref[column, p, pl.ds(by - 1, 1), :] = part[pl.ds(at + 1, 1), :]


def squares_kernel(bx, by, place, *refs):
    parts, out_ref = refs[:-1], refs[-1]
    _, _, squares, size = part_rows(bx, by)
    lane = lax.broadcasted_iota(jnp.int32, (1, LANES), 1)
    row = jnp.zeros((1, LANES), jnp.float32)
    for m, part in enumerate(parts):
        target = jnp.bitwise_xor(place[0] // 2, step_of(m, len(parts)))
        for n in range(2):
            row = jnp.where(lane == 2 * target + n, part[pl.ds(n * size + squares, 1), :], row)
    out_ref[...] = row


SMEM = pl.BlockSpec(memory_space=pltpu.SMEM)
VMEM = pl.BlockSpec(memory_space=pltpu.VMEM)


def local_kernel(kernel, name, scalars, arrays, outs, scratch=(), in_place=()):
    gy_size = lax.axis_size("gy")
    step = SLAB // HALO

    def placed(*refs):
        along, across = lax.axis_index("gx"), lax.axis_index("gy")
        kernel((lax.rem(along, step) * gy_size + across, along // step), *refs)

    return pl.pallas_call(
        placed,
        out_shape=[jax.ShapeDtypeStruct(shape, jnp.float32) for shape in outs],
        in_specs=[SMEM] * len(scalars) + [VMEM] * len(arrays),
        out_specs=[VMEM] * len(outs),
        scratch_shapes=[pltpu.VMEM(shape, jnp.float32) for shape in scratch],
        input_output_aliases={len(scalars) + n: k for k, n in enumerate(in_place)},
        compiler_params=pltpu.CompilerParams(vmem_limit_bytes=VMEM_LIMIT),
        name=name,
    )(*scalars, *arrays)


def swap_in_plane(pieces, unit):
    devices = lax.axis_size("gx") * lax.axis_size("gy")
    moved = [pieces[0]]
    for k in range(1, len(pieces)):
        pairs = [(i, i ^ (k * unit)) for i in range(devices)]
        moved.append(lax.ppermute(pieces[k], ("gx", "gy"), pairs))
    return moved


def swap_slabs(piece, step, slabs):
    size = lax.axis_size("gx")
    moved = [piece]
    for k in range(1, slabs):
        pairs = [(i, i ^ (step_of(k, slabs) * step)) for i in range(size)]
        moved.append(lax.ppermute(piece, "gx", pairs))
    return moved


def column_body(source, reaction, shifts, shift_index, velocity):
    columns, bx, by, nz = source.shape
    gx_size, gy_size = lax.axis_size("gx"), lax.axis_size("gy")
    nx, ny = bx * gx_size, by * gy_size
    step = columns // gy_size
    slabs = gx_size // step
    count = SLAB + 2 * HALO
    area = bx * by

    chips, chips_y = columns // 2, gy_size // 2
    cores = [(i, i ^ 1) for i in range(gy_size)]
    theirs = [lax.ppermute(source, "gy", cores), lax.ppermute(reaction, "gy", cores)]
    mine = jnp.concatenate([source, reaction[None]])
    (scalar_rows,) = local_kernel(
        scalars_kernel, "scalars", (shifts, shift_index, velocity), (), [(8 + columns, LANES)]
    )
    blocks = local_kernel(
        merge_kernel,
        "merge",
        (),
        (mine, *theirs),
        [(2, bx, 2 * by, nz)] * chips,
    )
    blocks = swap_in_plane(blocks, 2)

    edge = (2, NEAR, ny, nz)
    (own_half,) = local_kernel(
        functools.partial(half_kernel, chips_y),
        "half",
        (),
        blocks[:chips_y],
        [(2, HALO, ny, nz)],
    )
    slab, near = local_kernel(
        functools.partial(arrange_kernel, chips_y),
        "arrange",
        (),
        [blocks[m ^ (m >> 1)] for m in range(chips)],
        [(2, SLAB, ny, nz), edge],
    )

    def send_beside(piece, up):
        pairs = [(i, i + step if i % step == up else i - step) for i in range(gx_size)]
        return lax.ppermute(piece, "gx", [(i, j) for i, j in pairs if 0 <= j < gx_size])

    beside = [send_beside(own_half, 1), send_beside(near, 0)]
    grid, rimmed = (count, ny, nz), (count, ny + 16, nz)
    fields = [grid, grid, grid, rimmed, rimmed]
    fields_own = local_kernel(begin_kernel, "begin", (), (scalar_rows, slab), fields)
    f, r, w, _, v1, coarse, beyond = local_kernel(
        functools.partial(pre_kernel, slabs, chips_y),
        "pre",
        (),
        (scalar_rows, *fields_own, *beside, pool_matrix(0), pool_matrix(LANES // 2)),
        fields + [(SLAB // 2, ny // 2, nz), (NEAR, ny, nz)],
        [(SLAB, ny, nz), (2, SLAB // 2 * ny // 2, nz)],
        in_place=range(1, 1 + len(fields)),
    )
    (own_beyond,) = local_kernel(
        functools.partial(beyond_kernel, slabs, chips_y),
        "beyond",
        (),
        (scalar_rows, beside[0]),
        [(NEAR, ny, nz)],
        [(HALO, ny, nz)] * 3 + [(HALO, ny + 16, nz)],
    )
    gathered = swap_slabs(coarse, step, slabs)

    coarse_grid = (nx // 2, ny // 2, nz)
    coarse_rimmed = (nx // 2 + HALO, ny // 2 + 16, nz)
    window = (SLAB // 2 + HALO) * ny // 2
    (correction,) = local_kernel(
        functools.partial(coarse_kernel, (slabs, nx, ny, nz)),
        "coarse",
        (),
        (scalar_rows, pool_matrix(0), spread_matrix(), *gathered),
        [(window, nz)],
        [coarse_grid] * 3 + [coarse_rimmed] * 2 + [(nx // 4 * ny // 2, nz), (nx // 2, ny // 2, nz)],
    )
    result = (SLAB * ny + 8, nz)
    kept, sent = local_kernel(
        functools.partial(post_kernel, by, chips_y),
        "post",
        (),
        (scalar_rows, f, r, w, v1, correction, own_beyond, send_beside(beyond, 0)),
        [result, result],
        [rimmed] * 2 + [(SLAB, ny, nz)],
    )

    parts = local_kernel(
        functools.partial(merge_back_kernel, bx, by, chips_y),
        "merge_back",
        (),
        (kept, lax.ppermute(sent, "gy", cores)),
        [(2 * part_rows(bx, by)[3], nz)] * chips,
    )
    parts = swap_in_plane(parts, 2)
    parts = [parts[step_of(k, chips)] for k in range(chips)]
    (squares,) = local_kernel(
        functools.partial(squares_kernel, bx, by), "squares", (), parts, [(1, nz)]
    )
    iterate, residual = local_kernel(
        collect_kernel,
        "collect",
        (),
        (scalar_rows, source, reaction, *parts),
        [source.shape] * 2,
    )
    sums = swap_slabs(squares, step, slabs)
    sums = [*sums[1:], sums[0]]
    while len(sums) > 1:
        sums = [first + second for first, second in zip(sums[::2], sums[1::2])]
    (total,) = sums
    residual_rms = jnp.sqrt(total[0, :columns] / (nx * ny * nz) + EPSILON)
    return iterate, residual, residual_rms


def power_of_two(n):
    return n > 0 and n & (n - 1) == 0


def column_plan_fits(columns, bx, by, nz, gx_size, gy_size):
    if columns % gy_size or gx_size % (columns // gy_size):
        return False
    step = columns // gy_size
    slabs, ny = gx_size // step, by * gy_size
    whole = power_of_two(columns) and power_of_two(step) and power_of_two(slabs)
    small = slabs * ny * nz <= 2**15
    paired = step == 2 and bx == HALO and gy_size % 2 == 0
    return whole and small and paired and bx * step == SLAB and nz == LANES and by % 16 == 0


def solution(mesh):
    gx_size, gy_size = mesh.shape["gx"], mesh.shape["gy"]

    def body(source, reaction, shifts, shift_index, velocity):
        fits = column_plan_fits(*source.shape, gx_size, gy_size)
        plan = column_body if fits else halo_body
        return plan(source, reaction, shifts, shift_index, velocity)

    return jax.shard_map(
        body,
        mesh=mesh,
        in_specs=(P(None, "gx", "gy", None), P("gx", "gy", None), P(), P(), P()),
        out_specs=(P(None, "gx", "gy", None), P(None, "gx", "gy", None), P()),
        check_vma=False,
    )
```
